32 devices in a mesh: dp: 4 (over x, core), fsdp: 8 (over z, y).
Axes of the slice: x: 2, y: 2, z: 4, core: 2. Of those that a mesh axis runs over, the one named last changes fastest.
Arguments:
- tokens: bfloat16 [128, 128, 1024], P(('dp', 'fsdp')), may hold values from -6 to 6
- seq_counts: int32 [32], P(('dp', 'fsdp')), may hold values from 1 to 4, as said below
- segments: int32 [128, 128], P(('dp', 'fsdp')), may hold values from 0 to 31, as said below
- positions: int32 [128, 128], P(('dp', 'fsdp')), may hold values from 0 to 2428, as said below
- norm_first: bfloat16 [1024], P(('dp', 'fsdp')), may hold values from 0.5 to 1.5
- query_weight: bfloat16 [1024, 1024], P(('dp', 'fsdp')), may hold values from -0.25 to 0.25
- key_weight: bfloat16 [1024, 1024], P(('dp', 'fsdp')), may hold values from -0.1875 to 0.1875
- value_weight: bfloat16 [1024, 1024], P(('dp', 'fsdp')), may hold values from -0.1875 to 0.1875
- output_weight: bfloat16 [1024, 1024], P(('dp', 'fsdp')), may hold values from -0.75 to 0.75
- norm_second: bfloat16 [1024], P(('dp', 'fsdp')), may hold values from 0.5 to 1.5
- gate_weight: bfloat16 [1024, 2816], P(('dp', 'fsdp')), may hold values from -0.1875 to 0.1875
- up_weight: bfloat16 [1024, 2816], P(('dp', 'fsdp')), may hold values from -0.1875 to 0.1875
- down_weight: bfloat16 [2816, 1024], P(('dp', 'fsdp')), may hold values from -0.109375 to 0.109375
- out_cotangent: bfloat16 [128, 128, 1024], P(('dp', 'fsdp')), may hold values from -6 to 6
- value_cotangent: bfloat16 [128, 128, 1024], P(('dp', 'fsdp')), may hold values from -6 to 6
Outputs:
- block_output: bfloat16 [128, 128, 1024], P(('dp', 'fsdp'))
- first_values: bfloat16 [128, 128, 1024], P(('dp', 'fsdp'))
- token_grad: bfloat16 [128, 128, 1024], P(('dp', 'fsdp'))
- norm_first_grad: float32 [1024], P(('dp', 'fsdp'))
- query_grad: float32 [1024, 1024], P(('dp', 'fsdp'))
- key_grad: float32 [1024, 1024], P(('dp', 'fsdp'))
- value_grad: float32 [1024, 1024], P(('dp', 'fsdp'))
- output_grad: float32 [1024, 1024], P(('dp', 'fsdp'))
- norm_second_grad: float32 [1024], P(('dp', 'fsdp'))
- gate_grad: float32 [1024, 2816], P(('dp', 'fsdp'))
- up_grad: float32 [1024, 2816], P(('dp', 'fsdp'))
- down_grad: float32 [2816, 1024], P(('dp', 'fsdp'))
The draws below stay inside these ranges and needn't reach their ends.
Inputs may be any that keep to these rules, and one draw needn't show every extreme that they name: `seq_counts`: slots 0 to count - 1 of a device's 4 hold live sequences, the others are padding; some device holds 4 and some device 1. `segments`: starts at 0 in every sequence and rises by one at each new document's first token; documents begin only at token indices that are multiples of 4. `positions`: within a document rises by 1 to 3 from one token to the next; a document's first token has a position below 2048.
All inputs are finite; a program needn't handle non-finite values.
Results may differ from the reference program's by a relative error of at most 0.014.
Values may be sent and summed in bfloat16 or wider, within the bound.
A program may use at most 256 MiB of HBM per device.

```python
import math
import jax
import jax.numpy as jnp
from jax import lax

D = 1024
HD = 64
FF = 2816
SEQ = 128
CAP = 4
SEQS = 128
DEVICES = 32


def doc_starts(key):
    random_flags = jax.random.randint(jax.random.fold_in(key, 11), (SEQS, SEQ), 0, 8) == 0
    first_row = jax.random.randint(jax.random.fold_in(key, 12), (), 0, SEQS)
    second_row = (first_row + 1 + jax.random.randint(jax.random.fold_in(key, 13), (), 0, SEQS - 1)) % SEQS
    step_index = jnp.arange(SEQ, dtype=jnp.int32)
    row_index = jnp.arange(SEQS, dtype=jnp.int32)
    aligned = (step_index[None, :] % 4 == 0) & (step_index[None, :] > 0)
    flags = aligned & (random_flags | (row_index[:, None] == first_row))
    flags = flags & (row_index[:, None] != second_row)
    return (flags.astype(jnp.int32), first_row, second_row)


def draw_segments(key, part):
    flags, first_row, second_row = doc_starts(key)
    return jnp.cumsum(flags, axis=1).astype(jnp.int32)


def draw_positions(key, part):
    flags, first_row, second_row = doc_starts(key)
    key = jax.random.fold_in(key, 7)
    step_index = jnp.broadcast_to(jnp.arange(SEQ, dtype=jnp.int32)[None, :], (SEQS, SEQ))
    row_index = jnp.arange(SEQS, dtype=jnp.int32)
    starts = lax.cummax(jnp.where(flags == 1, step_index, 0), axis=1)
    doc_ids = jnp.cumsum(flags, axis=1).astype(jnp.int32)
    offsets = jax.random.randint(jax.random.fold_in(key, 1), (SEQS, SEQ), 0, 2048)
    offsets = jnp.where(row_index[:, None] == second_row, 2047, offsets)
    offsets = offsets.at[first_row, 0].set(0)
    increments = jax.random.randint(jax.random.fold_in(key, 2), (SEQS, SEQ), 1, 4)
    increments = jnp.where(row_index[:, None] == second_row, 3, increments)
    before = jnp.cumsum(increments, axis=1) - increments
    start_value = jnp.take_along_axis(before, starts, axis=1)
    return (jnp.take_along_axis(offsets, doc_ids, axis=1) + before - start_value).astype(jnp.int32)


def draw_seq_counts(key, part):
    key = jax.random.fold_in(key, 3)
    keys_all = jax.random.split(key, 4)
    base_counts = 1 + jax.random.randint(keys_all[0], (DEVICES,), 0, 2)
    full_pick = jax.random.randint(keys_all[1], (DEVICES,), 0, 4) == 0
    counts_now = jnp.where(full_pick, CAP, base_counts)
    first_pick = jax.random.randint(keys_all[2], (), 0, DEVICES)
    second_pick = (first_pick + 1 + jax.random.randint(keys_all[3], (), 0, DEVICES - 1)) % DEVICES
    counts_now = counts_now.at[first_pick].set(CAP).at[second_pick].set(1)
    return counts_now.astype(jnp.int32)


def levels(own_key, dims, pieces, least, high):
    factor_of, own = 1.0, jax.random.fold_in(own_key, 6)
    for position, shards_of in pieces:
        draws = jnp.exp(jax.random.uniform(jax.random.fold_in(own, position), (shards_of,), jnp.float32, least / len(pieces), high / len(pieces)))
        factor_of = factor_of * jnp.repeat(draws, dims[position] // shards_of).reshape([-1 if axis == position else 1 for axis in range(len(dims))])
    return factor_of


def bell_draw(rng, dims, spread, bound, cuts=(), kind=jnp.bfloat16):
    entries = spread * jax.random.normal(rng, dims, jnp.float32)
    if cuts:
        entries = entries * levels(rng, dims, cuts, -0.22, 0.18)
    return jnp.clip(entries, -bound, bound).astype(kind)


def setup_inputs(seed: int = 0) -> dict:
    keys = jax.random.split(jax.random.key(seed), 16)
    return {
        "tokens": bell_draw(keys[0], (SEQS, SEQ, D), 1.0, 6.0, ((0, 32),)),
        "seq_counts": draw_seq_counts(jax.random.fold_in(keys[15], 71), 0),
        "segments": draw_segments(jax.random.fold_in(keys[15], 71), 0),
        "positions": draw_positions(jax.random.fold_in(keys[15], 71), 0),
        "norm_first": jnp.clip(1.0 + 0.1 * jax.random.normal(keys[4], (D,), jnp.float32), 0.5, 1.5).astype(jnp.bfloat16),
        "query_weight": bell_draw(keys[5], (D, D), (D // 2) ** -0.5, 0.25, ((0, 32),)),
        "key_weight": bell_draw(keys[6], (D, D), D ** -0.5, 0.1875, ((0, 32),)),
        "value_weight": bell_draw(keys[7], (D, D), D ** -0.5, 0.1875, ((0, 32),)),
        "output_weight": bell_draw(keys[8], (D, D), (D // 16) ** -0.5, 0.75, ((0, 32),)),
        "norm_second": jnp.clip(1.0 + 0.1 * jax.random.normal(keys[9], (D,), jnp.float32), 0.5, 1.5).astype(jnp.bfloat16),
        "gate_weight": bell_draw(keys[10], (D, FF), D ** -0.5, 0.1875, ((0, 32),)),
        "up_weight": bell_draw(keys[11], (D, FF), D ** -0.5, 0.1875, ((0, 32),)),
        "down_weight": bell_draw(keys[12], (FF, D), FF ** -0.5, 0.109375, ((0, 32),)),
        "out_cotangent": bell_draw(keys[13], (SEQS, SEQ, D), 1.0, 6.0, ((0, 32),)),
        "value_cotangent": bell_draw(keys[14], (SEQS, SEQ, D), 1.0, 6.0, ((0, 32),)),
    }


@jax.custom_vjp
def low(v):
    return lax.optimization_barrier(v.astype(jnp.bfloat16)).astype(jnp.float32)

@jax.custom_vjp
def low_back(v):
    return v

def low_keep(v):
    return (low(v), None)

def low_pass(kept, grad):
    return (grad,)

def back_keep(v):
    return (v, None)

def back_low(kept, grad):
    return (low(grad),)
low.defvjp(low_keep, low_pass)
low_back.defvjp(back_keep, back_low)
eps = 1e-06

def rms_scale(values_in):
    return lax.rsqrt(lax.optimization_barrier(jnp.mean(values_in * values_in, axis=-1, keepdims=True)) + eps)

def rotate_table(positions):
    freq_index = jnp.arange(HD // 2, dtype=jnp.float32)
    inverse = jnp.exp(freq_index * (-2.0 * math.log(10000.0) / HD))
    angles = positions.astype(jnp.float32)[..., None] * inverse
    return (jnp.cos(angles), jnp.sin(angles))

def apply_rotary(values_in, cosine, sines):
    half_dim = values_in.shape[-1] // 2
    first_half = values_in[..., :half_dim]
    second_half = values_in[..., half_dim:]
    cosine = cosine[..., None, :]
    sines = sines[..., None, :]
    return jnp.concatenate([first_half * cosine - second_half * sines, second_half * cosine + first_half * sines], axis=-1)

def forward(params, inputs_f, segments, positions, live_rows):
    gain_one, query_weight, key_weight, value_weight, output_weight, gain_two, gate_weight, up_weight, down_weight = params
    group_size, seq_length, model_width = inputs_f.shape
    head_count = model_width // HD
    highest = lax.Precision.HIGHEST

    def project(left_arg, weight_arg):
        return jnp.einsum('gtd,de->gte', left_arg, weight_arg, precision=highest)

    def split_heads(values_in):
        return values_in.reshape(group_size, seq_length, head_count, HD)
    normed = low(inputs_f * rms_scale(inputs_f) * gain_one)
    cosine, sines = rotate_table(positions)
    queries = low(apply_rotary(split_heads(low_back(project(normed, query_weight))), cosine, sines))
    keys_rot = low(apply_rotary(split_heads(low_back(project(normed, key_weight))), cosine, sines))
    values_low = low(low_back(project(normed, value_weight)))
    step_index = jnp.arange(seq_length)
    allowed = (segments[:, :, None] == segments[:, None, :]) & (step_index[:, None] >= step_index[None, :])
    scores = jnp.einsum('gqhe,gkhe->ghqk', queries, keys_rot, precision=highest) * HD ** (-0.5)
    scores = low_back(jnp.where(allowed[:, None], scores, -1e+30))
    probs_low = low(jax.nn.softmax(scores, axis=-1))
    mixed_heads = jnp.einsum('ghqk,gkhe->gqhe', probs_low, split_heads(values_low), precision=highest)
    mixed_low = low(low_back(mixed_heads.reshape(group_size, seq_length, model_width)))
    middle = inputs_f + low_back(project(mixed_low, output_weight))
    normed_two = low(middle * rms_scale(middle) * gain_two)
    gate_pre = low_back(project(normed_two, gate_weight))
    upward = low_back(project(normed_two, up_weight))
    hidden = low(jax.nn.silu(gate_pre) * upward)
    branch = low_back(project(hidden, down_weight))
    live_mask = live_rows[:, None, None]
    return (live_mask * (middle + branch), live_mask * values_low)

def reference(tokens, seq_counts, segments, positions, norm_first, query_weight, key_weight, value_weight, output_weight, norm_second, gate_weight, up_weight, down_weight, out_cotangent, value_cotangent):
    seq_index = jnp.arange(SEQS, dtype=jnp.int32)
    live_rows = (seq_index % CAP < seq_counts[seq_index // CAP]).astype(jnp.float32)
    params = tuple((weight_arg.astype(jnp.float32) for weight_arg in (norm_first, query_weight, key_weight, value_weight, output_weight, norm_second, gate_weight, up_weight, down_weight)))
    group_count = SEQS // 32

    def regroup(values_in):
        return values_in.reshape((group_count, 32) + values_in.shape[1:])

    def one_group(totals, inputs_group):
        group_tokens, group_segments, group_positions, group_live, group_out, group_value = inputs_group

        def local_forward(weights_now, tokens_now):
            return forward(weights_now, tokens_now, group_segments, group_positions, group_live)
        outputs_now, pullback = jax.vjp(local_forward, params, group_tokens.astype(jnp.float32))
        grad_params, grad_tokens = pullback((group_out.astype(jnp.float32), group_value.astype(jnp.float32)))
        totals = jax.tree.map(jnp.add, totals, grad_params)
        return (totals, (outputs_now[0].astype(jnp.bfloat16), outputs_now[1].astype(jnp.bfloat16), grad_tokens.astype(jnp.bfloat16)))
    zeros_init = tuple((jnp.zeros_like(weight_arg) for weight_arg in params))
    scanned = (regroup(tokens), regroup(segments), regroup(positions), regroup(live_rows), regroup(out_cotangent), regroup(value_cotangent))
    totals, stacked = lax.scan(one_group, zeros_init, scanned)
    block_out = stacked[0].reshape(tokens.shape)
    first_values = stacked[1].reshape(tokens.shape)
    token_grad = stacked[2].reshape(tokens.shape)
    return (block_out, first_values, token_grad, totals[0], totals[1], totals[2], totals[3], totals[4], totals[5], totals[6], totals[7], totals[8])
```

```python
import math

import jax
import jax.numpy as jnp
from jax import lax
from jax.experimental import pallas as pl
from jax.experimental.pallas import tpu as pltpu
from jax.sharding import PartitionSpec as P

HD = 64
MESH = pl.DeviceIdType.MESH
BOTH = ("dp", "fsdp")

eps = 1e-06


class Place:
    def __init__(self, depth):
        dp, fsdp = lax.axis_index("dp"), lax.axis_index("fsdp")
        self.x, self.c = dp // 2, dp % 2
        self.z, self.y = fsdp // 2, fsdp % 2
        self.depth = depth

    def at(self, x, c, z, y):
        return (x * 2 + c, z * 2 + y)

    def across_x(self):
        return self.at(1 - self.x, self.c, self.z, self.y)

    def across_y(self):
        return self.at(self.x, self.c, self.z, 1 - self.y)

    def sibling(self):
        return self.at(self.x, 1 - self.c, self.z, self.y)

    def above(self):
        return self.at(self.x, self.c, self.z + 1, self.y)

    def below(self):
        return self.at(self.x, self.c, self.z - 1, self.y)

    def greet(self):
        barrier = pltpu.get_barrier_semaphore()

        def call(who):
            pl.semaphore_signal(barrier, inc=1, device_id=who, device_id_type=MESH)

        call(self.across_x())
        call(self.across_y())
        call(self.sibling())
        not_top = self.z < self.depth - 1
        not_low = self.z > 0
        pl.when(not_top)(lambda: call(self.above()))
        pl.when(not_low)(lambda: call(self.below()))
        peers = 3 + not_top.astype(jnp.int32) + not_low.astype(jnp.int32)
        pl.semaphore_wait(barrier, peers)


def remote(src, dst, send_sem, recv_sem, who):
    return pltpu.make_async_remote_copy(
        src_ref=src,
        dst_ref=dst,
        send_sem=send_sem,
        recv_sem=recv_sem,
        device_id=who,
        device_id_type=MESH,
    )


class Gather:
    def __init__(self, place, own, full, sems, order):
        self.p, self.own, self.full, self.sems, self.order = place, own, full, sems, order
        self.wide = full.shape[-1]

    def shard(self, x, y, z):
        return self.full.at[x, self.p.c, z, y]

    def zunit(self, z):
        if self.order == "zr":
            return self.full.at[self.p.x, self.p.c, z, self.p.y]
        return self.full.at[:, self.p.c, z]

    def runit(self, x, y, half=None):
        if self.order == "zr":
            if half is None:
                return self.full.at[x, self.p.c, :, y]
            count = self.p.depth // 2
            return self.full.at[x, self.p.c, half * count : (half + 1) * count, y]
        if half is None:
            return self.full.at[x, self.p.c, self.p.z, y]
        count = self.wide // 2
        return self.full.at[x, self.p.c, self.p.z, y, :, half * count : (half + 1) * count]

    def copy(self, ref, slot, who, src=None):
        return remote(ref if src is None else src, ref, self.sems.at[0, slot], self.sems.at[1, slot], who)

    def up(self, unit, src=None):
        return self.copy(self.zunit(unit), unit, self.p.above(), src)

    def down(self, unit, src=None):
        return self.copy(self.zunit(unit), self.p.depth + unit, self.p.below(), src)

    def place_own(self):
        p = self.p
        self.local = pltpu.make_async_copy(self.own, self.shard(p.x, p.y, p.z), self.sems.at[0, 22])
        self.local.start()

    def z_step(self, step):
        p = self.p
        top, low = p.depth - 1, 0
        src = self.own if (step == 0 and self.order == "zr") else None

        def from_below():
            if step > 0:
                self.up(p.z - step).wait_recv()
            pl.when(p.z < top)(lambda: self.up(p.z - step, src).start())

        def from_above():
            if step > 0:
                self.down(p.z + step).wait_recv()
            pl.when(p.z > low)(lambda: self.down(p.z + step, src).start())

        pl.when(p.z - step >= low)(from_below)
        pl.when(p.z + step <= top)(from_above)

    def ring_first(self):
        p, base = self.p, 2 * self.p.depth
        mine = self.runit(p.x, p.y)
        src = self.own if self.order == "rz" else None
        self.copy(mine, base, p.across_x(), src).start()
        self.copy(mine, base + 1, p.across_y(), src).start()

    def ring_second(self):
        p, base = self.p, 2 * self.p.depth
        from_x, from_y = self.runit(1 - p.x, p.y), self.runit(p.x, 1 - p.y)
        self.copy(from_x, base, p.across_x()).wait_recv()
        self.copy(self.runit(1 - p.x, p.y, 0), base + 2, p.across_y()).start()
        self.copy(from_y, base + 1, p.across_y()).wait_recv()
        self.copy(self.runit(p.x, 1 - p.y, 1), base + 3, p.across_x()).start()

    def ring_last(self):
        p, base = self.p, 2 * self.p.depth
        self.copy(self.runit(1 - p.x, 1 - p.y, 0), base + 2, p.across_y()).wait_recv()
        self.copy(self.runit(1 - p.x, 1 - p.y, 1), base + 3, p.across_x()).wait_recv()

    def give(self, ref, slot):
        self.copy(ref, 2 * self.p.depth + 4 + slot, self.p.sibling()).start()

    def sib_ref(self, kind):
        p, c = self.p, 1 - self.p.c
        if self.order == "zr":
            x = (p.x, 1 - p.x, p.x, 1 - p.x)[kind]
            y = (p.y, p.y, 1 - p.y, 1 - p.y)[kind]
            return self.full.at[x, c, :, y]
        return self.full.at[:, c, kind]

    def my_ref(self, kind):
        p, c = self.p, self.p.c
        if self.order == "zr":
            x = (p.x, 1 - p.x, p.x, 1 - p.x)[kind]
            y = (p.y, p.y, 1 - p.y, 1 - p.y)[kind]
            return self.full.at[x, c, :, y]
        return self.full.at[:, c, kind]

    def steps(self):
        p = self.p
        if self.order == "zr":
            return [
                lambda: (self.place_own(), self.z_step(0)),
                lambda: self.z_step(1),
                lambda: self.z_step(2),
                lambda: (self.z_step(3), self.local.wait(), self.ring_first(), self.give(self.my_ref(0), 0)),
                lambda: (self.ring_second(), self.give(self.my_ref(1), 1), self.give(self.my_ref(2), 2)),
                lambda: (self.ring_last(), self.give(self.my_ref(3), 3)),
                lambda: self.finish(),
            ]

        def pass_on(step):
            def low():
                self.give(self.full.at[:, p.c, p.z - step], p.z - step)

            def high():
                self.give(self.full.at[:, p.c, p.z + step], p.z + step)

            pl.when(p.z - step >= 0)(low)
            if step > 0:
                pl.when(p.z + step <= p.depth - 1)(high)

        return [
            lambda: (self.place_own(), self.ring_first()),
            lambda: self.ring_second(),
            lambda: (self.ring_last(), self.local.wait(), self.z_step(0), pass_on(0)),
            lambda: (self.z_step(1), pass_on(1)),
            lambda: (self.z_step(2), pass_on(2)),
            lambda: (self.z_step(3), pass_on(3)),
            lambda: self.finish(),
        ]

    def finish(self):
        p, base = self.p, 2 * self.p.depth
        for kind in range(4):
            self.copy(self.sib_ref(kind), base + 4 + kind, p.sibling()).wait_recv()
        top = p.depth - 1
        for unit in range(p.depth):
            pl.when((p.z < top) & (unit <= p.z))(lambda unit=unit: self.up(unit).wait_send())
            pl.when((p.z > 0) & (unit >= p.z))(lambda unit=unit: self.down(unit).wait_send())
        self.copy(self.runit(p.x, p.y), base, p.across_x()).wait_send()
        self.copy(self.runit(p.x, p.y), base + 1, p.across_y()).wait_send()
        self.copy(self.runit(1 - p.x, p.y, 0), base + 2, p.across_y()).wait_send()
        self.copy(self.runit(p.x, 1 - p.y, 1), base + 3, p.across_x()).wait_send()
        for kind in range(4):
            self.copy(self.my_ref(kind), base + 4 + kind, p.sibling()).wait_send()


GATHER_ORDERS = ("zr",) * 8


def gather_kernel(depth, count, *refs):
    owns, fulls, sems = refs[:count], refs[count : 2 * count], refs[2 * count]
    place = Place(depth)
    place.greet()
    jobs = [
        Gather(place, owns[i], fulls[i], sems.at[i], GATHER_ORDERS[i]).steps() for i in range(count)
    ]
    stages = len(jobs[0])
    for tick in range(count + stages - 1):
        for stage in reversed(range(stages)):
            if 0 <= tick - stage < count:
                jobs[tick - stage][stage]()


def gather_all(mesh, shards_in):
    depth = mesh.shape["fsdp"] // 2
    count = len(shards_in)
    return pl.pallas_call(
        lambda *refs: gather_kernel(depth, count, *refs),
        out_shape=tuple(
            jax.ShapeDtypeStruct((2, 2, depth, 2) + s.shape, s.dtype) for s in shards_in
        ),
        in_specs=[pl.BlockSpec(memory_space=pl.ANY)] * count,
        out_specs=tuple([pl.BlockSpec(memory_space=pl.ANY)] * count),
        scratch_shapes=[pltpu.SemaphoreType.DMA((count, 2, 24))],
        compiler_params=pltpu.CompilerParams(collective_id=1, has_side_effects=True),
        name="gather_weights",
    )(*shards_in)


class Reduce:
    def __init__(self, place, part, out, bufs, sems):
        self.p, self.part, self.out, self.sems = place, part, out, sems
        self.acc, self.sib, self.ring1, self.ring2, self.zed = bufs

    def copy(self, src, dst, slot, who):
        return remote(src, dst, self.sems.at[0, slot], self.sems.at[1, slot], who)

    def sib_copy(self):
        p = self.p
        return self.copy(self.part.at[:, 1 - p.c], self.sib, 0, p.sibling())

    def own_copy(self):
        return pltpu.make_async_copy(self.part.at[:, self.p.c], self.acc, self.sems.at[0, 1])

    def start(self):
        self.sib_copy().start()
        self.own_copy().start()

    def half1(self):
        p, half = self.p, self.p.depth // 2
        by_x = self.copy(self.acc.at[1 - p.x, :half, 1 - p.y], self.ring1.at[0], 2, p.across_x())
        by_y = self.copy(self.acc.at[1 - p.x, half:, 1 - p.y], self.ring1.at[1], 3, p.across_y())
        return by_x, by_y

    def half2(self):
        p = self.p
        to_x = self.copy(self.acc.at[1 - p.x, :, p.y], self.ring2.at[0], 4, p.across_x())
        to_y = self.copy(self.acc.at[p.x, :, 1 - p.y], self.ring2.at[1], 5, p.across_y())
        return to_x, to_y

    def after_sibling(self):
        self.own_copy().wait()
        self.sib_copy().wait_recv()
        p = self.p
        first = (1 - p.x, 1 - p.y)
        self.add_bundle(*first, self.sib)
        for cp in self.half1():
            cp.start()
        for x, y in ((1 - p.x, p.y), (p.x, 1 - p.y), (p.x, p.y)):
            self.add_bundle(x, y, self.sib)

    def add_bundle(self, x, y, other):
        for z in range(self.p.depth):
            self.acc[x, z, y] = self.acc[x, z, y] + other[x, z, y]

    def after_half(self):
        p, half = self.p, self.p.depth // 2
        by_x, by_y = self.half1()
        to_x, to_y = self.half2()
        by_x.wait_recv()
        for z in range(half):
            self.acc[p.x, z, 1 - p.y] = self.acc[p.x, z, 1 - p.y] + self.ring1[0, z]
        to_y.start()
        by_y.wait_recv()
        for z in range(half):
            self.acc[1 - p.x, half + z, p.y] = self.acc[1 - p.x, half + z, p.y] + self.ring1[1, z]
        to_x.start()

    def up(self, unit):
        p = self.p
        return self.copy(self.acc.at[p.x, unit, p.y], self.zed.at[0, unit], 6 + unit, p.above())

    def down(self, unit):
        p = self.p
        return self.copy(self.acc.at[p.x, unit, p.y], self.zed.at[1, unit], 6 + p.depth + unit, p.below())

    def after_ring(self):
        p = self.p
        to_x, to_y = self.half2()
        to_x.wait_recv()
        to_y.wait_recv()
        for z in range(p.depth):
            both = self.ring2[0, z].astype(jnp.float32) + self.ring2[1, z].astype(jnp.float32)
            mine = self.acc[p.x, z, p.y]
            self.acc[p.x, z, p.y] = (mine.astype(jnp.float32) + both).astype(mine.dtype)
        self.z_step(0)

    def z_step(self, step):
        p = self.p
        top = p.depth - 1

        def upward():
            if step > 0:
                for unit in range(step, p.depth):
                    self.up(unit).wait_recv()
                for unit in range(step + 1, p.depth):
                    self.acc[p.x, unit, p.y] = self.acc[p.x, unit, p.y] + self.zed[0, unit]
            if step < top:
                for unit in range(step + 1, p.depth):
                    self.up(unit).start()

        def downward():
            if step > 0:
                for unit in range(0, p.depth - step):
                    self.down(unit).wait_recv()
                for unit in range(0, p.depth - step - 1):
                    self.acc[p.x, unit, p.y] = self.acc[p.x, unit, p.y] + self.zed[1, unit]
            if step < top:
                for unit in range(0, p.depth - step - 1):
                    self.down(unit).start()

        pl.when(p.z == step)(upward)
        pl.when(p.z == top - step)(downward)

    def finish(self):
        p, top = self.p, self.p.depth - 1
        mine = self.acc[p.x, p.z, p.y].astype(jnp.float32)

        @pl.when(p.z == 0)
        def _():
            self.out[...] = mine + self.zed[1, p.z].astype(jnp.float32)

        @pl.when(p.z == top)
        def _():
            self.out[...] = mine + self.zed[0, p.z].astype(jnp.float32)

        @pl.when((p.z > 0) & (p.z < top))
        def _():
            self.out[...] = mine + (
                self.zed[0, p.z].astype(jnp.float32) + self.zed[1, p.z].astype(jnp.float32)
            )

        self.sib_copy().wait_send()
        for cp in self.half1() + self.half2():
            cp.wait_send()
        for unit in range(p.depth):
            if unit > 0:
                pl.when(p.z < unit)(lambda unit=unit: self.up(unit).wait_send())
            if unit < top:
                pl.when(p.z > unit)(lambda unit=unit: self.down(unit).wait_send())

    def steps(self):
        return [
            self.start,
            self.after_sibling,
            self.after_half,
            self.after_ring,
            lambda: self.z_step(1),
            lambda: self.z_step(2),
            lambda: (self.z_step(3), self.finish()),
        ]


def reduce_kernel(depth, count, *refs):
    parts, outs = refs[:count], refs[count : 2 * count]
    bufs = refs[2 * count : 2 * count + 5 * count]
    sems = refs[-1]
    place = Place(depth)
    place.greet()
    jobs = [
        Reduce(place, parts[i], outs[i], bufs[5 * i : 5 * i + 5], sems.at[i]).steps()
        for i in range(count)
    ]
    stages = len(jobs[0])
    for tick in range(count + stages - 1):
        for stage in reversed(range(stages)):
            if 0 <= tick - stage < count:
                jobs[tick - stage][stage]()


def reduce_all(mesh, parts):
    depth = mesh.shape["fsdp"] // 2
    count = len(parts)
    bufs = []
    for part in parts:
        block, kind = part.shape[4:], part.dtype
        bufs += [
            pltpu.VMEM((2, depth, 2) + block, kind),
            pltpu.VMEM((2, depth, 2) + block, kind),
            pltpu.VMEM((2, depth // 2) + block, kind),
            pltpu.VMEM((2, depth) + block, kind),
            pltpu.VMEM((2, depth) + block, kind),
        ]
    return pl.pallas_call(
        lambda *refs: reduce_kernel(depth, count, *refs),
        out_shape=tuple(jax.ShapeDtypeStruct(p.shape[4:], jnp.float32) for p in parts),
        in_specs=[pl.BlockSpec(memory_space=pl.ANY)] * count,
        out_specs=tuple([pl.BlockSpec(memory_space=pltpu.VMEM)] * count),
        scratch_shapes=bufs + [pltpu.SemaphoreType.DMA((count, 2, 16))],
        compiler_params=pltpu.CompilerParams(
            collective_id=2, has_side_effects=True, vmem_limit_bytes=60 * 2**20
        ),
        name="reduce_grads",
    )(*parts)


def rms_scale(values_in):
    return lax.rsqrt(jnp.mean(values_in * values_in, axis=-1, keepdims=True) + eps)


def rotate_table(positions):
    freq_index = jnp.arange(HD // 2, dtype=jnp.float32)
    inverse = jnp.exp(freq_index * (-2.0 * math.log(10000.0) / HD))
    angles = positions.astype(jnp.float32)[..., None] * inverse
    return (jnp.cos(angles), jnp.sin(angles))


def apply_rotary(values_in, cosine, sines):
    half_dim = values_in.shape[-1] // 2
    first_half = values_in[..., :half_dim]
    second_half = values_in[..., half_dim:]
    cosine = cosine[..., None, :]
    sines = sines[..., None, :]
    return jnp.concatenate(
        [first_half * cosine - second_half * sines, second_half * cosine + first_half * sines],
        axis=-1,
    )


def matmul(left_arg, right_arg):
    return jnp.dot(left_arg, right_arg, preferred_element_type=jnp.float32)


def stack_groups(values_in):
    row_count, model_width = values_in.shape
    return values_in.reshape(row_count, model_width // (4 * HD), 4 * HD).transpose(1, 0, 2)


def unstack_groups(values_in):
    group_count, row_count, group_width = values_in.shape
    return values_in.transpose(1, 0, 2).reshape(row_count, group_count * group_width)


def head_scores(query_grp, key_grp, allowed):
    row_count = query_grp.shape[0]
    query_heads = query_grp.reshape(row_count, 4, HD)
    key_heads = key_grp.reshape(row_count, 4, HD)
    scores = jnp.einsum(
        "qhe,khe->hqk", query_heads, key_heads, preferred_element_type=jnp.float32
    ) * HD ** (-0.5)
    return jnp.where(allowed[None], scores, -1e30)


def norm_back(grad_normed, inputs_f, scale_rows, gain_row):
    gain_term = jnp.sum(grad_normed * inputs_f * scale_rows, axis=0)
    scaled = grad_normed * gain_row
    grad_inputs = scale_rows * (
        scaled
        - inputs_f * scale_rows * scale_rows * jnp.mean(scaled * inputs_f, axis=-1, keepdims=True)
    )
    return (grad_inputs, gain_term)


def layer(
    gather_set,
    reduce_set,
    tokens,
    seq_counts,
    segments,
    positions,
    norm_first,
    query_weight,
    key_weight,
    value_weight,
    output_weight,
    norm_second,
    gate_weight,
    up_weight,
    down_weight,
    out_cotangent,
    value_cotangent,
):
    slot_count, seq_length, model_width = tokens.shape
    row_count = slot_count * seq_length
    head_count = model_width // HD
    weights = gather_set(
        norm_first,
        norm_second,
        query_weight,
        key_weight,
        value_weight,
        output_weight,
        gate_weight,
        up_weight,
        down_weight,
    )
    gain_one, gain_two, query_full, key_full, value_full, output_full = weights[:6]
    gate_full, up_full, down_full = weights[6:]
    row_index = jnp.arange(row_count, dtype=jnp.int32)
    slot_index = row_index // seq_length
    live_rows = (slot_index < seq_counts[0]).astype(jnp.float32)[:, None]
    flat_segments = segments.reshape(row_count)
    allowed = (
        (slot_index[:, None] == slot_index[None, :])
        & (flat_segments[:, None] == flat_segments[None, :])
        & (row_index[:, None] >= row_index[None, :])
    )
    inputs_f = tokens.reshape(row_count, model_width).astype(jnp.float32)
    scale_one = rms_scale(inputs_f)
    normed = (inputs_f * scale_one * gain_one.astype(jnp.float32)).astype(jnp.bfloat16)
    cosine, sines = rotate_table(positions.reshape(row_count))

    def rotated(values_in, turn_sign):
        turned = apply_rotary(
            values_in.reshape(row_count, head_count, HD), cosine, turn_sign * sines
        )
        return turned.reshape(row_count, model_width).astype(jnp.bfloat16)

    query_rot = rotated(matmul(normed, query_full), 1.0)
    key_rot = rotated(matmul(normed, key_full), 1.0)
    value_low = matmul(normed, value_full).astype(jnp.bfloat16)

    def attend_group(operands):
        query_grp, key_grp, value_grp = operands
        scores = head_scores(query_grp, key_grp, allowed)
        row_max = jnp.max(scores, axis=-1, keepdims=True)
        log_total = row_max + jnp.log(jnp.sum(jnp.exp(scores - row_max), axis=-1, keepdims=True))
        probs_low = jnp.exp(scores - log_total).astype(jnp.bfloat16)
        value_heads = value_grp.reshape(row_count, 4, HD)
        mixed_heads = jnp.einsum(
            "hqk,khe->qhe", probs_low, value_heads, preferred_element_type=jnp.float32
        )
        return (mixed_heads.reshape(row_count, 4 * HD), log_total)

    query_groups = stack_groups(query_rot)
    key_groups = stack_groups(key_rot)
    value_groups = stack_groups(value_low)
    mixed_groups, log_totals = lax.map(attend_group, (query_groups, key_groups, value_groups))
    mixed_low = unstack_groups(mixed_groups).astype(jnp.bfloat16)
    middle = inputs_f + matmul(mixed_low, output_full)
    scale_two = rms_scale(middle)
    normed_two = (middle * scale_two * gain_two.astype(jnp.float32)).astype(jnp.bfloat16)
    gate_pre = matmul(normed_two, gate_full)
    upward = matmul(normed_two, up_full)
    sigmoid_gate = jax.nn.sigmoid(gate_pre)
    silu_gate = gate_pre * sigmoid_gate
    hidden = (silu_gate * upward).astype(jnp.bfloat16)
    block_out = (live_rows * (middle + matmul(hidden, down_full))).astype(jnp.bfloat16)
    first_values = (live_rows * value_low.astype(jnp.float32)).astype(jnp.bfloat16)
    grad_y = live_rows * out_cotangent.reshape(row_count, model_width).astype(jnp.float32)
    grad_branch = grad_y.astype(jnp.bfloat16)
    down_term = jnp.einsum("rf,rd->fd", hidden, grad_branch, preferred_element_type=jnp.float32)
    grad_hidden = jnp.einsum(
        "rd,fd->rf", grad_branch, down_full, preferred_element_type=jnp.float32
    )
    grad_gate = (
        grad_hidden * upward * sigmoid_gate * (1.0 + gate_pre * (1.0 - sigmoid_gate))
    ).astype(jnp.bfloat16)
    grad_up = (grad_hidden * silu_gate).astype(jnp.bfloat16)
    gate_term = jnp.einsum("rd,rf->df", normed_two, grad_gate, preferred_element_type=jnp.float32)
    up_term = jnp.einsum("rd,rf->df", normed_two, grad_up, preferred_element_type=jnp.float32)
    grad_normed_two = jnp.einsum(
        "rf,df->rd", grad_gate, gate_full, preferred_element_type=jnp.float32
    ) + jnp.einsum("rf,df->rd", grad_up, up_full, preferred_element_type=jnp.float32)
    grad_middle_norm, gain_two_term = norm_back(
        grad_normed_two, middle, scale_two, gain_two.astype(jnp.float32)
    )
    grad_middle = grad_y + grad_middle_norm
    grad_attended = grad_middle.astype(jnp.bfloat16)
    output_term = jnp.einsum(
        "rd,re->de", mixed_low, grad_attended, preferred_element_type=jnp.float32
    )
    grad_mixed = jnp.einsum(
        "re,de->rd", grad_attended, output_full, preferred_element_type=jnp.float32
    ).astype(jnp.bfloat16)

    def attend_back(operands):
        query_grp, key_grp, value_grp, grad_grp, log_total = operands
        scores = head_scores(query_grp, key_grp, allowed)
        probs_full = jnp.exp(scores - log_total)
        probs_low = probs_full.astype(jnp.bfloat16)
        grad_heads = grad_grp.reshape(row_count, 4, HD)
        value_heads = value_grp.reshape(row_count, 4, HD)
        query_heads = query_grp.reshape(row_count, 4, HD)
        key_heads = key_grp.reshape(row_count, 4, HD)
        grad_probs = jnp.einsum(
            "qhe,khe->hqk", grad_heads, value_heads, preferred_element_type=jnp.float32
        )
        row_term = jnp.sum(probs_full * grad_probs, axis=-1, keepdims=True)
        grad_scores = (probs_full * (grad_probs - row_term)).astype(jnp.bfloat16)
        score_scale = HD ** (-0.5)
        grad_query = (
            jnp.einsum("hqk,khe->qhe", grad_scores, key_heads, preferred_element_type=jnp.float32)
            * score_scale
        )
        grad_key = (
            jnp.einsum("hqk,qhe->khe", grad_scores, query_heads, preferred_element_type=jnp.float32)
            * score_scale
        )
        grad_value = jnp.einsum(
            "hqk,qhe->khe", probs_low, grad_heads, preferred_element_type=jnp.float32
        )
        group_width = 4 * HD
        return (
            grad_query.reshape(row_count, group_width),
            grad_key.reshape(row_count, group_width),
            grad_value.reshape(row_count, group_width),
        )

    grad_q_groups, grad_k_groups, grad_v_groups = lax.map(
        attend_back, (query_groups, key_groups, value_groups, stack_groups(grad_mixed), log_totals)
    )
    grad_query = rotated(unstack_groups(grad_q_groups), -1.0)
    grad_key = rotated(unstack_groups(grad_k_groups), -1.0)
    grad_value = (
        unstack_groups(grad_v_groups)
        + live_rows * value_cotangent.reshape(row_count, model_width).astype(jnp.float32)
    ).astype(jnp.bfloat16)
    query_term = jnp.einsum("rd,re->de", normed, grad_query, preferred_element_type=jnp.float32)
    key_term = jnp.einsum("rd,re->de", normed, grad_key, preferred_element_type=jnp.float32)
    value_term = jnp.einsum("rd,re->de", normed, grad_value, preferred_element_type=jnp.float32)
    grad_normed = jnp.einsum(
        "re,de->rd", grad_query, query_full, preferred_element_type=jnp.float32
    )
    grad_normed = grad_normed + jnp.einsum(
        "re,de->rd", grad_key, key_full, preferred_element_type=jnp.float32
    )
    grad_normed = grad_normed + jnp.einsum(
        "re,de->rd", grad_value, value_full, preferred_element_type=jnp.float32
    )
    grad_inputs_norm, gain_one_term = norm_back(
        grad_normed, inputs_f, scale_one, gain_one.astype(jnp.float32)
    )
    token_grad = (grad_middle + grad_inputs_norm).astype(jnp.bfloat16).reshape(tokens.shape)
    grads = reduce_set(
        gain_one_term,
        gain_two_term,
        query_term,
        key_term,
        value_term,
        output_term,
        gate_term,
        up_term,
        down_term,
    )
    return (
        block_out.reshape(tokens.shape),
        first_values.reshape(tokens.shape),
        token_grad,
        grads[0],
        grads[2],
        grads[3],
        grads[4],
        grads[5],
        grads[1],
        grads[6],
        grads[7],
        grads[8],
    )


def plain_gather(*shards_in):
    return tuple(lax.all_gather(s, BOTH, axis=0, tiled=True) for s in shards_in)


def plain_reduce(*terms):
    return tuple(lax.psum_scatter(t, BOTH, scatter_dimension=0, tiled=True) for t in terms)


def linked_gather(mesh):
    def gather(gain_one, gain_two, *weights):
        down = weights[-1]
        rows, wide = down.shape
        gains = jnp.zeros((8, 128), jnp.float32)
        gains = gains.at[0, : gain_one.shape[0]].set(gain_one.astype(jnp.float32))
        gains = gains.at[1, : gain_two.shape[0]].set(gain_two.astype(jnp.float32))
        down = down.reshape(rows, 2, wide // 2).transpose(1, 0, 2).reshape(2 * rows, wide // 2)
        fulls = gather_all(mesh, (gains,) + weights[:-1] + (down,))
        gains_full = fulls[0].reshape(-1, 8, 128)
        ones = gains_full[:, 0, : gain_one.shape[0]].reshape(-1).astype(jnp.bfloat16)
        twos = gains_full[:, 1, : gain_two.shape[0]].reshape(-1).astype(jnp.bfloat16)
        whole = [f.reshape(-1, f.shape[-1]) for f in fulls[1:-1]]
        down = fulls[-1].reshape(-1, 2, rows, wide // 2).transpose(0, 2, 1, 3)
        return (ones, twos) + tuple(whole) + (down.reshape(-1, wide),)

    return gather


def linked_reduce(mesh):
    lead = (2, 2, mesh.shape["fsdp"] // 2, 2)
    count = mesh.size

    def reduce(gain_one, gain_two, *terms):
        each = gain_one.shape[0] // count
        gains = jnp.zeros((count, 8, 128), jnp.float32)
        gains = gains.at[:, 0, :each].set(gain_one.reshape(count, each))
        gains = gains.at[:, 1, :each].set(gain_two.reshape(count, each))
        low = [t.astype(jnp.bfloat16) for t in terms]
        parts = [t.reshape(lead + (t.shape[0] // count, t.shape[1])) for t in low[:-1]]
        rows, wide = low[-1].shape[0] // count, low[-1].shape[1]
        down = low[-1].reshape(count, rows, 2, wide // 2).transpose(0, 2, 1, 3)
        down = down.reshape(lead + (2 * rows, wide // 2))
        outs = reduce_all(mesh, [gains.reshape(lead + (8, 128))] + parts + [down])
        down = outs[-1].reshape(2, rows, wide // 2).transpose(1, 0, 2).reshape(rows, wide)
        return (outs[0][0, :each], outs[0][1, :each]) + tuple(outs[1:-1]) + (down,)

    return reduce


def solution(mesh):
    in_specs = (
        P(("dp", "fsdp"), None, None),
        P(("dp", "fsdp")),
        P(("dp", "fsdp"), None),
        P(("dp", "fsdp"), None),
        P(("dp", "fsdp")),
        P(("dp", "fsdp"), None),
        P(("dp", "fsdp"), None),
        P(("dp", "fsdp"), None),
        P(("dp", "fsdp"), None),
        P(("dp", "fsdp")),
        P(("dp", "fsdp"), None),
        P(("dp", "fsdp"), None),
        P(("dp", "fsdp"), None),
        P(("dp", "fsdp"), None, None),
        P(("dp", "fsdp"), None, None),
    )
    out_specs = (
        P(("dp", "fsdp"), None, None),
        P(("dp", "fsdp"), None, None),
        P(("dp", "fsdp"), None, None),
        P(("dp", "fsdp")),
        P(("dp", "fsdp"), None),
        P(("dp", "fsdp"), None),
        P(("dp", "fsdp"), None),
        P(("dp", "fsdp"), None),
        P(("dp", "fsdp")),
        P(("dp", "fsdp"), None),
        P(("dp", "fsdp"), None),
        P(("dp", "fsdp"), None),
    )
    if dict(mesh.shape) == {"dp": 4, "fsdp": 8}:
        sets = (linked_gather(mesh), linked_reduce(mesh))
    else:
        sets = (plain_gather, plain_reduce)

    def shards(*args):
        return layer(*sets, *args)

    return jax.shard_map(shards, mesh=mesh, in_specs=in_specs, out_specs=out_specs, check_vma=False)
```

```python
import math

import jax
import jax.numpy as jnp
import numpy as np
from jax import lax
from jax.experimental import pallas as pl
from jax.experimental.pallas import tpu as pltpu
from jax.sharding import PartitionSpec as P

HD = 64
MESH = pl.DeviceIdType.MESH
BOTH = ("dp", "fsdp")

eps = 1e-06


class Place:
    def __init__(self, depth):
        dp, fsdp = lax.axis_index("dp"), lax.axis_index("fsdp")
        self.x, self.c = dp // 2, dp % 2
        self.z, self.y = fsdp // 2, fsdp % 2
        self.depth = depth

    def at(self, x, c, z, y):
        return (x * 2 + c, z * 2 + y)

    def across_x(self):
        return self.at(1 - self.x, self.c, self.z, self.y)

    def across_y(self):
        return self.at(self.x, self.c, self.z, 1 - self.y)

    def sibling(self):
        return self.at(self.x, 1 - self.c, self.z, self.y)

    def above(self):
        return self.at(self.x, self.c, self.z + 1, self.y)

    def below(self):
        return self.at(self.x, self.c, self.z - 1, self.y)

    def greet(self):
        barrier = pltpu.get_barrier_semaphore()

        def call(who):
            pl.semaphore_signal(barrier, inc=1, device_id=who, device_id_type=MESH)

        call(self.across_x())
        call(self.across_y())
        call(self.sibling())
        not_top = self.z < self.depth - 1
        not_low = self.z > 0
        pl.when(not_top)(lambda: call(self.above()))
        pl.when(not_low)(lambda: call(self.below()))
        peers = 3 + not_top.astype(jnp.int32) + not_low.astype(jnp.int32)
        pl.semaphore_wait(barrier, peers)


def remote(src, dst, send_sem, recv_sem, who):
    return pltpu.make_async_remote_copy(
        src_ref=src,
        dst_ref=dst,
        send_sem=send_sem,
        recv_sem=recv_sem,
        device_id=who,
        device_id_type=MESH,
    )


class Gather:
    def __init__(self, place, own, full, sems, order):
        self.p, self.own, self.full, self.sems, self.order = place, own, full, sems, order
        self.wide = full.shape[-1]

    def shard(self, x, y, z):
        return self.full.at[x, self.p.c, z, y]

    def zunit(self, z):
        if self.order == "zr":
            return self.full.at[self.p.x, self.p.c, z, self.p.y]
        return self.full.at[:, self.p.c, z]

    def runit(self, x, y, half=None):
        if self.order == "zr":
            if half is None:
                return self.full.at[x, self.p.c, :, y]
            count = self.p.depth // 2
            return self.full.at[x, self.p.c, half * count : (half + 1) * count, y]
        if half is None:
            return self.full.at[x, self.p.c, self.p.z, y]
        count = self.wide // 2
        return self.full.at[x, self.p.c, self.p.z, y, :, half * count : (half + 1) * count]

    def copy(self, ref, slot, who, src=None):
        return remote(ref if src is None else src, ref, self.sems.at[0, slot], self.sems.at[1, slot], who)

    def up(self, unit, src=None):
        return self.copy(self.zunit(unit), unit, self.p.above(), src)

    def down(self, unit, src=None):
        return self.copy(self.zunit(unit), self.p.depth + unit, self.p.below(), src)

    def place_own(self):
        p = self.p
        self.local = pltpu.make_async_copy(self.own, self.shard(p.x, p.y, p.z), self.sems.at[0, 22])
        self.local.start()

    def z_step(self, step):
        p = self.p
        top, low = p.depth - 1, 0
        src = self.own if (step == 0 and self.order == "zr") else None

        def from_below():
            if step > 0:
                self.up(p.z - step).wait_recv()
            pl.when(p.z < top)(lambda: self.up(p.z - step, src).start())

        def from_above():
            if step > 0:
                self.down(p.z + step).wait_recv()
            pl.when(p.z > low)(lambda: self.down(p.z + step, src).start())

        pl.when(p.z - step >= low)(from_below)
        pl.when(p.z + step <= top)(from_above)

    def ring_first(self):
        p, base = self.p, 2 * self.p.depth
        mine = self.runit(p.x, p.y)
        src = self.own if self.order == "rz" else None
        self.copy(mine, base, p.across_x(), src).start()
        self.copy(mine, base + 1, p.across_y(), src).start()

    def ring_second(self):
        p, base = self.p, 2 * self.p.depth
        from_x, from_y = self.runit(1 - p.x, p.y), self.runit(p.x, 1 - p.y)
        self.copy(from_x, base, p.across_x()).wait_recv()
        self.copy(self.runit(1 - p.x, p.y, 0), base + 2, p.across_y()).start()
        self.copy(from_y, base + 1, p.across_y()).wait_recv()
        self.copy(self.runit(p.x, 1 - p.y, 1), base + 3, p.across_x()).start()

    def ring_last(self):
        p, base = self.p, 2 * self.p.depth
        self.copy(self.runit(1 - p.x, 1 - p.y, 0), base + 2, p.across_y()).wait_recv()
        self.copy(self.runit(1 - p.x, 1 - p.y, 1), base + 3, p.across_x()).wait_recv()

    def give(self, ref, slot):
        self.copy(ref, 2 * self.p.depth + 4 + slot, self.p.sibling()).start()

    def sib_ref(self, kind):
        p, c = self.p, 1 - self.p.c
        if self.order == "zr":
            x = (p.x, 1 - p.x, p.x, 1 - p.x)[kind]
            y = (p.y, p.y, 1 - p.y, 1 - p.y)[kind]
            return self.full.at[x, c, :, y]
        return self.full.at[:, c, kind]

    def my_ref(self, kind):
        p, c = self.p, self.p.c
        if self.order == "zr":
            x = (p.x, 1 - p.x, p.x, 1 - p.x)[kind]
            y = (p.y, p.y, 1 - p.y, 1 - p.y)[kind]
            return self.full.at[x, c, :, y]
        return self.full.at[:, c, kind]

    def steps(self):
        p = self.p
        if self.order == "zr":
            return [
                lambda: (self.place_own(), self.z_step(0)),
                lambda: self.z_step(1),
                lambda: self.z_step(2),
                lambda: (self.z_step(3), self.local.wait(), self.ring_first(), self.give(self.my_ref(0), 0)),
                lambda: (self.ring_second(), self.give(self.my_ref(1), 1), self.give(self.my_ref(2), 2)),
                lambda: (self.ring_last(), self.give(self.my_ref(3), 3)),
                lambda: self.finish(),
            ]

        def pass_on(step):
            def low():
                self.give(self.full.at[:, p.c, p.z - step], p.z - step)

            def high():
                self.give(self.full.at[:, p.c, p.z + step], p.z + step)

            pl.when(p.z - step >= 0)(low)
            if step > 0:
                pl.when(p.z + step <= p.depth - 1)(high)

        return [
            lambda: (self.place_own(), self.ring_first()),
            lambda: self.ring_second(),
            lambda: (self.ring_last(), self.local.wait(), self.z_step(0), pass_on(0)),
            lambda: (self.z_step(1), pass_on(1)),
            lambda: (self.z_step(2), pass_on(2)),
            lambda: (self.z_step(3), pass_on(3)),
            lambda: self.finish(),
        ]

    def finish(self):
        p, base = self.p, 2 * self.p.depth
        for kind in range(4):
            self.copy(self.sib_ref(kind), base + 4 + kind, p.sibling()).wait_recv()
        top = p.depth - 1
        for unit in range(p.depth):
            pl.when((p.z < top) & (unit <= p.z))(lambda unit=unit: self.up(unit).wait_send())
            pl.when((p.z > 0) & (unit >= p.z))(lambda unit=unit: self.down(unit).wait_send())
        self.copy(self.runit(p.x, p.y), base, p.across_x()).wait_send()
        self.copy(self.runit(p.x, p.y), base + 1, p.across_y()).wait_send()
        self.copy(self.runit(1 - p.x, p.y, 0), base + 2, p.across_y()).wait_send()
        self.copy(self.runit(p.x, 1 - p.y, 1), base + 3, p.across_x()).wait_send()
        for kind in range(4):
            self.copy(self.my_ref(kind), base + 4 + kind, p.sibling()).wait_send()


WIDE = 256


def iota(shape, dim):
    return lax.broadcasted_iota(jnp.int32, shape, dim)


def to_column(row):
    n = row.shape[1]
    eye = iota((n, n), 0) == iota((n, n), 1)
    return jnp.sum(jnp.where(eye, jnp.broadcast_to(row, (n, n)), 0.0), axis=1, keepdims=True)


def dot(a, b, dims=((1,), (0,))):
    return lax.dot_general(a, b, (dims, ((), ())), preferred_element_type=jnp.float32)


def turn(values, cosine, sines):
    outs = []
    first = iota((values.shape[0], 128), 1) % HD < HD // 2
    for g in range(values.shape[1] // 128):
        part = values[:, g * 128 : (g + 1) * 128]
        other = jnp.where(
            first, pltpu.roll(part, 128 - HD // 2, 1), pltpu.roll(part, HD // 2, 1)
        )
        outs.append(part * cosine + other * sines)
    return jnp.concatenate(outs, axis=1)


def gain_row(gains, row, each):
    count = gains.shape[0]
    rows = gains[:, row, :]
    whole = jnp.concatenate([rows] * (count * each // 128), axis=1)
    shape = whole.shape
    keep = iota(shape, 1) // each == iota(shape, 0)
    return jnp.sum(jnp.where(keep, whole, 0.0), axis=0, keepdims=True)


class Forward:
    def __init__(self, place, refs):
        self.p = place
        self.__dict__.update(refs)
        self.slots, self.length = self.segments.shape
        self.rows = self.slots * self.length

    def load(self, name, cols=None):
        full, dst = getattr(self, name + "_full"), getattr(self, name + "_v")
        slot = self.load_slots[(name, cols)]
        if cols is not None:
            lo, hi = cols
            full, dst = full.at[:, :, :, :, :, lo:hi], dst.at[:, :, :, :, :, lo:hi]
        return pltpu.make_async_copy(full, dst, self.load_sems.at[slot])

    def save(self, name):
        slot = self.save_slots[name]
        return pltpu.make_async_copy(
            getattr(self, name + "_v"), getattr(self, name + "_out"), self.save_sems.at[slot]
        )

    def tables(self):
        for b in range(self.slots):
            rows = pl.ds(b * self.length, self.length)
            angles = to_column(self.positions[b : b + 1, :].astype(jnp.float32)) * self.inverse[...]
            first = iota(angles.shape, 1) % HD < HD // 2
            sines = jnp.sin(angles)
            self.cos_v[rows, :] = jnp.cos(angles)
            self.sin_v[rows, :] = jnp.where(first, -sines, sines)
            seg = self.segments[b : b + 1, :].astype(jnp.float32)
            shape = (self.length, self.length)
            allowed = (to_column(seg) == seg) & (iota(shape, 0) >= iota(shape, 1))
            self.bias_v[b] = jnp.where(allowed, 0.0, -1e30)
        self.save("cos").start()
        self.save("sin").start()

    def gains(self):
        pltpu.make_async_copy(self.g_full, self.g_v, self.load_sems.at[0]).start()
        pltpu.make_async_copy(self.g_full, self.g_v, self.load_sems.at[0]).wait()
        count = math.prod(self.g_v.shape[:4])
        gains = self.g_v[...].reshape(count, 8, 128)
        each = self.width // count
        self.gain_v[0:1, :] = gain_row(gains, 0, each)
        self.gain_v[1:2, :] = gain_row(gains, 1, each)

    def norm_one(self):
        for b in range(self.slots):
            rows = pl.ds(b * self.length, self.length)
            inputs = self.tokens[rows, :].astype(jnp.float32)
            scale = lax.rsqrt(jnp.mean(inputs * inputs, axis=-1, keepdims=True) + eps)
            normed = (inputs * scale * self.gain_v[0:1, :]).astype(jnp.bfloat16)
            self.normed_v[rows, :] = normed
            self.normed_t_v[:, rows] = normed.T
        self.save("normed_t").start()

    def weight(self, name, cols):
        w = getattr(self, name + "_v")[:, :, :, :, :, cols]
        return w.reshape(math.prod(w.shape[:5]), w.shape[5])

    def project(self, name):
        self.load(name).wait()
        normed = self.normed_v[...]

        def tile(n, carry):
            cols = pl.ds(pl.multiple_of(n * WIDE, WIDE), WIDE)
            got = dot(normed, self.weight(name, cols))
            if name == "v":
                low = got.astype(jnp.bfloat16)
                self.v_low_v[:, cols] = low
                self.first_v[:, cols] = (self.live_v[...][:, 0:1] * low.astype(jnp.float32)).astype(jnp.bfloat16)
            else:
                turned = turn(got, self.cos_v[...], self.sin_v[...])
                getattr(self, name + "_rot_v")[:, cols] = turned.astype(jnp.bfloat16)
            return carry

        lax.fori_loop(0, self.width // WIDE, tile, 0)
        if name == "v":
            self.save("v_low").start()
            self.save("first").start()
        else:
            self.save(name + "_rot").start()

    def live(self):
        index = iota((self.rows, 128), 0) // self.length
        self.live_v[...] = (index < self.counts[0]).astype(jnp.float32)

    def attend(self, b):
        length = self.length
        rows = pl.ds(b * length, length)

        def pair(h, carry):
            cols = pl.ds(pl.multiple_of(h * 128, 128), 128)
            q, k, v = self.q_rot_v[rows, cols], self.k_rot_v[rows, cols], self.v_low_v[rows, cols]
            k2, v2 = split_pair(k), split_pair(v)
            scores = dot(q, k2, ((1,), (1,))) * HD ** (-0.5)
            bias = self.bias_v[b]
            probs = []
            for half in range(2):
                s = scores[:, half * length : (half + 1) * length] + bias
                e = jnp.exp(s - jnp.max(s, axis=-1, keepdims=True))
                probs.append(e * (1.0 / jnp.sum(e, axis=-1, keepdims=True)))
            probs = jnp.concatenate(probs, axis=1).astype(jnp.bfloat16)
            self.probs_v[b, h] = probs
            self.mixed_v[rows, cols] = dot(probs, v2).astype(jnp.bfloat16)
            return carry

        lax.fori_loop(0, self.width // 128, pair, 0)
        self.mixed_t_v[:, rows] = self.mixed_v[rows, :].T
        if b == self.slots - 1:
            self.save("probs").start()
            self.save("mixed_t").start()

    def join(self):
        self.load("o").wait()
        mixed = self.mixed_v[...]

        def tile(n, carry):
            cols = pl.ds(pl.multiple_of(n * WIDE, WIDE), WIDE)
            got = dot(mixed, self.weight("o", cols))
            self.middle_v[:, cols] = self.tokens[:, cols].astype(jnp.float32) + got
            return carry

        lax.fori_loop(0, self.width // WIDE, tile, 0)
        self.save("middle").start()

    def norm_two(self):
        for b in range(self.slots):
            rows = pl.ds(b * self.length, self.length)
            middle = self.middle_v[rows, :]
            scale = lax.rsqrt(jnp.mean(middle * middle, axis=-1, keepdims=True) + eps)
            normed = (middle * scale * self.gain_v[1:2, :]).astype(jnp.bfloat16)
            self.two_v[rows, :] = normed
            self.two_t_v[:, rows] = normed.T
        self.save("two_t").start()

    def hidden(self, part):
        lo, hi = part
        self.load("G", part).wait()
        self.load("U", part).wait()
        two = self.two_v[...]

        def tile(n, carry):
            at = pl.multiple_of(lo + n * WIDE, WIDE)
            cols = pl.ds(at, WIDE)
            gate = dot(two, self.weight("G", cols))
            upward = dot(two, self.weight("U", cols))
            sig = 1.0 / (1.0 + jnp.exp(-gate))
            silu = gate * sig
            low = (silu * upward).astype(jnp.bfloat16)
            self.hid_v[:, cols] = low
            self.hid_t_v[cols, :] = low.T
            self.t1_v[:, cols] = (upward * sig * (1.0 + gate * (1.0 - sig))).astype(jnp.bfloat16)
            self.t2_v[:, cols] = silu.astype(jnp.bfloat16)
            return carry

        lax.fori_loop(0, (hi - lo) // WIDE, tile, 0)

    def hidden_saves(self):
        for name in ("hid", "hid_t", "t1", "t2"):
            self.save(name).start()

    def finish(self):
        for name in self.save_slots:
            self.save(name).wait()


def split_pair(values):
    first = iota(values.shape, 1) < HD
    zero = jnp.zeros_like(values)
    return jnp.concatenate([jnp.where(first, values, zero), jnp.where(first, zero, values)], axis=0)


GATHER_JOBS = (
    ("D", "rz", (0, 256), (0, 6, 12, 18, 24, 30, 36)),
    ("g", "zr", None, (1, 4, 7, 10, 14, 18, 20)),
    ("q", "zr", None, (2, 5, 8, 11, 17, 22, 25)),
    ("k", "zr", None, (3, 8, 12, 16, 24, 30, 32)),
    ("v", "zr", None, (6, 12, 17, 22, 31, 37, 40)),
    ("o", "zr", None, (13, 18, 23, 29, 38, 46, 49)),
    ("G", "zr", (0, 1536), (18, 23, 29, 36, 47, 56, 60)),
    ("D", "rz", (256, 512), (24, 33, 40, 48, 57, 66, 75)),
    ("U", "zr", (0, 1536), (30, 36, 42, 50, 61, 70, 74)),
    ("G", "zr", (1536, 2816), (40, 46, 52, 63, 74, 83, 87)),
    ("U", "zr", (1536, 2816), (50, 56, 62, 76, 87, 96, 100)),
)
FORWARD_STEPS = (
    ("tables", (), 2.5),
    ("live", (), 2.6),
    ("gains", (), 20.5),
    ("norm_one", (), 20.6),
    ("load", ("q",), 25.1),
    ("project", ("q",), 25.2),
    ("load", ("k",), 32.1),
    ("project", ("k",), 32.2),
    ("load", ("v",), 40.1),
    ("project", ("v",), 40.2),
    ("attend", (0,), 45),
    ("attend", (1,), 48.5),
    ("load", ("o",), 49.2),
    ("attend", (2,), 52),
    ("attend", (3,), 55),
    ("join", (), 58),
    ("norm_two", (), 62),
    ("load", ("G", (0, 1536)), 60.1),
    ("load", ("U", (0, 1536)), 74.1),
    ("hidden", ((0, 1536),), 75.5),
    ("load", ("G", (1536, 2816)), 87.1),
    ("load", ("U", (1536, 2816)), 100.1),
    ("hidden", ((1536, 2816),), 100.2),
    ("hidden_saves", (), 100.3),
)
OWNS = ("g", "q", "k", "v", "o", "G", "U", "D")
SAVED = (
    "cos", "sin", "normed_t", "q_rot", "k_rot", "v_low", "first", "probs",
    "mixed_t", "middle", "two_t", "hid", "hid_t", "t1", "t2",
)


def forward_kernel(depth, *refs):
    refs = list(refs)

    def take(names):
        return {name: refs.pop(0) for name in names}

    plain = take(("tokens", "counts", "segments", "positions", "inverse"))
    owns = take(OWNS)
    fulls = take([n + "_full" for n in OWNS])
    outs = take([n + "_out" for n in SAVED])
    held = take([n + "_v" for n in SAVED])
    weights = take([n + "_v" for n in OWNS[:-1]])
    rest = take(("gain_v", "normed_v", "mixed_v", "two_v", "bias_v", "live_v"))
    sems = take(("gather_sems", "load_sems", "save_sems"))
    place = Place(depth)
    work = Forward(place, {**plain, **fulls, **outs, **held, **weights, **rest, **sems})
    work.width = held["middle_v"].shape[1]
    loads = [(args[0], args[1] if len(args) > 1 else None) for name, args, _ in FORWARD_STEPS if name == "load"]
    work.load_slots = {key: 1 + i for i, key in enumerate(loads)}
    work.save_slots = {name: i for i, name in enumerate(SAVED)}
    order = []
    for i, (name, way, cols, times) in enumerate(GATHER_JOBS):
        own, full = owns[name], fulls[name + "_full"]
        wide = full.shape[-1]
        if cols is not None:
            own, full = own.at[:, cols[0] : cols[1]], full.at[:, :, :, :, :, cols[0] : cols[1]]
            wide = cols[1] - cols[0]
        job = Gather(place, own, full, sems["gather_sems"].at[i], way)
        job.wide = wide
        order += list(zip(times, job.steps()))

    def step(name, args):
        if name == "load":
            return lambda: work.load(*args).start()
        return lambda: getattr(work, name)(*args)

    order += [(time, step(name, args)) for name, args, time in FORWARD_STEPS]
    place.greet()
    for _, action in sorted(order, key=lambda e: e[0]):
        action()
    work.finish()


def forward(mesh, tokens, counts, segments, positions, owns):
    depth = mesh.shape["fsdp"] // 2
    slots, length, width = tokens.shape
    rows, low, full = slots * length, jnp.bfloat16, jnp.float32
    hidden = owns["G"].shape[1]
    lead = (2, 2, depth, 2)
    saved = {
        "cos": ((rows, 128), full),
        "sin": ((rows, 128), full),
        "normed_t": ((width, rows), low),
        "q_rot": ((rows, width), low),
        "k_rot": ((rows, width), low),
        "v_low": ((rows, width), low),
        "first": ((rows, width), low),
        "probs": ((slots, width // 128, length, 2 * length), low),
        "mixed_t": ((width, rows), low),
        "middle": ((rows, width), full),
        "two_t": ((width, rows), low),
        "hid": ((rows, hidden), low),
        "hid_t": ((hidden, rows), low),
        "t1": ((rows, hidden), low),
        "t2": ((rows, hidden), low),
    }
    inverse = jnp.asarray(
        np.exp((np.arange(128) % (HD // 2)) * (-2.0 * math.log(10000.0) / HD)), jnp.float32
    )[None, :]
    vmem, anywhere = pl.BlockSpec(memory_space=pltpu.VMEM), pl.BlockSpec(memory_space=pl.ANY)
    smem = pl.BlockSpec(memory_space=pltpu.SMEM)
    fulls = [jax.ShapeDtypeStruct(lead + owns[n].shape, owns[n].dtype) for n in OWNS]
    outs = [jax.ShapeDtypeStruct(*saved[n]) for n in SAVED]
    got = pl.pallas_call(
        lambda *refs: forward_kernel(depth, *refs),
        out_shape=tuple(fulls + outs),
        in_specs=[vmem, smem, vmem, vmem, vmem] + [anywhere] * len(OWNS),
        out_specs=tuple([anywhere] * (len(OWNS) + len(SAVED))),
        scratch_shapes=[pltpu.VMEM(*saved[n]) for n in SAVED]
        + [pltpu.VMEM(lead + owns[n].shape, owns[n].dtype) for n in OWNS[:-1]]
        + [
            pltpu.VMEM((8, width), full),
            pltpu.VMEM((rows, width), low),
            pltpu.VMEM((rows, width), low),
            pltpu.VMEM((rows, width), low),
            pltpu.VMEM((slots, length, length), full),
            pltpu.VMEM((rows, 128), full),
            pltpu.SemaphoreType.DMA((len(GATHER_JOBS), 2, 24)),
            pltpu.SemaphoreType.DMA((16,)),
            pltpu.SemaphoreType.DMA((len(SAVED),)),
        ],
        compiler_params=pltpu.CompilerParams(
            collective_id=1, has_side_effects=True, vmem_limit_bytes=60 * 2**20
        ),
        cost_estimate=pl.CostEstimate(
            flops=2 * rows * width * (4 * width + 2 * hidden), bytes_accessed=80 * 2**20, transcendentals=2**22
        ),
        name="gather_and_forward",
    )(tokens.reshape(rows, width), counts, segments, positions, inverse, *[owns[n] for n in OWNS])
    names = [n + "_full" for n in OWNS] + list(SAVED)
    return dict(zip(names, got))


class Reduce:
    def __init__(self, place, part, out, bufs, sems):
        self.p, self.part, self.out, self.sems = place, part, out, sems
        self.acc, self.sib, self.ring1, self.ring2, self.zed = bufs

    def copy(self, src, dst, slot, who):
        return remote(src, dst, self.sems.at[0, slot], self.sems.at[1, slot], who)

    def sib_copy(self):
        p = self.p
        return self.copy(self.part.at[:, 1 - p.c], self.sib, 0, p.sibling())

    def own_copy(self):
        return pltpu.make_async_copy(self.part.at[:, self.p.c], self.acc, self.sems.at[0, 1])

    def start(self):
        self.sib_copy().start()
        self.own_copy().start()

    def half1(self):
        p, half = self.p, self.p.depth // 2
        by_x = self.copy(self.acc.at[1 - p.x, :half, 1 - p.y], self.ring1.at[0], 2, p.across_x())
        by_y = self.copy(self.acc.at[1 - p.x, half:, 1 - p.y], self.ring1.at[1], 3, p.across_y())
        return by_x, by_y

    def half2(self):
        p = self.p
        to_x = self.copy(self.acc.at[1 - p.x, :, p.y], self.ring2.at[0], 4, p.across_x())
        to_y = self.copy(self.acc.at[p.x, :, 1 - p.y], self.ring2.at[1], 5, p.across_y())
        return to_x, to_y

    def after_sibling(self):
        self.own_copy().wait()
        self.sib_copy().wait_recv()
        p = self.p
        first = (1 - p.x, 1 - p.y)
        self.add_bundle(*first, self.sib)
        for cp in self.half1():
            cp.start()
        for x, y in ((1 - p.x, p.y), (p.x, 1 - p.y), (p.x, p.y)):
            self.add_bundle(x, y, self.sib)

    def add_bundle(self, x, y, other):
        for z in range(self.p.depth):
            self.acc[x, z, y] = self.acc[x, z, y] + other[x, z, y]

    def after_half(self):
        p, half = self.p, self.p.depth // 2
        by_x, by_y = self.half1()
        to_x, to_y = self.half2()
        by_x.wait_recv()
        for z in range(half):
            self.acc[p.x, z, 1 - p.y] = self.acc[p.x, z, 1 - p.y] + self.ring1[0, z]
        to_y.start()
        by_y.wait_recv()
        for z in range(half):
            self.acc[1 - p.x, half + z, p.y] = self.acc[1 - p.x, half + z, p.y] + self.ring1[1, z]
        to_x.start()

    def up(self, unit):
        p = self.p
        return self.copy(self.acc.at[p.x, unit, p.y], self.zed.at[0, unit], 6 + unit, p.above())

    def down(self, unit):
        p = self.p
        return self.copy(self.acc.at[p.x, unit, p.y], self.zed.at[1, unit], 6 + p.depth + unit, p.below())

    def after_ring(self):
        p = self.p
        to_x, to_y = self.half2()
        to_x.wait_recv()
        to_y.wait_recv()
        for z in range(p.depth):
            both = self.ring2[0, z].astype(jnp.float32) + self.ring2[1, z].astype(jnp.float32)
            mine = self.acc[p.x, z, p.y]
            self.acc[p.x, z, p.y] = (mine.astype(jnp.float32) + both).astype(mine.dtype)
        self.z_step(0)

    def z_step(self, step):
        p = self.p
        top = p.depth - 1

        def upward():
            if step > 0:
                for unit in range(step, p.depth):
                    self.up(unit).wait_recv()
                for unit in range(step + 1, p.depth):
                    self.acc[p.x, unit, p.y] = self.acc[p.x, unit, p.y] + self.zed[0, unit]
            if step < top:
                for unit in range(step + 1, p.depth):
                    self.up(unit).start()

        def downward():
            if step > 0:
                for unit in range(0, p.depth - step):
                    self.down(unit).wait_recv()
                for unit in range(0, p.depth - step - 1):
                    self.acc[p.x, unit, p.y] = self.acc[p.x, unit, p.y] + self.zed[1, unit]
            if step < top:
                for unit in range(0, p.depth - step - 1):
                    self.down(unit).start()

        pl.when(p.z == step)(upward)
        pl.when(p.z == top - step)(downward)

    def finish(self):
        p, top = self.p, self.p.depth - 1
        mine = self.acc[p.x, p.z, p.y].astype(jnp.float32)

        @pl.when(p.z == 0)
        def _():
            self.out[...] = mine + self.zed[1, p.z].astype(jnp.float32)

        @pl.when(p.z == top)
        def _():
            self.out[...] = mine + self.zed[0, p.z].astype(jnp.float32)

        @pl.when((p.z > 0) & (p.z < top))
        def _():
            self.out[...] = mine + (
                self.zed[0, p.z].astype(jnp.float32) + self.zed[1, p.z].astype(jnp.float32)
            )

        self.sib_copy().wait_send()
        for cp in self.half1() + self.half2():
            cp.wait_send()
        for unit in range(p.depth):
            if unit > 0:
                pl.when(p.z < unit)(lambda unit=unit: self.up(unit).wait_send())
            if unit < top:
                pl.when(p.z > unit)(lambda unit=unit: self.down(unit).wait_send())

    def steps(self):
        return [
            self.start,
            self.after_sibling,
            self.after_half,
            self.after_ring,
            lambda: self.z_step(1),
            lambda: self.z_step(2),
            lambda: (self.z_step(3), self.finish()),
        ]


def reduce_kernel(depth, count, *refs):
    parts, outs = refs[:count], refs[count : 2 * count]
    bufs = refs[2 * count : 2 * count + 5 * count]
    sems = refs[-1]
    place = Place(depth)
    place.greet()
    jobs = [
        Reduce(place, parts[i], outs[i], bufs[5 * i : 5 * i + 5], sems.at[i]).steps()
        for i in range(count)
    ]
    stages = len(jobs[0])
    for tick in range(count + stages - 1):
        for stage in reversed(range(stages)):
            if 0 <= tick - stage < count:
                jobs[tick - stage][stage]()


def reduce_all(mesh, parts):
    depth = mesh.shape["fsdp"] // 2
    count = len(parts)
    bufs = []
    for part in parts:
        block, kind = part.shape[4:], part.dtype
        bufs += [
            pltpu.VMEM((2, depth, 2) + block, kind),
            pltpu.VMEM((2, depth, 2) + block, kind),
            pltpu.VMEM((2, depth // 2) + block, kind),
            pltpu.VMEM((2, depth) + block, kind),
            pltpu.VMEM((2, depth) + block, kind),
        ]
    return pl.pallas_call(
        lambda *refs: reduce_kernel(depth, count, *refs),
        out_shape=tuple(jax.ShapeDtypeStruct(p.shape[4:], jnp.float32) for p in parts),
        in_specs=[pl.BlockSpec(memory_space=pl.ANY)] * count,
        out_specs=tuple([pl.BlockSpec(memory_space=pltpu.VMEM)] * count),
        scratch_shapes=bufs + [pltpu.SemaphoreType.DMA((count, 2, 16))],
        compiler_params=pltpu.CompilerParams(
            collective_id=2, has_side_effects=True, vmem_limit_bytes=60 * 2**20
        ),
        name="reduce_grads",
    )(*parts)


def rms_scale(values_in):
    return lax.rsqrt(jnp.mean(values_in * values_in, axis=-1, keepdims=True) + eps)


def rotate_table(positions):
    freq_index = jnp.arange(HD // 2, dtype=jnp.float32)
    inverse = jnp.exp(freq_index * (-2.0 * math.log(10000.0) / HD))
    angles = positions.astype(jnp.float32)[..., None] * inverse
    return (jnp.cos(angles), jnp.sin(angles))


def apply_rotary(values_in, cosine, sines):
    half_dim = values_in.shape[-1] // 2
    first_half = values_in[..., :half_dim]
    second_half = values_in[..., half_dim:]
    cosine = cosine[..., None, :]
    sines = sines[..., None, :]
    return jnp.concatenate(
        [first_half * cosine - second_half * sines, second_half * cosine + first_half * sines],
        axis=-1,
    )


def matmul(left_arg, right_arg):
    return jnp.dot(left_arg, right_arg, preferred_element_type=jnp.float32)


def stack_groups(values_in):
    row_count, model_width = values_in.shape
    return values_in.reshape(row_count, model_width // (4 * HD), 4 * HD).transpose(1, 0, 2)


def unstack_groups(values_in):
    group_count, row_count, group_width = values_in.shape
    return values_in.transpose(1, 0, 2).reshape(row_count, group_count * group_width)


def head_scores(query_grp, key_grp, allowed):
    row_count = query_grp.shape[0]
    query_heads = query_grp.reshape(row_count, 4, HD)
    key_heads = key_grp.reshape(row_count, 4, HD)
    scores = jnp.einsum(
        "qhe,khe->hqk", query_heads, key_heads, preferred_element_type=jnp.float32
    ) * HD ** (-0.5)
    return jnp.where(allowed[None], scores, -1e30)


def norm_back(grad_normed, inputs_f, scale_rows, gain_row):
    gain_term = jnp.sum(grad_normed * inputs_f * scale_rows, axis=0)
    scaled = grad_normed * gain_row
    grad_inputs = scale_rows * (
        scaled
        - inputs_f * scale_rows * scale_rows * jnp.mean(scaled * inputs_f, axis=-1, keepdims=True)
    )
    return (grad_inputs, gain_term)


def layer(
    gather_set,
    reduce_set,
    tokens,
    seq_counts,
    segments,
    positions,
    norm_first,
    query_weight,
    key_weight,
    value_weight,
    output_weight,
    norm_second,
    gate_weight,
    up_weight,
    down_weight,
    out_cotangent,
    value_cotangent,
):
    slot_count, seq_length, model_width = tokens.shape
    row_count = slot_count * seq_length
    head_count = model_width // HD
    weights = gather_set(
        norm_first,
        norm_second,
        query_weight,
        key_weight,
        value_weight,
        output_weight,
        gate_weight,
        up_weight,
        down_weight,
    )
    gain_one, gain_two, query_full, key_full, value_full, output_full = weights[:6]
    gate_full, up_full, down_full = weights[6:]
    row_index = jnp.arange(row_count, dtype=jnp.int32)
    slot_index = row_index // seq_length
    live_rows = (slot_index < seq_counts[0]).astype(jnp.float32)[:, None]
    flat_segments = segments.reshape(row_count)
    allowed = (
        (slot_index[:, None] == slot_index[None, :])
        & (flat_segments[:, None] == flat_segments[None, :])
        & (row_index[:, None] >= row_index[None, :])
    )
    inputs_f = tokens.reshape(row_count, model_width).astype(jnp.float32)
    scale_one = rms_scale(inputs_f)
    normed = (inputs_f * scale_one * gain_one.astype(jnp.float32)).astype(jnp.bfloat16)
    cosine, sines = rotate_table(positions.reshape(row_count))

    def rotated(values_in, turn_sign):
        turned = apply_rotary(
            values_in.reshape(row_count, head_count, HD), cosine, turn_sign * sines
        )
        return turned.reshape(row_count, model_width).astype(jnp.bfloat16)

    query_rot = rotated(matmul(normed, query_full), 1.0)
    key_rot = rotated(matmul(normed, key_full), 1.0)
    value_low = matmul(normed, value_full).astype(jnp.bfloat16)

    def attend_group(operands):
        query_grp, key_grp, value_grp = operands
        scores = head_scores(query_grp, key_grp, allowed)
        row_max = jnp.max(scores, axis=-1, keepdims=True)
        log_total = row_max + jnp.log(jnp.sum(jnp.exp(scores - row_max), axis=-1, keepdims=True))
        probs_low = jnp.exp(scores - log_total).astype(jnp.bfloat16)
        value_heads = value_grp.reshape(row_count, 4, HD)
        mixed_heads = jnp.einsum(
            "hqk,khe->qhe", probs_low, value_heads, preferred_element_type=jnp.float32
        )
        return (mixed_heads.reshape(row_count, 4 * HD), log_total)

    query_groups = stack_groups(query_rot)
    key_groups = stack_groups(key_rot)
    value_groups = stack_groups(value_low)
    mixed_groups, log_totals = lax.map(attend_group, (query_groups, key_groups, value_groups))
    mixed_low = unstack_groups(mixed_groups).astype(jnp.bfloat16)
    middle = inputs_f + matmul(mixed_low, output_full)
    scale_two = rms_scale(middle)
    normed_two = (middle * scale_two * gain_two.astype(jnp.float32)).astype(jnp.bfloat16)
    gate_pre = matmul(normed_two, gate_full)
    upward = matmul(normed_two, up_full)
    sigmoid_gate = jax.nn.sigmoid(gate_pre)
    silu_gate = gate_pre * sigmoid_gate
    hidden = (silu_gate * upward).astype(jnp.bfloat16)
    block_out = (live_rows * (middle + matmul(hidden, down_full))).astype(jnp.bfloat16)
    first_values = (live_rows * value_low.astype(jnp.float32)).astype(jnp.bfloat16)
    grad_y = live_rows * out_cotangent.reshape(row_count, model_width).astype(jnp.float32)
    grad_branch = grad_y.astype(jnp.bfloat16)
    down_term = jnp.einsum("rf,rd->fd", hidden, grad_branch, preferred_element_type=jnp.float32)
    grad_hidden = jnp.einsum(
        "rd,fd->rf", grad_branch, down_full, preferred_element_type=jnp.float32
    )
    grad_gate = (
        grad_hidden * upward * sigmoid_gate * (1.0 + gate_pre * (1.0 - sigmoid_gate))
    ).astype(jnp.bfloat16)
    grad_up = (grad_hidden * silu_gate).astype(jnp.bfloat16)
    gate_term = jnp.einsum("rd,rf->df", normed_two, grad_gate, preferred_element_type=jnp.float32)
    up_term = jnp.einsum("rd,rf->df", normed_two, grad_up, preferred_element_type=jnp.float32)
    grad_normed_two = jnp.einsum(
        "rf,df->rd", grad_gate, gate_full, preferred_element_type=jnp.float32
    ) + jnp.einsum("rf,df->rd", grad_up, up_full, preferred_element_type=jnp.float32)
    grad_middle_norm, gain_two_term = norm_back(
        grad_normed_two, middle, scale_two, gain_two.astype(jnp.float32)
    )
    grad_middle = grad_y + grad_middle_norm
    grad_attended = grad_middle.astype(jnp.bfloat16)
    output_term = jnp.einsum(
        "rd,re->de", mixed_low, grad_attended, preferred_element_type=jnp.float32
    )
    grad_mixed = jnp.einsum(
        "re,de->rd", grad_attended, output_full, preferred_element_type=jnp.float32
    ).astype(jnp.bfloat16)

    def attend_back(operands):
        query_grp, key_grp, value_grp, grad_grp, log_total = operands
        scores = head_scores(query_grp, key_grp, allowed)
        probs_full = jnp.exp(scores - log_total)
        probs_low = probs_full.astype(jnp.bfloat16)
        grad_heads = grad_grp.reshape(row_count, 4, HD)
        value_heads = value_grp.reshape(row_count, 4, HD)
        query_heads = query_grp.reshape(row_count, 4, HD)
        key_heads = key_grp.reshape(row_count, 4, HD)
        grad_probs = jnp.einsum(
            "qhe,khe->hqk", grad_heads, value_heads, preferred_element_type=jnp.float32
        )
        row_term = jnp.sum(probs_full * grad_probs, axis=-1, keepdims=True)
        grad_scores = (probs_full * (grad_probs - row_term)).astype(jnp.bfloat16)
        score_scale = HD ** (-0.5)
        grad_query = (
            jnp.einsum("hqk,khe->qhe", grad_scores, key_heads, preferred_element_type=jnp.float32)
            * score_scale
        )
        grad_key = (
            jnp.einsum("hqk,qhe->khe", grad_scores, query_heads, preferred_element_type=jnp.float32)
            * score_scale
        )
        grad_value = jnp.einsum(
            "hqk,qhe->khe", probs_low, grad_heads, preferred_element_type=jnp.float32
        )
        group_width = 4 * HD
        return (
            grad_query.reshape(row_count, group_width),
            grad_key.reshape(row_count, group_width),
            grad_value.reshape(row_count, group_width),
        )

    grad_q_groups, grad_k_groups, grad_v_groups = lax.map(
        attend_back, (query_groups, key_groups, value_groups, stack_groups(grad_mixed), log_totals)
    )
    grad_query = rotated(unstack_groups(grad_q_groups), -1.0)
    grad_key = rotated(unstack_groups(grad_k_groups), -1.0)
    grad_value = (
        unstack_groups(grad_v_groups)
        + live_rows * value_cotangent.reshape(row_count, model_width).astype(jnp.float32)
    ).astype(jnp.bfloat16)
    query_term = jnp.einsum("rd,re->de", normed, grad_query, preferred_element_type=jnp.float32)
    key_term = jnp.einsum("rd,re->de", normed, grad_key, preferred_element_type=jnp.float32)
    value_term = jnp.einsum("rd,re->de", normed, grad_value, preferred_element_type=jnp.float32)
    grad_normed = jnp.einsum(
        "re,de->rd", grad_query, query_full, preferred_element_type=jnp.float32
    )
    grad_normed = grad_normed + jnp.einsum(
        "re,de->rd", grad_key, key_full, preferred_element_type=jnp.float32
    )
    grad_normed = grad_normed + jnp.einsum(
        "re,de->rd", grad_value, value_full, preferred_element_type=jnp.float32
    )
    grad_inputs_norm, gain_one_term = norm_back(
        grad_normed, inputs_f, scale_one, gain_one.astype(jnp.float32)
    )
    token_grad = (grad_middle + grad_inputs_norm).astype(jnp.bfloat16).reshape(tokens.shape)
    grads = reduce_set(
        gain_one_term,
        gain_two_term,
        query_term,
        key_term,
        value_term,
        output_term,
        gate_term,
        up_term,
        down_term,
    )
    return (
        block_out.reshape(tokens.shape),
        first_values.reshape(tokens.shape),
        token_grad,
        grads[0],
        grads[2],
        grads[3],
        grads[4],
        grads[5],
        grads[1],
        grads[6],
        grads[7],
        grads[8],
    )


def plain_gather(*shards_in):
    return tuple(lax.all_gather(s, BOTH, axis=0, tiled=True) for s in shards_in)


def plain_reduce(*terms):
    return tuple(lax.psum_scatter(t, BOTH, scatter_dimension=0, tiled=True) for t in terms)


def linked_reduce(mesh):
    lead = (2, 2, mesh.shape["fsdp"] // 2, 2)
    count = mesh.size

    def reduce(gain_one, gain_two, *terms):
        each = gain_one.shape[0] // count
        gains = jnp.zeros((count, 8, 128), jnp.float32)
        gains = gains.at[:, 0, :each].set(gain_one.reshape(count, each))
        gains = gains.at[:, 1, :each].set(gain_two.reshape(count, each))
        low = [t.astype(jnp.bfloat16) for t in terms]
        parts = [t.reshape(lead + (t.shape[0] // count, t.shape[1])) for t in low[:-1]]
        rows, wide = low[-1].shape[0] // count, low[-1].shape[1]
        down = low[-1].reshape(count, rows, 2, wide // 2).transpose(0, 2, 1, 3)
        down = down.reshape(lead + (2 * rows, wide // 2))
        outs = reduce_all(mesh, [gains.reshape(lead + (8, 128))] + parts + [down])
        down = outs[-1].reshape(2, rows, wide // 2).transpose(1, 0, 2).reshape(rows, wide)
        return (outs[0][0, :each], outs[0][1, :each]) + tuple(outs[1:-1]) + (down,)

    return reduce


def linked_layer(
    mesh,
    tokens,
    seq_counts,
    segments,
    positions,
    norm_first,
    query_weight,
    key_weight,
    value_weight,
    output_weight,
    norm_second,
    gate_weight,
    up_weight,
    down_weight,
    out_cotangent,
    value_cotangent,
):
    slot_count, seq_length, model_width = tokens.shape
    row_count = slot_count * seq_length
    head_count = model_width // HD
    rows, wide = down_weight.shape
    gains = jnp.zeros((8, 128), jnp.float32)
    gains = gains.at[0].set(jnp.tile(norm_first.astype(jnp.float32), 128 // norm_first.shape[0]))
    gains = gains.at[1].set(jnp.tile(norm_second.astype(jnp.float32), 128 // norm_second.shape[0]))
    owns = {
        "g": gains,
        "q": query_weight,
        "k": key_weight,
        "v": value_weight,
        "o": output_weight,
        "G": gate_weight,
        "U": up_weight,
        "D": down_weight.reshape(rows, 2, wide // 2).transpose(1, 0, 2).reshape(2 * rows, wide // 2),
    }
    got = forward(mesh, tokens, seq_counts, segments, positions, owns)
    whole = [got[n + "_full"].reshape(model_width, -1) for n in "qkvoGU"]
    query_full, key_full, value_full, output_full, gate_full, up_full = whole
    down_full = got["D_full"].reshape(-1, 2, rows, wide // 2).transpose(0, 2, 1, 3).reshape(-1, wide)
    gains_full = got["g_full"].reshape(-1, 8, 128)
    gain_one = gains_full[:, 0, : norm_first.shape[0]].reshape(-1)
    gain_two = gains_full[:, 1, : norm_first.shape[0]].reshape(-1)
    row_index = jnp.arange(row_count, dtype=jnp.int32)
    slot_index = row_index // seq_length
    live_rows = (slot_index < seq_counts[0]).astype(jnp.float32)[:, None]
    flat_segments = segments.reshape(row_count)
    allowed = (
        (slot_index[:, None] == slot_index[None, :])
        & (flat_segments[:, None] == flat_segments[None, :])
        & (row_index[:, None] >= row_index[None, :])
    )
    inputs_f = tokens.reshape(row_count, model_width).astype(jnp.float32)
    scale_one = rms_scale(inputs_f)
    cosine, sines = rotate_table(positions.reshape(row_count))

    def rotated(values_in, turn_sign):
        turned = apply_rotary(
            values_in.reshape(row_count, head_count, HD), cosine, turn_sign * sines
        )
        return turned.reshape(row_count, model_width).astype(jnp.bfloat16)

    normed = got["normed_t"].T
    query_rot, key_rot, value_low = got["q_rot"], got["k_rot"], got["v_low"]
    query_groups = stack_groups(query_rot)
    key_groups = stack_groups(key_rot)
    value_groups = stack_groups(value_low)
    mixed_low = got["mixed_t"].T
    middle = got["middle"]
    scale_two = rms_scale(middle)
    normed_two = got["two_t"].T
    hidden = got["hid"]
    block_out = (live_rows * (middle + matmul(hidden, down_full))).astype(jnp.bfloat16)
    first_values = got["first"]
    probs = got["probs"].reshape(slot_count, model_width // 256, 2, seq_length, 2, seq_length)
    probs = probs.transpose(1, 2, 4, 0, 3, 5).reshape(model_width // 256, 4, slot_count, seq_length, seq_length)
    spread = jnp.zeros((model_width // 256, 4, slot_count, seq_length, slot_count, seq_length), jnp.bfloat16)
    for s in range(slot_count):
        spread = spread.at[:, :, s, :, s].set(probs[:, :, s])
    probs = spread.reshape(model_width // 256, 4, row_count, row_count)
    reduce_set = linked_reduce(mesh)
    grad_y = live_rows * out_cotangent.reshape(row_count, model_width).astype(jnp.float32)
    grad_branch = grad_y.astype(jnp.bfloat16)
    down_term = jnp.einsum("rf,rd->fd", hidden, grad_branch, preferred_element_type=jnp.float32)
    grad_hidden = jnp.einsum(
        "rd,fd->rf", grad_branch, down_full, preferred_element_type=jnp.float32
    )
    grad_gate = (
        grad_hidden * got["t1"].astype(jnp.float32)
    ).astype(jnp.bfloat16)
    grad_up = (grad_hidden * got["t2"].astype(jnp.float32)).astype(jnp.bfloat16)
    gate_term = jnp.einsum("rd,rf->df", normed_two, grad_gate, preferred_element_type=jnp.float32)
    up_term = jnp.einsum("rd,rf->df", normed_two, grad_up, preferred_element_type=jnp.float32)
    grad_normed_two = jnp.einsum(
        "rf,df->rd", grad_gate, gate_full, preferred_element_type=jnp.float32
    ) + jnp.einsum("rf,df->rd", grad_up, up_full, preferred_element_type=jnp.float32)
    grad_middle_norm, gain_two_term = norm_back(
        grad_normed_two, middle, scale_two, gain_two.astype(jnp.float32)
    )
    grad_middle = grad_y + grad_middle_norm
    grad_attended = grad_middle.astype(jnp.bfloat16)
    output_term = jnp.einsum(
        "rd,re->de", mixed_low, grad_attended, preferred_element_type=jnp.float32
    )
    grad_mixed = jnp.einsum(
        "re,de->rd", grad_attended, output_full, preferred_element_type=jnp.float32
    ).astype(jnp.bfloat16)

    def attend_back(operands):
        query_grp, key_grp, value_grp, grad_grp, probs_low = operands
        probs_full = probs_low.astype(jnp.float32)
        grad_heads = grad_grp.reshape(row_count, 4, HD)
        value_heads = value_grp.reshape(row_count, 4, HD)
        query_heads = query_grp.reshape(row_count, 4, HD)
        key_heads = key_grp.reshape(row_count, 4, HD)
        grad_probs = jnp.einsum(
            "qhe,khe->hqk", grad_heads, value_heads, preferred_element_type=jnp.float32
        )
        row_term = jnp.sum(probs_full * grad_probs, axis=-1, keepdims=True)
        grad_scores = (probs_full * (grad_probs - row_term)).astype(jnp.bfloat16)
        score_scale = HD ** (-0.5)
        grad_query = (
            jnp.einsum("hqk,khe->qhe", grad_scores, key_heads, preferred_element_type=jnp.float32)
            * score_scale
        )
        grad_key = (
            jnp.einsum("hqk,qhe->khe", grad_scores, query_heads, preferred_element_type=jnp.float32)
            * score_scale
        )
        grad_value = jnp.einsum(
            "hqk,qhe->khe", probs_low, grad_heads, preferred_element_type=jnp.float32
        )
        group_width = 4 * HD
        return (
            grad_query.reshape(row_count, group_width),
            grad_key.reshape(row_count, group_width),
            grad_value.reshape(row_count, group_width),
        )

    grad_q_groups, grad_k_groups, grad_v_groups = lax.map(
        attend_back, (query_groups, key_groups, value_groups, stack_groups(grad_mixed), probs)
    )
    grad_query = rotated(unstack_groups(grad_q_groups), -1.0)
    grad_key = rotated(unstack_groups(grad_k_groups), -1.0)
    grad_value = (
        unstack_groups(grad_v_groups)
        + live_rows * value_cotangent.reshape(row_count, model_width).astype(jnp.float32)
    ).astype(jnp.bfloat16)
    query_term = jnp.einsum("rd,re->de", normed, grad_query, preferred_element_type=jnp.float32)
    key_term = jnp.einsum("rd,re->de", normed, grad_key, preferred_element_type=jnp.float32)
    value_term = jnp.einsum("rd,re->de", normed, grad_value, preferred_element_type=jnp.float32)
    grad_normed = jnp.einsum(
        "re,de->rd", grad_query, query_full, preferred_element_type=jnp.float32
    )
    grad_normed = grad_normed + jnp.einsum(
        "re,de->rd", grad_key, key_full, preferred_element_type=jnp.float32
    )
    grad_normed = grad_normed + jnp.einsum(
        "re,de->rd", grad_value, value_full, preferred_element_type=jnp.float32
    )
    grad_inputs_norm, gain_one_term = norm_back(
        grad_normed, inputs_f, scale_one, gain_one.astype(jnp.float32)
    )
    token_grad = (grad_middle + grad_inputs_norm).astype(jnp.bfloat16).reshape(tokens.shape)
    grads = reduce_set(
        gain_one_term,
        gain_two_term,
        query_term,
        key_term,
        value_term,
        output_term,
        gate_term,
        up_term,
        down_term,
    )
    return (
        block_out.reshape(tokens.shape),
        first_values.reshape(tokens.shape),
        token_grad,
        grads[0],
        grads[2],
        grads[3],
        grads[4],
        grads[5],
        grads[1],
        grads[6],
        grads[7],
        grads[8],
    )


def solution(mesh):
    in_specs = (
        P(("dp", "fsdp"), None, None),
        P(("dp", "fsdp")),
        P(("dp", "fsdp"), None),
        P(("dp", "fsdp"), None),
        P(("dp", "fsdp")),
        P(("dp", "fsdp"), None),
        P(("dp", "fsdp"), None),
        P(("dp", "fsdp"), None),
        P(("dp", "fsdp"), None),
        P(("dp", "fsdp")),
        P(("dp", "fsdp"), None),
        P(("dp", "fsdp"), None),
        P(("dp", "fsdp"), None),
        P(("dp", "fsdp"), None, None),
        P(("dp", "fsdp"), None, None),
    )
    out_specs = (
        P(("dp", "fsdp"), None, None),
        P(("dp", "fsdp"), None, None),
        P(("dp", "fsdp"), None, None),
        P(("dp", "fsdp")),
        P(("dp", "fsdp"), None),
        P(("dp", "fsdp"), None),
        P(("dp", "fsdp"), None),
        P(("dp", "fsdp"), None),
        P(("dp", "fsdp")),
        P(("dp", "fsdp"), None),
        P(("dp", "fsdp"), None),
        P(("dp", "fsdp"), None),
    )
    if dict(mesh.shape) == {"dp": 4, "fsdp": 8}:
        whole_layer = lambda *args: linked_layer(mesh, *args)
    else:
        whole_layer = lambda *args: layer(plain_gather, plain_reduce, *args)

    def shards(*args):
        return whole_layer(*args)

    return jax.shard_map(shards, mesh=mesh, in_specs=in_specs, out_specs=out_specs, check_vma=False)
```

```python
import math
from typing import Any, NamedTuple

import jax
import jax.numpy as jnp
import numpy as np
from jax import lax
from jax.experimental import pallas as pl
from jax.experimental.pallas import tpu as pltpu
from jax.sharding import PartitionSpec as P

HD = 64
MESH = pl.DeviceIdType.MESH
DP, FSDP = "dp", "fsdp"
BOTH = (DP, FSDP)
LOW, FULL = jnp.bfloat16, jnp.float32
WIDE = 256

eps = 1e-06


class Weights(NamedTuple):
    gains: Any
    query: Any
    key: Any
    value: Any
    output: Any
    gate: Any
    up: Any
    down: Any


class Saved(NamedTuple):
    cos: Any
    sin: Any
    normed_t: Any
    q_rot: Any
    k_rot: Any
    v_low: Any
    probs: Any
    mixed_t: Any
    middle: Any
    two_t: Any
    hid_t: Any
    t1: Any
    t2: Any
    first: Any


W = Weights._make(range(len(Weights._fields)))
S = Saved._make(range(len(Saved._fields)))


class Place:
    def __init__(self, depth):
        dp, fsdp = lax.axis_index(DP), lax.axis_index(FSDP)
        self.x, self.c = dp // 2, dp % 2
        self.z, self.y = fsdp // 2, fsdp % 2
        self.depth = depth

    def at(self, x, c, z, y):
        return (x * 2 + c, z * 2 + y)

    def across_x(self):
        return self.at(1 - self.x, self.c, self.z, self.y)

    def across_y(self):
        return self.at(self.x, self.c, self.z, 1 - self.y)

    def sibling(self):
        return self.at(self.x, 1 - self.c, self.z, self.y)

    def above(self):
        return self.at(self.x, self.c, self.z + 1, self.y)

    def below(self):
        return self.at(self.x, self.c, self.z - 1, self.y)

    def greet(self):
        barrier = pltpu.get_barrier_semaphore()

        def call(who):
            pl.semaphore_signal(barrier, inc=1, device_id=who, device_id_type=MESH)

        call(self.across_x())
        call(self.across_y())
        call(self.sibling())
        not_top = self.z < self.depth - 1
        not_low = self.z > 0
        pl.when(not_top)(lambda: call(self.above()))
        pl.when(not_low)(lambda: call(self.below()))
        peers = 3 + not_top.astype(jnp.int32) + not_low.astype(jnp.int32)
        pl.semaphore_wait(barrier, peers)


def remote(src, dst, send_sem, recv_sem, who):
    return pltpu.make_async_remote_copy(
        src_ref=src,
        dst_ref=dst,
        send_sem=send_sem,
        recv_sem=recv_sem,
        device_id=who,
        device_id_type=MESH,
    )


def iota(shape, dim):
    return lax.broadcasted_iota(jnp.int32, shape, dim)


def dot(a, b, dims=((1,), (0,))):
    return lax.dot_general(a, b, (dims, ((), ())), preferred_element_type=FULL)


def to_column(row):
    n = row.shape[1]
    eye = iota((n, n), 0) == iota((n, n), 1)
    return jnp.sum(jnp.where(eye, jnp.broadcast_to(row, (n, n)), 0.0), axis=1, keepdims=True)


def turn(values, cosine, sines):
    outs = []
    first = iota((values.shape[0], 128), 1) % HD < HD // 2
    for g in range(values.shape[1] // 128):
        part = values[:, g * 128 : (g + 1) * 128]
        other = jnp.where(
            first, pltpu.roll(part, 128 - HD // 2, 1), pltpu.roll(part, HD // 2, 1)
        )
        outs.append(part * cosine + other * sines)
    return jnp.concatenate(outs, axis=1)


def gain_row(gains, row, each):
    count = gains.shape[0]
    rows = gains[:, row, :]
    whole = jnp.concatenate([rows] * (count * each // 128), axis=1)
    shape = whole.shape
    keep = iota(shape, 1) // each == iota(shape, 0)
    return jnp.sum(jnp.where(keep, whole, 0.0), axis=0, keepdims=True)


def split_pair(values):
    first = iota(values.shape, 1) < HD
    zero = jnp.zeros_like(values)
    return jnp.concatenate([jnp.where(first, values, zero), jnp.where(first, zero, values)], axis=0)


class Gather:
    def __init__(self, place, own, full, sends, receipts, local_sem, z_first):
        self.p, self.own, self.full, self.z_first = place, own, full, z_first
        self.sends, self.receipts, self.local_sem = sends, receipts, local_sem
        self.wide = own.shape[-1]

    def shard(self, x, y, z):
        return self.full.at[x, self.p.c, z, y]

    def zunit(self, z):
        if self.z_first:
            return self.full.at[self.p.x, self.p.c, z, self.p.y]
        return self.full.at[:, self.p.c, z]

    def runit(self, x, y, half=None):
        if self.z_first:
            if half is None:
                return self.full.at[x, self.p.c, :, y]
            count = self.p.depth // 2
            return self.full.at[x, self.p.c, half * count : (half + 1) * count, y]
        if half is None:
            return self.full.at[x, self.p.c, self.p.z, y]
        count = self.wide // 2
        return self.full.at[x, self.p.c, self.p.z, y, :, half * count : (half + 1) * count]

    def copy(self, ref, slot, who, src=None):
        return remote(ref if src is None else src, ref, self.sends.at[slot], self.receipts.at[slot], who)

    def up(self, unit, src=None):
        return self.copy(self.zunit(unit), unit, self.p.above(), src)

    def down(self, unit, src=None):
        return self.copy(self.zunit(unit), self.p.depth - 2 + unit, self.p.below(), src)

    def ring_slot(self, i):
        return 2 * (self.p.depth - 1) + i

    def keep_own(self):
        p = self.p
        return pltpu.make_async_copy(self.own, self.shard(p.x, p.y, p.z), self.local_sem)

    def z_step(self, step):
        p = self.p
        top, low = p.depth - 1, 0
        src = self.own if (step == 0 and self.z_first) else None

        def from_below():
            if step > 0:
                self.up(p.z - step).wait_recv()
            if step < top:
                pl.when(p.z < top)(lambda: self.up(p.z - step, src).start())

        def from_above():
            if step > 0:
                self.down(p.z + step).wait_recv()
            if step < top:
                pl.when(p.z > low)(lambda: self.down(p.z + step, src).start())

        pl.when(p.z - step >= low)(from_below)
        pl.when(p.z + step <= top)(from_above)

    def ring_first(self):
        p = self.p
        mine = self.runit(p.x, p.y)
        src = None if self.z_first else self.own
        self.copy(mine, self.ring_slot(0), p.across_x(), src).start()
        self.copy(mine, self.ring_slot(1), p.across_y(), src).start()

    def ring_second(self):
        p = self.p
        from_x, from_y = self.runit(1 - p.x, p.y), self.runit(p.x, 1 - p.y)
        self.copy(from_x, self.ring_slot(0), p.across_x()).wait_recv()
        self.copy(self.runit(1 - p.x, p.y, 0), self.ring_slot(2), p.across_y()).start()
        self.copy(from_y, self.ring_slot(1), p.across_y()).wait_recv()
        self.copy(self.runit(p.x, 1 - p.y, 1), self.ring_slot(3), p.across_x()).start()

    def ring_last(self):
        p = self.p
        self.copy(self.runit(1 - p.x, 1 - p.y, 0), self.ring_slot(2), p.across_y()).wait_recv()
        self.copy(self.runit(1 - p.x, 1 - p.y, 1), self.ring_slot(3), p.across_x()).wait_recv()

    def given(self, kind, core):
        p = self.p
        if self.z_first:
            x = (p.x, 1 - p.x, p.x, 1 - p.x)[kind]
            y = (p.y, p.y, 1 - p.y, 1 - p.y)[kind]
            return self.full.at[x, core, :, y]
        return self.full.at[:, core, kind]

    def give(self, ref, kind):
        self.copy(ref, self.ring_slot(4 + kind), self.p.sibling()).start()

    def pass_on(self, step):
        p = self.p

        def low():
            self.give(self.full.at[:, p.c, p.z - step], p.z - step)

        def high():
            self.give(self.full.at[:, p.c, p.z + step], p.z + step)

        pl.when(p.z - step >= 0)(low)
        if step > 0:
            pl.when(p.z + step <= p.depth - 1)(high)

    def steps(self):
        mine = lambda kind: self.give(self.given(kind, self.p.c), kind)
        if self.z_first:
            return [
                lambda: (self.keep_own().start(), self.z_step(0)),
                lambda: self.z_step(1),
                lambda: self.z_step(2),
                lambda: (self.z_step(3), self.keep_own().wait(), self.ring_first(), mine(0)),
                lambda: (self.ring_second(), mine(1), mine(2)),
                lambda: (self.ring_last(), mine(3)),
                self.finish,
            ]
        return [
            lambda: (self.keep_own().start(), self.ring_first()),
            self.ring_second,
            lambda: (self.ring_last(), self.keep_own().wait(), self.z_step(0), self.pass_on(0)),
            lambda: (self.z_step(1), self.pass_on(1)),
            lambda: (self.z_step(2), self.pass_on(2)),
            lambda: (self.z_step(3), self.pass_on(3)),
            self.finish,
        ]

    def finish(self):
        p = self.p
        for kind in range(4):
            self.copy(self.given(kind, 1 - p.c), self.ring_slot(4 + kind), p.sibling()).wait_recv()

    def sent(self):
        p = self.p
        top = p.depth - 1
        for unit in range(p.depth):
            if unit < top:
                pl.when((p.z < top) & (unit <= p.z))(lambda unit=unit: self.up(unit).wait_send())
            if unit > 0:
                pl.when((p.z > 0) & (unit >= p.z))(lambda unit=unit: self.down(unit).wait_send())
        self.copy(self.runit(p.x, p.y), self.ring_slot(0), p.across_x()).wait_send()
        self.copy(self.runit(p.x, p.y), self.ring_slot(1), p.across_y()).wait_send()
        self.copy(self.runit(1 - p.x, p.y, 0), self.ring_slot(2), p.across_y()).wait_send()
        self.copy(self.runit(p.x, 1 - p.y, 1), self.ring_slot(3), p.across_x()).wait_send()
        for kind in range(4):
            self.copy(self.given(kind, p.c), self.ring_slot(4 + kind), p.sibling()).wait_send()


GATHER_JOBS = (
    (W.gains, True, None),
    (W.query, True, None),
    (W.key, True, None),
    (W.value, True, None),
    (W.output, True, None),
    (W.down, False, (0, 1)),
    (W.down, False, (1, 2)),
    (W.gate, True, (0, 6)),
    (W.up, True, (0, 6)),
    (W.gate, True, (6, 11)),
    (W.up, True, (6, 11)),
)
FORWARD_ORDER = (
    14, 35, 70, 42, 15, 7, 16, 21, 43, 36, 17, 8, 0, 77, 9, 49, 22, 1, 10, 18, 23, 28, 2, 3, 24, 71, 50, 11, 56, 63,
    57, 29, 51, 72, 25, 19, 20, 4, 52, 5, 12, 58, 6, 78, 30, 64, 13, 82, 37, 79, 59, 31, 80, 44, 26, 27, 81, 84, 65,
    53, 83, 85, 60, 32, 45, 86, 66, 38, 73, 87, 54, 88, 61, 62, 94, 33, 55, 93, 34, 90, 46, 89, 91, 67, 92, 39, 47,
    74, 95, 68, 75, 69, 96, 48, 40, 76, 97, 41, 98,
)


class Forward:
    def __init__(self, place, **refs):
        self.p = place
        self.__dict__.update(refs)
        self.slots, self.length = self.segments.shape
        self.rows, self.width = self.slots * self.length, self.v.middle.shape[1]
        self.loads = 0

    def loader(self, which, cols=None):
        full, near = self.full[which], self.near[which]
        if cols is not None:
            cut = slice(*cols)
            full, near = full.at[:, :, :, :, :, cut], near.at[:, :, :, :, :, cut]
        copy = lambda slot=self.loads: pltpu.make_async_copy(full, near, self.load_sems.at[slot])
        self.loads += 1
        return (lambda: copy().start()), (lambda: copy().wait())

    def save(self, *which):
        for i in which:
            pltpu.make_async_copy(self.v[i], self.o[i], self.save_sems.at[i]).start()

    def own_shards(self):
        each = self.norm_first.shape[1]
        spread = (iota((each, 128), 1) % each == iota((each, 128), 0)).astype(LOW)
        sub = iota((8, 128), 0)
        one, two = dot(self.norm_first[...], spread), dot(self.norm_second[...], spread)
        self.own_gains[...] = jnp.where(sub == 0, one, jnp.where(sub == 1, two, 0.0))
        rows, half = self.down_weight.shape[0], self.down_weight.shape[1] // 2
        down = self.down_weight[...].astype(FULL)
        self.own_down[...] = jnp.concatenate([down[:, :half], down[:, half:]], axis=0).astype(LOW)

    def tables(self):
        for b in range(self.slots):
            rows = pl.ds(b * self.length, self.length)
            angles = to_column(self.positions[b : b + 1, :].astype(FULL)) * self.inverse[...]
            first = iota(angles.shape, 1) % HD < HD // 2
            sines = jnp.sin(angles)
            self.v.cos[rows, :] = jnp.cos(angles)
            self.v.sin[rows, :] = jnp.where(first, -sines, sines)
            seg = self.segments[b : b + 1, :].astype(FULL)
            shape = (self.length, self.length)
            allowed = (to_column(seg) == seg) & (iota(shape, 0) >= iota(shape, 1))
            self.bias[b] = jnp.where(allowed, 0.0, -1e30)
        self.live[...] = (iota((self.rows, 128), 0) // self.length < self.counts[0]).astype(FULL)
        self.save(S.cos, S.sin)

    def gain_rows(self):
        start, wait = self.loader(W.gains)
        start()
        wait()
        near = self.near.gains
        count = math.prod(near.shape[:4])
        gains = near[...].reshape(count, 8, 128)
        self.gain[0:1, :] = gain_row(gains, 0, self.width // count)
        self.gain[1:2, :] = gain_row(gains, 1, self.width // count)

    def norm_one(self):
        for b in range(self.slots):
            rows = pl.ds(b * self.length, self.length)
            inputs = self.tokens[rows, :].astype(FULL)
            scale = lax.rsqrt(jnp.mean(inputs * inputs, axis=-1, keepdims=True) + eps)
            normed = (inputs * scale * self.gain[0:1, :]).astype(LOW)
            self.normed[rows, :] = normed
            self.v.normed_t[:, rows] = normed.T
        self.save(S.normed_t)

    def weight(self, which, cols):
        w = self.near[which][:, :, :, :, :, cols]
        return w.reshape(math.prod(w.shape[:5]), w.shape[5])

    def project(self, which, wait):
        wait()
        normed = self.normed[...]

        def tile(n, carry):
            cols = pl.ds(pl.multiple_of(n * WIDE, WIDE), WIDE)
            got = dot(normed, self.weight(which, cols))
            if which == W.value:
                low = got.astype(LOW)
                self.v.v_low[:, cols] = low
                self.v.first[:, cols] = (self.live[...][:, 0:1] * low.astype(FULL)).astype(LOW)
            else:
                into = self.v.q_rot if which == W.query else self.v.k_rot
                into[:, cols] = turn(got, self.v.cos[...], self.v.sin[...]).astype(LOW)
            return carry

        lax.fori_loop(0, self.width // WIDE, tile, 0)
        if which == W.value:
            self.save(S.v_low, S.first)
        else:
            self.save(S.q_rot if which == W.query else S.k_rot)

    def attend(self, b):
        length = self.length
        rows = pl.ds(b * length, length)

        def pair(h, carry):
            cols = pl.ds(pl.multiple_of(h * 128, 128), 128)
            q, k, v = self.v.q_rot[rows, cols], self.v.k_rot[rows, cols], self.v.v_low[rows, cols]
            k2, v2 = split_pair(k), split_pair(v)
            scores = dot(q, k2, ((1,), (1,))) * HD ** (-0.5)
            bias = self.bias[b]
            probs = []
            for half in range(2):
                s = scores[:, half * length : (half + 1) * length] + bias
                e = jnp.exp(s - jnp.max(s, axis=-1, keepdims=True))
                probs.append(e * (1.0 / jnp.sum(e, axis=-1, keepdims=True)))
            probs = jnp.concatenate(probs, axis=1).astype(LOW)
            self.v.probs[b, h] = probs
            self.mixed[rows, cols] = dot(probs, v2).astype(LOW)
            return carry

        lax.fori_loop(0, self.width // 128, pair, 0)
        self.v.mixed_t[:, rows] = self.mixed[rows, :].T
        if b == self.slots - 1:
            self.save(S.probs, S.mixed_t)

    def join(self, wait):
        wait()
        mixed = self.mixed[...]

        def tile(n, carry):
            cols = pl.ds(pl.multiple_of(n * WIDE, WIDE), WIDE)
            got = dot(mixed, self.weight(W.output, cols))
            self.v.middle[:, cols] = self.tokens[:, cols].astype(FULL) + got
            return carry

        lax.fori_loop(0, self.width // WIDE, tile, 0)
        self.save(S.middle)

    def norm_two(self):
        for b in range(self.slots):
            rows = pl.ds(b * self.length, self.length)
            middle = self.v.middle[rows, :]
            scale = lax.rsqrt(jnp.mean(middle * middle, axis=-1, keepdims=True) + eps)
            normed = (middle * scale * self.gain[1:2, :]).astype(LOW)
            self.two[rows, :] = normed
            self.v.two_t[:, rows] = normed.T
        self.save(S.two_t)

    def hidden(self, lo, hi, wait_gate, wait_up):
        wait_gate()
        wait_up()
        two = self.two[...]

        def tile(n, carry):
            cols = pl.ds(pl.multiple_of(lo + n * WIDE, WIDE), WIDE)
            gate = dot(two, self.weight(W.gate, cols))
            upward = dot(two, self.weight(W.up, cols))
            sig = 1.0 / (1.0 + jnp.exp(-gate))
            silu = gate * sig
            self.v.hid_t[cols, :] = (silu * upward).astype(LOW).T
            self.v.t1[:, cols] = (upward * sig * (1.0 + gate * (1.0 - sig))).astype(LOW)
            self.v.t2[:, cols] = silu.astype(LOW)
            return carry

        lax.fori_loop(0, (hi - lo) // WIDE, tile, 0)
        if hi == self.v.hid_t.shape[0]:
            self.save(S.hid_t, S.t1, S.t2)

    def steps(self):
        todo = [self.tables, self.gain_rows, self.norm_one]

        def after(which, action, *args):
            start, wait = self.loader(which)
            todo.extend([start, lambda: action(*args, wait)])

        for which in (W.query, W.key, W.value):
            after(which, self.project, which)
        for b in range(self.slots):
            todo.append(lambda b=b: self.attend(b))
        after(W.output, self.join)
        todo.append(self.norm_two)
        for which, _, cols in GATHER_JOBS:
            if which == W.gate:
                cols = (cols[0] * WIDE, cols[1] * WIDE)
                gate, up = self.loader(W.gate, cols), self.loader(W.up, cols)
                todo += [gate[0], up[0], lambda c=cols, g=gate, u=up: self.hidden(*c, g[1], u[1])]
        return todo


def forward_kernel(depth, *refs):
    refs = list(refs)

    def take(count):
        got = refs[:count]
        del refs[:count]
        return got

    kinds = len(Weights._fields)
    tokens, counts, segments, positions, inverse, norm_first, norm_second = take(7)
    given = take(kinds - 1)
    full = Weights._make(take(kinds))
    o = Saved._make(take(len(Saved._fields)))
    v = Saved._make(take(len(Saved._fields)))
    near = Weights._make(take(kinds - 1) + [None])
    gain, normed, mixed, two, bias, live, own_gains, own_down = take(8)
    sends, receipts, local_sems, load_sems, save_sems = take(5)
    place = Place(depth)
    work = Forward(
        place, tokens=tokens, counts=counts, segments=segments, positions=positions, inverse=inverse,
        norm_first=norm_first, norm_second=norm_second, down_weight=given[-1], full=full, o=o, v=v, near=near,
        gain=gain, normed=normed, mixed=mixed, two=two, bias=bias, live=live, own_gains=own_gains,
        own_down=own_down, load_sems=load_sems, save_sems=save_sems,
    )
    owns = Weights._make([own_gains] + given[:-1] + [own_down])
    jobs = []
    for i, (which, z_first, cols) in enumerate(GATHER_JOBS):
        own, whole = owns[which], full[which]
        if cols is not None:
            cut = slice(cols[0] * WIDE, cols[1] * WIDE)
            own, whole = own.at[:, cut], whole.at[:, :, :, :, :, cut]
        jobs.append(Gather(place, own, whole, sends.at[i], receipts.at[i], local_sems.at[i], z_first))
    actions = [step for job in jobs for step in job.steps()] + work.steps()
    assert sorted(FORWARD_ORDER) == list(range(len(actions)))
    work.own_shards()
    place.greet()
    for i in FORWARD_ORDER:
        actions[i]()
    for job in jobs:
        job.sent()
    for i in range(len(v)):
        pltpu.make_async_copy(v[i], o[i], save_sems.at[i]).wait()


def forward(mesh, tokens, counts, segments, positions, norm_first, norm_second, weights):
    depth = mesh.shape[FSDP] // 2
    slots, length, width = tokens.shape
    rows, each = slots * length, norm_first.shape[0]
    down_rows, hidden = weights[-1].shape[0], weights[W.gate - 1].shape[1]
    lead = (2, 2, depth, 2)
    flat, tall = ((rows, width), LOW), ((width, rows), LOW)
    saved = Saved(
        cos=((rows, 128), FULL),
        sin=((rows, 128), FULL),
        normed_t=tall,
        q_rot=flat,
        k_rot=flat,
        v_low=flat,
        probs=((slots, width // 128, length, 2 * length), LOW),
        mixed_t=tall,
        middle=((rows, width), FULL),
        two_t=tall,
        hid_t=((hidden, rows), LOW),
        t1=((rows, hidden), LOW),
        t2=((rows, hidden), LOW),
        first=flat,
    )
    owns = [((8, 128), FULL)] + [(w.shape, LOW) for w in weights[:-1]] + [((2 * down_rows, width // 2), LOW)]
    fulls = [(lead + shape, kind) for shape, kind in owns]
    inverse = jnp.asarray(
        np.exp((np.arange(128) % (HD // 2)) * (-2.0 * math.log(10000.0) / HD)), FULL
    )[None, :]
    vmem, anywhere = pl.BlockSpec(memory_space=pltpu.VMEM), pl.BlockSpec(memory_space=pl.ANY)
    smem = pl.BlockSpec(memory_space=pltpu.SMEM)
    jobs = len(GATHER_JOBS)
    got = pl.pallas_call(
        lambda *refs: forward_kernel(depth, *refs),
        out_shape=tuple(jax.ShapeDtypeStruct(*a) for a in fulls + list(saved)),
        in_specs=[vmem, smem] + [vmem] * 5 + [anywhere] * (len(weights) - 1) + [vmem],
        out_specs=tuple([anywhere] * (len(fulls) + len(saved))),
        scratch_shapes=[pltpu.VMEM(*a) for a in list(saved) + fulls[:-1]]
        + [
            pltpu.VMEM((8, width), FULL),
            pltpu.VMEM(*flat),
            pltpu.VMEM(*flat),
            pltpu.VMEM(*flat),
            pltpu.VMEM((slots, length, length), FULL),
            pltpu.VMEM((rows, 128), FULL),
            pltpu.VMEM(*owns[0]),
            pltpu.VMEM(*owns[-1]),
            pltpu.SemaphoreType.DMA((jobs, 2 * (depth - 1) + 8)),
            pltpu.SemaphoreType.DMA((jobs, 2 * (depth - 1) + 8)),
            pltpu.SemaphoreType.DMA((jobs,)),
            pltpu.SemaphoreType.DMA((5 + 2 * sum(job[0] == W.gate for job in GATHER_JOBS),)),
            pltpu.SemaphoreType.DMA((len(saved),)),
        ],
        compiler_params=pltpu.CompilerParams(
            collective_id=1, has_side_effects=True, vmem_limit_bytes=60 * 2**20
        ),
        cost_estimate=pl.CostEstimate(
            flops=2 * rows * width * (4 * width + 2 * hidden), bytes_accessed=80 * 2**20, transcendentals=2**22
        ),
        name="gather_and_forward",
    )(
        tokens.reshape(rows, width), counts, segments, positions, inverse,
        norm_first.reshape(1, each), norm_second.reshape(1, each), *weights,
    )
    return Weights._make(got[: len(fulls)]), Saved._make(got[len(fulls) :])


def add_block(into, other):
    into[...] = into[...] + other[...]


class Buffers(NamedTuple):
    acc: Any
    stage: Any
    sib: Any
    ring1: Any
    ring2: Any
    zed: Any
    sends: Any
    receipts: Any
    credit: Any


class Reduce:
    def __init__(self, place, index, count, slots, z_first, buffers, emit):
        self.p, self.z_first, self.b, self.emit = place, z_first, buffers, emit
        self.k, self.count, self.slots = index, count, slots
        rows = buffers.acc.shape[3]
        self.cut = (rows // 2 + 15) // 16 * 16

    def copy(self, src, dst, slot, who):
        return remote(src, dst, self.b.sends.at[slot], self.b.receipts.at[slot], who)

    def sib_copy(self):
        return self.copy(self.b.stage, self.b.sib, 0, self.p.sibling())

    def free_stage(self):
        self.sib_copy().wait_send()

    def send(self):
        if self.k >= self.slots:
            pl.semaphore_wait(self.b.credit, 1)
        self.sib_copy().start()

    def merge(self):
        self.sib_copy().wait_recv()
        depth = self.p.depth

        def block(i, carry):
            at = (i // (2 * depth), i // 2 % depth, i % 2)
            self.b.acc[at] = self.b.acc[at] + self.b.sib[at]
            return carry

        lax.fori_loop(0, 4 * depth, block, 0)
        if self.k + self.slots < self.count:
            pl.semaphore_signal(
                self.b.credit, inc=1, device_id=self.p.sibling(), device_id_type=MESH
            )

    def bundle(self, x, y):
        if self.z_first:
            return self.b.acc.at[x, self.p.z, y]
        return self.b.acc.at[x, :, y]

    def halves(self, ref):
        cut = self.cut if self.z_first else self.p.depth // 2
        return ref.at[:cut], ref.at[cut:]

    def first_copies(self):
        p = self.p
        low, high = self.halves(self.bundle(1 - p.x, 1 - p.y))
        to_low, to_high = self.halves(self.b.ring1)
        return (
            self.copy(low, to_low, 1, p.across_x()),
            self.copy(high, to_high, 2, p.across_y()),
        )

    def second_copies(self):
        p = self.p
        return (
            self.copy(self.bundle(1 - p.x, p.y), self.b.ring2.at[0], 3, p.across_x()),
            self.copy(self.bundle(p.x, 1 - p.y), self.b.ring2.at[1], 4, p.across_y()),
        )

    def ring_first(self):
        for copy in self.first_copies():
            copy.start()

    def ring_second(self):
        p = self.p
        by_x, by_y = self.first_copies()
        to_x, to_y = self.second_copies()
        got_low, got_high = self.halves(self.b.ring1)
        by_x.wait_recv()
        add_block(self.halves(self.bundle(p.x, 1 - p.y))[0], got_low)
        to_y.start()
        by_y.wait_recv()
        add_block(self.halves(self.bundle(1 - p.x, p.y))[1], got_high)
        to_x.start()

    def ring_last(self):
        p = self.p
        for copy in self.second_copies():
            copy.wait_recv()
        both = self.b.ring2[0].astype(FULL) + self.b.ring2[1].astype(FULL)
        return self.bundle(p.x, p.y)[...].astype(FULL) + both

    def zunits(self, units):
        if self.z_first:
            return self.b.acc.at[:, units]
        return self.b.acc.at[self.p.x, units, self.p.y]

    def landing(self, side, units):
        if self.z_first:
            return self.b.zed.at[side, :, units]
        return self.b.zed.at[side, units]

    def up(self, step):
        top = self.p.depth - 1
        return self.copy(self.zunits(slice(step + 1, top + 1)), self.landing(0, slice(step, top)), 5, self.p.above())

    def down(self, step):
        count = self.p.depth - 1 - step
        return self.copy(self.zunits(slice(0, count)), self.landing(1, slice(0, count)), 6, self.p.below())

    def z_step(self, step):
        p, top = self.p, self.p.depth - 1

        def upward():
            if step > 0:
                self.up(step - 1).wait_recv()
            if step < top:
                if step > 0:
                    add_block(self.zunits(slice(step + 1, top + 1)), self.landing(0, slice(step, top)))
                self.up(step).start()

        def downward():
            if step > 0:
                self.down(step - 1).wait_recv()
            if step < top:
                if step > 0:
                    add_block(self.zunits(slice(0, top - step)), self.landing(1, slice(0, top - step)))
                self.down(step).start()

        pl.when(p.z == step)(upward)
        pl.when(p.z == top - step)(downward)

    def z_sum(self, put):
        p, top = self.p, self.p.depth - 1
        mine = self.zunits(p.z)[...].astype(FULL)

        @pl.when(p.z == 0)
        def _():
            put(mine + self.landing(1, 0)[...].astype(FULL))

        @pl.when(p.z == top)
        def _():
            put(mine + self.landing(0, top - 1)[...].astype(FULL))

        @pl.when((p.z > 0) & (p.z < top))
        def _():
            low, high = self.landing(0, p.z - 1)[...], self.landing(1, p.z)[...]
            put(mine + (low.astype(FULL) + high.astype(FULL)))

    def steps(self):
        kind = self.b.acc.dtype

        def keep_ring():
            self.bundle(self.p.x, self.p.y)[...] = self.ring_last().astype(kind)
            self.z_step(0)

        def keep_z(values):
            self.zunits(self.p.z)[...] = values.astype(kind)

        if self.z_first:
            return [
                self.send,
                lambda: (self.merge(), self.z_step(0)),
                lambda: self.z_step(1),
                lambda: self.z_step(2),
                lambda: (self.z_step(3), self.z_sum(keep_z), self.ring_first()),
                self.ring_second,
                lambda: self.emit(self.ring_last()),
            ]
        return [
            self.send,
            lambda: (self.merge(), self.ring_first()),
            self.ring_second,
            keep_ring,
            lambda: self.z_step(1),
            lambda: self.z_step(2),
            lambda: (self.z_step(3), self.z_sum(self.emit)),
        ]

    def sent(self):
        p, top = self.p, self.p.depth - 1
        if self.k + self.slots >= self.count:
            self.free_stage()
        for copy in self.first_copies() + self.second_copies():
            copy.wait_send()
        for step in range(top):
            pl.when(p.z == step)(lambda step=step: self.up(step).wait_send())
            pl.when(p.z == top - step)(lambda step=step: self.down(step).wait_send())


DOWN, SIDE, GAIN = range(3)
SLOTS = (2, 3, 1)
Z_FIRST = (True, False, False)
BACKWARD_ORDER = (
    168, 169, 0, 170, 171, 172, 1, 173, 174, 7, 175, 176, 177, 28, 178, 35, 29, 8, 179, 42, 36, 180, 30, 43, 49, 14,
    181, 37, 50, 15, 56, 182, 63, 183, 70, 57, 64, 184, 21, 77, 44, 71, 185, 84, 58, 186, 187, 9, 51, 31, 78, 85, 72,
    188, 189, 91, 16, 190, 191, 65, 98, 2, 92, 105, 22, 79, 192, 112, 99, 193, 86, 194, 17, 106, 113, 80, 100, 23, 93,
    10, 73, 195, 3, 81, 45, 66, 38, 74, 107, 196, 24, 67, 114, 46, 197, 119, 198, 199, 11, 126, 133, 87, 120, 4, 32,
    59, 75, 127, 94, 200, 140, 201, 202, 134, 52, 47, 147, 154, 5, 12, 203, 141, 135, 60, 204, 25, 121, 53, 76, 115,
    148, 101, 142, 205, 206, 116, 88, 128, 108, 207, 39, 68, 18, 61, 161, 117, 95, 6, 122, 208, 155, 136, 123, 149,
    54, 137, 102, 96, 33, 109, 209, 143, 162, 156, 89, 13, 129, 97, 118, 82, 150, 55, 130, 19, 40, 144, 151, 103, 48,
    138, 163, 69, 26, 157, 110, 158, 124, 164, 165, 145, 139, 27, 146, 131, 111, 20, 152, 125, 159, 104, 41, 34, 90,
    153, 83, 166, 62, 132, 160, 167,
)


def chunk_list(tiles, width):
    halves = width // (2 * WIDE)
    chunks = [(DOWN, W.down, n) for n in range(width // WIDE)]
    chunks += [(SIDE, W.gate, f) for f in range(tiles)]
    chunks += [(SIDE, w, half) for w in (W.output, W.query, W.key, W.value) for half in range(halves)]
    return chunks + [(GAIN, W.gains, 0)]


class First(NamedTuple):
    hid_t: Any
    branch: Any
    raw: Any
    down: Any
    two_t: Any
    middle: Any
    tile: Any
    t: Any
    both: Any


class Second(NamedTuple):
    w: Any
    mixed_t: Any
    normed_t: Any
    v_low: Any
    probs: Any
    cos: Any
    sin: Any
    tokens: Any
    gmixed: Any
    gq: Any
    gk: Any
    gv: Any
    gnormed: Any


class Third(NamedTuple):
    hid_t: Any
    down: Any
    middle: Any
    out: Any


class Backward:
    def __init__(self, place, **refs):
        self.p = place
        self.__dict__.update(refs)
        self.rows, self.width = self.tokens.shape
        self.tiles = self.full.gate.shape[-1] // WIDE
        self.loads = 0
        self.pending = {}

    def fetch(self, key, src, dst):
        copy = pltpu.make_async_copy(src, dst, self.load_sems.at[self.loads])
        self.loads += 1
        self.pending[key] = copy
        copy.start()

    def arrived(self, *keys):
        for key in keys:
            self.pending.pop(key).wait()

    def block_rows(self, b):
        return pl.ds(b * self.length, self.length)

    def live(self, b):
        return (jnp.int32(b) < self.counts[0]).astype(FULL)

    def spread(self, job, part):
        p = self.p
        if job.before is not None:
            job.before.free_stage()
        for x in range(2):
            part(x, 1 - p.c, job.b.stage)
            part(x, p.c, job.b.acc)

    def side_by_side(self, job, left, right):
        count = self.width // 4

        def part(x, c, into):
            at = pl.multiple_of((x * 2 + c) * count, count)
            got = dot(left[pl.ds(at, count), :], right[...]).astype(LOW)
            got = got.reshape(self.p.depth, 2, -1, 2 * WIDE)
            each = got.shape[2]
            into[x, :, :, :each, :] = got[..., :WIDE]
            into[x, :, :, each:, :] = got[..., WIDE:]

        self.spread(job, part)

    def begin(self):
        h, s = self.h, self.s
        self.fetch(-1, self.out_cotangent, h.branch)
        self.fetch(S.hid_t, s.hid_t, h.hid_t)
        self.fetch((W.down, 0), self.full.down.at[0, 0], h.raw)
        self.fetch(S.two_t, s.two_t, h.two_t)
        self.tile_loads(0)
        self.fetch(S.middle, s.middle, h.middle)
        self.fetch((W.gains,), self.full.gains, self.gains_near)
        self.arrived(-1)
        for b in range(self.slots):
            rows = self.block_rows(b)
            h.branch[rows, :] = (h.branch[rows, :].astype(FULL) * self.live(b)).astype(LOW)

    def down_chunk(self, n):
        h = self.h
        if n == 0:
            self.arrived(S.hid_t)
        right = h.branch[:, n * WIDE : (n + 1) * WIDE]
        count = h.hid_t.shape[0] // 4

        def part(x, c, into):
            at = pl.multiple_of((x * 2 + c) * count, 16)
            got = dot(h.hid_t[pl.ds(at, count), :], right)
            got = got.reshape(2 * self.p.depth, -1, WIDE)
            got = jnp.concatenate([got[:, :, : WIDE // 2], got[:, :, WIDE // 2 :]], axis=1)
            into[x] = got.astype(LOW).reshape(into.shape[1:])

        self.spread(self.job[W.down, n], part)

    def down_weight(self, i):
        self.arrived((W.down, i))
        depth, raw, down = self.p.depth, self.h.raw, self.h.down
        rows, half = raw.shape[2] // 2, raw.shape[3]
        for z in range(depth):
            pair = raw[z].astype(FULL)
            for side in range(2):
                part = pair[:, side * rows : (side + 1) * rows, :].reshape(2 * rows, half)
                at = (i * depth + z) * 2 * rows
                down[at : at + 2 * rows, side * half : (side + 1) * half] = part.astype(LOW)
        j = i + 1
        if j < 4:
            self.fetch((W.down, j), self.full.down.at[j // 2, j % 2], raw)
        else:
            self.fetch((W.down,), down, self.down_kept)

    def tile_loads(self, f):
        cols, slot = pl.ds(f * WIDE, WIDE), f % 2
        for which, side in ((W.gate, 0), (W.up, 1)):
            into = self.h.tile.at[slot, :, :, :, :, :, side * WIDE : (side + 1) * WIDE]
            self.fetch((which, f), self.full[which].at[:, :, :, :, :, cols], into)
        for which, side in ((S.t1, 0), (S.t2, 1)):
            self.fetch((f, side, 0), self.s[which].at[:, cols], self.h.t.at[slot, side])

    def ff_tile(self, f):
        h, slot = self.h, f % 2
        self.arrived((W.gate, f), (W.up, f), (f, 0, 0), (f, 1, 0))
        if f + 1 < self.tiles:
            self.tile_loads(f + 1)
        if f == 0:
            self.arrived(S.two_t)
        grad = dot(h.branch[...], h.down[f * WIDE : (f + 1) * WIDE, :], ((1,), (1,)))
        h.both[:, :WIDE] = (grad * h.t[slot, 0].astype(FULL)).astype(LOW)
        h.both[:, WIDE:] = (grad * h.t[slot, 1].astype(FULL)).astype(LOW)
        self.side_by_side(self.job[W.gate, f], h.two_t, h.both)
        count = self.width // 4
        for xc in range(4):
            cols = slice(xc * count, (xc + 1) * count)
            weight = h.tile[slot, xc // 2, xc % 2].reshape(count, 2 * WIDE)
            got = dot(h.both[...], weight, ((1,), (1,)))
            if f == 0:
                self.grad[:, cols] = got
            else:
                self.grad[:, cols] += got

    def norm_back(self, grads, inputs, gain):
        scale = lax.rsqrt(jnp.mean(inputs * inputs, axis=-1, keepdims=True) + eps)
        total = jnp.sum(grads * inputs * scale, axis=0, keepdims=True)
        scaled = grads * gain
        mean = jnp.mean(scaled * inputs, axis=-1, keepdims=True)
        return scale * (scaled - inputs * (scale * scale * mean)), total

    def norm_two(self):
        h = self.h
        self.arrived((W.gains,), S.middle)
        count = math.prod(self.gains_near.shape[:4])
        gains = self.gains_near[...].reshape(count, 8, 128)
        self.gain[0:1, :] = gain_row(gains, 0, self.width // count)
        self.gain[1:2, :] = gain_row(gains, 1, self.width // count)
        total = jnp.zeros((1, self.width), FULL)
        for b in range(self.slots):
            rows = self.block_rows(b)
            got, part = self.norm_back(self.grad[rows, :], h.middle[rows, :], self.gain[1:2, :])
            grad = h.branch[rows, :].astype(FULL) + got
            self.grad[rows, :] = grad
            self.attended[rows, :] = grad.astype(LOW)
            total = total + part
        self.gain_sum[1:2, :] = total
        self.arrived((W.down,))

    def second(self):
        h, s = self.h, self.s
        self.fetch((W.output,), self.full.output, h.w.at[0])
        self.fetch(S.mixed_t, s.mixed_t, h.mixed_t)
        self.fetch(S.v_low, s.v_low, h.v_low)
        self.fetch(S.probs, s.probs, h.probs)
        self.fetch(S.q_rot, s.q_rot, h.gq)
        self.fetch(S.k_rot, s.k_rot, h.gk)
        self.fetch(-2, self.value_cotangent, h.gv)
        self.fetch(S.cos, s.cos, h.cos)
        self.fetch(S.sin, s.sin, h.sin)
        self.fetch(S.normed_t, s.normed_t, h.normed_t)
        self.fetch(-3, self.tokens, h.tokens)
        self.fetch((W.query,), self.full.query, h.w.at[1])

    def weight_rows(self, slot, xc):
        return self.h.w[slot, xc // 2, xc % 2].reshape(self.width // 4, self.width)

    def mixed_back(self):
        self.arrived((W.output,))
        for xc in range(4):
            got = dot(self.attended[...], self.weight_rows(0, xc), ((1,), (1,)))
            count = self.width // 4
            self.h.gmixed[:, xc * count : (xc + 1) * count] = got.astype(LOW)
        self.fetch((W.key,), self.full.key, self.h.w.at[0])

    def weight_chunk(self, which, half):
        h = self.h
        if half == 0 and which in (W.output, W.query):
            self.arrived(S.mixed_t if which == W.output else S.normed_t)
        left = h.mixed_t if which == W.output else h.normed_t
        right = {W.output: self.attended, W.query: h.gq, W.key: h.gk, W.value: h.gv}[which]
        cols = slice(half * 2 * WIDE, (half + 1) * 2 * WIDE)
        self.side_by_side(self.job[which, half], left, right.at[:, cols])

    def attend_back(self, b):
        h = self.h
        if b == 0:
            self.arrived(S.v_low, S.probs, S.q_rot, S.k_rot, -2, S.cos, S.sin)
        rows, length = self.block_rows(b), self.length
        first = iota((length, 128), 1) < HD
        live = self.live(b)
        cosine, sines = h.cos[rows, :], h.sin[rows, :]

        def fold(values):
            return jnp.where(first, values[:length], values[length:])

        def pair(n, carry):
            cols = pl.ds(pl.multiple_of(n * 128, 128), 128)
            q, k, v = h.gq[rows, cols], h.gk[rows, cols], h.v_low[rows, cols]
            grad = h.gmixed[rows, cols]
            probs = h.probs[b, n]
            k2, v2 = split_pair(k), split_pair(v)
            grad_probs = dot(grad, v2, ((1,), (1,)))
            parts = []
            for half in range(2):
                at = slice(half * length, (half + 1) * length)
                full, gp = probs[:, at].astype(FULL), grad_probs[:, at]
                parts.append(full * (gp - jnp.sum(full * gp, axis=-1, keepdims=True)))
            scores = jnp.concatenate(parts, axis=1).astype(LOW)
            grad_q = dot(scores, k2) * HD ** (-0.5)
            grad_k = fold(dot(scores, q, ((0,), (0,)))) * HD ** (-0.5)
            grad_v = fold(dot(probs, grad, ((0,), (0,))))
            grad_v = grad_v + live * h.gv[rows, cols].astype(FULL)
            h.gq[rows, cols] = turn(grad_q, cosine, -sines).astype(LOW)
            h.gk[rows, cols] = turn(grad_k, cosine, -sines).astype(LOW)
            h.gv[rows, cols] = grad_v.astype(LOW)
            return carry

        lax.fori_loop(0, self.width // 128, pair, 0)

    def normed_back(self, which):
        h = self.h
        self.arrived((which,))
        slot, grad = {W.query: (1, h.gq), W.key: (0, h.gk), W.value: (1, h.gv)}[which]
        for xc in range(4):
            got = dot(grad[...], self.weight_rows(slot, xc), ((1,), (1,)))
            count = self.width // 4
            cols = slice(xc * count, (xc + 1) * count)
            if which == W.query:
                h.gnormed[:, cols] = got
            else:
                h.gnormed[:, cols] += got
        if which == W.query:
            self.fetch((W.value,), self.full.value, h.w.at[1])

    def norm_one(self):
        h = self.h
        self.arrived(-3)
        total = jnp.zeros((1, self.width), FULL)
        for b in range(self.slots):
            rows = self.block_rows(b)
            inputs = h.tokens[rows, :].astype(FULL)
            got, part = self.norm_back(h.gnormed[rows, :], inputs, self.gain[0:1, :])
            h.tokens[rows, :] = (self.grad[rows, :] + got).astype(LOW)
            total = total + part
        self.gain_sum[0:1, :] = total
        self.fetch(-4, h.tokens, self.token_grad)

    def gain_chunk(self):
        depth = self.p.depth
        count = 4 * 2 * depth
        each = self.width // count
        shape = (count, self.width)
        keep = iota(shape, 1) // each == iota(shape, 0)
        folded = []
        for row in range(2):
            whole = jnp.where(keep, jnp.broadcast_to(self.gain_sum[row : row + 1, :], shape), 0.0)
            folded.append(sum(whole[:, i * 128 : (i + 1) * 128] for i in range(self.width // 128)))
        sub = iota((8, 128), 0)
        mine = []
        for i in range(count):
            one = jnp.broadcast_to(folded[0][i : i + 1, :], (8, 128))
            two = jnp.broadcast_to(folded[1][i : i + 1, :], (8, 128))
            mine.append(jnp.where(sub == 0, one, jnp.where(sub == 1, two, 0.0)))

        def part(x, c, into):
            for core in range(2):

                @pl.when(c == core)
                def _(core=core):
                    for z in range(depth):
                        for y in range(2):
                            into[x, z, y] = mine[(x * 2 + core) * 2 * depth + z * 2 + y]

        self.spread(self.job[W.gains, 0], part)
        self.arrived(-4)

    def third(self):
        h = self.h
        self.fetch(S.hid_t, self.s.hid_t, h.hid_t)
        self.fetch((W.down,), self.down_kept, h.down)
        self.fetch(S.middle, self.s.middle, h.middle)

    def block_output(self):
        h = self.h
        self.arrived(S.hid_t, (W.down,), S.middle)
        for b in range(self.slots // 2):
            rows = pl.ds(b * 2 * self.length, 2 * self.length)
            hidden = h.hid_t[:, rows].T
            live = jnp.concatenate(
                [jnp.full((self.length, 1), 1.0, FULL) * self.live(2 * b + i) for i in range(2)], axis=0
            )

            def tile(n, carry, rows=rows, hidden=hidden, live=live):
                cols = pl.ds(pl.multiple_of(n * WIDE, WIDE), WIDE)
                got = dot(hidden, h.down[:, cols])
                h.out[rows, cols] = (live * (h.middle[rows, cols] + got)).astype(LOW)
                return carry

            lax.fori_loop(0, self.width // WIDE, tile, 0)
        self.fetch(-5, h.out, self.block_out)

    def finish(self):
        self.arrived(-5)

    def steps(self):
        todo, halves = [self.begin], self.width // (2 * WIDE)
        for n in range(self.width // WIDE):
            todo += [lambda n=n: self.down_chunk(n), lambda n=n: self.down_weight(n)]
        todo += [lambda f=f: self.ff_tile(f) for f in range(self.tiles)] + [self.norm_two]
        second = len(todo)
        todo += [self.second, self.mixed_back]
        todo += [lambda h=h: self.weight_chunk(W.output, h) for h in range(halves)]
        todo += [lambda b=b: self.attend_back(b) for b in range(self.slots)]
        todo += [lambda w=w, h=h: self.weight_chunk(w, h) for w in (W.query, W.key, W.value) for h in range(halves)]
        todo += [lambda w=w: self.normed_back(w) for w in (W.query, W.key, W.value)]
        todo += [self.norm_one, self.gain_chunk]
        third = len(todo)
        todo += [self.third, self.block_output]
        return todo, second, third


def emitter(outs, kind, which, n):
    def emit(values):
        each = values.shape[0] // 2
        if kind == GAIN:
            outs.gains[...] = values
        elif kind == DOWN:
            half = WIDE // 2
            outs.down[:, n * WIDE : n * WIDE + half] = values[:each]
            outs.down[:, n * WIDE + half : (n + 1) * WIDE] = values[each:]
        elif which == W.gate:
            outs.gate[:, n * WIDE : (n + 1) * WIDE] = values[:each]
            outs.up[:, n * WIDE : (n + 1) * WIDE] = values[each:]
        else:
            outs[which][:, 2 * n * WIDE : (2 * n + 1) * WIDE] = values[:each]
            outs[which][:, (2 * n + 1) * WIDE : (2 * n + 2) * WIDE] = values[each:]

    return emit


def backward_kernel(depth, slots, length, *refs):
    refs = list(refs)

    def take(count):
        got = refs[:count]
        del refs[:count]
        return got

    counts, tokens, out_cotangent, value_cotangent = take(4)
    full = Weights._make(take(len(Weights._fields)))
    s = Saved._make(take(len(Saved._fields) - 1) + [None])
    block_out, token_grad, down_kept = take(3)
    outs = Weights._make(take(len(Weights._fields)))
    grad, attended, gain, gain_sum, gains_near = take(5)
    kinds = [Buffers._make(take(len(Buffers._fields))) for _ in SLOTS]
    (load_sems,) = refs
    place = Place(depth)
    work = Backward(
        place, counts=counts, tokens=tokens, out_cotangent=out_cotangent, value_cotangent=value_cotangent, full=full,
        s=s, block_out=block_out, token_grad=token_grad, down_kept=down_kept, grad=grad, attended=attended, gain=gain,
        gain_sum=gain_sum, gains_near=gains_near, load_sems=load_sems, slots=slots, length=length,
    )
    rows, width = work.rows, work.width
    chunks = chunk_list(work.tiles, width)
    work.job, by_kind = {}, [[] for _ in SLOTS]
    for kind, which, n in chunks:
        b, k, many = kinds[kind], len(by_kind[kind]), SLOTS[kind]
        own = Buffers._make([ref.at[k % many if i in (1, 2) else k] for i, ref in enumerate(b[:-1])] + [b.credit])
        count = sum(chunk[0] == kind for chunk in chunks)
        job = Reduce(place, k, count, many, Z_FIRST[kind], own, emitter(outs, kind, which, n))
        job.before = by_kind[kind][k - many] if k >= many else None
        by_kind[kind].append(job)
        work.job[which, n] = job
    todo, second, third = work.steps()
    actions = [step for job in work.job.values() for step in job.steps()]
    borders = [len(actions) + second, len(actions) + third]
    actions += todo
    assert sorted(BACKWARD_ORDER) == list(range(len(actions)))
    place.greet()
    flat, tall = pltpu.VMEM((rows, width), LOW), pltpu.VMEM((width, rows), LOW)
    table, wide = pltpu.VMEM((rows, 128), FULL), pltpu.VMEM((rows, width), FULL)
    down = pltpu.VMEM((work.tiles * WIDE, width), LOW)
    hid_t = pltpu.VMEM((work.tiles * WIDE, rows), LOW)
    held = (
        First(
            hid_t=hid_t, branch=flat, raw=pltpu.VMEM(full.down.shape[2:], LOW), down=down, two_t=tall, middle=wide,
            tile=pltpu.VMEM((2,) + full.gate.shape[:5] + (2 * WIDE,), LOW), t=pltpu.VMEM((2, 2, rows, WIDE), LOW),
            both=pltpu.VMEM((rows, 2 * WIDE), LOW),
        ),
        Second(
            w=pltpu.VMEM((2,) + full.query.shape, LOW), mixed_t=tall, normed_t=tall, v_low=flat,
            probs=pltpu.VMEM(s.probs.shape, LOW), cos=table, sin=table, tokens=flat, gmixed=flat, gq=flat, gk=flat,
            gv=flat, gnormed=wide,
        ),
        Third(hid_t=hid_t, down=down, middle=wide, out=flat),
    )
    cuts = [0] + [BACKWARD_ORDER.index(border) for border in borders] + [len(BACKWARD_ORDER)]
    for part, types in enumerate(held):

        def run(*buffers, part=part, types=types):
            work.h = type(types)._make(buffers)
            for i in BACKWARD_ORDER[cuts[part] : cuts[part + 1]]:
                actions[i]()
            if part == len(held) - 1:
                work.finish()

        pl.run_scoped(run, *types)
    for job in work.job.values():
        job.sent()


def backward(mesh, full, saved, tokens, counts, out_cotangent, value_cotangent, down_rows):
    depth = mesh.shape[FSDP] // 2
    slots, length, width = tokens.shape
    rows, hidden = slots * length, saved.hid_t.shape[0]
    tiles, each = hidden // WIDE, full.query.shape[4]
    chunks = chunk_list(tiles, width)
    scratch = [
        pltpu.VMEM((rows, width), FULL),
        pltpu.VMEM((rows, width), LOW),
        pltpu.VMEM((8, width), FULL),
        pltpu.VMEM((8, width), FULL),
        pltpu.VMEM(full.gains.shape, FULL),
    ]
    blocks = (((2 * down_rows, WIDE // 2), LOW), ((2 * each, WIDE), LOW), ((8, 128), FULL))
    for kind, (block, dtype) in enumerate(blocks):
        count, many = sum(chunk[0] == kind for chunk in chunks), SLOTS[kind]
        whole = (2, depth, 2) + block
        if Z_FIRST[kind]:
            ring1, ring2, zed = block, (2,) + block, (2, 2, depth - 1, 2) + block
        else:
            ring1, ring2, zed = (depth,) + block, (2, depth) + block, (2, depth - 1) + block
        scratch += [
            pltpu.VMEM((count,) + whole, dtype),
            pltpu.VMEM((many,) + whole, dtype),
            pltpu.VMEM((many,) + whole, dtype),
            pltpu.VMEM((count,) + ring1, dtype),
            pltpu.VMEM((count,) + ring2, dtype),
            pltpu.VMEM((count,) + zed, dtype),
            pltpu.SemaphoreType.DMA((count, 7)),
            pltpu.SemaphoreType.DMA((count, 7)),
            pltpu.SemaphoreType.REGULAR,
        ]
    scratch += [pltpu.SemaphoreType.DMA((32 + 4 * tiles,))]
    vmem, anywhere = pl.BlockSpec(memory_space=pltpu.VMEM), pl.BlockSpec(memory_space=pl.ANY)
    smem = pl.BlockSpec(memory_space=pltpu.SMEM)
    outs = [((rows, width), LOW), ((rows, width), LOW), ((hidden, width), LOW), ((8, 128), FULL)]
    outs += [((each, width), FULL)] * 4 + [((each, hidden), FULL)] * 2 + [((down_rows, width), FULL)]
    return pl.pallas_call(
        lambda *refs: backward_kernel(depth, slots, length, *refs),
        out_shape=tuple(jax.ShapeDtypeStruct(*a) for a in outs),
        in_specs=[smem] + [anywhere] * (3 + len(full) + len(saved) - 1),
        out_specs=tuple([anywhere] * 3 + [vmem] * len(full)),
        scratch_shapes=scratch,
        compiler_params=pltpu.CompilerParams(
            collective_id=2, has_side_effects=True, vmem_limit_bytes=63 * 2**20
        ),
        cost_estimate=pl.CostEstimate(
            flops=4 * rows * width * (4 * width + 3 * hidden), bytes_accessed=80 * 2**20, transcendentals=2**20
        ),
        name="backward_and_reduce",
    )(
        counts,
        tokens.reshape(rows, width),
        out_cotangent.reshape(rows, width),
        value_cotangent.reshape(rows, width),
        *full,
        *saved[:-1],
    )


def hand_over_kernel(count, each, *refs):
    gains, ins = refs[0], refs[1 : count + 1]
    one, two, outs = refs[count + 1], refs[count + 2], refs[count + 3 : 2 * count + 3]
    held, sems = refs[2 * count + 3 : -1], refs[-1]
    takes = [pltpu.make_async_copy(a, b, sems.at[0, i]) for i, (a, b) in enumerate(zip(ins, held))]
    gives = [pltpu.make_async_copy(a, b, sems.at[1, i]) for i, (a, b) in enumerate(zip(held, outs))]
    for take in takes:
        take.start()
    total, shift = gains[...], each
    while shift < 128:
        total = total + pltpu.roll(total, shift, 1)
        shift *= 2
    one[...] = total[0:1, :each]
    two[...] = total[1:2, :each]
    for take, give in zip(takes, gives):
        take.wait()
        give.start()
    for give in gives:
        give.wait()


def hand_over(gains, each, arrays):
    vmem, anywhere = pl.BlockSpec(memory_space=pltpu.VMEM), pl.BlockSpec(memory_space=pl.ANY)
    count = len(arrays)
    return pl.pallas_call(
        lambda *refs: hand_over_kernel(count, each, *refs),
        out_shape=tuple([jax.ShapeDtypeStruct((1, each), FULL)] * 2)
        + tuple(jax.ShapeDtypeStruct(a.shape, a.dtype) for a in arrays),
        in_specs=[vmem] + [anywhere] * count,
        out_specs=tuple([vmem] * 2 + [anywhere] * count),
        scratch_shapes=[pltpu.VMEM(a.shape, a.dtype) for a in arrays] + [pltpu.SemaphoreType.DMA((2, count))],
        compiler_params=pltpu.CompilerParams(vmem_limit_bytes=60 * 2**20),
        name="hand_over",
    )(gains, *arrays)


def rms_scale(values_in):
    return lax.rsqrt(jnp.mean(values_in * values_in, axis=-1, keepdims=True) + eps)


def rotate_table(positions):
    freq_index = jnp.arange(HD // 2, dtype=jnp.float32)
    inverse = jnp.exp(freq_index * (-2.0 * math.log(10000.0) / HD))
    angles = positions.astype(jnp.float32)[..., None] * inverse
    return (jnp.cos(angles), jnp.sin(angles))


def apply_rotary(values_in, cosine, sines):
    half_dim = values_in.shape[-1] // 2
    first_half = values_in[..., :half_dim]
    second_half = values_in[..., half_dim:]
    cosine = cosine[..., None, :]
    sines = sines[..., None, :]
    return jnp.concatenate(
        [first_half * cosine - second_half * sines, second_half * cosine + first_half * sines],
        axis=-1,
    )


def matmul(left_arg, right_arg):
    return jnp.dot(left_arg, right_arg, preferred_element_type=jnp.float32)


def stack_groups(values_in):
    row_count, model_width = values_in.shape
    return values_in.reshape(row_count, model_width // (4 * HD), 4 * HD).transpose(1, 0, 2)


def unstack_groups(values_in):
    group_count, row_count, group_width = values_in.shape
    return values_in.transpose(1, 0, 2).reshape(row_count, group_count * group_width)


def head_scores(query_grp, key_grp, allowed):
    row_count = query_grp.shape[0]
    query_heads = query_grp.reshape(row_count, 4, HD)
    key_heads = key_grp.reshape(row_count, 4, HD)
    scores = jnp.einsum(
        "qhe,khe->hqk", query_heads, key_heads, preferred_element_type=jnp.float32
    ) * HD ** (-0.5)
    return jnp.where(allowed[None], scores, -1e30)


def norm_back(grad_normed, inputs_f, scale_rows, gain_row):
    gain_term = jnp.sum(grad_normed * inputs_f * scale_rows, axis=0)
    scaled = grad_normed * gain_row
    grad_inputs = scale_rows * (
        scaled
        - inputs_f * scale_rows * scale_rows * jnp.mean(scaled * inputs_f, axis=-1, keepdims=True)
    )
    return (grad_inputs, gain_term)


def layer(
    gather_set,
    reduce_set,
    tokens,
    seq_counts,
    segments,
    positions,
    norm_first,
    query_weight,
    key_weight,
    value_weight,
    output_weight,
    norm_second,
    gate_weight,
    up_weight,
    down_weight,
    out_cotangent,
    value_cotangent,
):
    slot_count, seq_length, model_width = tokens.shape
    row_count = slot_count * seq_length
    head_count = model_width // HD
    weights = gather_set(
        norm_first,
        norm_second,
        query_weight,
        key_weight,
        value_weight,
        output_weight,
        gate_weight,
        up_weight,
        down_weight,
    )
    gain_one, gain_two, query_full, key_full, value_full, output_full = weights[:6]
    gate_full, up_full, down_full = weights[6:]
    row_index = jnp.arange(row_count, dtype=jnp.int32)
    slot_index = row_index // seq_length
    live_rows = (slot_index < seq_counts[0]).astype(jnp.float32)[:, None]
    flat_segments = segments.reshape(row_count)
    allowed = (
        (slot_index[:, None] == slot_index[None, :])
        & (flat_segments[:, None] == flat_segments[None, :])
        & (row_index[:, None] >= row_index[None, :])
    )
    inputs_f = tokens.reshape(row_count, model_width).astype(jnp.float32)
    scale_one = rms_scale(inputs_f)
    normed = (inputs_f * scale_one * gain_one.astype(jnp.float32)).astype(jnp.bfloat16)
    cosine, sines = rotate_table(positions.reshape(row_count))

    def rotated(values_in, turn_sign):
        turned = apply_rotary(
            values_in.reshape(row_count, head_count, HD), cosine, turn_sign * sines
        )
        return turned.reshape(row_count, model_width).astype(jnp.bfloat16)

    query_rot = rotated(matmul(normed, query_full), 1.0)
    key_rot = rotated(matmul(normed, key_full), 1.0)
    value_low = matmul(normed, value_full).astype(jnp.bfloat16)

    def attend_group(operands):
        query_grp, key_grp, value_grp = operands
        scores = head_scores(query_grp, key_grp, allowed)
        row_max = jnp.max(scores, axis=-1, keepdims=True)
        log_total = row_max + jnp.log(jnp.sum(jnp.exp(scores - row_max), axis=-1, keepdims=True))
        probs_low = jnp.exp(scores - log_total).astype(jnp.bfloat16)
        value_heads = value_grp.reshape(row_count, 4, HD)
        mixed_heads = jnp.einsum(
            "hqk,khe->qhe", probs_low, value_heads, preferred_element_type=jnp.float32
        )
        return (mixed_heads.reshape(row_count, 4 * HD), log_total)

    query_groups = stack_groups(query_rot)
    key_groups = stack_groups(key_rot)
    value_groups = stack_groups(value_low)
    mixed_groups, log_totals = lax.map(attend_group, (query_groups, key_groups, value_groups))
    mixed_low = unstack_groups(mixed_groups).astype(jnp.bfloat16)
    middle = inputs_f + matmul(mixed_low, output_full)
    scale_two = rms_scale(middle)
    normed_two = (middle * scale_two * gain_two.astype(jnp.float32)).astype(jnp.bfloat16)
    gate_pre = matmul(normed_two, gate_full)
    upward = matmul(normed_two, up_full)
    sigmoid_gate = jax.nn.sigmoid(gate_pre)
    silu_gate = gate_pre * sigmoid_gate
    hidden = (silu_gate * upward).astype(jnp.bfloat16)
    block_out = (live_rows * (middle + matmul(hidden, down_full))).astype(jnp.bfloat16)
    first_values = (live_rows * value_low.astype(jnp.float32)).astype(jnp.bfloat16)
    grad_y = live_rows * out_cotangent.reshape(row_count, model_width).astype(jnp.float32)
    grad_branch = grad_y.astype(jnp.bfloat16)
    down_term = jnp.einsum("rf,rd->fd", hidden, grad_branch, preferred_element_type=jnp.float32)
    grad_hidden = jnp.einsum(
        "rd,fd->rf", grad_branch, down_full, preferred_element_type=jnp.float32
    )
    grad_gate = (
        grad_hidden * upward * sigmoid_gate * (1.0 + gate_pre * (1.0 - sigmoid_gate))
    ).astype(jnp.bfloat16)
    grad_up = (grad_hidden * silu_gate).astype(jnp.bfloat16)
    gate_term = jnp.einsum("rd,rf->df", normed_two, grad_gate, preferred_element_type=jnp.float32)
    up_term = jnp.einsum("rd,rf->df", normed_two, grad_up, preferred_element_type=jnp.float32)
    grad_normed_two = jnp.einsum(
        "rf,df->rd", grad_gate, gate_full, preferred_element_type=jnp.float32
    ) + jnp.einsum("rf,df->rd", grad_up, up_full, preferred_element_type=jnp.float32)
    grad_middle_norm, gain_two_term = norm_back(
        grad_normed_two, middle, scale_two, gain_two.astype(jnp.float32)
    )
    grad_middle = grad_y + grad_middle_norm
    grad_attended = grad_middle.astype(jnp.bfloat16)
    output_term = jnp.einsum(
        "rd,re->de", mixed_low, grad_attended, preferred_element_type=jnp.float32
    )
    grad_mixed = jnp.einsum(
        "re,de->rd", grad_attended, output_full, preferred_element_type=jnp.float32
    ).astype(jnp.bfloat16)

    def attend_back(operands):
        query_grp, key_grp, value_grp, grad_grp, log_total = operands
        scores = head_scores(query_grp, key_grp, allowed)
        probs_full = jnp.exp(scores - log_total)
        probs_low = probs_full.astype(jnp.bfloat16)
        grad_heads = grad_grp.reshape(row_count, 4, HD)
        value_heads = value_grp.reshape(row_count, 4, HD)
        query_heads = query_grp.reshape(row_count, 4, HD)
        key_heads = key_grp.reshape(row_count, 4, HD)
        grad_probs = jnp.einsum(
            "qhe,khe->hqk", grad_heads, value_heads, preferred_element_type=jnp.float32
        )
        row_term = jnp.sum(probs_full * grad_probs, axis=-1, keepdims=True)
        grad_scores = (probs_full * (grad_probs - row_term)).astype(jnp.bfloat16)
        score_scale = HD ** (-0.5)
        grad_query = (
            jnp.einsum("hqk,khe->qhe", grad_scores, key_heads, preferred_element_type=jnp.float32)
            * score_scale
        )
        grad_key = (
            jnp.einsum("hqk,qhe->khe", grad_scores, query_heads, preferred_element_type=jnp.float32)
            * score_scale
        )
        grad_value = jnp.einsum(
            "hqk,qhe->khe", probs_low, grad_heads, preferred_element_type=jnp.float32
        )
        group_width = 4 * HD
        return (
            grad_query.reshape(row_count, group_width),
            grad_key.reshape(row_count, group_width),
            grad_value.reshape(row_count, group_width),
        )

    grad_q_groups, grad_k_groups, grad_v_groups = lax.map(
        attend_back, (query_groups, key_groups, value_groups, stack_groups(grad_mixed), log_totals)
    )
    grad_query = rotated(unstack_groups(grad_q_groups), -1.0)
    grad_key = rotated(unstack_groups(grad_k_groups), -1.0)
    grad_value = (
        unstack_groups(grad_v_groups)
        + live_rows * value_cotangent.reshape(row_count, model_width).astype(jnp.float32)
    ).astype(jnp.bfloat16)
    query_term = jnp.einsum("rd,re->de", normed, grad_query, preferred_element_type=jnp.float32)
    key_term = jnp.einsum("rd,re->de", normed, grad_key, preferred_element_type=jnp.float32)
    value_term = jnp.einsum("rd,re->de", normed, grad_value, preferred_element_type=jnp.float32)
    grad_normed = jnp.einsum(
        "re,de->rd", grad_query, query_full, preferred_element_type=jnp.float32
    )
    grad_normed = grad_normed + jnp.einsum(
        "re,de->rd", grad_key, key_full, preferred_element_type=jnp.float32
    )
    grad_normed = grad_normed + jnp.einsum(
        "re,de->rd", grad_value, value_full, preferred_element_type=jnp.float32
    )
    grad_inputs_norm, gain_one_term = norm_back(
        grad_normed, inputs_f, scale_one, gain_one.astype(jnp.float32)
    )
    token_grad = (grad_middle + grad_inputs_norm).astype(jnp.bfloat16).reshape(tokens.shape)
    grads = reduce_set(
        gain_one_term,
        gain_two_term,
        query_term,
        key_term,
        value_term,
        output_term,
        gate_term,
        up_term,
        down_term,
    )
    return (
        block_out.reshape(tokens.shape),
        first_values.reshape(tokens.shape),
        token_grad,
        grads[0],
        grads[2],
        grads[3],
        grads[4],
        grads[5],
        grads[1],
        grads[6],
        grads[7],
        grads[8],
    )


def plain_gather(*shards_in):
    return tuple(lax.all_gather(s, BOTH, axis=0, tiled=True) for s in shards_in)


def plain_reduce(*terms):
    return tuple(lax.psum_scatter(t, BOTH, scatter_dimension=0, tiled=True) for t in terms)


def linked_layer(mesh, *args):
    tokens, counts, segments, positions, norm_first = args[:5]
    norm_second, out_cotangent, value_cotangent = args[9], args[13], args[14]
    weights = args[5:9] + args[10:13]
    each = norm_first.shape[0]
    full, saved = forward(mesh, tokens, counts, segments, positions, norm_first, norm_second, weights)
    block, token_grad, _, gains, *grads = backward(
        mesh, full, saved, tokens, counts, out_cotangent, value_cotangent, weights[-1].shape[0]
    )
    one, two, block, first, token_grad, *grads = hand_over(gains, each, [block, saved.first, token_grad] + grads)
    streams = tuple(a.reshape(tokens.shape) for a in (block, first, token_grad))
    return streams + (one.reshape(each), *grads[:4], two.reshape(each), *grads[4:])


def fits(mesh, tokens, weights):
    return (
        dict(mesh.shape) == {DP: 4, FSDP: 8}
        and tokens == (4, 128, 1024)
        and all(w == (32, 1024) for w in weights[:4])
        and weights[4:] == ((32, 2816), (32, 2816), (88, 1024))
    )


def solution(mesh):
    one, two, three = P(BOTH), P(BOTH, None), P(BOTH, None, None)
    in_specs = (three, one, two, two, one, two, two, two, two, one, two, two, two, three, three)
    out_specs = (three, three, three, one, two, two, two, two, one, two, two, two)

    def shards(*args):
        weights = tuple(w.shape for w in args[5:9] + args[10:13])
        if fits(mesh, args[0].shape, weights):
            return linked_layer(mesh, *args)
        return layer(plain_gather, plain_reduce, *args)

    return jax.shard_map(shards, mesh=mesh, in_specs=in_specs, out_specs=out_specs, check_vma=False)
```

```python
import math
from typing import Any, NamedTuple

import jax
import jax.numpy as jnp
import numpy as np
from jax import lax
from jax.experimental import pallas as pl
from jax.experimental.pallas import tpu as pltpu
from jax.sharding import PartitionSpec as P

HD = 64
MESH = pl.DeviceIdType.MESH
DP, FSDP = "dp", "fsdp"
BOTH = (DP, FSDP)
LOW, FULL = jnp.bfloat16, jnp.float32
WIDE = 256

eps = 1e-06


class Weights(NamedTuple):
    gains: Any
    query: Any
    key: Any
    value: Any
    output: Any
    gate: Any
    up: Any
    down: Any


class Saved(NamedTuple):
    cos: Any
    sin: Any
    normed_t: Any
    q_rot: Any
    k_rot: Any
    v_low: Any
    probs: Any
    mixed_t: Any
    middle: Any
    two_t: Any
    hid_t: Any
    t1: Any
    t2: Any
    first: Any


W = Weights._make(range(len(Weights._fields)))
S = Saved._make(range(len(Saved._fields)))


class Place:
    def __init__(self, depth):
        dp, fsdp = lax.axis_index(DP), lax.axis_index(FSDP)
        self.x, self.c = dp // 2, dp % 2
        self.z, self.y = fsdp // 2, fsdp % 2
        self.depth = depth

    def at(self, x, c, z, y):
        return (x * 2 + c, z * 2 + y)

    def across_x(self):
        return self.at(1 - self.x, self.c, self.z, self.y)

    def across_y(self):
        return self.at(self.x, self.c, self.z, 1 - self.y)

    def sibling(self):
        return self.at(self.x, 1 - self.c, self.z, self.y)

    def above(self):
        return self.at(self.x, self.c, self.z + 1, self.y)

    def below(self):
        return self.at(self.x, self.c, self.z - 1, self.y)

    def greet(self):
        barrier = pltpu.get_barrier_semaphore()

        def call(who):
            pl.semaphore_signal(barrier, inc=1, device_id=who, device_id_type=MESH)

        call(self.across_x())
        call(self.across_y())
        call(self.sibling())
        not_top = self.z < self.depth - 1
        not_low = self.z > 0
        pl.when(not_top)(lambda: call(self.above()))
        pl.when(not_low)(lambda: call(self.below()))
        peers = 3 + not_top.astype(jnp.int32) + not_low.astype(jnp.int32)
        pl.semaphore_wait(barrier, peers)


def remote(src, dst, send_sem, recv_sem, who):
    return pltpu.make_async_remote_copy(
        src_ref=src,
        dst_ref=dst,
        send_sem=send_sem,
        recv_sem=recv_sem,
        device_id=who,
        device_id_type=MESH,
    )


def iota(shape, dim):
    return lax.broadcasted_iota(jnp.int32, shape, dim)


def dot(a, b, dims=((1,), (0,))):
    return lax.dot_general(a, b, (dims, ((), ())), preferred_element_type=FULL)


def to_column(row):
    n = row.shape[1]
    eye = iota((n, n), 0) == iota((n, n), 1)
    return jnp.sum(jnp.where(eye, jnp.broadcast_to(row, (n, n)), 0.0), axis=1, keepdims=True)


def turn(values, cosine, sines):
    outs = []
    first = iota((values.shape[0], 128), 1) % HD < HD // 2
    for g in range(values.shape[1] // 128):
        part = values[:, g * 128 : (g + 1) * 128]
        other = jnp.where(
            first, pltpu.roll(part, 128 - HD // 2, 1), pltpu.roll(part, HD // 2, 1)
        )
        outs.append(part * cosine + other * sines)
    return jnp.concatenate(outs, axis=1)


def gain_row(gains, row, each):
    count = gains.shape[0]
    rows = gains[:, row, :]
    whole = jnp.concatenate([rows] * (count * each // 128), axis=1)
    shape = whole.shape
    keep = iota(shape, 1) // each == iota(shape, 0)
    return jnp.sum(jnp.where(keep, whole, 0.0), axis=0, keepdims=True)


def split_pair(values):
    first = iota(values.shape, 1) < HD
    zero = jnp.zeros_like(values)
    return jnp.concatenate([jnp.where(first, values, zero), jnp.where(first, zero, values)], axis=0)


class Gather:
    def __init__(self, place, own, full, sends, receipts, local_sem, z_first):
        self.p, self.own, self.full, self.z_first = place, own, full, z_first
        self.sends, self.receipts, self.local_sem = sends, receipts, local_sem
        self.wide = own.shape[-1]

    def shard(self, x, y, z):
        return self.full.at[x, self.p.c, z, y]

    def zunit(self, z):
        if self.z_first:
            return self.full.at[self.p.x, self.p.c, z, self.p.y]
        return self.full.at[:, self.p.c, z]

    def runit(self, x, y, half=None):
        if self.z_first:
            if half is None:
                return self.full.at[x, self.p.c, :, y]
            count = self.p.depth // 2
            return self.full.at[x, self.p.c, half * count : (half + 1) * count, y]
        if half is None:
            return self.full.at[x, self.p.c, self.p.z, y]
        count = self.wide // 2
        return self.full.at[x, self.p.c, self.p.z, y, :, half * count : (half + 1) * count]

    def copy(self, ref, slot, who, src=None):
        return remote(ref if src is None else src, ref, self.sends.at[slot], self.receipts.at[slot], who)

    def up(self, unit, src=None):
        return self.copy(self.zunit(unit), unit, self.p.above(), src)

    def down(self, unit, src=None):
        return self.copy(self.zunit(unit), self.p.depth - 2 + unit, self.p.below(), src)

    def ring_slot(self, i):
        return 2 * (self.p.depth - 1) + i

    def keep_own(self):
        p = self.p
        return pltpu.make_async_copy(self.own, self.shard(p.x, p.y, p.z), self.local_sem)

    def z_step(self, step):
        p = self.p
        top, low = p.depth - 1, 0
        src = self.own if (step == 0 and self.z_first) else None

        def from_below():
            if step > 0:
                self.up(p.z - step).wait_recv()
            if step < top:
                pl.when(p.z < top)(lambda: self.up(p.z - step, src).start())

        def from_above():
            if step > 0:
                self.down(p.z + step).wait_recv()
            if step < top:
                pl.when(p.z > low)(lambda: self.down(p.z + step, src).start())

        pl.when(p.z - step >= low)(from_below)
        pl.when(p.z + step <= top)(from_above)

    def ring_first(self):
        p = self.p
        mine = self.runit(p.x, p.y)
        src = None if self.z_first else self.own
        self.copy(mine, self.ring_slot(0), p.across_x(), src).start()
        self.copy(mine, self.ring_slot(1), p.across_y(), src).start()

    def ring_second(self):
        p = self.p
        from_x, from_y = self.runit(1 - p.x, p.y), self.runit(p.x, 1 - p.y)
        self.copy(from_x, self.ring_slot(0), p.across_x()).wait_recv()
        self.copy(self.runit(1 - p.x, p.y, 0), self.ring_slot(2), p.across_y()).start()
        self.copy(from_y, self.ring_slot(1), p.across_y()).wait_recv()
        self.copy(self.runit(p.x, 1 - p.y, 1), self.ring_slot(3), p.across_x()).start()

    def ring_last(self):
        p = self.p
        self.copy(self.runit(1 - p.x, 1 - p.y, 0), self.ring_slot(2), p.across_y()).wait_recv()
        self.copy(self.runit(1 - p.x, 1 - p.y, 1), self.ring_slot(3), p.across_x()).wait_recv()

    def given(self, kind, core):
        p = self.p
        if self.z_first:
            x = (p.x, 1 - p.x, p.x, 1 - p.x)[kind]
            y = (p.y, p.y, 1 - p.y, 1 - p.y)[kind]
            return self.full.at[x, core, :, y]
        return self.full.at[:, core, kind]

    def give(self, ref, kind):
        self.copy(ref, self.ring_slot(4 + kind), self.p.sibling()).start()

    def pass_on(self, step):
        p = self.p

        def low():
            self.give(self.full.at[:, p.c, p.z - step], p.z - step)

        def high():
            self.give(self.full.at[:, p.c, p.z + step], p.z + step)

        pl.when(p.z - step >= 0)(low)
        if step > 0:
            pl.when(p.z + step <= p.depth - 1)(high)

    def steps(self):
        mine = lambda kind: self.give(self.given(kind, self.p.c), kind)
        if self.z_first:
            return [
                lambda: (self.keep_own().start(), self.z_step(0)),
                lambda: self.z_step(1),
                lambda: self.z_step(2),
                lambda: (self.z_step(3), self.keep_own().wait(), self.ring_first(), mine(0)),
                lambda: (self.ring_second(), mine(1), mine(2)),
                lambda: (self.ring_last(), mine(3)),
                self.finish,
            ]
        return [
            lambda: (self.keep_own().start(), self.ring_first()),
            self.ring_second,
            lambda: (self.ring_last(), self.keep_own().wait(), self.z_step(0), self.pass_on(0)),
            lambda: (self.z_step(1), self.pass_on(1)),
            lambda: (self.z_step(2), self.pass_on(2)),
            lambda: (self.z_step(3), self.pass_on(3)),
            self.finish,
        ]

    def finish(self):
        p = self.p
        for kind in range(4):
            self.copy(self.given(kind, 1 - p.c), self.ring_slot(4 + kind), p.sibling()).wait_recv()

    def sent(self):
        p = self.p
        top = p.depth - 1
        for unit in range(p.depth):
            if unit < top:
                pl.when((p.z < top) & (unit <= p.z))(lambda unit=unit: self.up(unit).wait_send())
            if unit > 0:
                pl.when((p.z > 0) & (unit >= p.z))(lambda unit=unit: self.down(unit).wait_send())
        self.copy(self.runit(p.x, p.y), self.ring_slot(0), p.across_x()).wait_send()
        self.copy(self.runit(p.x, p.y), self.ring_slot(1), p.across_y()).wait_send()
        self.copy(self.runit(1 - p.x, p.y, 0), self.ring_slot(2), p.across_y()).wait_send()
        self.copy(self.runit(p.x, 1 - p.y, 1), self.ring_slot(3), p.across_x()).wait_send()
        for kind in range(4):
            self.copy(self.given(kind, p.c), self.ring_slot(4 + kind), p.sibling()).wait_send()


GATHER_JOBS = (
    (W.gains, True, None),
    (W.query, True, None),
    (W.key, True, None),
    (W.value, True, None),
    (W.output, True, None),
    (W.down, False, (0, 1)),
    (W.down, False, (1, 2)),
    (W.gate, True, (0, 6)),
    (W.up, True, (0, 6)),
    (W.gate, True, (6, 9)),
    (W.up, True, (6, 9)),
    (W.gate, True, (9, 11)),
    (W.up, True, (9, 11)),
)
FORWARD_ORDER = (
    0, 63, 14, 42, 1, 35, 64, 2, 65, 15, 3, 43, 7, 36, 4, 66, 16, 17, 28, 8, 84, 91, 5, 6, 9, 49, 29, 21, 10, 30, 77,
    18, 56, 50, 31, 22, 85, 70, 23, 11, 92, 19, 57, 71, 51, 44, 24, 32, 12, 20, 72, 93, 58, 25, 52, 96, 37, 13, 94,
    95, 78, 59, 26, 27, 86, 97, 33, 45, 53, 98, 34, 79, 99, 100, 101, 60, 104, 38, 73, 102, 80, 103, 105, 46, 54, 55,
    107, 87, 61, 62, 108, 39, 106, 74, 67, 109, 47, 81, 75, 88, 76, 111, 68, 82, 69, 110, 83, 113, 89, 48, 40, 90,
    114, 112, 41, 115,
)


class Forward:
    def __init__(self, place, **refs):
        self.p = place
        self.__dict__.update(refs)
        self.slots, self.length = self.segments.shape
        self.rows, self.width = self.slots * self.length, self.v.middle.shape[1]
        self.loads = 0

    def loader(self, which, cols=None):
        full, near = self.full[which], self.near[which]
        if cols is not None:
            cut = slice(*cols)
            full, near = full.at[:, :, :, :, :, cut], near.at[:, :, :, :, :, cut]
        copy = lambda slot=self.loads: pltpu.make_async_copy(full, near, self.load_sems.at[slot])
        self.loads += 1
        return (lambda: copy().start()), (lambda: copy().wait())

    def save(self, *which):
        for i in which:
            pltpu.make_async_copy(self.v[i], self.o[i], self.save_sems.at[i]).start()

    def own_shards(self):
        each = self.norm_first.shape[1]
        spread = (iota((each, 128), 1) % each == iota((each, 128), 0)).astype(LOW)
        sub = iota((8, 128), 0)
        one, two = dot(self.norm_first[...], spread), dot(self.norm_second[...], spread)
        self.own_gains[...] = jnp.where(sub == 0, one, jnp.where(sub == 1, two, 0.0))
        rows, half = self.down_weight.shape[0], self.down_weight.shape[1] // 2
        down = self.down_weight[...].astype(FULL)
        self.own_down[...] = jnp.concatenate([down[:, :half], down[:, half:]], axis=0).astype(LOW)

    def tables(self):
        for b in range(self.slots):
            rows = pl.ds(b * self.length, self.length)
            angles = to_column(self.positions[b : b + 1, :].astype(FULL)) * self.inverse[...]
            first = iota(angles.shape, 1) % HD < HD // 2
            sines = jnp.sin(angles)
            self.v.cos[rows, :] = jnp.cos(angles)
            self.v.sin[rows, :] = jnp.where(first, -sines, sines)
            seg = self.segments[b : b + 1, :].astype(FULL)
            shape = (self.length, self.length)
            allowed = (to_column(seg) == seg) & (iota(shape, 0) >= iota(shape, 1))
            self.bias[b] = jnp.where(allowed, 0.0, -1e30)
        self.live[...] = (iota((self.rows, 128), 0) // self.length < self.counts[0]).astype(FULL)
        self.save(S.cos, S.sin)

    def gain_rows(self):
        start, wait = self.loader(W.gains)
        start()
        wait()
        near = self.near.gains
        count = math.prod(near.shape[:4])
        gains = near[...].reshape(count, 8, 128)
        self.gain[0:1, :] = gain_row(gains, 0, self.width // count)
        self.gain[1:2, :] = gain_row(gains, 1, self.width // count)

    def norm_one(self):
        for b in range(self.slots):
            rows = pl.ds(b * self.length, self.length)
            inputs = self.tokens[rows, :].astype(FULL)
            scale = lax.rsqrt(jnp.mean(inputs * inputs, axis=-1, keepdims=True) + eps)
            normed = (inputs * scale * self.gain[0:1, :]).astype(LOW)
            self.normed[rows, :] = normed
            self.v.normed_t[:, rows] = normed.T
        self.save(S.normed_t)

    def weight(self, which, cols):
        w = self.near[which][:, :, :, :, :, cols]
        return w.reshape(math.prod(w.shape[:5]), w.shape[5])

    def project(self, which, wait):
        wait()
        normed = self.normed[...]

        def tile(n, carry):
            cols = pl.ds(pl.multiple_of(n * WIDE, WIDE), WIDE)
            got = dot(normed, self.weight(which, cols))
            if which == W.value:
                low = got.astype(LOW)
                self.v.v_low[:, cols] = low
                self.v.first[:, cols] = (self.live[...][:, 0:1] * low.astype(FULL)).astype(LOW)
            else:
                into = self.v.q_rot if which == W.query else self.v.k_rot
                into[:, cols] = turn(got, self.v.cos[...], self.v.sin[...]).astype(LOW)
            return carry

        lax.fori_loop(0, self.width // WIDE, tile, 0)
        if which == W.value:
            self.save(S.v_low, S.first)
        else:
            self.save(S.q_rot if which == W.query else S.k_rot)

    def attend(self, b):
        length = self.length
        rows = pl.ds(b * length, length)

        def pair(h, carry):
            cols = pl.ds(pl.multiple_of(h * 128, 128), 128)
            q, k, v = self.v.q_rot[rows, cols], self.v.k_rot[rows, cols], self.v.v_low[rows, cols]
            k2, v2 = split_pair(k), split_pair(v)
            scores = dot(q, k2, ((1,), (1,))) * HD ** (-0.5)
            bias = self.bias[b]
            probs = []
            for half in range(2):
                s = scores[:, half * length : (half + 1) * length] + bias
                e = jnp.exp(s - jnp.max(s, axis=-1, keepdims=True))
                probs.append(e * (1.0 / jnp.sum(e, axis=-1, keepdims=True)))
            probs = jnp.concatenate(probs, axis=1).astype(LOW)
            self.v.probs[b, h] = probs
            self.mixed[rows, cols] = dot(probs, v2).astype(LOW)
            return carry

        lax.fori_loop(0, self.width // 128, pair, 0, unroll=True)
        self.v.mixed_t[:, rows] = self.mixed[rows, :].T
        if b == self.slots - 1:
            self.save(S.probs, S.mixed_t)

    def join(self, wait):
        wait()
        mixed = self.mixed[...]

        def tile(n, carry):
            cols = pl.ds(pl.multiple_of(n * WIDE, WIDE), WIDE)
            got = dot(mixed, self.weight(W.output, cols))
            self.v.middle[:, cols] = self.tokens[:, cols].astype(FULL) + got
            return carry

        lax.fori_loop(0, self.width // WIDE, tile, 0)
        self.save(S.middle)

    def norm_two(self):
        for b in range(self.slots):
            rows = pl.ds(b * self.length, self.length)
            middle = self.v.middle[rows, :]
            scale = lax.rsqrt(jnp.mean(middle * middle, axis=-1, keepdims=True) + eps)
            normed = (middle * scale * self.gain[1:2, :]).astype(LOW)
            self.two[rows, :] = normed
            self.v.two_t[:, rows] = normed.T
        self.save(S.two_t)

    def hidden(self, lo, hi, wait_gate, wait_up):
        wait_gate()
        wait_up()
        two = self.two[...]

        def tile(n, carry):
            cols = pl.ds(pl.multiple_of(lo + n * WIDE, WIDE), WIDE)
            gate = dot(two, self.weight(W.gate, cols))
            upward = dot(two, self.weight(W.up, cols))
            sig = 1.0 / (1.0 + jnp.exp(-gate))
            silu = gate * sig
            self.v.hid_t[cols, :] = (silu * upward).astype(LOW).T
            self.v.t1[:, cols] = (upward * sig * (1.0 + gate * (1.0 - sig))).astype(LOW)
            self.v.t2[:, cols] = silu.astype(LOW)
            for i, at in ((S.hid_t, (cols,)), (S.t1, (slice(None), cols)), (S.t2, (slice(None), cols))):
                pltpu.make_async_copy(self.v[i].at[at], self.o[i].at[at], self.save_sems.at[i]).start()
            return carry

        lax.fori_loop(0, (hi - lo) // WIDE, tile, 0)

    def steps(self):
        todo = [self.tables, self.gain_rows, self.norm_one]

        def after(which, action, *args):
            start, wait = self.loader(which)
            todo.extend([start, lambda: action(*args, wait)])

        for which in (W.query, W.key, W.value):
            after(which, self.project, which)
        for b in range(self.slots):
            todo.append(lambda b=b: self.attend(b))
        after(W.output, self.join)
        todo.append(self.norm_two)
        for which, _, cols in GATHER_JOBS:
            if which == W.gate:
                cols = (cols[0] * WIDE, cols[1] * WIDE)
                gate, up = self.loader(W.gate, cols), self.loader(W.up, cols)
                todo += [gate[0], up[0], lambda c=cols, g=gate, u=up: self.hidden(*c, g[1], u[1])]
        return todo


def forward_kernel(depth, *refs):
    refs = list(refs)

    def take(count):
        got = refs[:count]
        del refs[:count]
        return got

    kinds = len(Weights._fields)
    tokens, counts, segments, positions, inverse, norm_first, norm_second = take(7)
    given = take(kinds - 1)
    full = Weights._make(take(kinds))
    o = Saved._make(take(len(Saved._fields)))
    v = Saved._make(take(len(Saved._fields)))
    near = Weights._make(take(kinds - 1) + [None])
    gain, normed, mixed, two, bias, live, own_gains, own_down = take(8)
    sends, receipts, local_sems, load_sems, save_sems = take(5)
    place = Place(depth)
    work = Forward(
        place, tokens=tokens, counts=counts, segments=segments, positions=positions, inverse=inverse,
        norm_first=norm_first, norm_second=norm_second, down_weight=given[-1], full=full, o=o, v=v, near=near,
        gain=gain, normed=normed, mixed=mixed, two=two, bias=bias, live=live, own_gains=own_gains,
        own_down=own_down, load_sems=load_sems, save_sems=save_sems,
    )
    owns = Weights._make([own_gains] + given[:-1] + [own_down])
    jobs = []
    for i, (which, z_first, cols) in enumerate(GATHER_JOBS):
        own, whole = owns[which], full[which]
        if cols is not None:
            cut = slice(cols[0] * WIDE, cols[1] * WIDE)
            own, whole = own.at[:, cut], whole.at[:, :, :, :, :, cut]
        jobs.append(Gather(place, own, whole, sends.at[i], receipts.at[i], local_sems.at[i], z_first))
    actions = [step for job in jobs for step in job.steps()] + work.steps()
    assert sorted(FORWARD_ORDER) == list(range(len(actions)))
    work.own_shards()
    place.greet()
    for i in FORWARD_ORDER:
        actions[i]()
    for job in jobs:
        job.sent()
    for i in range(len(v)):
        pltpu.make_async_copy(v[i], o[i], save_sems.at[i]).wait()


def forward(mesh, tokens, counts, segments, positions, norm_first, norm_second, weights):
    depth = mesh.shape[FSDP] // 2
    slots, length, width = tokens.shape
    rows, each = slots * length, norm_first.shape[0]
    down_rows, hidden = weights[-1].shape[0], weights[W.gate - 1].shape[1]
    lead = (2, 2, depth, 2)
    flat, tall = ((rows, width), LOW), ((width, rows), LOW)
    saved = Saved(
        cos=((rows, 128), FULL),
        sin=((rows, 128), FULL),
        normed_t=tall,
        q_rot=flat,
        k_rot=flat,
        v_low=flat,
        probs=((slots, width // 128, length, 2 * length), LOW),
        mixed_t=tall,
        middle=((rows, width), FULL),
        two_t=tall,
        hid_t=((hidden, rows), LOW),
        t1=((rows, hidden), LOW),
        t2=((rows, hidden), LOW),
        first=flat,
    )
    owns = [((8, 128), FULL)] + [(w.shape, LOW) for w in weights[:-1]] + [((2 * down_rows, width // 2), LOW)]
    fulls = [(lead + shape, kind) for shape, kind in owns]
    inverse = jnp.asarray(
        np.exp((np.arange(128) % (HD // 2)) * (-2.0 * math.log(10000.0) / HD)), FULL
    )[None, :]
    vmem, anywhere = pl.BlockSpec(memory_space=pltpu.VMEM), pl.BlockSpec(memory_space=pl.ANY)
    smem = pl.BlockSpec(memory_space=pltpu.SMEM)
    jobs = len(GATHER_JOBS)
    got = pl.pallas_call(
        lambda *refs: forward_kernel(depth, *refs),
        out_shape=tuple(jax.ShapeDtypeStruct(*a) for a in fulls + list(saved)),
        in_specs=[vmem, smem] + [vmem] * 5 + [anywhere] * (len(weights) - 1) + [vmem],
        out_specs=tuple([anywhere] * (len(fulls) + len(saved))),
        scratch_shapes=[pltpu.VMEM(*a) for a in list(saved) + fulls[:-1]]
        + [
            pltpu.VMEM((8, width), FULL),
            pltpu.VMEM(*flat),
            pltpu.VMEM(*flat),
            pltpu.VMEM(*flat),
            pltpu.VMEM((slots, length, length), FULL),
            pltpu.VMEM((rows, 128), FULL),
            pltpu.VMEM(*owns[0]),
            pltpu.VMEM(*owns[-1]),
            pltpu.SemaphoreType.DMA((jobs, 2 * (depth - 1) + 8)),
            pltpu.SemaphoreType.DMA((jobs, 2 * (depth - 1) + 8)),
            pltpu.SemaphoreType.DMA((jobs,)),
            pltpu.SemaphoreType.DMA((5 + 2 * sum(job[0] == W.gate for job in GATHER_JOBS),)),
            pltpu.SemaphoreType.DMA((len(saved),)),
        ],
        compiler_params=pltpu.CompilerParams(
            collective_id=1, has_side_effects=True, vmem_limit_bytes=60 * 2**20
        ),
        cost_estimate=pl.CostEstimate(
            flops=2 * rows * width * (4 * width + 2 * hidden), bytes_accessed=80 * 2**20, transcendentals=2**22
        ),
        name="gather_and_forward",
    )(
        tokens.reshape(rows, width), counts, segments, positions, inverse,
        norm_first.reshape(1, each), norm_second.reshape(1, each), *weights,
    )
    return Weights._make(got[: len(fulls)]), Saved._make(got[len(fulls) :])


def add_block(into, other):
    into[...] = into[...] + other[...]


class Buffers(NamedTuple):
    acc: Any
    stage: Any
    sib: Any
    ring1: Any
    ring2: Any
    zed: Any
    sends: Any
    receipts: Any
    credit: Any


class Reduce:
    def __init__(self, place, index, count, slots, z_first, buffers, emit):
        self.p, self.z_first, self.b, self.emit = place, z_first, buffers, emit
        self.k, self.count, self.slots = index, count, slots
        rows = buffers.acc.shape[3]
        self.cut = (rows // 2 + 15) // 16 * 16

    def copy(self, src, dst, slot, who):
        return remote(src, dst, self.b.sends.at[slot], self.b.receipts.at[slot], who)

    def sib_copy(self):
        return self.copy(self.b.stage, self.b.sib, 0, self.p.sibling())

    def free_stage(self):
        self.sib_copy().wait_send()

    def send(self):
        if self.k >= self.slots:
            pl.semaphore_wait(self.b.credit, 1)
        self.sib_copy().start()

    def merge(self):
        self.sib_copy().wait_recv()
        depth = self.p.depth

        def block(i, carry):
            at = (i // (2 * depth), i // 2 % depth, i % 2)
            self.b.acc[at] = self.b.acc[at] + self.b.sib[at]
            return carry

        lax.fori_loop(0, 4 * depth, block, 0)
        if self.k + self.slots < self.count:
            pl.semaphore_signal(
                self.b.credit, inc=1, device_id=self.p.sibling(), device_id_type=MESH
            )

    def bundle(self, x, y):
        if self.z_first:
            return self.b.acc.at[x, self.p.z, y]
        return self.b.acc.at[x, :, y]

    def halves(self, ref):
        cut = self.cut if self.z_first else self.p.depth // 2
        return ref.at[:cut], ref.at[cut:]

    def first_copies(self):
        p = self.p
        low, high = self.halves(self.bundle(1 - p.x, 1 - p.y))
        to_low, to_high = self.halves(self.b.ring1)
        return (
            self.copy(low, to_low, 1, p.across_x()),
            self.copy(high, to_high, 2, p.across_y()),
        )

    def second_copies(self):
        p = self.p
        return (
            self.copy(self.bundle(1 - p.x, p.y), self.b.ring2.at[0], 3, p.across_x()),
            self.copy(self.bundle(p.x, 1 - p.y), self.b.ring2.at[1], 4, p.across_y()),
        )

    def ring_first(self):
        for copy in self.first_copies():
            copy.start()

    def ring_second(self):
        p = self.p
        by_x, by_y = self.first_copies()
        to_x, to_y = self.second_copies()
        got_low, got_high = self.halves(self.b.ring1)
        by_x.wait_recv()
        add_block(self.halves(self.bundle(p.x, 1 - p.y))[0], got_low)
        to_y.start()
        by_y.wait_recv()
        add_block(self.halves(self.bundle(1 - p.x, p.y))[1], got_high)
        to_x.start()

    def ring_last(self):
        p = self.p
        for copy in self.second_copies():
            copy.wait_recv()
        both = self.b.ring2[0].astype(FULL) + self.b.ring2[1].astype(FULL)
        return self.bundle(p.x, p.y)[...].astype(FULL) + both

    def zunits(self, units):
        if self.z_first:
            return self.b.acc.at[:, units]
        return self.b.acc.at[self.p.x, units, self.p.y]

    def landing(self, side, units):
        if self.z_first:
            return self.b.zed.at[side, :, units]
        return self.b.zed.at[side, units]

    def up(self, step):
        top = self.p.depth - 1
        return self.copy(self.zunits(slice(step + 1, top + 1)), self.landing(0, slice(step, top)), 5, self.p.above())

    def down(self, step):
        count = self.p.depth - 1 - step
        return self.copy(self.zunits(slice(0, count)), self.landing(1, slice(0, count)), 6, self.p.below())

    def z_step(self, step):
        p, top = self.p, self.p.depth - 1

        def upward():
            if step > 0:
                self.up(step - 1).wait_recv()
            if step < top:
                if step > 0:
                    add_block(self.zunits(slice(step + 1, top + 1)), self.landing(0, slice(step, top)))
                self.up(step).start()

        def downward():
            if step > 0:
                self.down(step - 1).wait_recv()
            if step < top:
                if step > 0:
                    add_block(self.zunits(slice(0, top - step)), self.landing(1, slice(0, top - step)))
                self.down(step).start()

        pl.when(p.z == step)(upward)
        pl.when(p.z == top - step)(downward)

    def z_sum(self, put):
        p, top = self.p, self.p.depth - 1
        mine = self.zunits(p.z)[...].astype(FULL)

        @pl.when(p.z == 0)
        def _():
            put(mine + self.landing(1, 0)[...].astype(FULL))

        @pl.when(p.z == top)
        def _():
            put(mine + self.landing(0, top - 1)[...].astype(FULL))

        @pl.when((p.z > 0) & (p.z < top))
        def _():
            low, high = self.landing(0, p.z - 1)[...], self.landing(1, p.z)[...]
            put(mine + (low.astype(FULL) + high.astype(FULL)))

    def steps(self):
        kind = self.b.acc.dtype

        def keep_ring():
            self.bundle(self.p.x, self.p.y)[...] = self.ring_last().astype(kind)
            self.z_step(0)

        def keep_z(values):
            self.zunits(self.p.z)[...] = values.astype(kind)

        if self.z_first:
            return [
                self.send,
                lambda: (self.merge(), self.z_step(0)),
                lambda: self.z_step(1),
                lambda: self.z_step(2),
                lambda: (self.z_step(3), self.z_sum(keep_z), self.ring_first()),
                self.ring_second,
                lambda: self.emit(self.ring_last()),
            ]
        return [
            self.send,
            lambda: (self.merge(), self.ring_first()),
            self.ring_second,
            keep_ring,
            lambda: self.z_step(1),
            lambda: self.z_step(2),
            lambda: (self.z_step(3), self.z_sum(self.emit)),
        ]

    def sent(self):
        p, top = self.p, self.p.depth - 1
        if self.k + self.slots >= self.count:
            self.free_stage()
        for copy in self.first_copies() + self.second_copies():
            copy.wait_send()
        for step in range(top):
            pl.when(p.z == step)(lambda step=step: self.up(step).wait_send())
            pl.when(p.z == top - step)(lambda step=step: self.down(step).wait_send())


DOWN, SIDE, GAIN = range(3)
SLOTS = (2, 3, 1)
Z_FIRST = (True, False, False)
BACKWARD_ORDER = (
    168, 169, 0, 170, 171, 172, 173, 174, 7, 175, 1, 176, 177, 28, 178, 35, 29, 14, 179, 36, 8, 21, 15, 42, 30, 180,
    49, 43, 37, 181, 56, 50, 182, 57, 44, 63, 183, 70, 51, 184, 64, 71, 185, 58, 45, 77, 84, 186, 91, 65, 78, 85, 187,
    22, 188, 92, 98, 2, 189, 16, 72, 99, 46, 190, 191, 105, 192, 112, 9, 79, 193, 52, 106, 113, 31, 93, 100, 194, 195,
    114, 80, 53, 59, 196, 197, 107, 32, 198, 119, 3, 199, 66, 126, 200, 86, 73, 38, 120, 17, 133, 201, 202, 127, 94,
    140, 23, 134, 54, 203, 147, 141, 154, 10, 47, 108, 39, 33, 101, 87, 67, 204, 74, 128, 60, 121, 148, 155, 205, 206,
    207, 109, 81, 135, 129, 24, 208, 102, 142, 95, 75, 115, 149, 88, 130, 122, 209, 61, 156, 68, 116, 40, 110, 131,
    136, 55, 137, 143, 96, 161, 18, 162, 123, 25, 11, 4, 117, 144, 150, 151, 34, 157, 76, 163, 132, 103, 138, 12, 82,
    158, 19, 124, 164, 5, 62, 165, 145, 26, 125, 152, 69, 41, 89, 48, 159, 13, 139, 146, 111, 153, 20, 166, 27, 6, 90,
    104, 97, 118, 83, 160, 167,
)


def chunk_list(tiles, width):
    halves = width // (2 * WIDE)
    chunks = [(DOWN, W.down, n) for n in range(width // WIDE)]
    chunks += [(SIDE, W.gate, f) for f in range(tiles)]
    chunks += [(SIDE, w, half) for w in (W.output, W.query, W.key, W.value) for half in range(halves)]
    return chunks + [(GAIN, W.gains, 0)]


class First(NamedTuple):
    hid_t: Any
    branch: Any
    raw: Any
    down: Any
    two_t: Any
    middle: Any
    tile: Any
    t: Any
    both: Any


class Second(NamedTuple):
    w: Any
    mixed_t: Any
    normed_t: Any
    v_low: Any
    probs: Any
    cos: Any
    sin: Any
    tokens: Any
    gmixed: Any
    gq: Any
    gk: Any
    gv: Any
    gnormed: Any


class Third(NamedTuple):
    hid_t: Any
    down: Any
    middle: Any
    out: Any


class Backward:
    def __init__(self, place, **refs):
        self.p = place
        self.__dict__.update(refs)
        self.rows, self.width = self.tokens.shape
        self.tiles = self.full.gate.shape[-1] // WIDE
        self.loads = 0
        self.pending = {}

    def fetch(self, key, src, dst):
        copy = pltpu.make_async_copy(src, dst, self.load_sems.at[self.loads])
        self.loads += 1
        self.pending[key] = copy
        copy.start()

    def arrived(self, *keys):
        for key in keys:
            self.pending.pop(key).wait()

    def block_rows(self, b):
        return pl.ds(b * self.length, self.length)

    def live(self, b):
        return (jnp.int32(b) < self.counts[0]).astype(FULL)

    def spread(self, job, part):
        p = self.p
        if job.before is not None:
            job.before.free_stage()
        for x in range(2):
            part(x, 1 - p.c, job.b.stage)
            part(x, p.c, job.b.acc)

    def side_by_side(self, job, left, right):
        count = self.width // 4

        def part(x, c, into):
            at = pl.multiple_of((x * 2 + c) * count, count)
            got = dot(left[pl.ds(at, count), :], right[...]).astype(LOW)
            got = got.reshape(self.p.depth, 2, -1, 2 * WIDE)
            each = got.shape[2]
            into[x, :, :, :each, :] = got[..., :WIDE]
            into[x, :, :, each:, :] = got[..., WIDE:]

        self.spread(job, part)

    def begin(self):
        h, s = self.h, self.s
        self.fetch(-1, self.out_cotangent, h.branch)
        self.fetch(S.hid_t, s.hid_t, h.hid_t)
        self.fetch((W.down, 0), self.full.down.at[0, 0], h.raw)
        self.fetch(S.two_t, s.two_t, h.two_t)
        self.tile_loads(0)
        self.fetch(S.middle, s.middle, h.middle)
        self.fetch((W.gains,), self.full.gains, self.gains_near)
        self.arrived(-1)
        for b in range(self.slots):
            rows = self.block_rows(b)
            h.branch[rows, :] = (h.branch[rows, :].astype(FULL) * self.live(b)).astype(LOW)

    def down_chunk(self, n):
        h = self.h
        if n == 0:
            self.arrived(S.hid_t)
        right = h.branch[:, n * WIDE : (n + 1) * WIDE]
        count = h.hid_t.shape[0] // 4

        def part(x, c, into):
            at = pl.multiple_of((x * 2 + c) * count, 16)
            got = dot(h.hid_t[pl.ds(at, count), :], right)
            got = got.reshape(2 * self.p.depth, -1, WIDE)
            got = jnp.concatenate([got[:, :, : WIDE // 2], got[:, :, WIDE // 2 :]], axis=1)
            into[x] = got.astype(LOW).reshape(into.shape[1:])

        self.spread(self.job[W.down, n], part)

    def down_weight(self, i):
        self.arrived((W.down, i))
        depth, raw, down = self.p.depth, self.h.raw, self.h.down
        rows, half = raw.shape[2] // 2, raw.shape[3]
        for z in range(depth):
            pair = raw[z].astype(FULL)
            for side in range(2):
                part = pair[:, side * rows : (side + 1) * rows, :].reshape(2 * rows, half)
                at = (i * depth + z) * 2 * rows
                down[at : at + 2 * rows, side * half : (side + 1) * half] = part.astype(LOW)
        j = i + 1
        if j < 4:
            self.fetch((W.down, j), self.full.down.at[j // 2, j % 2], raw)
        else:
            self.fetch((W.down,), down, self.down_kept)

    def tile_loads(self, f):
        cols, slot = pl.ds(f * WIDE, WIDE), f % 2
        for which, side in ((W.gate, 0), (W.up, 1)):
            into = self.h.tile.at[slot, :, :, :, :, :, side * WIDE : (side + 1) * WIDE]
            self.fetch((which, f), self.full[which].at[:, :, :, :, :, cols], into)
        for which, side in ((S.t1, 0), (S.t2, 1)):
            self.fetch((f, side, 0), self.s[which].at[:, cols], self.h.t.at[slot, side])

    def ff_tile(self, f):
        h, slot = self.h, f % 2
        self.arrived((W.gate, f), (W.up, f), (f, 0, 0), (f, 1, 0))
        if f + 1 < self.tiles:
            self.tile_loads(f + 1)
        if f == 0:
            self.arrived(S.two_t)
        grad = dot(h.branch[...], h.down[f * WIDE : (f + 1) * WIDE, :], ((1,), (1,)))
        h.both[:, :WIDE] = (grad * h.t[slot, 0].astype(FULL)).astype(LOW)
        h.both[:, WIDE:] = (grad * h.t[slot, 1].astype(FULL)).astype(LOW)
        self.side_by_side(self.job[W.gate, f], h.two_t, h.both)
        count = self.width // 4
        for xc in range(4):
            cols = slice(xc * count, (xc + 1) * count)
            weight = h.tile[slot, xc // 2, xc % 2].reshape(count, 2 * WIDE)
            got = dot(h.both[...], weight, ((1,), (1,)))
            if f == 0:
                self.grad[:, cols] = got
            else:
                self.grad[:, cols] += got

    def norm_back(self, grads, inputs, gain):
        scale = lax.rsqrt(jnp.mean(inputs * inputs, axis=-1, keepdims=True) + eps)
        total = jnp.sum(grads * inputs * scale, axis=0, keepdims=True)
        scaled = grads * gain
        mean = jnp.mean(scaled * inputs, axis=-1, keepdims=True)
        return scale * (scaled - inputs * (scale * scale * mean)), total

    def norm_two(self):
        h = self.h
        self.arrived((W.gains,), S.middle)
        count = math.prod(self.gains_near.shape[:4])
        gains = self.gains_near[...].reshape(count, 8, 128)
        self.gain[0:1, :] = gain_row(gains, 0, self.width // count)
        self.gain[1:2, :] = gain_row(gains, 1, self.width // count)
        total = jnp.zeros((1, self.width), FULL)
        for b in range(self.slots):
            rows = self.block_rows(b)
            got, part = self.norm_back(self.grad[rows, :], h.middle[rows, :], self.gain[1:2, :])
            grad = h.branch[rows, :].astype(FULL) + got
            self.grad[rows, :] = grad
            self.attended[rows, :] = grad.astype(LOW)
            total = total + part
        self.gain_sum[1:2, :] = total
        self.arrived((W.down,))

    def second(self):
        h, s = self.h, self.s
        self.fetch((W.output,), self.full.output, h.w.at[0])
        self.fetch(S.mixed_t, s.mixed_t, h.mixed_t)
        self.fetch(S.v_low, s.v_low, h.v_low)
        self.fetch(S.probs, s.probs, h.probs)
        self.fetch(S.q_rot, s.q_rot, h.gq)
        self.fetch(S.k_rot, s.k_rot, h.gk)
        self.fetch(-2, self.value_cotangent, h.gv)
        self.fetch(S.cos, s.cos, h.cos)
        self.fetch(S.sin, s.sin, h.sin)
        self.fetch(S.normed_t, s.normed_t, h.normed_t)
        self.fetch(-3, self.tokens, h.tokens)
        self.fetch((W.query,), self.full.query, h.w.at[1])

    def weight_rows(self, slot, xc):
        return self.h.w[slot, xc // 2, xc % 2].reshape(self.width // 4, self.width)

    def mixed_back(self):
        self.arrived((W.output,))
        for xc in range(4):
            got = dot(self.attended[...], self.weight_rows(0, xc), ((1,), (1,)))
            count = self.width // 4
            self.h.gmixed[:, xc * count : (xc + 1) * count] = got.astype(LOW)
        self.fetch((W.key,), self.full.key, self.h.w.at[0])

    def weight_chunk(self, which, half):
        h = self.h
        if half == 0 and which in (W.output, W.query):
            self.arrived(S.mixed_t if which == W.output else S.normed_t)
        left = h.mixed_t if which == W.output else h.normed_t
        right = {W.output: self.attended, W.query: h.gq, W.key: h.gk, W.value: h.gv}[which]
        cols = slice(half * 2 * WIDE, (half + 1) * 2 * WIDE)
        self.side_by_side(self.job[which, half], left, right.at[:, cols])

    def attend_back(self, b):
        h = self.h
        if b == 0:
            self.arrived(S.v_low, S.probs, S.q_rot, S.k_rot, -2, S.cos, S.sin)
        rows, length = self.block_rows(b), self.length
        first = iota((length, 128), 1) < HD
        live = self.live(b)
        cosine, sines = h.cos[rows, :], h.sin[rows, :]

        def fold(values):
            return jnp.where(first, values[:length], values[length:])

        def pair(n, carry):
            cols = pl.ds(pl.multiple_of(n * 128, 128), 128)
            q, k, v = h.gq[rows, cols], h.gk[rows, cols], h.v_low[rows, cols]
            grad = h.gmixed[rows, cols]
            probs = h.probs[b, n]
            k2, v2 = split_pair(k), split_pair(v)
            grad_probs = dot(grad, v2, ((1,), (1,)))
            parts = []
            for half in range(2):
                at = slice(half * length, (half + 1) * length)
                full, gp = probs[:, at].astype(FULL), grad_probs[:, at]
                parts.append(full * (gp - jnp.sum(full * gp, axis=-1, keepdims=True)))
            scores = jnp.concatenate(parts, axis=1).astype(LOW)
            grad_q = dot(scores, k2) * HD ** (-0.5)
            grad_k = fold(dot(scores, q, ((0,), (0,)))) * HD ** (-0.5)
            grad_v = fold(dot(probs, grad, ((0,), (0,))))
            grad_v = grad_v + live * h.gv[rows, cols].astype(FULL)
            h.gq[rows, cols] = turn(grad_q, cosine, -sines).astype(LOW)
            h.gk[rows, cols] = turn(grad_k, cosine, -sines).astype(LOW)
            h.gv[rows, cols] = grad_v.astype(LOW)
            return carry

        lax.fori_loop(0, self.width // 128, pair, 0, unroll=True)

    def normed_back(self, which):
        h = self.h
        self.arrived((which,))
        slot, grad = {W.query: (1, h.gq), W.key: (0, h.gk), W.value: (1, h.gv)}[which]
        for xc in range(4):
            got = dot(grad[...], self.weight_rows(slot, xc), ((1,), (1,)))
            count = self.width // 4
            cols = slice(xc * count, (xc + 1) * count)
            if which == W.query:
                h.gnormed[:, cols] = got
            else:
                h.gnormed[:, cols] += got
        if which == W.query:
            self.fetch((W.value,), self.full.value, h.w.at[1])

    def norm_one(self):
        h = self.h
        self.arrived(-3)
        total = jnp.zeros((1, self.width), FULL)
        for b in range(self.slots):
            rows = self.block_rows(b)
            inputs = h.tokens[rows, :].astype(FULL)
            got, part = self.norm_back(h.gnormed[rows, :], inputs, self.gain[0:1, :])
            h.tokens[rows, :] = (self.grad[rows, :] + got).astype(LOW)
            total = total + part
        self.gain_sum[0:1, :] = total
        self.fetch(-4, h.tokens, self.token_grad)

    def gain_chunk(self):
        depth = self.p.depth
        count = 4 * 2 * depth
        each = self.width // count
        shape = (count, self.width)
        keep = iota(shape, 1) // each == iota(shape, 0)
        folded = []
        for row in range(2):
            whole = jnp.where(keep, jnp.broadcast_to(self.gain_sum[row : row + 1, :], shape), 0.0)
            folded.append(sum(whole[:, i * 128 : (i + 1) * 128] for i in range(self.width // 128)))
        sub = iota((8, 128), 0)
        mine = []
        for i in range(count):
            one = jnp.broadcast_to(folded[0][i : i + 1, :], (8, 128))
            two = jnp.broadcast_to(folded[1][i : i + 1, :], (8, 128))
            mine.append(jnp.where(sub == 0, one, jnp.where(sub == 1, two, 0.0)))

        def part(x, c, into):
            for core in range(2):

                @pl.when(c == core)
                def _(core=core):
                    for z in range(depth):
                        for y in range(2):
                            into[x, z, y] = mine[(x * 2 + core) * 2 * depth + z * 2 + y]

        self.spread(self.job[W.gains, 0], part)
        self.arrived(-4)

    def third(self):
        h = self.h
        self.fetch(S.hid_t, self.s.hid_t, h.hid_t)
        self.fetch((W.down,), self.down_kept, h.down)
        self.fetch(S.middle, self.s.middle, h.middle)

    def block_output(self):
        h = self.h
        self.arrived(S.hid_t, (W.down,), S.middle)
        for b in range(self.slots // 2):
            rows = pl.ds(b * 2 * self.length, 2 * self.length)
            hidden = h.hid_t[:, rows].T
            live = jnp.concatenate(
                [jnp.full((self.length, 1), 1.0, FULL) * self.live(2 * b + i) for i in range(2)], axis=0
            )

            def tile(n, carry, rows=rows, hidden=hidden, live=live):
                cols = pl.ds(pl.multiple_of(n * WIDE, WIDE), WIDE)
                got = dot(hidden, h.down[:, cols])
                h.out[rows, cols] = (live * (h.middle[rows, cols] + got)).astype(LOW)
                return carry

            lax.fori_loop(0, self.width // WIDE, tile, 0)
        self.fetch(-5, h.out, self.block_out)

    def finish(self):
        self.arrived(-5)

    def steps(self):
        todo, halves = [self.begin], self.width // (2 * WIDE)
        for n in range(self.width // WIDE):
            todo += [lambda n=n: self.down_chunk(n), lambda n=n: self.down_weight(n)]
        todo += [lambda f=f: self.ff_tile(f) for f in range(self.tiles)] + [self.norm_two]
        second = len(todo)
        todo += [self.second, self.mixed_back]
        todo += [lambda h=h: self.weight_chunk(W.output, h) for h in range(halves)]
        todo += [lambda b=b: self.attend_back(b) for b in range(self.slots)]
        todo += [lambda w=w, h=h: self.weight_chunk(w, h) for w in (W.query, W.key, W.value) for h in range(halves)]
        todo += [lambda w=w: self.normed_back(w) for w in (W.query, W.key, W.value)]
        todo += [self.norm_one, self.gain_chunk]
        third = len(todo)
        todo += [self.third, self.block_output]
        return todo, second, third


def emitter(outs, kind, which, n):
    def emit(values):
        each = values.shape[0] // 2
        if kind == GAIN:
            outs.gains[...] = values
        elif kind == DOWN:
            half = WIDE // 2
            outs.down[:, n * WIDE : n * WIDE + half] = values[:each]
            outs.down[:, n * WIDE + half : (n + 1) * WIDE] = values[each:]
        elif which == W.gate:
            outs.gate[:, n * WIDE : (n + 1) * WIDE] = values[:each]
            outs.up[:, n * WIDE : (n + 1) * WIDE] = values[each:]
        else:
            outs[which][:, 2 * n * WIDE : (2 * n + 1) * WIDE] = values[:each]
            outs[which][:, (2 * n + 1) * WIDE : (2 * n + 2) * WIDE] = values[each:]

    return emit


def backward_kernel(depth, slots, length, *refs):
    refs = list(refs)

    def take(count):
        got = refs[:count]
        del refs[:count]
        return got

    counts, tokens, out_cotangent, value_cotangent = take(4)
    full = Weights._make(take(len(Weights._fields)))
    s = Saved._make(take(len(Saved._fields) - 1) + [None])
    block_out, token_grad, down_kept = take(3)
    outs = Weights._make(take(len(Weights._fields)))
    grad, attended, gain, gain_sum, gains_near = take(5)
    kinds = [Buffers._make(take(len(Buffers._fields))) for _ in SLOTS]
    (load_sems,) = refs
    place = Place(depth)
    work = Backward(
        place, counts=counts, tokens=tokens, out_cotangent=out_cotangent, value_cotangent=value_cotangent, full=full,
        s=s, block_out=block_out, token_grad=token_grad, down_kept=down_kept, grad=grad, attended=attended, gain=gain,
        gain_sum=gain_sum, gains_near=gains_near, load_sems=load_sems, slots=slots, length=length,
    )
    rows, width = work.rows, work.width
    chunks = chunk_list(work.tiles, width)
    work.job, by_kind = {}, [[] for _ in SLOTS]
    for kind, which, n in chunks:
        b, k, many = kinds[kind], len(by_kind[kind]), SLOTS[kind]
        own = Buffers._make([ref.at[k % many if i in (1, 2) else k] for i, ref in enumerate(b[:-1])] + [b.credit])
        count = sum(chunk[0] == kind for chunk in chunks)
        job = Reduce(place, k, count, many, Z_FIRST[kind], own, emitter(outs, kind, which, n))
        job.before = by_kind[kind][k - many] if k >= many else None
        by_kind[kind].append(job)
        work.job[which, n] = job
    todo, second, third = work.steps()
    actions = [step for job in work.job.values() for step in job.steps()]
    borders = [len(actions) + second, len(actions) + third]
    actions += todo
    assert sorted(BACKWARD_ORDER) == list(range(len(actions)))
    place.greet()
    flat, tall = pltpu.VMEM((rows, width), LOW), pltpu.VMEM((width, rows), LOW)
    table, wide = pltpu.VMEM((rows, 128), FULL), pltpu.VMEM((rows, width), FULL)
    down = pltpu.VMEM((work.tiles * WIDE, width), LOW)
    hid_t = pltpu.VMEM((work.tiles * WIDE, rows), LOW)
    held = (
        First(
            hid_t=hid_t, branch=flat, raw=pltpu.VMEM(full.down.shape[2:], LOW), down=down, two_t=tall, middle=wide,
            tile=pltpu.VMEM((2,) + full.gate.shape[:5] + (2 * WIDE,), LOW), t=pltpu.VMEM((2, 2, rows, WIDE), LOW),
            both=pltpu.VMEM((rows, 2 * WIDE), LOW),
        ),
        Second(
            w=pltpu.VMEM((2,) + full.query.shape, LOW), mixed_t=tall, normed_t=tall, v_low=flat,
            probs=pltpu.VMEM(s.probs.shape, LOW), cos=table, sin=table, tokens=flat, gmixed=flat, gq=flat, gk=flat,
            gv=flat, gnormed=wide,
        ),
        Third(hid_t=hid_t, down=down, middle=wide, out=flat),
    )
    cuts = [0] + [BACKWARD_ORDER.index(border) for border in borders] + [len(BACKWARD_ORDER)]
    for part, types in enumerate(held):

        def run(*buffers, part=part, types=types):
            work.h = type(types)._make(buffers)
            for i in BACKWARD_ORDER[cuts[part] : cuts[part + 1]]:
                actions[i]()
            if part == len(held) - 1:
                work.finish()

        pl.run_scoped(run, *types)
    for job in work.job.values():
        job.sent()


def backward(mesh, full, saved, tokens, counts, out_cotangent, value_cotangent, down_rows):
    depth = mesh.shape[FSDP] // 2
    slots, length, width = tokens.shape
    rows, hidden = slots * length, saved.hid_t.shape[0]
    tiles, each = hidden // WIDE, full.query.shape[4]
    chunks = chunk_list(tiles, width)
    scratch = [
        pltpu.VMEM((rows, width), FULL),
        pltpu.VMEM((rows, width), LOW),
        pltpu.VMEM((8, width), FULL),
        pltpu.VMEM((8, width), FULL),
        pltpu.VMEM(full.gains.shape, FULL),
    ]
    blocks = (((2 * down_rows, WIDE // 2), LOW), ((2 * each, WIDE), LOW), ((8, 128), FULL))
    for kind, (block, dtype) in enumerate(blocks):
        count, many = sum(chunk[0] == kind for chunk in chunks), SLOTS[kind]
        whole = (2, depth, 2) + block
        if Z_FIRST[kind]:
            ring1, ring2, zed = block, (2,) + block, (2, 2, depth - 1, 2) + block
        else:
            ring1, ring2, zed = (depth,) + block, (2, depth) + block, (2, depth - 1) + block
        scratch += [
            pltpu.VMEM((count,) + whole, dtype),
            pltpu.VMEM((many,) + whole, dtype),
            pltpu.VMEM((many,) + whole, dtype),
            pltpu.VMEM((count,) + ring1, dtype),
            pltpu.VMEM((count,) + ring2, dtype),
            pltpu.VMEM((count,) + zed, dtype),
            pltpu.SemaphoreType.DMA((count, 7)),
            pltpu.SemaphoreType.DMA((count, 7)),
            pltpu.SemaphoreType.REGULAR,
        ]
    scratch += [pltpu.SemaphoreType.DMA((32 + 4 * tiles,))]
    vmem, anywhere = pl.BlockSpec(memory_space=pltpu.VMEM), pl.BlockSpec(memory_space=pl.ANY)
    smem = pl.BlockSpec(memory_space=pltpu.SMEM)
    outs = [((rows, width), LOW), ((rows, width), LOW), ((hidden, width), LOW), ((8, 128), FULL)]
    outs += [((each, width), FULL)] * 4 + [((each, hidden), FULL)] * 2 + [((down_rows, width), FULL)]
    return pl.pallas_call(
        lambda *refs: backward_kernel(depth, slots, length, *refs),
        out_shape=tuple(jax.ShapeDtypeStruct(*a) for a in outs),
        in_specs=[smem] + [anywhere] * (3 + len(full) + len(saved) - 1),
        out_specs=tuple([anywhere] * 3 + [vmem] * len(full)),
        scratch_shapes=scratch,
        compiler_params=pltpu.CompilerParams(
            collective_id=2, has_side_effects=True, vmem_limit_bytes=63 * 2**20
        ),
        cost_estimate=pl.CostEstimate(
            flops=4 * rows * width * (4 * width + 3 * hidden), bytes_accessed=80 * 2**20, transcendentals=2**20
        ),
        name="backward_and_reduce",
    )(
        counts,
        tokens.reshape(rows, width),
        out_cotangent.reshape(rows, width),
        value_cotangent.reshape(rows, width),
        *full,
        *saved[:-1],
    )


def hand_over_kernel(count, each, *refs):
    gains, ins = refs[0], refs[1 : count + 1]
    one, two, outs = refs[count + 1], refs[count + 2], refs[count + 3 : 2 * count + 3]
    held, sems = refs[2 * count + 3 : -1], refs[-1]
    takes = [pltpu.make_async_copy(a, b, sems.at[0, i]) for i, (a, b) in enumerate(zip(ins, held))]
    gives = [pltpu.make_async_copy(a, b, sems.at[1, i]) for i, (a, b) in enumerate(zip(held, outs))]
    for take in takes:
        take.start()
    total, shift = gains[...], each
    while shift < 128:
        total = total + pltpu.roll(total, shift, 1)
        shift *= 2
    one[...] = total[0:1, :each]
    two[...] = total[1:2, :each]
    for take, give in zip(takes, gives):
        take.wait()
        give.start()
    for give in gives:
        give.wait()


def hand_over(gains, each, arrays):
    vmem, anywhere = pl.BlockSpec(memory_space=pltpu.VMEM), pl.BlockSpec(memory_space=pl.ANY)
    count = len(arrays)
    return pl.pallas_call(
        lambda *refs: hand_over_kernel(count, each, *refs),
        out_shape=tuple([jax.ShapeDtypeStruct((1, each), FULL)] * 2)
        + tuple(jax.ShapeDtypeStruct(a.shape, a.dtype) for a in arrays),
        in_specs=[vmem] + [anywhere] * count,
        out_specs=tuple([vmem] * 2 + [anywhere] * count),
        scratch_shapes=[pltpu.VMEM(a.shape, a.dtype) for a in arrays] + [pltpu.SemaphoreType.DMA((2, count))],
        compiler_params=pltpu.CompilerParams(vmem_limit_bytes=60 * 2**20),
        name="hand_over",
    )(gains, *arrays)


def rms_scale(values_in):
    return lax.rsqrt(jnp.mean(values_in * values_in, axis=-1, keepdims=True) + eps)


def rotate_table(positions):
    freq_index = jnp.arange(HD // 2, dtype=jnp.float32)
    inverse = jnp.exp(freq_index * (-2.0 * math.log(10000.0) / HD))
    angles = positions.astype(jnp.float32)[..., None] * inverse
    return (jnp.cos(angles), jnp.sin(angles))


def apply_rotary(values_in, cosine, sines):
    half_dim = values_in.shape[-1] // 2
    first_half = values_in[..., :half_dim]
    second_half = values_in[..., half_dim:]
    cosine = cosine[..., None, :]
    sines = sines[..., None, :]
    return jnp.concatenate(
        [first_half * cosine - second_half * sines, second_half * cosine + first_half * sines],
        axis=-1,
    )


def matmul(left_arg, right_arg):
    return jnp.dot(left_arg, right_arg, preferred_element_type=jnp.float32)


def stack_groups(values_in):
    row_count, model_width = values_in.shape
    return values_in.reshape(row_count, model_width // (4 * HD), 4 * HD).transpose(1, 0, 2)


def unstack_groups(values_in):
    group_count, row_count, group_width = values_in.shape
    return values_in.transpose(1, 0, 2).reshape(row_count, group_count * group_width)


def head_scores(query_grp, key_grp, allowed):
    row_count = query_grp.shape[0]
    query_heads = query_grp.reshape(row_count, 4, HD)
    key_heads = key_grp.reshape(row_count, 4, HD)
    scores = jnp.einsum(
        "qhe,khe->hqk", query_heads, key_heads, preferred_element_type=jnp.float32
    ) * HD ** (-0.5)
    return jnp.where(allowed[None], scores, -1e30)


def norm_back(grad_normed, inputs_f, scale_rows, gain_row):
    gain_term = jnp.sum(grad_normed * inputs_f * scale_rows, axis=0)
    scaled = grad_normed * gain_row
    grad_inputs = scale_rows * (
        scaled
        - inputs_f * scale_rows * scale_rows * jnp.mean(scaled * inputs_f, axis=-1, keepdims=True)
    )
    return (grad_inputs, gain_term)


def layer(
    gather_set,
    reduce_set,
    tokens,
    seq_counts,
    segments,
    positions,
    norm_first,
    query_weight,
    key_weight,
    value_weight,
    output_weight,
    norm_second,
    gate_weight,
    up_weight,
    down_weight,
    out_cotangent,
    value_cotangent,
):
    slot_count, seq_length, model_width = tokens.shape
    row_count = slot_count * seq_length
    head_count = model_width // HD
    weights = gather_set(
        norm_first,
        norm_second,
        query_weight,
        key_weight,
        value_weight,
        output_weight,
        gate_weight,
        up_weight,
        down_weight,
    )
    gain_one, gain_two, query_full, key_full, value_full, output_full = weights[:6]
    gate_full, up_full, down_full = weights[6:]
    row_index = jnp.arange(row_count, dtype=jnp.int32)
    slot_index = row_index // seq_length
    live_rows = (slot_index < seq_counts[0]).astype(jnp.float32)[:, None]
    flat_segments = segments.reshape(row_count)
    allowed = (
        (slot_index[:, None] == slot_index[None, :])
        & (flat_segments[:, None] == flat_segments[None, :])
        & (row_index[:, None] >= row_index[None, :])
    )
    inputs_f = tokens.reshape(row_count, model_width).astype(jnp.float32)
    scale_one = rms_scale(inputs_f)
    normed = (inputs_f * scale_one * gain_one.astype(jnp.float32)).astype(jnp.bfloat16)
    cosine, sines = rotate_table(positions.reshape(row_count))

    def rotated(values_in, turn_sign):
        turned = apply_rotary(
            values_in.reshape(row_count, head_count, HD), cosine, turn_sign * sines
        )
        return turned.reshape(row_count, model_width).astype(jnp.bfloat16)

    query_rot = rotated(matmul(normed, query_full), 1.0)
    key_rot = rotated(matmul(normed, key_full), 1.0)
    value_low = matmul(normed, value_full).astype(jnp.bfloat16)

    def attend_group(operands):
        query_grp, key_grp, value_grp = operands
        scores = head_scores(query_grp, key_grp, allowed)
        row_max = jnp.max(scores, axis=-1, keepdims=True)
        log_total = row_max + jnp.log(jnp.sum(jnp.exp(scores - row_max), axis=-1, keepdims=True))
        probs_low = jnp.exp(scores - log_total).astype(jnp.bfloat16)
        value_heads = value_grp.reshape(row_count, 4, HD)
        mixed_heads = jnp.einsum(
            "hqk,khe->qhe", probs_low, value_heads, preferred_element_type=jnp.float32
        )
        return (mixed_heads.reshape(row_count, 4 * HD), log_total)

    query_groups = stack_groups(query_rot)
    key_groups = stack_groups(key_rot)
    value_groups = stack_groups(value_low)
    mixed_groups, log_totals = lax.map(attend_group, (query_groups, key_groups, value_groups))
    mixed_low = unstack_groups(mixed_groups).astype(jnp.bfloat16)
    middle = inputs_f + matmul(mixed_low, output_full)
    scale_two = rms_scale(middle)
    normed_two = (middle * scale_two * gain_two.astype(jnp.float32)).astype(jnp.bfloat16)
    gate_pre = matmul(normed_two, gate_full)
    upward = matmul(normed_two, up_full)
    sigmoid_gate = jax.nn.sigmoid(gate_pre)
    silu_gate = gate_pre * sigmoid_gate
    hidden = (silu_gate * upward).astype(jnp.bfloat16)
    block_out = (live_rows * (middle + matmul(hidden, down_full))).astype(jnp.bfloat16)
    first_values = (live_rows * value_low.astype(jnp.float32)).astype(jnp.bfloat16)
    grad_y = live_rows * out_cotangent.reshape(row_count, model_width).astype(jnp.float32)
    grad_branch = grad_y.astype(jnp.bfloat16)
    down_term = jnp.einsum("rf,rd->fd", hidden, grad_branch, preferred_element_type=jnp.float32)
    grad_hidden = jnp.einsum(
        "rd,fd->rf", grad_branch, down_full, preferred_element_type=jnp.float32
    )
    grad_gate = (
        grad_hidden * upward * sigmoid_gate * (1.0 + gate_pre * (1.0 - sigmoid_gate))
    ).astype(jnp.bfloat16)
    grad_up = (grad_hidden * silu_gate).astype(jnp.bfloat16)
    gate_term = jnp.einsum("rd,rf->df", normed_two, grad_gate, preferred_element_type=jnp.float32)
    up_term = jnp.einsum("rd,rf->df", normed_two, grad_up, preferred_element_type=jnp.float32)
    grad_normed_two = jnp.einsum(
        "rf,df->rd", grad_gate, gate_full, preferred_element_type=jnp.float32
    ) + jnp.einsum("rf,df->rd", grad_up, up_full, preferred_element_type=jnp.float32)
    grad_middle_norm, gain_two_term = norm_back(
        grad_normed_two, middle, scale_two, gain_two.astype(jnp.float32)
    )
    grad_middle = grad_y + grad_middle_norm
    grad_attended = grad_middle.astype(jnp.bfloat16)
    output_term = jnp.einsum(
        "rd,re->de", mixed_low, grad_attended, preferred_element_type=jnp.float32
    )
    grad_mixed = jnp.einsum(
        "re,de->rd", grad_attended, output_full, preferred_element_type=jnp.float32
    ).astype(jnp.bfloat16)

    def attend_back(operands):
        query_grp, key_grp, value_grp, grad_grp, log_total = operands
        scores = head_scores(query_grp, key_grp, allowed)
        probs_full = jnp.exp(scores - log_total)
        probs_low = probs_full.astype(jnp.bfloat16)
        grad_heads = grad_grp.reshape(row_count, 4, HD)
        value_heads = value_grp.reshape(row_count, 4, HD)
        query_heads = query_grp.reshape(row_count, 4, HD)
        key_heads = key_grp.reshape(row_count, 4, HD)
        grad_probs = jnp.einsum(
            "qhe,khe->hqk", grad_heads, value_heads, preferred_element_type=jnp.float32
        )
        row_term = jnp.sum(probs_full * grad_probs, axis=-1, keepdims=True)
        grad_scores = (probs_full * (grad_probs - row_term)).astype(jnp.bfloat16)
        score_scale = HD ** (-0.5)
        grad_query = (
            jnp.einsum("hqk,khe->qhe", grad_scores, key_heads, preferred_element_type=jnp.float32)
            * score_scale
        )
        grad_key = (
            jnp.einsum("hqk,qhe->khe", grad_scores, query_heads, preferred_element_type=jnp.float32)
            * score_scale
        )
        grad_value = jnp.einsum(
            "hqk,qhe->khe", probs_low, grad_heads, preferred_element_type=jnp.float32
        )
        group_width = 4 * HD
        return (
            grad_query.reshape(row_count, group_width),
            grad_key.reshape(row_count, group_width),
            grad_value.reshape(row_count, group_width),
        )

    grad_q_groups, grad_k_groups, grad_v_groups = lax.map(
        attend_back, (query_groups, key_groups, value_groups, stack_groups(grad_mixed), log_totals)
    )
    grad_query = rotated(unstack_groups(grad_q_groups), -1.0)
    grad_key = rotated(unstack_groups(grad_k_groups), -1.0)
    grad_value = (
        unstack_groups(grad_v_groups)
        + live_rows * value_cotangent.reshape(row_count, model_width).astype(jnp.float32)
    ).astype(jnp.bfloat16)
    query_term = jnp.einsum("rd,re->de", normed, grad_query, preferred_element_type=jnp.float32)
    key_term = jnp.einsum("rd,re->de", normed, grad_key, preferred_element_type=jnp.float32)
    value_term = jnp.einsum("rd,re->de", normed, grad_value, preferred_element_type=jnp.float32)
    grad_normed = jnp.einsum(
        "re,de->rd", grad_query, query_full, preferred_element_type=jnp.float32
    )
    grad_normed = grad_normed + jnp.einsum(
        "re,de->rd", grad_key, key_full, preferred_element_type=jnp.float32
    )
    grad_normed = grad_normed + jnp.einsum(
        "re,de->rd", grad_value, value_full, preferred_element_type=jnp.float32
    )
    grad_inputs_norm, gain_one_term = norm_back(
        grad_normed, inputs_f, scale_one, gain_one.astype(jnp.float32)
    )
    token_grad = (grad_middle + grad_inputs_norm).astype(jnp.bfloat16).reshape(tokens.shape)
    grads = reduce_set(
        gain_one_term,
        gain_two_term,
        query_term,
        key_term,
        value_term,
        output_term,
        gate_term,
        up_term,
        down_term,
    )
    return (
        block_out.reshape(tokens.shape),
        first_values.reshape(tokens.shape),
        token_grad,
        grads[0],
        grads[2],
        grads[3],
        grads[4],
        grads[5],
        grads[1],
        grads[6],
        grads[7],
        grads[8],
    )


def plain_gather(*shards_in):
    return tuple(lax.all_gather(s, BOTH, axis=0, tiled=True) for s in shards_in)


def plain_reduce(*terms):
    return tuple(lax.psum_scatter(t, BOTH, scatter_dimension=0, tiled=True) for t in terms)


def linked_layer(mesh, *args):
    tokens, counts, segments, positions, norm_first = args[:5]
    norm_second, out_cotangent, value_cotangent = args[9], args[13], args[14]
    weights = args[5:9] + args[10:13]
    each = norm_first.shape[0]
    full, saved = forward(mesh, tokens, counts, segments, positions, norm_first, norm_second, weights)
    block, token_grad, _, gains, *grads = backward(
        mesh, full, saved, tokens, counts, out_cotangent, value_cotangent, weights[-1].shape[0]
    )
    one, two, block, first, token_grad, *grads = hand_over(gains, each, [block, saved.first, token_grad] + grads)
    streams = tuple(a.reshape(tokens.shape) for a in (block, first, token_grad))
    return streams + (one.reshape(each), *grads[:4], two.reshape(each), *grads[4:])


def fits(mesh, tokens, weights):
    return (
        dict(mesh.shape) == {DP: 4, FSDP: 8}
        and tokens == (4, 128, 1024)
        and all(w == (32, 1024) for w in weights[:4])
        and weights[4:] == ((32, 2816), (32, 2816), (88, 1024))
    )


def solution(mesh):
    one, two, three = P(BOTH), P(BOTH, None), P(BOTH, None, None)
    in_specs = (three, one, two, two, one, two, two, two, two, one, two, two, two, three, three)
    out_specs = (three, three, three, one, two, two, two, two, one, two, two, two)

    def shards(*args):
        weights = tuple(w.shape for w in args[5:9] + args[10:13])
        if fits(mesh, args[0].shape, weights):
            return linked_layer(mesh, *args)
        return layer(plain_gather, plain_reduce, *args)

    return jax.shard_map(shards, mesh=mesh, in_specs=in_specs, out_specs=out_specs, check_vma=False)
```

```python
import math
from typing import Any, NamedTuple

import jax
import jax.numpy as jnp
import numpy as np
from jax import lax
from jax.experimental import pallas as pl
from jax.experimental.pallas import tpu as pltpu
from jax.sharding import PartitionSpec as P

HD = 64
MESH = pl.DeviceIdType.MESH
DP, FSDP = "dp", "fsdp"
BOTH = (DP, FSDP)
LOW, FULL = jnp.bfloat16, jnp.float32
WIDE = 256

eps = 1e-06


class Weights(NamedTuple):
    gains: Any
    query: Any
    key: Any
    value: Any
    output: Any
    gate: Any
    up: Any
    down: Any


class Saved(NamedTuple):
    cos: Any
    sin: Any
    normed_t: Any
    q_rot: Any
    k_rot: Any
    v_low: Any
    probs: Any
    mixed_t: Any
    middle: Any
    two: Any
    two_t: Any
    first: Any
    hid_t: Any
    down: Any


W = Weights._make(range(len(Weights._fields)))
S = Saved._make(range(len(Saved._fields)))


class Place:
    def __init__(self, depth):
        dp, fsdp = lax.axis_index(DP), lax.axis_index(FSDP)
        self.x, self.c = dp // 2, dp % 2
        self.z, self.y = fsdp // 2, fsdp % 2
        self.depth = depth

    def at(self, x, c, z, y):
        return (x * 2 + c, z * 2 + y)

    def across_x(self):
        return self.at(1 - self.x, self.c, self.z, self.y)

    def across_y(self):
        return self.at(self.x, self.c, self.z, 1 - self.y)

    def sibling(self):
        return self.at(self.x, 1 - self.c, self.z, self.y)

    def above(self):
        return self.at(self.x, self.c, self.z + 1, self.y)

    def below(self):
        return self.at(self.x, self.c, self.z - 1, self.y)

    def greet(self):
        barrier = pltpu.get_barrier_semaphore()

        def call(who):
            pl.semaphore_signal(barrier, inc=1, device_id=who, device_id_type=MESH)

        call(self.across_x())
        call(self.across_y())
        call(self.sibling())
        not_top = self.z < self.depth - 1
        not_low = self.z > 0
        pl.when(not_top)(lambda: call(self.above()))
        pl.when(not_low)(lambda: call(self.below()))
        peers = 3 + not_top.astype(jnp.int32) + not_low.astype(jnp.int32)
        pl.semaphore_wait(barrier, peers)


def remote(src, dst, send_sem, recv_sem, who):
    return pltpu.make_async_remote_copy(
        src_ref=src,
        dst_ref=dst,
        send_sem=send_sem,
        recv_sem=recv_sem,
        device_id=who,
        device_id_type=MESH,
    )


def iota(shape, dim):
    return lax.broadcasted_iota(jnp.int32, shape, dim)


def dot(a, b, dims=((1,), (0,))):
    return lax.dot_general(a, b, (dims, ((), ())), preferred_element_type=FULL)


def to_column(row):
    n = row.shape[1]
    eye = iota((n, n), 0) == iota((n, n), 1)
    return jnp.sum(jnp.where(eye, jnp.broadcast_to(row, (n, n)), 0.0), axis=1, keepdims=True)


def turn(values, cosine, sines):
    outs = []
    first = iota((values.shape[0], 128), 1) % HD < HD // 2
    for g in range(values.shape[1] // 128):
        part = values[:, g * 128 : (g + 1) * 128]
        other = jnp.where(
            first, pltpu.roll(part, 128 - HD // 2, 1), pltpu.roll(part, HD // 2, 1)
        )
        outs.append(part * cosine + other * sines)
    return jnp.concatenate(outs, axis=1)


def gain_row(gains, row, each):
    count = gains.shape[0]
    rows = gains[:, row, :]
    whole = jnp.concatenate([rows] * (count * each // 128), axis=1)
    shape = whole.shape
    keep = iota(shape, 1) // each == iota(shape, 0)
    return jnp.sum(jnp.where(keep, whole, 0.0), axis=0, keepdims=True)


def split_pair(values):
    first = iota(values.shape, 1) < HD
    zero = jnp.zeros_like(values)
    return jnp.concatenate([jnp.where(first, values, zero), jnp.where(first, zero, values)], axis=0)


class Gather:
    def __init__(self, place, own, full, sends, receipts, local_sem, z_first):
        self.p, self.own, self.full, self.z_first = place, own, full, z_first
        self.sends, self.receipts, self.local_sem = sends, receipts, local_sem
        self.wide = own.shape[-1]

    def shard(self, x, y, z):
        return self.full.at[x, self.p.c, z, y]

    def zunit(self, z):
        if self.z_first:
            return self.full.at[self.p.x, self.p.c, z, self.p.y]
        return self.full.at[:, self.p.c, z]

    def runit(self, x, y, half=None):
        if self.z_first:
            if half is None:
                return self.full.at[x, self.p.c, :, y]
            count = self.p.depth // 2
            return self.full.at[x, self.p.c, half * count : (half + 1) * count, y]
        if half is None:
            return self.full.at[x, self.p.c, self.p.z, y]
        count = self.wide // 2
        return self.full.at[x, self.p.c, self.p.z, y, :, half * count : (half + 1) * count]

    def copy(self, ref, slot, who, src=None):
        return remote(ref if src is None else src, ref, self.sends.at[slot], self.receipts.at[slot], who)

    def up(self, unit, src=None):
        return self.copy(self.zunit(unit), unit, self.p.above(), src)

    def down(self, unit, src=None):
        return self.copy(self.zunit(unit), self.p.depth - 2 + unit, self.p.below(), src)

    def ring_slot(self, i):
        return 2 * (self.p.depth - 1) + i

    def keep_own(self):
        p = self.p
        return pltpu.make_async_copy(self.own, self.shard(p.x, p.y, p.z), self.local_sem)

    def z_step(self, step):
        p = self.p
        top, low = p.depth - 1, 0
        src = self.own if (step == 0 and self.z_first) else None

        def from_below():
            if step > 0:
                self.up(p.z - step).wait_recv()
            if step < top:
                pl.when(p.z < top)(lambda: self.up(p.z - step, src).start())

        def from_above():
            if step > 0:
                self.down(p.z + step).wait_recv()
            if step < top:
                pl.when(p.z > low)(lambda: self.down(p.z + step, src).start())

        pl.when(p.z - step >= low)(from_below)
        pl.when(p.z + step <= top)(from_above)

    def ring_first(self):
        p = self.p
        mine = self.runit(p.x, p.y)
        src = None if self.z_first else self.own
        self.copy(mine, self.ring_slot(0), p.across_x(), src).start()
        self.copy(mine, self.ring_slot(1), p.across_y(), src).start()

    def ring_second(self):
        p = self.p
        from_x, from_y = self.runit(1 - p.x, p.y), self.runit(p.x, 1 - p.y)
        self.copy(from_x, self.ring_slot(0), p.across_x()).wait_recv()
        self.copy(self.runit(1 - p.x, p.y, 0), self.ring_slot(2), p.across_y()).start()
        self.copy(from_y, self.ring_slot(1), p.across_y()).wait_recv()
        self.copy(self.runit(p.x, 1 - p.y, 1), self.ring_slot(3), p.across_x()).start()

    def ring_last(self):
        p = self.p
        self.copy(self.runit(1 - p.x, 1 - p.y, 0), self.ring_slot(2), p.across_y()).wait_recv()
        self.copy(self.runit(1 - p.x, 1 - p.y, 1), self.ring_slot(3), p.across_x()).wait_recv()

    def given(self, kind, core):
        p = self.p
        if self.z_first:
            x = (p.x, 1 - p.x, p.x, 1 - p.x)[kind]
            y = (p.y, p.y, 1 - p.y, 1 - p.y)[kind]
            return self.full.at[x, core, :, y]
        return self.full.at[:, core, kind]

    def give(self, ref, kind):
        self.copy(ref, self.ring_slot(4 + kind), self.p.sibling()).start()

    def pass_on(self, step):
        p = self.p

        def low():
            self.give(self.full.at[:, p.c, p.z - step], p.z - step)

        def high():
            self.give(self.full.at[:, p.c, p.z + step], p.z + step)

        pl.when(p.z - step >= 0)(low)
        if step > 0:
            pl.when(p.z + step <= p.depth - 1)(high)

    def steps(self):
        mine = lambda kind: self.give(self.given(kind, self.p.c), kind)
        if self.z_first:
            return [
                lambda: (self.keep_own().start(), self.z_step(0)),
                lambda: self.z_step(1),
                lambda: self.z_step(2),
                lambda: (self.z_step(3), self.keep_own().wait(), self.ring_first(), mine(0)),
                lambda: (self.ring_second(), mine(1), mine(2)),
                lambda: (self.ring_last(), mine(3)),
                self.finish,
            ]
        return [
            lambda: (self.keep_own().start(), self.ring_first()),
            self.ring_second,
            lambda: (self.ring_last(), self.keep_own().wait(), self.z_step(0), self.pass_on(0)),
            lambda: (self.z_step(1), self.pass_on(1)),
            lambda: (self.z_step(2), self.pass_on(2)),
            lambda: (self.z_step(3), self.pass_on(3)),
            self.finish,
        ]

    def finish(self):
        p = self.p
        for kind in range(4):
            self.copy(self.given(kind, 1 - p.c), self.ring_slot(4 + kind), p.sibling()).wait_recv()

    def sent(self):
        p = self.p
        top = p.depth - 1
        for unit in range(p.depth):
            if unit < top:
                pl.when((p.z < top) & (unit <= p.z))(lambda unit=unit: self.up(unit).wait_send())
            if unit > 0:
                pl.when((p.z > 0) & (unit >= p.z))(lambda unit=unit: self.down(unit).wait_send())
        self.copy(self.runit(p.x, p.y), self.ring_slot(0), p.across_x()).wait_send()
        self.copy(self.runit(p.x, p.y), self.ring_slot(1), p.across_y()).wait_send()
        self.copy(self.runit(1 - p.x, p.y, 0), self.ring_slot(2), p.across_y()).wait_send()
        self.copy(self.runit(p.x, 1 - p.y, 1), self.ring_slot(3), p.across_x()).wait_send()
        for kind in range(4):
            self.copy(self.given(kind, p.c), self.ring_slot(4 + kind), p.sibling()).wait_send()


def add_block(into, other):
    into[...] = into[...] + other[...]


class Buffers(NamedTuple):
    acc: Any
    stage: Any
    sib: Any
    ring1: Any
    ring2: Any
    zed: Any
    sends: Any
    receipts: Any
    credit: Any


class Reduce:
    def __init__(self, place, index, count, slots, z_first, buffers, emit):
        self.p, self.z_first, self.b, self.emit = place, z_first, buffers, emit
        self.k, self.count, self.slots = index, count, slots
        rows = buffers.acc.shape[3]
        self.cut = (rows // 2 + 15) // 16 * 16

    def copy(self, src, dst, slot, who):
        return remote(src, dst, self.b.sends.at[slot], self.b.receipts.at[slot], who)

    def sib_copy(self):
        return self.copy(self.b.stage, self.b.sib, 0, self.p.sibling())

    def free_stage(self):
        self.sib_copy().wait_send()

    def send(self):
        if self.k >= self.slots:
            pl.semaphore_wait(self.b.credit, 1)
        self.sib_copy().start()

    def merge(self):
        self.sib_copy().wait_recv()
        depth = self.p.depth

        def block(i, carry):
            at = (i // (2 * depth), i // 2 % depth, i % 2)
            self.b.acc[at] = self.b.acc[at] + self.b.sib[at]
            return carry

        lax.fori_loop(0, 4 * depth, block, 0)
        if self.k + self.slots < self.count:
            pl.semaphore_signal(
                self.b.credit, inc=1, device_id=self.p.sibling(), device_id_type=MESH
            )

    def bundle(self, x, y):
        if self.z_first:
            return self.b.acc.at[x, self.p.z, y]
        return self.b.acc.at[x, :, y]

    def halves(self, ref):
        cut = self.cut if self.z_first else self.p.depth // 2
        return ref.at[:cut], ref.at[cut:]

    def first_copies(self):
        p = self.p
        low, high = self.halves(self.bundle(1 - p.x, 1 - p.y))
        to_low, to_high = self.halves(self.b.ring1)
        return (
            self.copy(low, to_low, 1, p.across_x()),
            self.copy(high, to_high, 2, p.across_y()),
        )

    def second_copies(self):
        p = self.p
        return (
            self.copy(self.bundle(1 - p.x, p.y), self.b.ring2.at[0], 3, p.across_x()),
            self.copy(self.bundle(p.x, 1 - p.y), self.b.ring2.at[1], 4, p.across_y()),
        )

    def ring_first(self):
        for copy in self.first_copies():
            copy.start()

    def ring_second(self):
        p = self.p
        by_x, by_y = self.first_copies()
        to_x, to_y = self.second_copies()
        got_low, got_high = self.halves(self.b.ring1)
        by_x.wait_recv()
        add_block(self.halves(self.bundle(p.x, 1 - p.y))[0], got_low)
        to_y.start()
        by_y.wait_recv()
        add_block(self.halves(self.bundle(1 - p.x, p.y))[1], got_high)
        to_x.start()

    def ring_last(self):
        p = self.p
        for copy in self.second_copies():
            copy.wait_recv()
        both = self.b.ring2[0].astype(FULL) + self.b.ring2[1].astype(FULL)
        return self.bundle(p.x, p.y)[...].astype(FULL) + both

    def zunits(self, units):
        if self.z_first:
            return self.b.acc.at[:, units]
        return self.b.acc.at[self.p.x, units, self.p.y]

    def landing(self, side, units):
        if self.z_first:
            return self.b.zed.at[side, :, units]
        return self.b.zed.at[side, units]

    def up(self, step):
        top = self.p.depth - 1
        return self.copy(self.zunits(slice(step + 1, top + 1)), self.landing(0, slice(step, top)), 5, self.p.above())

    def down(self, step):
        count = self.p.depth - 1 - step
        return self.copy(self.zunits(slice(0, count)), self.landing(1, slice(0, count)), 6, self.p.below())

    def z_step(self, step):
        p, top = self.p, self.p.depth - 1

        def upward():
            if step > 0:
                self.up(step - 1).wait_recv()
            if step < top:
                if step > 0:
                    add_block(self.zunits(slice(step + 1, top + 1)), self.landing(0, slice(step, top)))
                self.up(step).start()

        def downward():
            if step > 0:
                self.down(step - 1).wait_recv()
            if step < top:
                if step > 0:
                    add_block(self.zunits(slice(0, top - step)), self.landing(1, slice(0, top - step)))
                self.down(step).start()

        pl.when(p.z == step)(upward)
        pl.when(p.z == top - step)(downward)

    def z_sum(self, put):
        p, top = self.p, self.p.depth - 1
        mine = self.zunits(p.z)[...].astype(FULL)

        @pl.when(p.z == 0)
        def _():
            put(mine + self.landing(1, 0)[...].astype(FULL))

        @pl.when(p.z == top)
        def _():
            put(mine + self.landing(0, top - 1)[...].astype(FULL))

        @pl.when((p.z > 0) & (p.z < top))
        def _():
            low, high = self.landing(0, p.z - 1)[...], self.landing(1, p.z)[...]
            put(mine + (low.astype(FULL) + high.astype(FULL)))

    def steps(self):
        kind = self.b.acc.dtype

        def keep_ring():
            self.bundle(self.p.x, self.p.y)[...] = self.ring_last().astype(kind)
            self.z_step(0)

        def keep_z(values):
            self.zunits(self.p.z)[...] = values.astype(kind)

        if self.z_first:
            return [
                self.send,
                lambda: (self.merge(), self.z_step(0)),
                lambda: self.z_step(1),
                lambda: self.z_step(2),
                lambda: (self.z_step(3), self.z_sum(keep_z), self.ring_first()),
                self.ring_second,
                lambda: self.emit(self.ring_last()),
            ]
        return [
            self.send,
            lambda: (self.merge(), self.ring_first()),
            self.ring_second,
            keep_ring,
            lambda: self.z_step(1),
            lambda: self.z_step(2),
            lambda: (self.z_step(3), self.z_sum(self.emit)),
        ]

    def sent(self):
        p, top = self.p, self.p.depth - 1
        if self.k + self.slots >= self.count:
            self.free_stage()
        for copy in self.first_copies() + self.second_copies():
            copy.wait_send()
        for step in range(top):
            pl.when(p.z == step)(lambda step=step: self.up(step).wait_send())
            pl.when(p.z == top - step)(lambda step=step: self.down(step).wait_send())


GATHER_JOBS = (
    (W.gains, True, None),
    (W.query, True, None),
    (W.key, True, None),
    (W.value, True, None),
    (W.output, True, None),
    (W.down, False, (0, 1)),
    (W.down, True, (1, 2)),
    (W.gate, True, (0, 3)),
    (W.up, True, (0, 3)),
    (W.gate, True, (3, 6)),
    (W.up, True, (3, 6)),
    (W.gate, True, (6, 9)),
    (W.up, True, (6, 9)),
    (W.gate, False, (9, 11)),
    (W.up, False, (9, 11)),
)
DOWN, SIDE, SIDE_Z, GAIN = range(4)
SLOTS = (2, 2, 2, 1)
Z_FIRST = (False, False, True, False)
Z_CHUNKS = ((W.gate, 0), (W.gate, 2), (W.gate, 4), (W.gate, 6), (W.gate, 8))
ORDER = (
    0, 14, 91, 35, 98, 28, 1, 15, 2, 3, 7, 92, 36, 99, 16, 29, 4, 21, 17, 63, 30, 56, 31, 8, 22, 18, 5, 42, 6, 9, 77,
    10, 23, 37, 273, 274, 49, 43, 275, 70, 24, 57, 11, 25, 19, 32, 44, 45, 58, 71, 50, 59, 20, 64, 38, 278, 12, 13,
    276, 26, 27, 277, 280, 33, 93, 279, 281, 282, 51, 52, 34, 286, 39, 65, 46, 78, 283, 284, 285, 287, 60, 84, 40, 53,
    100, 66, 72, 94, 288, 41, 47, 289, 85, 48, 290, 61, 62, 54, 291, 79, 73, 55, 295, 292, 293, 294, 95, 86, 297, 67,
    296, 74, 133, 101, 96, 80, 298, 68, 97, 299, 75, 87, 134, 140, 102, 69, 76, 301, 300, 303, 147, 81, 302, 305, 154,
    141, 103, 88, 304, 161, 82, 306, 89, 168, 148, 162, 83, 90, 307, 155, 104, 309, 169, 142, 308, 311, 310, 182, 313,
    156, 312, 183, 315, 170, 314, 196, 184, 316, 203, 197, 317, 105, 204, 318, 112, 106, 163, 319, 119, 198, 175, 113,
    189, 143, 205, 320, 176, 120, 107, 321, 126, 322, 190, 323, 149, 324, 114, 325, 210, 326, 327, 217, 127, 199, 177,
    211, 218, 206, 328, 121, 329, 330, 224, 331, 231, 178, 191, 185, 200, 128, 108, 207, 332, 333, 135, 164, 225, 115,
    232, 238, 219, 122, 334, 245, 335, 109, 239, 246, 252, 157, 150, 336, 337, 212, 338, 186, 144, 129, 116, 339, 253,
    130, 259, 240, 158, 220, 123, 171, 187, 340, 266, 221, 260, 226, 136, 233, 341, 213, 247, 214, 192, 254, 241, 242,
    342, 131, 188, 261, 267, 215, 227, 228, 151, 179, 159, 234, 248, 124, 201, 172, 193, 243, 110, 249, 229, 235, 255,
    165, 262, 145, 268, 256, 180, 208, 137, 160, 152, 216, 222, 250, 125, 263, 236, 194, 269, 117, 244, 202, 230, 111,
    270, 223, 138, 166, 237, 146, 153, 257, 258, 173, 251, 132, 195, 209, 264, 181, 174, 118, 271, 139, 167, 265, 272,
)


def chunk_list(tiles, width):
    halves = width // (2 * WIDE)
    sides = [(W.gate, f) for f in range(tiles)]
    sides += [(w, half) for w in (W.output, W.query, W.key, W.value) for half in range(halves)]
    chunks = [(DOWN, W.down, n) for n in range(width // WIDE)]
    chunks += [(SIDE_Z if side in Z_CHUNKS else SIDE, *side) for side in sides]
    return chunks + [(GAIN, W.gains, 0)]


class Ahead(NamedTuple):
    tokens: Any
    normed: Any
    normed_t: Any
    q_rot: Any
    k_rot: Any
    v_low: Any
    first: Any
    probs: Any
    mixed: Any
    mixed_t: Any
    w: Any
    middle: Any
    two: Any
    two_t: Any
    cos: Any
    sin: Any
    bias: Any
    live: Any


class Hidden(NamedTuple):
    hid_t: Any
    branch: Any
    raw: Any
    down: Any
    two: Any
    two_t: Any
    middle: Any
    tile: Any
    both: Any


class Attention(NamedTuple):
    w: Any
    mixed_t: Any
    normed_t: Any
    v_low: Any
    probs: Any
    cos: Any
    sin: Any
    tokens: Any
    gmixed: Any
    gq: Any
    gk: Any
    gv: Any
    gnormed: Any


class Last(NamedTuple):
    hid_t: Any
    down: Any
    middle: Any
    out: Any


class Layer:
    def __init__(self, place, **refs):
        self.p = place
        self.__dict__.update(refs)
        self.slots, self.length = self.segments.shape
        self.rows, self.width = self.tokens.shape
        self.tiles = self.full.gate.shape[-1] // WIDE
        self.loads = 0
        self.pending = {}
        self.saving = []

    def fetch(self, key, src, dst):
        copy = pltpu.make_async_copy(src, dst, self.load_sems.at[self.loads])
        self.loads += 1
        self.pending[key] = copy
        copy.start()

    def arrived(self, *keys):
        for key in keys:
            self.pending.pop(key).wait()

    def save(self, *which):
        for i in which:
            copy = pltpu.make_async_copy(getattr(self.h, Saved._fields[i]), self.s[i], self.save_sems.at[i])
            copy.start()
            self.saving.append(copy)

    def saved(self):
        for copy in self.saving:
            copy.wait()
        self.saving = []

    def block_rows(self, b):
        return pl.ds(b * self.length, self.length)

    def live(self, b):
        return (jnp.int32(b) < self.counts[0]).astype(FULL)

    def own_shards(self):
        each = self.norm_first.shape[1]
        spread = (iota((each, 128), 1) % each == iota((each, 128), 0)).astype(LOW)
        sub = iota((8, 128), 0)
        one, two = dot(self.norm_first[...], spread), dot(self.norm_second[...], spread)
        self.own_gains[...] = jnp.where(sub == 0, one, jnp.where(sub == 1, two, 0.0))
        rows, half = self.down_weight.shape[0], self.down_weight.shape[1] // 2
        down = self.down_weight[...].astype(FULL)
        self.own_down[...] = jnp.concatenate([down[:, :half], down[:, half:]], axis=0).astype(LOW)

    def tables(self):
        h = self.h
        for b in range(self.slots):
            rows = pl.ds(b * self.length, self.length)
            angles = to_column(self.positions[b : b + 1, :].astype(FULL)) * self.inverse[...]
            first = iota(angles.shape, 1) % HD < HD // 2
            sines = jnp.sin(angles)
            h.cos[rows, :] = jnp.cos(angles)
            h.sin[rows, :] = jnp.where(first, -sines, sines)
            seg = self.segments[b : b + 1, :].astype(FULL)
            shape = (self.length, self.length)
            allowed = (to_column(seg) == seg) & (iota(shape, 0) >= iota(shape, 1))
            h.bias[b] = jnp.where(allowed, 0.0, -1e30)
        h.live[...] = (iota((self.rows, 128), 0) // self.length < self.counts[0]).astype(FULL)
        self.save(S.cos, S.sin)

    def gain_rows(self):
        self.fetch((W.gains,), self.full.gains, self.gains_near)
        self.arrived((W.gains,))
        near = self.gains_near
        count = math.prod(near.shape[:4])
        gains = near[...].reshape(count, 8, 128)
        self.gain[0:1, :] = gain_row(gains, 0, self.width // count)
        self.gain[1:2, :] = gain_row(gains, 1, self.width // count)

    def norm_one(self):
        h = self.h
        self.arrived(-3)
        for b in range(self.slots):
            rows = pl.ds(b * self.length, self.length)
            inputs = h.tokens[rows, :].astype(FULL)
            scale = lax.rsqrt(jnp.mean(inputs * inputs, axis=-1, keepdims=True) + eps)
            normed = (inputs * scale * self.gain[0:1, :]).astype(LOW)
            h.normed[rows, :] = normed
            h.normed_t[:, rows] = normed.T
        self.save(S.normed_t)

    def take(self, which):
        self.fetch((which,), self.full[which], self.h.w.at[which % 2])

    def weight(self, which, cols):
        w = self.h.w[which % 2, :, :, :, :, :, cols]
        return w.reshape(math.prod(w.shape[:5]), w.shape[5])

    def project(self, which):
        h = self.h
        self.arrived((which,))
        normed = h.normed[...]

        def tile(n, carry):
            cols = pl.ds(pl.multiple_of(n * WIDE, WIDE), WIDE)
            got = dot(normed, self.weight(which, cols))
            if which == W.value:
                low = got.astype(LOW)
                h.v_low[:, cols] = low
                h.first[:, cols] = (h.live[...][:, 0:1] * low.astype(FULL)).astype(LOW)
            else:
                into = h.q_rot if which == W.query else h.k_rot
                into[:, cols] = turn(got, h.cos[...], h.sin[...]).astype(LOW)
            return carry

        lax.fori_loop(0, self.width // WIDE, tile, 0)
        if which == W.value:
            self.save(S.v_low, S.first)
        else:
            self.save(S.q_rot if which == W.query else S.k_rot)

    def attend(self, b):
        h = self.h
        length = self.length
        rows = pl.ds(b * length, length)

        def pair(n, carry):
            cols = pl.ds(pl.multiple_of(n * 128, 128), 128)
            q, k, v = h.q_rot[rows, cols], h.k_rot[rows, cols], h.v_low[rows, cols]
            k2, v2 = split_pair(k), split_pair(v)
            scores = dot(q, k2, ((1,), (1,))) * HD ** (-0.5)
            bias = h.bias[b]
            probs = []
            for half in range(2):
                s = scores[:, half * length : (half + 1) * length] + bias
                e = jnp.exp(s - jnp.max(s, axis=-1, keepdims=True))
                probs.append(e * (1.0 / jnp.sum(e, axis=-1, keepdims=True)))
            probs = jnp.concatenate(probs, axis=1).astype(LOW)
            h.probs[b, n] = probs
            h.mixed[rows, cols] = dot(probs, v2).astype(LOW)
            return carry

        lax.fori_loop(0, self.width // 128, pair, 0, unroll=True)
        h.mixed_t[:, rows] = h.mixed[rows, :].T
        if b == self.slots - 1:
            self.save(S.probs, S.mixed_t)

    def join(self):
        h = self.h
        self.arrived((W.output,))
        mixed = h.mixed[...]

        def tile(n, carry):
            cols = pl.ds(pl.multiple_of(n * WIDE, WIDE), WIDE)
            got = dot(mixed, self.weight(W.output, cols))
            h.middle[:, cols] = h.tokens[:, cols].astype(FULL) + got
            return carry

        lax.fori_loop(0, self.width // WIDE, tile, 0)
        self.save(S.middle)

    def norm_two(self):
        h = self.h
        for b in range(self.slots):
            rows = pl.ds(b * self.length, self.length)
            middle = h.middle[rows, :]
            scale = lax.rsqrt(jnp.mean(middle * middle, axis=-1, keepdims=True) + eps)
            normed = (middle * scale * self.gain[1:2, :]).astype(LOW)
            h.two[rows, :] = normed
            h.two_t[:, rows] = normed.T
        self.save(S.two, S.two_t)

    def enter(self):
        h, s = self.h, self.s
        self.fetch(S.two, s.two, h.two)
        self.fetch(-1, self.out_cotangent, h.branch)
        self.fetch(S.two_t, s.two_t, h.two_t)
        self.fetch(S.middle, s.middle, h.middle)
        self.arrived(-1)
        for b in range(self.slots):
            rows = self.block_rows(b)
            h.branch[rows, :] = (h.branch[rows, :].astype(FULL) * self.live(b)).astype(LOW)

    def raw(self):
        self.fetch((W.down, 0), self.full.down.at[0, 0], self.h.raw)

    def down_quarter(self, i):
        self.arrived((W.down, i))
        depth, raw, down = self.p.depth, self.h.raw, self.h.down
        rows, half = raw.shape[2] // 2, raw.shape[3]
        for z in range(depth):
            pair = raw[z].astype(FULL)
            for side in range(2):
                part = pair[:, side * rows : (side + 1) * rows, :].reshape(2 * rows, half)
                at = (i * depth + z) * 2 * rows
                down[at : at + 2 * rows, side * half : (side + 1) * half] = part.astype(LOW)
        j = i + 1
        if j < 4:
            self.fetch((W.down, j), self.full.down.at[j // 2, j % 2], raw)
        else:
            self.save(S.down)

    def tile_load(self, f):
        cols = pl.ds(f * WIDE, WIDE)
        for which, side in ((W.gate, 0), (W.up, 1)):
            into = self.h.tile.at[f % 2, :, :, :, :, :, side * WIDE : (side + 1) * WIDE]
            self.fetch((which, f), self.full[which].at[:, :, :, :, :, cols], into)

    def ff_tile(self, f):
        h, slot = self.h, f % 2
        self.arrived((W.gate, f), (W.up, f))
        if f == 0:
            self.arrived(S.two, S.two_t)
        count = self.width // 4
        both = dot(h.two[...], h.tile[slot].reshape(self.width, 2 * WIDE))
        gate, upward = both[:, :WIDE], both[:, WIDE:]
        sig = 1.0 / (1.0 + jnp.exp(-gate))
        silu = gate * sig
        rows = slice(f * WIDE, (f + 1) * WIDE)
        h.hid_t[rows, :] = (silu * upward).astype(LOW).T
        grad = dot(h.branch[...], h.down[rows, :], ((1,), (1,)))
        h.both[:, :WIDE] = (grad * upward * sig * (1.0 + gate * (1.0 - sig))).astype(LOW)
        h.both[:, WIDE:] = (grad * silu).astype(LOW)
        self.side_by_side(self.job[W.gate, f], h.two_t, h.both)
        for xc in range(4):
            cols = slice(xc * count, (xc + 1) * count)
            weight = h.tile[slot, xc // 2, xc % 2].reshape(count, 2 * WIDE)
            got = dot(h.both[...], weight, ((1,), (1,)))
            if f == 0:
                self.grad[:, cols] = got
            else:
                self.grad[:, cols] += got
        if f == self.tiles - 1:
            self.save(S.hid_t)

    def spread(self, job, part):
        p = self.p
        if job.before is not None:
            job.before.free_stage()
        for x in range(2):
            part(x, 1 - p.c, job.b.stage)
            part(x, p.c, job.b.acc)

    def side_by_side(self, job, left, right):
        count = self.width // 4

        def part(x, c, into):
            at = pl.multiple_of((x * 2 + c) * count, count)
            got = dot(left[pl.ds(at, count), :], right[...]).astype(LOW)
            got = got.reshape(self.p.depth, 2, -1, 2 * WIDE)
            each = got.shape[2]
            into[x, :, :, :each, :] = got[..., :WIDE]
            into[x, :, :, each:, :] = got[..., WIDE:]

        self.spread(job, part)

    def down_chunk(self, n):
        h = self.h
        right = h.branch[:, n * WIDE : (n + 1) * WIDE]
        count = h.hid_t.shape[0] // 4

        def part(x, c, into):
            at = pl.multiple_of((x * 2 + c) * count, 16)
            got = dot(h.hid_t[pl.ds(at, count), :], right)
            got = got.reshape(2 * self.p.depth, -1, WIDE)
            got = jnp.concatenate([got[:, :, : WIDE // 2], got[:, :, WIDE // 2 :]], axis=1)
            into[x] = got.astype(LOW).reshape(into.shape[1:])

        self.spread(self.job[W.down, n], part)

    def norm_back(self, grads, inputs, gain):
        scale = lax.rsqrt(jnp.mean(inputs * inputs, axis=-1, keepdims=True) + eps)
        total = jnp.sum(grads * inputs * scale, axis=0, keepdims=True)
        scaled = grads * gain
        mean = jnp.mean(scaled * inputs, axis=-1, keepdims=True)
        return scale * (scaled - inputs * (scale * scale * mean)), total

    def norm_two_back(self):
        h = self.h
        self.arrived(S.middle)
        total = jnp.zeros((1, self.width), FULL)
        for b in range(self.slots):
            rows = self.block_rows(b)
            got, part = self.norm_back(self.grad[rows, :], h.middle[rows, :], self.gain[1:2, :])
            grad = h.branch[rows, :].astype(FULL) + got
            self.grad[rows, :] = grad
            self.attended[rows, :] = grad.astype(LOW)
            total = total + part
        self.gain_sum[1:2, :] = total

    def second(self):
        h, s = self.h, self.s
        self.fetch((W.output,), self.full.output, h.w.at[0])
        self.fetch(S.mixed_t, s.mixed_t, h.mixed_t)
        self.fetch(S.v_low, s.v_low, h.v_low)
        self.fetch(S.probs, s.probs, h.probs)
        self.fetch(S.q_rot, s.q_rot, h.gq)
        self.fetch(S.k_rot, s.k_rot, h.gk)
        self.fetch(-2, self.value_cotangent, h.gv)
        self.fetch(S.cos, s.cos, h.cos)
        self.fetch(S.sin, s.sin, h.sin)
        self.fetch(S.normed_t, s.normed_t, h.normed_t)
        self.fetch(-3, self.tokens, h.tokens)
        self.fetch((W.query,), self.full.query, h.w.at[1])

    def weight_rows(self, slot, xc):
        return self.h.w[slot, xc // 2, xc % 2].reshape(self.width // 4, self.width)

    def mixed_back(self):
        self.arrived((W.output,))
        for xc in range(4):
            got = dot(self.attended[...], self.weight_rows(0, xc), ((1,), (1,)))
            count = self.width // 4
            self.h.gmixed[:, xc * count : (xc + 1) * count] = got.astype(LOW)
        self.fetch((W.key,), self.full.key, self.h.w.at[0])

    def weight_chunk(self, which, half):
        h = self.h
        if half == 0 and which in (W.output, W.query):
            self.arrived(S.mixed_t if which == W.output else S.normed_t)
        left = h.mixed_t if which == W.output else h.normed_t
        right = {W.output: self.attended, W.query: h.gq, W.key: h.gk, W.value: h.gv}[which]
        cols = slice(half * 2 * WIDE, (half + 1) * 2 * WIDE)
        self.side_by_side(self.job[which, half], left, right.at[:, cols])

    def attend_back(self, b):
        h = self.h
        if b == 0:
            self.arrived(S.v_low, S.probs, S.q_rot, S.k_rot, -2, S.cos, S.sin)
        rows, length = self.block_rows(b), self.length
        first = iota((length, 128), 1) < HD
        live = self.live(b)
        cosine, sines = h.cos[rows, :], h.sin[rows, :]

        def fold(values):
            return jnp.where(first, values[:length], values[length:])

        def pair(n, carry):
            cols = pl.ds(pl.multiple_of(n * 128, 128), 128)
            q, k, v = h.gq[rows, cols], h.gk[rows, cols], h.v_low[rows, cols]
            grad = h.gmixed[rows, cols]
            probs = h.probs[b, n]
            k2, v2 = split_pair(k), split_pair(v)
            grad_probs = dot(grad, v2, ((1,), (1,)))
            parts = []
            for half in range(2):
                at = slice(half * length, (half + 1) * length)
                full, gp = probs[:, at].astype(FULL), grad_probs[:, at]
                parts.append(full * (gp - jnp.sum(full * gp, axis=-1, keepdims=True)))
            scores = jnp.concatenate(parts, axis=1).astype(LOW)
            grad_q = dot(scores, k2) * HD ** (-0.5)
            grad_k = fold(dot(scores, q, ((0,), (0,)))) * HD ** (-0.5)
            grad_v = fold(dot(probs, grad, ((0,), (0,))))
            grad_v = grad_v + live * h.gv[rows, cols].astype(FULL)
            h.gq[rows, cols] = turn(grad_q, cosine, -sines).astype(LOW)
            h.gk[rows, cols] = turn(grad_k, cosine, -sines).astype(LOW)
            h.gv[rows, cols] = grad_v.astype(LOW)
            return carry

        lax.fori_loop(0, self.width // 128, pair, 0, unroll=True)

    def normed_back(self, which):
        h = self.h
        self.arrived((which,))
        slot, grad = {W.query: (1, h.gq), W.key: (0, h.gk), W.value: (1, h.gv)}[which]
        for xc in range(4):
            got = dot(grad[...], self.weight_rows(slot, xc), ((1,), (1,)))
            count = self.width // 4
            cols = slice(xc * count, (xc + 1) * count)
            if which == W.query:
                h.gnormed[:, cols] = got
            else:
                h.gnormed[:, cols] += got
        if which == W.query:
            self.fetch((W.value,), self.full.value, h.w.at[1])

    def norm_one_back(self):
        h = self.h
        self.arrived(-3)
        total = jnp.zeros((1, self.width), FULL)
        for b in range(self.slots):
            rows = self.block_rows(b)
            inputs = h.tokens[rows, :].astype(FULL)
            got, part = self.norm_back(h.gnormed[rows, :], inputs, self.gain[0:1, :])
            h.tokens[rows, :] = (self.grad[rows, :] + got).astype(LOW)
            total = total + part
        self.gain_sum[0:1, :] = total
        self.fetch(-4, h.tokens, self.token_grad)

    def gain_chunk(self):
        depth = self.p.depth
        count = 4 * 2 * depth
        each = self.width // count
        shape = (count, self.width)
        keep = iota(shape, 1) // each == iota(shape, 0)
        folded = []
        for row in range(2):
            whole = jnp.where(keep, jnp.broadcast_to(self.gain_sum[row : row + 1, :], shape), 0.0)
            folded.append(sum(whole[:, i * 128 : (i + 1) * 128] for i in range(self.width // 128)))
        sub = iota((8, 128), 0)
        mine = []
        for i in range(count):
            one = jnp.broadcast_to(folded[0][i : i + 1, :], (8, 128))
            two = jnp.broadcast_to(folded[1][i : i + 1, :], (8, 128))
            mine.append(jnp.where(sub == 0, one, jnp.where(sub == 1, two, 0.0)))

        def part(x, c, into):
            for core in range(2):

                @pl.when(c == core)
                def _(core=core):
                    for z in range(depth):
                        for y in range(2):
                            into[x, z, y] = mine[(x * 2 + core) * 2 * depth + z * 2 + y]

        self.spread(self.job[W.gains, 0], part)
        self.arrived(-4)

    def third(self):
        h = self.h
        self.fetch(S.hid_t, self.s.hid_t, h.hid_t)
        self.fetch((W.down,), self.s.down, h.down)
        self.fetch(S.middle, self.s.middle, h.middle)

    def block_output(self):
        h = self.h
        self.arrived(S.hid_t, (W.down,), S.middle)
        for b in range(self.slots // 2):
            rows = pl.ds(b * 2 * self.length, 2 * self.length)
            hidden = h.hid_t[:, rows].T
            live = jnp.concatenate(
                [jnp.full((self.length, 1), 1.0, FULL) * self.live(2 * b + i) for i in range(2)], axis=0
            )

            def tile(n, carry, rows=rows, hidden=hidden, live=live):
                cols = pl.ds(pl.multiple_of(n * WIDE, WIDE), WIDE)
                got = dot(hidden, h.down[:, cols])
                h.out[rows, cols] = (live * (h.middle[rows, cols] + got)).astype(LOW)
                return carry

            lax.fori_loop(0, self.width // WIDE, tile, 0)
        self.fetch(-5, h.out, self.block_out)

    def leave(self, part):
        self.saved()
        if part == 3:
            self.arrived(-5)

    def begin(self):
        self.fetch(-3, self.tokens, self.h.tokens)

    def steps(self):
        halves, slots = range(self.width // (2 * WIDE)), range(self.slots)
        qkv, quarters = (W.query, W.key, W.value), range(4)
        todo, borders = [self.tables, self.gain_rows, self.norm_one], []

        def add(action, *args):
            todo.append(lambda: action(*args))

        for w in qkv:
            add(self.take, w)
            add(self.project, w)
        for b in slots:
            add(self.attend, b)
        add(self.take, W.output)
        add(self.join)
        add(self.norm_two)
        borders.append(len(todo))
        add(self.enter)
        add(self.raw)
        for i in quarters:
            add(self.down_quarter, i)
        for f in range(self.tiles):
            add(self.tile_load, f)
            add(self.ff_tile, f)
        for n in range(self.width // WIDE):
            add(self.down_chunk, n)
        add(self.norm_two_back)
        borders.append(len(todo))
        add(self.second)
        add(self.mixed_back)
        for half in halves:
            add(self.weight_chunk, W.output, half)
        for b in slots:
            add(self.attend_back, b)
        for w in qkv:
            for half in halves:
                add(self.weight_chunk, w, half)
        for w in qkv:
            add(self.normed_back, w)
        add(self.norm_one_back)
        add(self.gain_chunk)
        borders.append(len(todo))
        add(self.third)
        add(self.block_output)
        return todo, borders


def emitter(outs, kind, which, n):
    def emit(values):
        each = values.shape[0] // 2
        if kind == GAIN:
            outs.gains[...] = values
        elif kind == DOWN:
            half = WIDE // 2
            outs.down[:, n * WIDE : n * WIDE + half] = values[:each]
            outs.down[:, n * WIDE + half : (n + 1) * WIDE] = values[each:]
        elif which == W.gate:
            outs.gate[:, n * WIDE : (n + 1) * WIDE] = values[:each]
            outs.up[:, n * WIDE : (n + 1) * WIDE] = values[each:]
        else:
            outs[which][:, 2 * n * WIDE : (2 * n + 1) * WIDE] = values[:each]
            outs[which][:, (2 * n + 1) * WIDE : (2 * n + 2) * WIDE] = values[each:]

    return emit


def layer_kernel(depth, *refs):
    refs = list(refs)

    def take(count):
        got = refs[:count]
        del refs[:count]
        return got

    kinds = len(Weights._fields)
    counts, segments, positions, inverse, norm_first, norm_second = take(6)
    tokens, out_cotangent, value_cotangent = take(3)
    given = take(kinds - 1)
    full = Weights._make(take(kinds))
    s = Saved._make(take(len(Saved._fields)))
    block_out, token_grad = take(2)
    outs = Weights._make(take(kinds))
    grad, attended, gain, gain_sum, gains_near, own_gains, own_down = take(7)
    buffers = [Buffers._make(take(len(Buffers._fields))) for _ in SLOTS]
    sends, receipts, local_sems, load_sems, save_sems = refs
    place = Place(depth)
    work = Layer(
        place, counts=counts, segments=segments, positions=positions, inverse=inverse, norm_first=norm_first,
        norm_second=norm_second, tokens=tokens, out_cotangent=out_cotangent, value_cotangent=value_cotangent,
        down_weight=given[-1], full=full, s=s, block_out=block_out, token_grad=token_grad, grad=grad,
        attended=attended, gain=gain, gain_sum=gain_sum, gains_near=gains_near, own_gains=own_gains,
        own_down=own_down, load_sems=load_sems, save_sems=save_sems,
    )
    owns = Weights._make([own_gains] + given[:-1] + [own_down])
    gathers = []
    for i, (which, z_first, cols) in enumerate(GATHER_JOBS):
        own, whole = owns[which], full[which]
        if cols is not None:
            cut = slice(cols[0] * WIDE, cols[1] * WIDE)
            own, whole = own.at[:, cut], whole.at[:, :, :, :, :, cut]
        gathers.append(Gather(place, own, whole, sends.at[i], receipts.at[i], local_sems.at[i], z_first))
    rows, width = work.rows, work.width
    chunks = chunk_list(work.tiles, width)
    work.job, by_kind = {}, [[] for _ in SLOTS]
    for kind, which, n in chunks:
        b, k, many = buffers[kind], len(by_kind[kind]), SLOTS[kind]
        own = Buffers._make([ref.at[k % many if i in (1, 2) else k] for i, ref in enumerate(b[:-1])] + [b.credit])
        count = sum(chunk[0] == kind for chunk in chunks)
        job = Reduce(place, k, count, many, Z_FIRST[kind], own, emitter(outs, kind, which, n))
        job.before = by_kind[kind][k - many] if k >= many else None
        by_kind[kind].append(job)
        work.job[which, n] = job
    todo, borders = work.steps()
    actions = [step for job in gathers + list(work.job.values()) for step in job.steps()]
    borders = [len(actions) + border for border in borders]
    actions += todo
    assert sorted(ORDER) == list(range(len(actions)))
    work.own_shards()
    place.greet()
    flat, tall = pltpu.VMEM((rows, width), LOW), pltpu.VMEM((width, rows), LOW)
    table, wide = pltpu.VMEM((rows, 128), FULL), pltpu.VMEM((rows, width), FULL)
    down = pltpu.VMEM((work.tiles * WIDE, width), LOW)
    hid_t = pltpu.VMEM((work.tiles * WIDE, rows), LOW)
    pairs = pltpu.VMEM(s.probs.shape, LOW)
    two_weights = pltpu.VMEM((2,) + full.query.shape, LOW)
    held = (
        Ahead(
            tokens=flat, normed=flat, normed_t=tall, q_rot=flat, k_rot=flat, v_low=flat, first=flat, probs=pairs,
            mixed=flat, mixed_t=tall, w=two_weights, middle=wide, two=flat, two_t=tall, cos=table, sin=table,
            bias=pltpu.VMEM((work.slots, work.length, work.length), FULL), live=table,
        ),
        Hidden(
            hid_t=hid_t, branch=flat, raw=pltpu.VMEM(full.down.shape[2:], LOW), down=down, two=flat, two_t=tall,
            middle=wide, tile=pltpu.VMEM((2,) + full.gate.shape[:5] + (2 * WIDE,), LOW),
            both=pltpu.VMEM((rows, 2 * WIDE), LOW),
        ),
        Attention(
            w=two_weights, mixed_t=tall, normed_t=tall, v_low=flat, probs=pairs, cos=table, sin=table, tokens=flat,
            gmixed=flat, gq=flat, gk=flat, gv=flat, gnormed=wide,
        ),
        Last(hid_t=hid_t, down=down, middle=wide, out=flat),
    )
    cuts = [0] + [ORDER.index(border) for border in borders] + [len(ORDER)]
    for part, types in enumerate(held):

        def run(*mine, part=part, types=types):
            work.h = type(types)._make(mine)
            if part == 0:
                work.begin()
            for i in ORDER[cuts[part] : cuts[part + 1]]:
                actions[i]()
            work.leave(part)

        pl.run_scoped(run, *types)
    for job in gathers + list(work.job.values()):
        job.sent()


def whole_layer(mesh, tokens, counts, segments, positions, norm_first, norm_second, weights, cotangents):
    depth = mesh.shape[FSDP] // 2
    slots, length, width = tokens.shape
    rows, each = slots * length, norm_first.shape[0]
    down_rows, hidden = weights[-1].shape[0], weights[W.gate - 1].shape[1]
    tiles, lead = hidden // WIDE, (2, 2, depth, 2)
    flat, tall, table = ((rows, width), LOW), ((width, rows), LOW), ((rows, 128), FULL)
    saved = Saved(
        cos=table,
        sin=table,
        normed_t=tall,
        q_rot=flat,
        k_rot=flat,
        v_low=flat,
        probs=((slots, width // 128, length, 2 * length), LOW),
        mixed_t=tall,
        middle=((rows, width), FULL),
        two=flat,
        two_t=tall,
        first=flat,
        hid_t=((hidden, rows), LOW),
        down=((hidden, width), LOW),
    )
    owns = [((8, 128), FULL)] + [(w.shape, LOW) for w in weights[:-1]] + [((2 * down_rows, width // 2), LOW)]
    fulls = [(lead + shape, kind) for shape, kind in owns]
    grads = [((8, 128), FULL)] + [(w.shape, FULL) for w in weights]
    scratch = [
        pltpu.VMEM((rows, width), FULL),
        pltpu.VMEM(*flat),
        pltpu.VMEM((8, width), FULL),
        pltpu.VMEM((8, width), FULL),
        pltpu.VMEM(*fulls[0]),
        pltpu.VMEM(*owns[0]),
        pltpu.VMEM(*owns[-1]),
    ]
    chunks = chunk_list(tiles, width)
    side = ((2 * each, WIDE), LOW)
    blocks = (((2 * down_rows, WIDE // 2), LOW), side, side, ((8, 128), FULL))
    for kind, (block, dtype) in enumerate(blocks):
        count, many = sum(chunk[0] == kind for chunk in chunks), SLOTS[kind]
        whole = (2, depth, 2) + block
        if Z_FIRST[kind]:
            ring1, ring2, zed = block, (2,) + block, (2, 2, depth - 1, 2) + block
        else:
            ring1, ring2, zed = (depth,) + block, (2, depth) + block, (2, depth - 1) + block
        scratch += [
            pltpu.VMEM((count,) + whole, dtype),
            pltpu.VMEM((many,) + whole, dtype),
            pltpu.VMEM((many,) + whole, dtype),
            pltpu.VMEM((count,) + ring1, dtype),
            pltpu.VMEM((count,) + ring2, dtype),
            pltpu.VMEM((count,) + zed, dtype),
            pltpu.SemaphoreType.DMA((count, 7)),
            pltpu.SemaphoreType.DMA((count, 7)),
            pltpu.SemaphoreType.REGULAR,
        ]
    jobs = len(GATHER_JOBS)
    scratch += [
        pltpu.SemaphoreType.DMA((jobs, 2 * (depth - 1) + 8)),
        pltpu.SemaphoreType.DMA((jobs, 2 * (depth - 1) + 8)),
        pltpu.SemaphoreType.DMA((jobs,)),
        pltpu.SemaphoreType.DMA((36 + 2 * tiles,)),
        pltpu.SemaphoreType.DMA((len(saved),)),
    ]
    inverse = jnp.asarray(
        np.exp((np.arange(128) % (HD // 2)) * (-2.0 * math.log(10000.0) / HD)), FULL
    )[None, :]
    vmem, anywhere = pl.BlockSpec(memory_space=pltpu.VMEM), pl.BlockSpec(memory_space=pl.ANY)
    smem = pl.BlockSpec(memory_space=pltpu.SMEM)
    shapes = fulls + list(saved) + [flat, flat] + grads
    got = pl.pallas_call(
        lambda *refs: layer_kernel(depth, *refs),
        out_shape=tuple(jax.ShapeDtypeStruct(*a) for a in shapes),
        in_specs=[smem] + [vmem] * 5 + [anywhere] * (3 + len(weights) - 1) + [vmem],
        out_specs=tuple([anywhere] * (len(fulls) + len(saved) + 2) + [vmem] * len(grads)),
        scratch_shapes=scratch,
        compiler_params=pltpu.CompilerParams(
            collective_id=1, has_side_effects=True, vmem_limit_bytes=63 * 2**20
        ),
        cost_estimate=pl.CostEstimate(
            flops=6 * rows * width * (4 * width + 3 * hidden), bytes_accessed=160 * 2**20, transcendentals=2**22
        ),
        name="layer",
    )(
        counts, segments, positions, inverse, norm_first.reshape(1, each), norm_second.reshape(1, each),
        tokens.reshape(rows, width), *[a.reshape(rows, width) for a in cotangents], *weights,
    )
    first = got[len(fulls) + S.first]
    block, token_grad, gains, *grads = got[len(fulls) + len(saved) :]
    return first, block, token_grad, gains, grads


def hand_over_kernel(count, each, *refs):
    gains, ins = refs[0], refs[1 : count + 1]
    one, two, outs = refs[count + 1], refs[count + 2], refs[count + 3 : 2 * count + 3]
    held, sems = refs[2 * count + 3 : -1], refs[-1]
    takes = [pltpu.make_async_copy(a, b, sems.at[0, i]) for i, (a, b) in enumerate(zip(ins, held))]
    gives = [pltpu.make_async_copy(a, b, sems.at[1, i]) for i, (a, b) in enumerate(zip(held, outs))]
    for take in takes:
        take.start()
    total, shift = gains[...], each
    while shift < 128:
        total = total + pltpu.roll(total, shift, 1)
        shift *= 2
    one[...] = total[0:1, :each]
    two[...] = total[1:2, :each]
    for take, give in zip(takes, gives):
        take.wait()
        give.start()
    for give in gives:
        give.wait()


def hand_over(gains, each, arrays):
    vmem, anywhere = pl.BlockSpec(memory_space=pltpu.VMEM), pl.BlockSpec(memory_space=pl.ANY)
    count = len(arrays)
    return pl.pallas_call(
        lambda *refs: hand_over_kernel(count, each, *refs),
        out_shape=tuple([jax.ShapeDtypeStruct((1, each), FULL)] * 2)
        + tuple(jax.ShapeDtypeStruct(a.shape, a.dtype) for a in arrays),
        in_specs=[vmem] + [anywhere] * count,
        out_specs=tuple([vmem] * 2 + [anywhere] * count),
        scratch_shapes=[pltpu.VMEM(a.shape, a.dtype) for a in arrays] + [pltpu.SemaphoreType.DMA((2, count))],
        compiler_params=pltpu.CompilerParams(vmem_limit_bytes=60 * 2**20),
        name="hand_over",
    )(gains, *arrays)


def rms_scale(values_in):
    return lax.rsqrt(jnp.mean(values_in * values_in, axis=-1, keepdims=True) + eps)


def rotate_table(positions):
    freq_index = jnp.arange(HD // 2, dtype=jnp.float32)
    inverse = jnp.exp(freq_index * (-2.0 * math.log(10000.0) / HD))
    angles = positions.astype(jnp.float32)[..., None] * inverse
    return (jnp.cos(angles), jnp.sin(angles))


def apply_rotary(values_in, cosine, sines):
    half_dim = values_in.shape[-1] // 2
    first_half = values_in[..., :half_dim]
    second_half = values_in[..., half_dim:]
    cosine = cosine[..., None, :]
    sines = sines[..., None, :]
    return jnp.concatenate(
        [first_half * cosine - second_half * sines, second_half * cosine + first_half * sines],
        axis=-1,
    )


def matmul(left_arg, right_arg):
    return jnp.dot(left_arg, right_arg, preferred_element_type=jnp.float32)


def stack_groups(values_in):
    row_count, model_width = values_in.shape
    return values_in.reshape(row_count, model_width // (4 * HD), 4 * HD).transpose(1, 0, 2)


def unstack_groups(values_in):
    group_count, row_count, group_width = values_in.shape
    return values_in.transpose(1, 0, 2).reshape(row_count, group_count * group_width)


def head_scores(query_grp, key_grp, allowed):
    row_count = query_grp.shape[0]
    query_heads = query_grp.reshape(row_count, 4, HD)
    key_heads = key_grp.reshape(row_count, 4, HD)
    scores = jnp.einsum(
        "qhe,khe->hqk", query_heads, key_heads, preferred_element_type=jnp.float32
    ) * HD ** (-0.5)
    return jnp.where(allowed[None], scores, -1e30)


def norm_back(grad_normed, inputs_f, scale_rows, gain_row):
    gain_term = jnp.sum(grad_normed * inputs_f * scale_rows, axis=0)
    scaled = grad_normed * gain_row
    grad_inputs = scale_rows * (
        scaled
        - inputs_f * scale_rows * scale_rows * jnp.mean(scaled * inputs_f, axis=-1, keepdims=True)
    )
    return (grad_inputs, gain_term)


def layer(
    gather_set,
    reduce_set,
    tokens,
    seq_counts,
    segments,
    positions,
    norm_first,
    query_weight,
    key_weight,
    value_weight,
    output_weight,
    norm_second,
    gate_weight,
    up_weight,
    down_weight,
    out_cotangent,
    value_cotangent,
):
    slot_count, seq_length, model_width = tokens.shape
    row_count = slot_count * seq_length
    head_count = model_width // HD
    weights = gather_set(
        norm_first,
        norm_second,
        query_weight,
        key_weight,
        value_weight,
        output_weight,
        gate_weight,
        up_weight,
        down_weight,
    )
    gain_one, gain_two, query_full, key_full, value_full, output_full = weights[:6]
    gate_full, up_full, down_full = weights[6:]
    row_index = jnp.arange(row_count, dtype=jnp.int32)
    slot_index = row_index // seq_length
    live_rows = (slot_index < seq_counts[0]).astype(jnp.float32)[:, None]
    flat_segments = segments.reshape(row_count)
    allowed = (
        (slot_index[:, None] == slot_index[None, :])
        & (flat_segments[:, None] == flat_segments[None, :])
        & (row_index[:, None] >= row_index[None, :])
    )
    inputs_f = tokens.reshape(row_count, model_width).astype(jnp.float32)
    scale_one = rms_scale(inputs_f)
    normed = (inputs_f * scale_one * gain_one.astype(jnp.float32)).astype(jnp.bfloat16)
    cosine, sines = rotate_table(positions.reshape(row_count))

    def rotated(values_in, turn_sign):
        turned = apply_rotary(
            values_in.reshape(row_count, head_count, HD), cosine, turn_sign * sines
        )
        return turned.reshape(row_count, model_width).astype(jnp.bfloat16)

    query_rot = rotated(matmul(normed, query_full), 1.0)
    key_rot = rotated(matmul(normed, key_full), 1.0)
    value_low = matmul(normed, value_full).astype(jnp.bfloat16)

    def attend_group(operands):
        query_grp, key_grp, value_grp = operands
        scores = head_scores(query_grp, key_grp, allowed)
        row_max = jnp.max(scores, axis=-1, keepdims=True)
        log_total = row_max + jnp.log(jnp.sum(jnp.exp(scores - row_max), axis=-1, keepdims=True))
        probs_low = jnp.exp(scores - log_total).astype(jnp.bfloat16)
        value_heads = value_grp.reshape(row_count, 4, HD)
        mixed_heads = jnp.einsum(
            "hqk,khe->qhe", probs_low, value_heads, preferred_element_type=jnp.float32
        )
        return (mixed_heads.reshape(row_count, 4 * HD), log_total)

    query_groups = stack_groups(query_rot)
    key_groups = stack_groups(key_rot)
    value_groups = stack_groups(value_low)
    mixed_groups, log_totals = lax.map(attend_group, (query_groups, key_groups, value_groups))
    mixed_low = unstack_groups(mixed_groups).astype(jnp.bfloat16)
    middle = inputs_f + matmul(mixed_low, output_full)
    scale_two = rms_scale(middle)
    normed_two = (middle * scale_two * gain_two.astype(jnp.float32)).astype(jnp.bfloat16)
    gate_pre = matmul(normed_two, gate_full)
    upward = matmul(normed_two, up_full)
    sigmoid_gate = jax.nn.sigmoid(gate_pre)
    silu_gate = gate_pre * sigmoid_gate
    hidden = (silu_gate * upward).astype(jnp.bfloat16)
    block_out = (live_rows * (middle + matmul(hidden, down_full))).astype(jnp.bfloat16)
    first_values = (live_rows * value_low.astype(jnp.float32)).astype(jnp.bfloat16)
    grad_y = live_rows * out_cotangent.reshape(row_count, model_width).astype(jnp.float32)
    grad_branch = grad_y.astype(jnp.bfloat16)
    down_term = jnp.einsum("rf,rd->fd", hidden, grad_branch, preferred_element_type=jnp.float32)
    grad_hidden = jnp.einsum(
        "rd,fd->rf", grad_branch, down_full, preferred_element_type=jnp.float32
    )
    grad_gate = (
        grad_hidden * upward * sigmoid_gate * (1.0 + gate_pre * (1.0 - sigmoid_gate))
    ).astype(jnp.bfloat16)
    grad_up = (grad_hidden * silu_gate).astype(jnp.bfloat16)
    gate_term = jnp.einsum("rd,rf->df", normed_two, grad_gate, preferred_element_type=jnp.float32)
    up_term = jnp.einsum("rd,rf->df", normed_two, grad_up, preferred_element_type=jnp.float32)
    grad_normed_two = jnp.einsum(
        "rf,df->rd", grad_gate, gate_full, preferred_element_type=jnp.float32
    ) + jnp.einsum("rf,df->rd", grad_up, up_full, preferred_element_type=jnp.float32)
    grad_middle_norm, gain_two_term = norm_back(
        grad_normed_two, middle, scale_two, gain_two.astype(jnp.float32)
    )
    grad_middle = grad_y + grad_middle_norm
    grad_attended = grad_middle.astype(jnp.bfloat16)
    output_term = jnp.einsum(
        "rd,re->de", mixed_low, grad_attended, preferred_element_type=jnp.float32
    )
    grad_mixed = jnp.einsum(
        "re,de->rd", grad_attended, output_full, preferred_element_type=jnp.float32
    ).astype(jnp.bfloat16)

    def attend_back(operands):
        query_grp, key_grp, value_grp, grad_grp, log_total = operands
        scores = head_scores(query_grp, key_grp, allowed)
        probs_full = jnp.exp(scores - log_total)
        probs_low = probs_full.astype(jnp.bfloat16)
        grad_heads = grad_grp.reshape(row_count, 4, HD)
        value_heads = value_grp.reshape(row_count, 4, HD)
        query_heads = query_grp.reshape(row_count, 4, HD)
        key_heads = key_grp.reshape(row_count, 4, HD)
        grad_probs = jnp.einsum(
            "qhe,khe->hqk", grad_heads, value_heads, preferred_element_type=jnp.float32
        )
        row_term = jnp.sum(probs_full * grad_probs, axis=-1, keepdims=True)
        grad_scores = (probs_full * (grad_probs - row_term)).astype(jnp.bfloat16)
        score_scale = HD ** (-0.5)
        grad_query = (
            jnp.einsum("hqk,khe->qhe", grad_scores, key_heads, preferred_element_type=jnp.float32)
            * score_scale
        )
        grad_key = (
            jnp.einsum("hqk,qhe->khe", grad_scores, query_heads, preferred_element_type=jnp.float32)
            * score_scale
        )
        grad_value = jnp.einsum(
            "hqk,qhe->khe", probs_low, grad_heads, preferred_element_type=jnp.float32
        )
        group_width = 4 * HD
        return (
            grad_query.reshape(row_count, group_width),
            grad_key.reshape(row_count, group_width),
            grad_value.reshape(row_count, group_width),
        )

    grad_q_groups, grad_k_groups, grad_v_groups = lax.map(
        attend_back, (query_groups, key_groups, value_groups, stack_groups(grad_mixed), log_totals)
    )
    grad_query = rotated(unstack_groups(grad_q_groups), -1.0)
    grad_key = rotated(unstack_groups(grad_k_groups), -1.0)
    grad_value = (
        unstack_groups(grad_v_groups)
        + live_rows * value_cotangent.reshape(row_count, model_width).astype(jnp.float32)
    ).astype(jnp.bfloat16)
    query_term = jnp.einsum("rd,re->de", normed, grad_query, preferred_element_type=jnp.float32)
    key_term = jnp.einsum("rd,re->de", normed, grad_key, preferred_element_type=jnp.float32)
    value_term = jnp.einsum("rd,re->de", normed, grad_value, preferred_element_type=jnp.float32)
    grad_normed = jnp.einsum(
        "re,de->rd", grad_query, query_full, preferred_element_type=jnp.float32
    )
    grad_normed = grad_normed + jnp.einsum(
        "re,de->rd", grad_key, key_full, preferred_element_type=jnp.float32
    )
    grad_normed = grad_normed + jnp.einsum(
        "re,de->rd", grad_value, value_full, preferred_element_type=jnp.float32
    )
    grad_inputs_norm, gain_one_term = norm_back(
        grad_normed, inputs_f, scale_one, gain_one.astype(jnp.float32)
    )
    token_grad = (grad_middle + grad_inputs_norm).astype(jnp.bfloat16).reshape(tokens.shape)
    grads = reduce_set(
        gain_one_term,
        gain_two_term,
        query_term,
        key_term,
        value_term,
        output_term,
        gate_term,
        up_term,
        down_term,
    )
    return (
        block_out.reshape(tokens.shape),
        first_values.reshape(tokens.shape),
        token_grad,
        grads[0],
        grads[2],
        grads[3],
        grads[4],
        grads[5],
        grads[1],
        grads[6],
        grads[7],
        grads[8],
    )


def plain_gather(*shards_in):
    return tuple(lax.all_gather(s, BOTH, axis=0, tiled=True) for s in shards_in)


def plain_reduce(*terms):
    return tuple(lax.psum_scatter(t, BOTH, scatter_dimension=0, tiled=True) for t in terms)


def linked_layer(mesh, *args):
    tokens, counts, segments, positions, norm_first = args[:5]
    norm_second, out_cotangent, value_cotangent = args[9], args[13], args[14]
    weights = args[5:9] + args[10:13]
    each = norm_first.shape[0]
    first, block, token_grad, gains, grads = whole_layer(
        mesh, tokens, counts, segments, positions, norm_first, norm_second, weights, (out_cotangent, value_cotangent)
    )
    one, two, block, first, token_grad, *grads = hand_over(gains, each, [block, first, token_grad] + grads)
    streams = tuple(a.reshape(tokens.shape) for a in (block, first, token_grad))
    return streams + (one.reshape(each), *grads[:4], two.reshape(each), *grads[4:])


def fits(mesh, tokens, weights):
    return (
        dict(mesh.shape) == {DP: 4, FSDP: 8}
        and tokens == (4, 128, 1024)
        and all(w == (32, 1024) for w in weights[:4])
        and weights[4:] == ((32, 2816), (32, 2816), (88, 1024))
    )


def solution(mesh):
    one, two, three = P(BOTH), P(BOTH, None), P(BOTH, None, None)
    in_specs = (three, one, two, two, one, two, two, two, two, one, two, two, two, three, three)
    out_specs = (three, three, three, one, two, two, two, two, one, two, two, two)

    def shards(*args):
        weights = tuple(w.shape for w in args[5:9] + args[10:13])
        if fits(mesh, args[0].shape, weights):
            return linked_layer(mesh, *args)
        return layer(plain_gather, plain_reduce, *args)

    return jax.shard_map(shards, mesh=mesh, in_specs=in_specs, out_specs=out_specs, check_vma=False)
```

```python
import math
from typing import Any, NamedTuple

import jax
import jax.numpy as jnp
import numpy as np
from jax import lax
from jax.experimental import pallas as pl
from jax.experimental.pallas import tpu as pltpu
from jax.sharding import PartitionSpec as P

HD = 64
MESH = pl.DeviceIdType.MESH
DP, FSDP = "dp", "fsdp"
BOTH = (DP, FSDP)
LOW, FULL = jnp.bfloat16, jnp.float32
WIDE = 256

eps = 1e-06


class Weights(NamedTuple):
    gains: Any
    query: Any
    key: Any
    value: Any
    output: Any
    gate: Any
    up: Any
    down: Any


class Saved(NamedTuple):
    cos: Any
    sin: Any
    normed_t: Any
    q_rot: Any
    k_rot: Any
    v_low: Any
    probs: Any
    mixed_t: Any
    middle: Any
    two: Any
    two_t: Any
    first: Any
    hid_t: Any
    down: Any


W = Weights._make(range(len(Weights._fields)))
S = Saved._make(range(len(Saved._fields)))


class Place:
    def __init__(self, depth):
        dp, fsdp = lax.axis_index(DP), lax.axis_index(FSDP)
        self.x, self.c = dp // 2, dp % 2
        self.z, self.y = fsdp // 2, fsdp % 2
        self.depth = depth

    def at(self, x, c, z, y):
        return (x * 2 + c, z * 2 + y)

    def across_x(self):
        return self.at(1 - self.x, self.c, self.z, self.y)

    def across_y(self):
        return self.at(self.x, self.c, self.z, 1 - self.y)

    def sibling(self):
        return self.at(self.x, 1 - self.c, self.z, self.y)

    def above(self):
        return self.at(self.x, self.c, self.z + 1, self.y)

    def below(self):
        return self.at(self.x, self.c, self.z - 1, self.y)

    def greet(self):
        barrier = pltpu.get_barrier_semaphore()

        def call(who):
            pl.semaphore_signal(barrier, inc=1, device_id=who, device_id_type=MESH)

        call(self.across_x())
        call(self.across_y())
        call(self.sibling())
        not_top = self.z < self.depth - 1
        not_low = self.z > 0
        pl.when(not_top)(lambda: call(self.above()))
        pl.when(not_low)(lambda: call(self.below()))
        peers = 3 + not_top.astype(jnp.int32) + not_low.astype(jnp.int32)
        pl.semaphore_wait(barrier, peers)


def remote(src, dst, send_sem, recv_sem, who):
    return pltpu.make_async_remote_copy(
        src_ref=src,
        dst_ref=dst,
        send_sem=send_sem,
        recv_sem=recv_sem,
        device_id=who,
        device_id_type=MESH,
    )


def iota(shape, dim):
    return lax.broadcasted_iota(jnp.int32, shape, dim)


def dot(a, b, dims=((1,), (0,))):
    return lax.dot_general(a, b, (dims, ((), ())), preferred_element_type=FULL)


def to_column(row):
    n = row.shape[1]
    eye = iota((n, n), 0) == iota((n, n), 1)
    return jnp.sum(jnp.where(eye, jnp.broadcast_to(row, (n, n)), 0.0), axis=1, keepdims=True)


def turn(values, cosine, sines):
    outs = []
    first = iota((values.shape[0], 128), 1) % HD < HD // 2
    for g in range(values.shape[1] // 128):
        part = values[:, g * 128 : (g + 1) * 128]
        other = jnp.where(
            first, pltpu.roll(part, 128 - HD // 2, 1), pltpu.roll(part, HD // 2, 1)
        )
        outs.append(part * cosine + other * sines)
    return jnp.concatenate(outs, axis=1)


def gain_row(gains, row, each):
    count = gains.shape[0]
    rows = gains[:, row, :]
    whole = jnp.concatenate([rows] * (count * each // 128), axis=1)
    shape = whole.shape
    keep = iota(shape, 1) // each == iota(shape, 0)
    return jnp.sum(jnp.where(keep, whole, 0.0), axis=0, keepdims=True)


def split_pair(values):
    first = iota(values.shape, 1) < HD
    zero = jnp.zeros_like(values)
    return jnp.concatenate([jnp.where(first, values, zero), jnp.where(first, zero, values)], axis=0)


class Gather:
    def __init__(self, place, own, full, sends, receipts, local_sem, z_first):
        self.p, self.own, self.full, self.z_first = place, own, full, z_first
        self.sends, self.receipts, self.local_sem = sends, receipts, local_sem
        self.wide = own.shape[-1]

    def shard(self, x, y, z):
        return self.full.at[x, self.p.c, z, y]

    def zunit(self, z):
        if self.z_first:
            return self.full.at[self.p.x, self.p.c, z, self.p.y]
        return self.full.at[:, self.p.c, z]

    def runit(self, x, y, half=None):
        if self.z_first:
            if half is None:
                return self.full.at[x, self.p.c, :, y]
            count = self.p.depth // 2
            return self.full.at[x, self.p.c, half * count : (half + 1) * count, y]
        if half is None:
            return self.full.at[x, self.p.c, self.p.z, y]
        count = self.wide // 2
        return self.full.at[x, self.p.c, self.p.z, y, :, half * count : (half + 1) * count]

    def copy(self, ref, sent, slot, who, src=None):
        return remote(ref if src is None else src, ref, self.sends.at[sent], self.receipts.at[slot], who)

    def up(self, unit, src=None):
        return self.copy(self.zunit(unit), 0, unit, self.p.above(), src)

    def down(self, unit, src=None):
        return self.copy(self.zunit(unit), 1, unit - 1, self.p.below(), src)

    def ring(self, ref, i, who, src=None):
        return self.copy(ref, 2, self.p.depth - 1 + i, who, src)

    def sib(self, ref):
        return self.copy(ref, 3, self.p.depth + 3, self.p.sibling())

    def keep_own(self):
        p = self.p
        return pltpu.make_async_copy(self.own, self.shard(p.x, p.y, p.z), self.local_sem)

    def z_step(self, step):
        p = self.p
        top, low = p.depth - 1, 0
        src = self.own if (step == 0 and self.z_first) else None

        def from_below():
            if step > 0:
                self.up(p.z - step).wait_recv()
            if step < top:
                pl.when(p.z < top)(lambda: self.up(p.z - step, src).start())

        def from_above():
            if step > 0:
                self.down(p.z + step).wait_recv()
            if step < top:
                pl.when(p.z > low)(lambda: self.down(p.z + step, src).start())

        pl.when(p.z - step >= low)(from_below)
        pl.when(p.z + step <= top)(from_above)

    def ring_first(self):
        p = self.p
        mine = self.runit(p.x, p.y)
        src = None if self.z_first else self.own
        self.ring(mine, 0, p.across_x(), src).start()
        self.ring(mine, 1, p.across_y(), src).start()

    def ring_second(self):
        p = self.p
        from_x, from_y = self.runit(1 - p.x, p.y), self.runit(p.x, 1 - p.y)
        self.ring(from_x, 0, p.across_x()).wait_recv()
        self.ring(self.runit(1 - p.x, p.y, 0), 2, p.across_y()).start()
        self.ring(from_y, 1, p.across_y()).wait_recv()
        self.ring(self.runit(p.x, 1 - p.y, 1), 3, p.across_x()).start()

    def ring_last(self):
        p = self.p
        self.ring(self.runit(1 - p.x, 1 - p.y, 0), 2, p.across_y()).wait_recv()
        self.ring(self.runit(1 - p.x, 1 - p.y, 1), 3, p.across_x()).wait_recv()

    def mine(self, kind):
        p = self.p
        x, y = (1 - p.x if kind % 2 else p.x), (1 - p.y if kind // 2 else p.y)
        self.sib(self.full.at[x, p.c, :, y]).start()

    def pass_on(self, step):
        p = self.p

        def low():
            self.sib(self.full.at[:, p.c, p.z - step]).start()

        def high():
            self.sib(self.full.at[:, p.c, p.z + step]).start()

        pl.when(p.z - step >= 0)(low)
        if step > 0:
            pl.when(p.z + step <= p.depth - 1)(high)

    def steps(self):
        mine = self.mine
        if self.z_first:
            return [
                lambda: (self.keep_own().start(), self.z_step(0)),
                lambda: self.z_step(1),
                lambda: self.z_step(2),
                lambda: (self.z_step(3), self.keep_own().wait(), self.ring_first(), mine(0)),
                lambda: (self.ring_second(), mine(1), mine(2)),
                lambda: (self.ring_last(), mine(3)),
                self.finish,
            ]
        return [
            lambda: (self.keep_own().start(), self.ring_first()),
            self.ring_second,
            lambda: (self.ring_last(), self.keep_own().wait(), self.z_step(0), self.pass_on(0)),
            lambda: (self.z_step(1), self.pass_on(1)),
            lambda: (self.z_step(2), self.pass_on(2)),
            lambda: (self.z_step(3), self.pass_on(3)),
            self.finish,
        ]

    def finish(self):
        self.sib(self.full.at[:, 1 - self.p.c]).wait_recv()

    def sent(self):
        p = self.p
        top = p.depth - 1

        def units(count):
            if self.z_first:
                return self.full.at[p.x, p.c, :count, p.y]
            return self.full.at[:, p.c, :count]

        for z in range(top):
            pl.when(p.z == z)(lambda z=z: self.copy(units(z + 1), 0, 0, p.above()).wait_send())
        for z in range(1, p.depth):
            pl.when(p.z == z)(lambda z=z: self.copy(units(p.depth - z), 1, 0, p.below()).wait_send())
        three = self.full.at[:, p.c, :3] if self.z_first else self.full.at[p.x, p.c, :3, p.y]
        self.ring(three, 0, p.across_x()).wait_send()
        self.sib(self.full.at[:, p.c]).wait_send()


def add_block(into, other):
    into[...] = into[...] + other[...]


class Buffers(NamedTuple):
    acc: Any
    stage: Any
    sib: Any
    ring1: Any
    ring2: Any
    zed: Any
    sends: Any
    receipts: Any
    credit: Any


class Reduce:
    def __init__(self, place, index, count, slots, z_first, buffers, emit):
        self.p, self.z_first, self.b, self.emit = place, z_first, buffers, emit
        self.k, self.count, self.slots = index, count, slots
        rows = buffers.acc.shape[3]
        self.cut = (rows // 2 + 15) // 16 * 16

    def copy(self, src, dst, slot, who):
        sent = 0 if slot == 0 else 1 if slot < 5 else 2
        return remote(src, dst, self.b.sends.at[sent], self.b.receipts.at[slot], who)

    def sib_copy(self):
        return self.copy(self.b.stage, self.b.sib, 0, self.p.sibling())

    def free_stage(self):
        self.sib_copy().wait_send()

    def send(self):
        if self.k >= self.slots:
            pl.semaphore_wait(self.b.credit, 1)
        self.sib_copy().start()

    def merge(self):
        self.sib_copy().wait_recv()
        depth = self.p.depth

        def block(i, carry):
            at = (i // (2 * depth), i // 2 % depth, i % 2)
            self.b.acc[at] = self.b.acc[at] + self.b.sib[at]
            return carry

        lax.fori_loop(0, 4 * depth, block, 0)
        if self.k + self.slots < self.count:
            pl.semaphore_signal(
                self.b.credit, inc=1, device_id=self.p.sibling(), device_id_type=MESH
            )

    def bundle(self, x, y):
        if self.z_first:
            return self.b.acc.at[x, self.p.z, y]
        return self.b.acc.at[x, :, y]

    def halves(self, ref):
        cut = self.cut if self.z_first else self.p.depth // 2
        return ref.at[:cut], ref.at[cut:]

    def first_copies(self):
        p = self.p
        low, high = self.halves(self.bundle(1 - p.x, 1 - p.y))
        to_low, to_high = self.halves(self.b.ring1)
        return (
            self.copy(low, to_low, 1, p.across_x()),
            self.copy(high, to_high, 2, p.across_y()),
        )

    def second_copies(self):
        p = self.p
        return (
            self.copy(self.bundle(1 - p.x, p.y), self.b.ring2.at[0], 3, p.across_x()),
            self.copy(self.bundle(p.x, 1 - p.y), self.b.ring2.at[1], 4, p.across_y()),
        )

    def ring_first(self):
        for copy in self.first_copies():
            copy.start()

    def ring_second(self):
        p = self.p
        by_x, by_y = self.first_copies()
        to_x, to_y = self.second_copies()
        got_low, got_high = self.halves(self.b.ring1)
        by_x.wait_recv()
        add_block(self.halves(self.bundle(p.x, 1 - p.y))[0], got_low)
        to_y.start()
        by_y.wait_recv()
        add_block(self.halves(self.bundle(1 - p.x, p.y))[1], got_high)
        to_x.start()

    def ring_last(self):
        p = self.p
        for copy in self.second_copies():
            copy.wait_recv()
        both = self.b.ring2[0].astype(FULL) + self.b.ring2[1].astype(FULL)
        return self.bundle(p.x, p.y)[...].astype(FULL) + both

    def zunits(self, units):
        if self.z_first:
            return self.b.acc.at[:, units]
        return self.b.acc.at[self.p.x, units, self.p.y]

    def landing(self, side, units):
        if self.z_first:
            return self.b.zed.at[side, :, units]
        return self.b.zed.at[side, units]

    def up(self, step):
        top = self.p.depth - 1
        return self.copy(self.zunits(slice(step + 1, top + 1)), self.landing(0, slice(step, top)), 5, self.p.above())

    def down(self, step):
        count = self.p.depth - 1 - step
        return self.copy(self.zunits(slice(0, count)), self.landing(1, slice(0, count)), 6, self.p.below())

    def z_step(self, step):
        p, top = self.p, self.p.depth - 1

        def upward():
            if step > 0:
                self.up(step - 1).wait_recv()
            if step < top:
                if step > 0:
                    add_block(self.zunits(slice(step + 1, top + 1)), self.landing(0, slice(step, top)))
                self.up(step).start()

        def downward():
            if step > 0:
                self.down(step - 1).wait_recv()
            if step < top:
                if step > 0:
                    add_block(self.zunits(slice(0, top - step)), self.landing(1, slice(0, top - step)))
                self.down(step).start()

        pl.when(p.z == step)(upward)
        pl.when(p.z == top - step)(downward)

    def z_sum(self, put):
        p, top = self.p, self.p.depth - 1
        mine = self.zunits(p.z)[...].astype(FULL)

        @pl.when(p.z == 0)
        def _():
            put(mine + self.landing(1, 0)[...].astype(FULL))

        @pl.when(p.z == top)
        def _():
            put(mine + self.landing(0, top - 1)[...].astype(FULL))

        @pl.when((p.z > 0) & (p.z < top))
        def _():
            low, high = self.landing(0, p.z - 1)[...], self.landing(1, p.z)[...]
            put(mine + (low.astype(FULL) + high.astype(FULL)))

    def steps(self):
        kind = self.b.acc.dtype

        def keep_ring():
            self.bundle(self.p.x, self.p.y)[...] = self.ring_last().astype(kind)
            self.z_step(0)

        def keep_z(values):
            self.zunits(self.p.z)[...] = values.astype(kind)

        if self.z_first:
            return [
                self.send,
                lambda: (self.merge(), self.z_step(0)),
                lambda: self.z_step(1),
                lambda: self.z_step(2),
                lambda: (self.z_step(3), self.z_sum(keep_z), self.ring_first()),
                self.ring_second,
                lambda: self.emit(self.ring_last()),
            ]
        return [
            self.send,
            lambda: (self.merge(), self.ring_first()),
            self.ring_second,
            keep_ring,
            lambda: self.z_step(1),
            lambda: self.z_step(2),
            lambda: (self.z_step(3), self.z_sum(self.emit)),
        ]

    def sent(self):
        p = self.p
        if self.k + self.slots >= self.count:
            self.free_stage()
        three = self.b.acc.at[0, :3, 0] if self.z_first else self.b.acc.at[:, :3]
        self.copy(three, three, 1, p.across_x()).wait_send()
        units = self.zunits(slice(0, p.depth - 1))
        self.copy(units, units, 5, p.sibling()).wait_send()


GATHER_JOBS = (
    (W.gains, True, None),
    (W.query, True, None),
    (W.key, True, None),
    (W.value, True, None),
    (W.output, True, None),
    (W.down, False, (0, 1)),
    (W.down, True, (1, 2)),
    (W.gate, True, (0, 3)),
    (W.up, True, (0, 3)),
    (W.gate, True, (3, 6)),
    (W.up, True, (3, 6)),
    (W.gate, True, (6, 9)),
    (W.up, True, (6, 9)),
    (W.gate, False, (9, 11)),
    (W.up, False, (9, 11)),
)
DOWN, SIDE, SIDE_Z, GAIN = range(4)
SLOTS = (2, 2, 2, 1)
Z_FIRST = (False, False, True, False)
Z_CHUNKS = ((W.gate, 0), (W.gate, 2), (W.gate, 4), (W.gate, 6), (W.gate, 8))
ORDER = (
    0, 14, 91, 35, 98, 28, 1, 15, 2, 3, 7, 92, 36, 99, 16, 29, 4, 21, 17, 63, 30, 56, 31, 8, 22, 18, 5, 42, 6, 9, 77,
    10, 23, 37, 273, 274, 49, 43, 275, 70, 24, 57, 11, 25, 19, 32, 44, 45, 58, 71, 50, 59, 20, 64, 38, 278, 12, 13,
    276, 26, 27, 277, 280, 33, 93, 279, 281, 282, 51, 52, 34, 286, 39, 65, 46, 78, 283, 284, 285, 287, 60, 84, 40, 53,
    100, 66, 72, 94, 288, 41, 47, 289, 85, 48, 290, 61, 62, 54, 291, 79, 73, 55, 295, 292, 293, 294, 95, 86, 297, 67,
    296, 74, 133, 101, 96, 80, 298, 68, 97, 299, 75, 87, 134, 140, 102, 69, 76, 301, 300, 303, 147, 81, 302, 305, 154,
    141, 103, 88, 304, 161, 82, 306, 89, 168, 148, 162, 83, 90, 307, 155, 104, 309, 169, 142, 308, 311, 310, 182, 313,
    156, 312, 183, 315, 170, 314, 196, 184, 316, 203, 197, 317, 105, 204, 318, 112, 106, 163, 319, 119, 198, 175, 113,
    189, 143, 205, 320, 176, 120, 107, 321, 126, 322, 190, 323, 149, 324, 114, 325, 210, 326, 327, 217, 127, 199, 177,
    211, 218, 206, 328, 121, 329, 330, 224, 331, 231, 178, 191, 185, 200, 128, 108, 207, 332, 333, 135, 164, 225, 115,
    232, 238, 219, 122, 334, 245, 335, 109, 239, 246, 252, 157, 150, 336, 337, 212, 338, 186, 144, 129, 116, 339, 253,
    130, 259, 240, 158, 220, 123, 171, 187, 340, 266, 221, 260, 226, 136, 233, 341, 213, 247, 214, 192, 254, 241, 242,
    342, 131, 188, 261, 267, 215, 227, 228, 151, 179, 159, 234, 248, 124, 201, 172, 193, 243, 110, 249, 229, 235, 255,
    165, 262, 145, 268, 256, 180, 208, 137, 160, 152, 216, 222, 250, 125, 263, 236, 194, 269, 117, 244, 202, 230, 111,
    270, 223, 138, 166, 237, 146, 153, 257, 258, 173, 251, 132, 195, 209, 264, 181, 174, 118, 271, 139, 167, 265, 272,
)


def chunk_list(tiles, width):
    halves = width // (2 * WIDE)
    sides = [(W.gate, f) for f in range(tiles)]
    sides += [(w, half) for w in (W.output, W.query, W.key, W.value) for half in range(halves)]
    chunks = [(DOWN, W.down, n) for n in range(width // WIDE)]
    chunks += [(SIDE_Z if side in Z_CHUNKS else SIDE, *side) for side in sides]
    return chunks + [(GAIN, W.gains, 0)]


class Ahead(NamedTuple):
    tokens: Any
    normed: Any
    normed_t: Any
    q_rot: Any
    k_rot: Any
    v_low: Any
    first: Any
    probs: Any
    mixed: Any
    mixed_t: Any
    w: Any
    middle: Any
    two: Any
    two_t: Any
    cos: Any
    sin: Any
    bias: Any
    live: Any


class Hidden(NamedTuple):
    hid_t: Any
    branch: Any
    raw: Any
    down: Any
    two: Any
    two_t: Any
    middle: Any
    tile: Any
    both: Any


class Attention(NamedTuple):
    w: Any
    mixed_t: Any
    normed_t: Any
    v_low: Any
    probs: Any
    cos: Any
    sin: Any
    tokens: Any
    gmixed: Any
    gq: Any
    gk: Any
    gv: Any
    gnormed: Any


class Last(NamedTuple):
    hid_t: Any
    down: Any
    middle: Any
    out: Any


class Layer:
    def __init__(self, place, **refs):
        self.p = place
        self.__dict__.update(refs)
        self.slots, self.length = self.segments.shape
        self.rows, self.width = self.tokens.shape
        self.tiles = self.full.gate.shape[-1] // WIDE
        self.loads = 0
        self.pending = {}
        self.saving = []

    def fetch(self, key, src, dst):
        copy = pltpu.make_async_copy(src, dst, self.load_sems.at[self.loads])
        self.loads += 1
        self.pending[key] = copy
        copy.start()

    def arrived(self, *keys):
        for key in keys:
            self.pending.pop(key).wait()

    def save(self, *which):
        for i in which:
            copy = pltpu.make_async_copy(getattr(self.h, Saved._fields[i]), self.s[i], self.save_sems.at[i])
            copy.start()
            self.saving.append(copy)

    def saved(self):
        for copy in self.saving:
            copy.wait()
        self.saving = []

    def block_rows(self, b):
        return pl.ds(b * self.length, self.length)

    def live(self, b):
        return (jnp.int32(b) < self.counts[0]).astype(FULL)

    def own_shards(self):
        each = self.norm_first.shape[1]
        spread = (iota((each, 128), 1) % each == iota((each, 128), 0)).astype(LOW)
        sub = iota((8, 128), 0)
        one, two = dot(self.norm_first[...], spread), dot(self.norm_second[...], spread)
        self.own_gains[...] = jnp.where(sub == 0, one, jnp.where(sub == 1, two, 0.0))
        rows, half = self.down_weight.shape[0], self.down_weight.shape[1] // 2
        down = self.down_weight[...].astype(FULL)
        self.own_down[...] = jnp.concatenate([down[:, :half], down[:, half:]], axis=0).astype(LOW)

    def tables(self):
        h = self.h
        for b in range(self.slots):
            rows = pl.ds(b * self.length, self.length)
            angles = to_column(self.positions[b : b + 1, :].astype(FULL)) * self.inverse[...]
            first = iota(angles.shape, 1) % HD < HD // 2
            sines = jnp.sin(angles)
            h.cos[rows, :] = jnp.cos(angles)
            h.sin[rows, :] = jnp.where(first, -sines, sines)
            seg = self.segments[b : b + 1, :].astype(FULL)
            shape = (self.length, self.length)
            allowed = (to_column(seg) == seg) & (iota(shape, 0) >= iota(shape, 1))
            h.bias[b] = jnp.where(allowed, 0.0, -1e30)
        h.live[...] = (iota((self.rows, 128), 0) // self.length < self.counts[0]).astype(FULL)
        self.save(S.cos, S.sin)

    def gain_rows(self):
        self.fetch((W.gains,), self.full.gains, self.gains_near)
        self.arrived((W.gains,))
        near = self.gains_near
        count = math.prod(near.shape[:4])
        gains = near[...].reshape(count, 8, 128)
        self.gain[0:1, :] = gain_row(gains, 0, self.width // count)
        self.gain[1:2, :] = gain_row(gains, 1, self.width // count)

    def norm_one(self):
        h = self.h
        self.arrived(-3)
        for b in range(self.slots):
            rows = pl.ds(b * self.length, self.length)
            inputs = h.tokens[rows, :].astype(FULL)
            scale = lax.rsqrt(jnp.mean(inputs * inputs, axis=-1, keepdims=True) + eps)
            normed = (inputs * scale * self.gain[0:1, :]).astype(LOW)
            h.normed[rows, :] = normed
            h.normed_t[:, rows] = normed.T
        self.save(S.normed_t)

    def take(self, which):
        self.fetch((which,), self.full[which], self.h.w.at[which % 2])

    def weight(self, which, cols):
        w = self.h.w[which % 2, :, :, :, :, :, cols]
        return w.reshape(math.prod(w.shape[:5]), w.shape[5])

    def project(self, which):
        h = self.h
        self.arrived((which,))
        normed = h.normed[...]

        def tile(n, carry):
            cols = pl.ds(pl.multiple_of(n * WIDE, WIDE), WIDE)
            got = dot(normed, self.weight(which, cols))
            if which == W.value:
                low = got.astype(LOW)
                h.v_low[:, cols] = low
                h.first[:, cols] = (h.live[...][:, 0:1] * low.astype(FULL)).astype(LOW)
            else:
                into = h.q_rot if which == W.query else h.k_rot
                into[:, cols] = turn(got, h.cos[...], h.sin[...]).astype(LOW)
            return carry

        lax.fori_loop(0, self.width // WIDE, tile, 0)
        if which == W.value:
            self.save(S.v_low, S.first)
        else:
            self.save(S.q_rot if which == W.query else S.k_rot)

    def attend(self, b):
        h = self.h
        length = self.length
        rows = pl.ds(b * length, length)

        def pair(n, carry):
            cols = pl.ds(pl.multiple_of(n * 128, 128), 128)
            q, k, v = h.q_rot[rows, cols], h.k_rot[rows, cols], h.v_low[rows, cols]
            k2, v2 = split_pair(k), split_pair(v)
            scores = dot(q, k2, ((1,), (1,))) * HD ** (-0.5)
            bias = h.bias[b]
            probs = []
            for half in range(2):
                s = scores[:, half * length : (half + 1) * length] + bias
                e = jnp.exp(s - jnp.max(s, axis=-1, keepdims=True))
                probs.append(e * (1.0 / jnp.sum(e, axis=-1, keepdims=True)))
            probs = jnp.concatenate(probs, axis=1).astype(LOW)
            h.probs[b, n] = probs
            h.mixed[rows, cols] = dot(probs, v2).astype(LOW)
            return carry

        lax.fori_loop(0, self.width // 128, pair, 0, unroll=True)
        h.mixed_t[:, rows] = h.mixed[rows, :].T
        if b == self.slots - 1:
            self.save(S.probs, S.mixed_t)

    def join(self):
        h = self.h
        self.arrived((W.output,))
        mixed = h.mixed[...]

        def tile(n, carry):
            cols = pl.ds(pl.multiple_of(n * WIDE, WIDE), WIDE)
            got = dot(mixed, self.weight(W.output, cols))
            h.middle[:, cols] = h.tokens[:, cols].astype(FULL) + got
            return carry

        lax.fori_loop(0, self.width // WIDE, tile, 0)
        self.save(S.middle)

    def norm_two(self):
        h = self.h
        for b in range(self.slots):
            rows = pl.ds(b * self.length, self.length)
            middle = h.middle[rows, :]
            scale = lax.rsqrt(jnp.mean(middle * middle, axis=-1, keepdims=True) + eps)
            normed = (middle * scale * self.gain[1:2, :]).astype(LOW)
            h.two[rows, :] = normed
            h.two_t[:, rows] = normed.T
        self.save(S.two, S.two_t)

    def enter(self):
        h, s = self.h, self.s
        self.fetch(S.two, s.two, h.two)
        self.fetch(-1, self.out_cotangent, h.branch)
        self.fetch(S.two_t, s.two_t, h.two_t)
        self.fetch(S.middle, s.middle, h.middle)
        self.arrived(-1)
        for b in range(self.slots):
            rows = self.block_rows(b)
            h.branch[rows, :] = (h.branch[rows, :].astype(FULL) * self.live(b)).astype(LOW)

    def raw(self):
        self.fetch((W.down, 0), self.full.down.at[0, 0], self.h.raw)

    def down_quarter(self, i):
        self.arrived((W.down, i))
        depth, raw, down = self.p.depth, self.h.raw, self.h.down
        rows, half = raw.shape[2] // 2, raw.shape[3]
        for z in range(depth):
            pair = raw[z].astype(FULL)
            for side in range(2):
                part = pair[:, side * rows : (side + 1) * rows, :].reshape(2 * rows, half)
                at = (i * depth + z) * 2 * rows
                down[at : at + 2 * rows, side * half : (side + 1) * half] = part.astype(LOW)
        j = i + 1
        if j < 4:
            self.fetch((W.down, j), self.full.down.at[j // 2, j % 2], raw)
        else:
            self.save(S.down)

    def tile_load(self, f):
        cols = pl.ds(f * WIDE, WIDE)
        for which, side in ((W.gate, 0), (W.up, 1)):
            into = self.h.tile.at[f % 2, :, :, :, :, :, side * WIDE : (side + 1) * WIDE]
            self.fetch((which, f), self.full[which].at[:, :, :, :, :, cols], into)

    def ff_tile(self, f):
        h, slot = self.h, f % 2
        self.arrived((W.gate, f), (W.up, f))
        if f == 0:
            self.arrived(S.two, S.two_t)
        count = self.width // 4
        both = dot(h.two[...], h.tile[slot].reshape(self.width, 2 * WIDE))
        gate, upward = both[:, :WIDE], both[:, WIDE:]
        sig = 1.0 / (1.0 + jnp.exp(-gate))
        silu = gate * sig
        rows = slice(f * WIDE, (f + 1) * WIDE)
        h.hid_t[rows, :] = (silu * upward).astype(LOW).T
        grad = dot(h.branch[...], h.down[rows, :], ((1,), (1,)))
        h.both[:, :WIDE] = (grad * upward * sig * (1.0 + gate * (1.0 - sig))).astype(LOW)
        h.both[:, WIDE:] = (grad * silu).astype(LOW)
        self.side_by_side(self.job[W.gate, f], h.two_t, h.both)
        for xc in range(4):
            cols = slice(xc * count, (xc + 1) * count)
            weight = h.tile[slot, xc // 2, xc % 2].reshape(count, 2 * WIDE)
            got = dot(h.both[...], weight, ((1,), (1,)))
            if f == 0:
                self.grad[:, cols] = got
            else:
                self.grad[:, cols] += got
        if f == self.tiles - 1:
            self.save(S.hid_t)

    def spread(self, job, part):
        p = self.p
        if job.before is not None:
            job.before.free_stage()
        for x in range(2):
            part(x, 1 - p.c, job.b.stage)
            part(x, p.c, job.b.acc)

    def side_by_side(self, job, left, right):
        count = self.width // 4

        def part(x, c, into):
            at = pl.multiple_of((x * 2 + c) * count, count)
            got = dot(left[pl.ds(at, count), :], right[...]).astype(LOW)
            got = got.reshape(self.p.depth, 2, -1, 2 * WIDE)
            each = got.shape[2]
            into[x, :, :, :each, :] = got[..., :WIDE]
            into[x, :, :, each:, :] = got[..., WIDE:]

        self.spread(job, part)

    def down_chunk(self, n):
        h = self.h
        right = h.branch[:, n * WIDE : (n + 1) * WIDE]
        count = h.hid_t.shape[0] // 4

        def part(x, c, into):
            at = pl.multiple_of((x * 2 + c) * count, 16)
            got = dot(h.hid_t[pl.ds(at, count), :], right)
            got = got.reshape(2 * self.p.depth, -1, WIDE)
            got = jnp.concatenate([got[:, :, : WIDE // 2], got[:, :, WIDE // 2 :]], axis=1)
            into[x] = got.astype(LOW).reshape(into.shape[1:])

        self.spread(self.job[W.down, n], part)

    def norm_back(self, grads, inputs, gain):
        scale = lax.rsqrt(jnp.mean(inputs * inputs, axis=-1, keepdims=True) + eps)
        total = jnp.sum(grads * inputs * scale, axis=0, keepdims=True)
        scaled = grads * gain
        mean = jnp.mean(scaled * inputs, axis=-1, keepdims=True)
        return scale * (scaled - inputs * (scale * scale * mean)), total

    def norm_two_back(self):
        h = self.h
        self.arrived(S.middle)
        total = jnp.zeros((1, self.width), FULL)
        for b in range(self.slots):
            rows = self.block_rows(b)
            got, part = self.norm_back(self.grad[rows, :], h.middle[rows, :], self.gain[1:2, :])
            grad = h.branch[rows, :].astype(FULL) + got
            self.grad[rows, :] = grad
            self.attended[rows, :] = grad.astype(LOW)
            total = total + part
        self.gain_sum[1:2, :] = total

    def second(self):
        h, s = self.h, self.s
        self.fetch((W.output,), self.full.output, h.w.at[0])
        self.fetch(S.mixed_t, s.mixed_t, h.mixed_t)
        self.fetch(S.v_low, s.v_low, h.v_low)
        self.fetch(S.probs, s.probs, h.probs)
        self.fetch(S.q_rot, s.q_rot, h.gq)
        self.fetch(S.k_rot, s.k_rot, h.gk)
        self.fetch(-2, self.value_cotangent, h.gv)
        self.fetch(S.cos, s.cos, h.cos)
        self.fetch(S.sin, s.sin, h.sin)
        self.fetch(S.normed_t, s.normed_t, h.normed_t)
        self.fetch(-3, self.tokens, h.tokens)
        self.fetch((W.query,), self.full.query, h.w.at[1])

    def weight_rows(self, slot, xc):
        return self.h.w[slot, xc // 2, xc % 2].reshape(self.width // 4, self.width)

    def mixed_back(self):
        self.arrived((W.output,))
        for xc in range(4):
            got = dot(self.attended[...], self.weight_rows(0, xc), ((1,), (1,)))
            count = self.width // 4
            self.h.gmixed[:, xc * count : (xc + 1) * count] = got.astype(LOW)
        self.fetch((W.key,), self.full.key, self.h.w.at[0])

    def weight_chunk(self, which, half):
        h = self.h
        if half == 0 and which in (W.output, W.query):
            self.arrived(S.mixed_t if which == W.output else S.normed_t)
        left = h.mixed_t if which == W.output else h.normed_t
        right = {W.output: self.attended, W.query: h.gq, W.key: h.gk, W.value: h.gv}[which]
        cols = slice(half * 2 * WIDE, (half + 1) * 2 * WIDE)
        self.side_by_side(self.job[which, half], left, right.at[:, cols])

    def attend_back(self, b):
        h = self.h
        if b == 0:
            self.arrived(S.v_low, S.probs, S.q_rot, S.k_rot, -2, S.cos, S.sin)
        rows, length = self.block_rows(b), self.length
        first = iota((length, 128), 1) < HD
        live = self.live(b)
        cosine, sines = h.cos[rows, :], h.sin[rows, :]

        def fold(values):
            return jnp.where(first, values[:length], values[length:])

        def pair(n, carry):
            cols = pl.ds(pl.multiple_of(n * 128, 128), 128)
            q, k, v = h.gq[rows, cols], h.gk[rows, cols], h.v_low[rows, cols]
            grad = h.gmixed[rows, cols]
            probs = h.probs[b, n]
            k2, v2 = split_pair(k), split_pair(v)
            grad_probs = dot(grad, v2, ((1,), (1,)))
            parts = []
            for half in range(2):
                at = slice(half * length, (half + 1) * length)
                full, gp = probs[:, at].astype(FULL), grad_probs[:, at]
                parts.append(full * (gp - jnp.sum(full * gp, axis=-1, keepdims=True)))
            scores = jnp.concatenate(parts, axis=1).astype(LOW)
            grad_q = dot(scores, k2) * HD ** (-0.5)
            grad_k = fold(dot(scores, q, ((0,), (0,)))) * HD ** (-0.5)
            grad_v = fold(dot(probs, grad, ((0,), (0,))))
            grad_v = grad_v + live * h.gv[rows, cols].astype(FULL)
            h.gq[rows, cols] = turn(grad_q, cosine, -sines).astype(LOW)
            h.gk[rows, cols] = turn(grad_k, cosine, -sines).astype(LOW)
            h.gv[rows, cols] = grad_v.astype(LOW)
            return carry

        lax.fori_loop(0, self.width // 128, pair, 0, unroll=True)

    def normed_back(self, which):
        h = self.h
        self.arrived((which,))
        slot, grad = {W.query: (1, h.gq), W.key: (0, h.gk), W.value: (1, h.gv)}[which]
        for xc in range(4):
            got = dot(grad[...], self.weight_rows(slot, xc), ((1,), (1,)))
            count = self.width // 4
            cols = slice(xc * count, (xc + 1) * count)
            if which == W.query:
                h.gnormed[:, cols] = got
            else:
                h.gnormed[:, cols] += got
        if which == W.query:
            self.fetch((W.value,), self.full.value, h.w.at[1])

    def norm_one_back(self):
        h = self.h
        self.arrived(-3)
        total = jnp.zeros((1, self.width), FULL)
        for b in range(self.slots):
            rows = self.block_rows(b)
            inputs = h.tokens[rows, :].astype(FULL)
            got, part = self.norm_back(h.gnormed[rows, :], inputs, self.gain[0:1, :])
            h.tokens[rows, :] = (self.grad[rows, :] + got).astype(LOW)
            total = total + part
        self.gain_sum[0:1, :] = total
        self.fetch(-4, h.tokens, self.token_grad)

    def gain_chunk(self):
        depth = self.p.depth
        count = 4 * 2 * depth
        each = self.width // count
        shape = (count, self.width)
        keep = iota(shape, 1) // each == iota(shape, 0)
        folded = []
        for row in range(2):
            whole = jnp.where(keep, jnp.broadcast_to(self.gain_sum[row : row + 1, :], shape), 0.0)
            folded.append(sum(whole[:, i * 128 : (i + 1) * 128] for i in range(self.width // 128)))
        sub = iota((8, 128), 0)
        mine = []
        for i in range(count):
            one = jnp.broadcast_to(folded[0][i : i + 1, :], (8, 128))
            two = jnp.broadcast_to(folded[1][i : i + 1, :], (8, 128))
            mine.append(jnp.where(sub == 0, one, jnp.where(sub == 1, two, 0.0)))

        def part(x, c, into):
            for core in range(2):

                @pl.when(c == core)
                def _(core=core):
                    for z in range(depth):
                        for y in range(2):
                            into[x, z, y] = mine[(x * 2 + core) * 2 * depth + z * 2 + y]

        self.spread(self.job[W.gains, 0], part)
        self.arrived(-4)

    def third(self):
        h = self.h
        self.fetch(S.hid_t, self.s.hid_t, h.hid_t)
        self.fetch((W.down,), self.s.down, h.down)
        self.fetch(S.middle, self.s.middle, h.middle)

    def block_output(self):
        h = self.h
        self.arrived(S.hid_t, (W.down,), S.middle)
        for b in range(self.slots // 2):
            rows = pl.ds(b * 2 * self.length, 2 * self.length)
            hidden = h.hid_t[:, rows].T
            live = jnp.concatenate(
                [jnp.full((self.length, 1), 1.0, FULL) * self.live(2 * b + i) for i in range(2)], axis=0
            )

            def tile(n, carry, rows=rows, hidden=hidden, live=live):
                cols = pl.ds(pl.multiple_of(n * WIDE, WIDE), WIDE)
                got = dot(hidden, h.down[:, cols])
                h.out[rows, cols] = (live * (h.middle[rows, cols] + got)).astype(LOW)
                return carry

            lax.fori_loop(0, self.width // WIDE, tile, 0)
        self.fetch(-5, h.out, self.block_out)

    def leave(self, part):
        self.saved()
        if part == 3:
            self.arrived(-5)

    def begin(self):
        self.fetch(-3, self.tokens, self.h.tokens)

    def steps(self):
        halves, slots = range(self.width // (2 * WIDE)), range(self.slots)
        qkv, quarters = (W.query, W.key, W.value), range(4)
        todo, borders = [self.tables, self.gain_rows, self.norm_one], []

        def add(action, *args):
            todo.append(lambda: action(*args))

        for w in qkv:
            add(self.take, w)
            add(self.project, w)
        for b in slots:
            add(self.attend, b)
        add(self.take, W.output)
        add(self.join)
        add(self.norm_two)
        borders.append(len(todo))
        add(self.enter)
        add(self.raw)
        for i in quarters:
            add(self.down_quarter, i)
        for f in range(self.tiles):
            add(self.tile_load, f)
            add(self.ff_tile, f)
        for n in range(self.width // WIDE):
            add(self.down_chunk, n)
        add(self.norm_two_back)
        borders.append(len(todo))
        add(self.second)
        add(self.mixed_back)
        for half in halves:
            add(self.weight_chunk, W.output, half)
        for b in slots:
            add(self.attend_back, b)
        for w in qkv:
            for half in halves:
                add(self.weight_chunk, w, half)
        for w in qkv:
            add(self.normed_back, w)
        add(self.norm_one_back)
        add(self.gain_chunk)
        borders.append(len(todo))
        add(self.third)
        add(self.block_output)
        return todo, borders


def emitter(outs, kind, which, n):
    def emit(values):
        each = values.shape[0] // 2
        if kind == GAIN:
            outs.gains[...] = values
        elif kind == DOWN:
            half = WIDE // 2
            outs.down[:, n * WIDE : n * WIDE + half] = values[:each]
            outs.down[:, n * WIDE + half : (n + 1) * WIDE] = values[each:]
        elif which == W.gate:
            outs.gate[:, n * WIDE : (n + 1) * WIDE] = values[:each]
            outs.up[:, n * WIDE : (n + 1) * WIDE] = values[each:]
        else:
            outs[which][:, 2 * n * WIDE : (2 * n + 1) * WIDE] = values[:each]
            outs[which][:, (2 * n + 1) * WIDE : (2 * n + 2) * WIDE] = values[each:]

    return emit


def layer_kernel(depth, *refs):
    refs = list(refs)

    def take(count):
        got = refs[:count]
        del refs[:count]
        return got

    kinds = len(Weights._fields)
    counts, segments, positions, inverse, norm_first, norm_second = take(6)
    tokens, out_cotangent, value_cotangent = take(3)
    given = take(kinds - 1)
    full = Weights._make(take(kinds))
    s = Saved._make(take(len(Saved._fields)))
    block_out, token_grad = take(2)
    outs = Weights._make(take(kinds))
    grad, attended, gain, gain_sum, gains_near, own_gains, own_down = take(7)
    buffers = [Buffers._make(take(len(Buffers._fields))) for _ in SLOTS]
    sends, receipts, local_sems, load_sems, save_sems = refs
    place = Place(depth)
    work = Layer(
        place, counts=counts, segments=segments, positions=positions, inverse=inverse, norm_first=norm_first,
        norm_second=norm_second, tokens=tokens, out_cotangent=out_cotangent, value_cotangent=value_cotangent,
        down_weight=given[-1], full=full, s=s, block_out=block_out, token_grad=token_grad, grad=grad,
        attended=attended, gain=gain, gain_sum=gain_sum, gains_near=gains_near, own_gains=own_gains,
        own_down=own_down, load_sems=load_sems, save_sems=save_sems,
    )
    owns = Weights._make([own_gains] + given[:-1] + [own_down])
    gathers = []
    for i, (which, z_first, cols) in enumerate(GATHER_JOBS):
        own, whole = owns[which], full[which]
        if cols is not None:
            cut = slice(cols[0] * WIDE, cols[1] * WIDE)
            own, whole = own.at[:, cut], whole.at[:, :, :, :, :, cut]
        gathers.append(Gather(place, own, whole, sends.at[i], receipts.at[i], local_sems.at[i], z_first))
    rows, width = work.rows, work.width
    chunks = chunk_list(work.tiles, width)
    work.job, by_kind = {}, [[] for _ in SLOTS]
    for kind, which, n in chunks:
        b, k, many = buffers[kind], len(by_kind[kind]), SLOTS[kind]
        own = Buffers._make([ref.at[k % many if i in (1, 2) else k] for i, ref in enumerate(b[:-1])] + [b.credit])
        count = sum(chunk[0] == kind for chunk in chunks)
        job = Reduce(place, k, count, many, Z_FIRST[kind], own, emitter(outs, kind, which, n))
        job.before = by_kind[kind][k - many] if k >= many else None
        by_kind[kind].append(job)
        work.job[which, n] = job
    todo, borders = work.steps()
    actions = [step for job in gathers + list(work.job.values()) for step in job.steps()]
    borders = [len(actions) + border for border in borders]
    actions += todo
    assert sorted(ORDER) == list(range(len(actions)))
    work.own_shards()
    place.greet()
    flat, tall = pltpu.VMEM((rows, width), LOW), pltpu.VMEM((width, rows), LOW)
    table, wide = pltpu.VMEM((rows, 128), FULL), pltpu.VMEM((rows, width), FULL)
    down = pltpu.VMEM((work.tiles * WIDE, width), LOW)
    hid_t = pltpu.VMEM((work.tiles * WIDE, rows), LOW)
    pairs = pltpu.VMEM(s.probs.shape, LOW)
    two_weights = pltpu.VMEM((2,) + full.query.shape, LOW)
    held = (
        Ahead(
            tokens=flat, normed=flat, normed_t=tall, q_rot=flat, k_rot=flat, v_low=flat, first=flat, probs=pairs,
            mixed=flat, mixed_t=tall, w=two_weights, middle=wide, two=flat, two_t=tall, cos=table, sin=table,
            bias=pltpu.VMEM((work.slots, work.length, work.length), FULL), live=table,
        ),
        Hidden(
            hid_t=hid_t, branch=flat, raw=pltpu.VMEM(full.down.shape[2:], LOW), down=down, two=flat, two_t=tall,
            middle=wide, tile=pltpu.VMEM((2,) + full.gate.shape[:5] + (2 * WIDE,), LOW),
            both=pltpu.VMEM((rows, 2 * WIDE), LOW),
        ),
        Attention(
            w=two_weights, mixed_t=tall, normed_t=tall, v_low=flat, probs=pairs, cos=table, sin=table, tokens=flat,
            gmixed=flat, gq=flat, gk=flat, gv=flat, gnormed=wide,
        ),
        Last(hid_t=hid_t, down=down, middle=wide, out=flat),
    )
    cuts = [0] + [ORDER.index(border) for border in borders] + [len(ORDER)]
    for part, types in enumerate(held):

        def run(*mine, part=part, types=types):
            work.h = type(types)._make(mine)
            if part == 0:
                work.begin()
            for i in ORDER[cuts[part] : cuts[part + 1]]:
                actions[i]()
            work.leave(part)

        pl.run_scoped(run, *types)
    for job in gathers + list(work.job.values()):
        job.sent()


def whole_layer(mesh, tokens, counts, segments, positions, norm_first, norm_second, weights, cotangents):
    depth = mesh.shape[FSDP] // 2
    slots, length, width = tokens.shape
    rows, each = slots * length, norm_first.shape[0]
    down_rows, hidden = weights[-1].shape[0], weights[W.gate - 1].shape[1]
    tiles, lead = hidden // WIDE, (2, 2, depth, 2)
    flat, tall, table = ((rows, width), LOW), ((width, rows), LOW), ((rows, 128), FULL)
    saved = Saved(
        cos=table,
        sin=table,
        normed_t=tall,
        q_rot=flat,
        k_rot=flat,
        v_low=flat,
        probs=((slots, width // 128, length, 2 * length), LOW),
        mixed_t=tall,
        middle=((rows, width), FULL),
        two=flat,
        two_t=tall,
        first=flat,
        hid_t=((hidden, rows), LOW),
        down=((hidden, width), LOW),
    )
    owns = [((8, 128), FULL)] + [(w.shape, LOW) for w in weights[:-1]] + [((2 * down_rows, width // 2), LOW)]
    fulls = [(lead + shape, kind) for shape, kind in owns]
    grads = [((8, 128), FULL)] + [(w.shape, FULL) for w in weights]
    scratch = [
        pltpu.VMEM((rows, width), FULL),
        pltpu.VMEM(*flat),
        pltpu.VMEM((8, width), FULL),
        pltpu.VMEM((8, width), FULL),
        pltpu.VMEM(*fulls[0]),
        pltpu.VMEM(*owns[0]),
        pltpu.VMEM(*owns[-1]),
    ]
    chunks = chunk_list(tiles, width)
    side = ((2 * each, WIDE), LOW)
    blocks = (((2 * down_rows, WIDE // 2), LOW), side, side, ((8, 128), FULL))
    for kind, (block, dtype) in enumerate(blocks):
        count, many = sum(chunk[0] == kind for chunk in chunks), SLOTS[kind]
        whole = (2, depth, 2) + block
        if Z_FIRST[kind]:
            ring1, ring2, zed = block, (2,) + block, (2, 2, depth - 1, 2) + block
        else:
            ring1, ring2, zed = (depth,) + block, (2, depth) + block, (2, depth - 1) + block
        scratch += [
            pltpu.VMEM((count,) + whole, dtype),
            pltpu.VMEM((many,) + whole, dtype),
            pltpu.VMEM((many,) + whole, dtype),
            pltpu.VMEM((count,) + ring1, dtype),
            pltpu.VMEM((count,) + ring2, dtype),
            pltpu.VMEM((count,) + zed, dtype),
            pltpu.SemaphoreType.DMA((count, 3)),
            pltpu.SemaphoreType.DMA((count, 7)),
            pltpu.SemaphoreType.REGULAR,
        ]
    jobs = len(GATHER_JOBS)
    scratch += [
        pltpu.SemaphoreType.DMA((jobs, 4)),
        pltpu.SemaphoreType.DMA((jobs, depth + 4)),
        pltpu.SemaphoreType.DMA((jobs,)),
        pltpu.SemaphoreType.DMA((36 + 2 * tiles,)),
        pltpu.SemaphoreType.DMA((len(saved),)),
    ]
    inverse = jnp.asarray(
        np.exp((np.arange(128) % (HD // 2)) * (-2.0 * math.log(10000.0) / HD)), FULL
    )[None, :]
    vmem, anywhere = pl.BlockSpec(memory_space=pltpu.VMEM), pl.BlockSpec(memory_space=pl.ANY)
    smem = pl.BlockSpec(memory_space=pltpu.SMEM)
    shapes = fulls + list(saved) + [flat, flat] + grads
    got = pl.pallas_call(
        lambda *refs: layer_kernel(depth, *refs),
        out_shape=tuple(jax.ShapeDtypeStruct(*a) for a in shapes),
        in_specs=[smem] + [vmem] * 5 + [anywhere] * (3 + len(weights) - 1) + [vmem],
        out_specs=tuple([anywhere] * (len(fulls) + len(saved) + 2) + [vmem] * len(grads)),
        scratch_shapes=scratch,
        compiler_params=pltpu.CompilerParams(
            collective_id=1, has_side_effects=True, vmem_limit_bytes=63 * 2**20
        ),
        cost_estimate=pl.CostEstimate(
            flops=6 * rows * width * (4 * width + 3 * hidden), bytes_accessed=160 * 2**20, transcendentals=2**22
        ),
        name="layer",
    )(
        counts, segments, positions, inverse, norm_first.reshape(1, each), norm_second.reshape(1, each),
        tokens.reshape(rows, width), *[a.reshape(rows, width) for a in cotangents], *weights,
    )
    first = got[len(fulls) + S.first]
    block, token_grad, gains, *grads = got[len(fulls) + len(saved) :]
    return first, block, token_grad, gains, grads


def hand_over_kernel(count, each, *refs):
    gains, ins = refs[0], refs[1 : count + 1]
    one, two, outs = refs[count + 1], refs[count + 2], refs[count + 3 : 2 * count + 3]
    held, sems = refs[2 * count + 3 : -1], refs[-1]
    takes = [pltpu.make_async_copy(a, b, sems.at[0, i]) for i, (a, b) in enumerate(zip(ins, held))]
    gives = [pltpu.make_async_copy(a, b, sems.at[1, i]) for i, (a, b) in enumerate(zip(held, outs))]
    for take in takes:
        take.start()
    total, shift = gains[...], each
    while shift < 128:
        total = total + pltpu.roll(total, shift, 1)
        shift *= 2
    one[...] = total[0:1, :each]
    two[...] = total[1:2, :each]
    for take, give in zip(takes, gives):
        take.wait()
        give.start()
    for give in gives:
        give.wait()


def hand_over(gains, each, arrays):
    vmem, anywhere = pl.BlockSpec(memory_space=pltpu.VMEM), pl.BlockSpec(memory_space=pl.ANY)
    count = len(arrays)
    return pl.pallas_call(
        lambda *refs: hand_over_kernel(count, each, *refs),
        out_shape=tuple([jax.ShapeDtypeStruct((1, each), FULL)] * 2)
        + tuple(jax.ShapeDtypeStruct(a.shape, a.dtype) for a in arrays),
        in_specs=[vmem] + [anywhere] * count,
        out_specs=tuple([vmem] * 2 + [anywhere] * count),
        scratch_shapes=[pltpu.VMEM(a.shape, a.dtype) for a in arrays] + [pltpu.SemaphoreType.DMA((2, count))],
        compiler_params=pltpu.CompilerParams(vmem_limit_bytes=60 * 2**20),
        name="hand_over",
    )(gains, *arrays)


def rms_scale(values_in):
    return lax.rsqrt(jnp.mean(values_in * values_in, axis=-1, keepdims=True) + eps)


def rotate_table(positions):
    freq_index = jnp.arange(HD // 2, dtype=jnp.float32)
    inverse = jnp.exp(freq_index * (-2.0 * math.log(10000.0) / HD))
    angles = positions.astype(jnp.float32)[..., None] * inverse
    return (jnp.cos(angles), jnp.sin(angles))


def apply_rotary(values_in, cosine, sines):
    half_dim = values_in.shape[-1] // 2
    first_half = values_in[..., :half_dim]
    second_half = values_in[..., half_dim:]
    cosine = cosine[..., None, :]
    sines = sines[..., None, :]
    return jnp.concatenate(
        [first_half * cosine - second_half * sines, second_half * cosine + first_half * sines],
        axis=-1,
    )


def matmul(left_arg, right_arg):
    return jnp.dot(left_arg, right_arg, preferred_element_type=jnp.float32)


def stack_groups(values_in):
    row_count, model_width = values_in.shape
    return values_in.reshape(row_count, model_width // (4 * HD), 4 * HD).transpose(1, 0, 2)


def unstack_groups(values_in):
    group_count, row_count, group_width = values_in.shape
    return values_in.transpose(1, 0, 2).reshape(row_count, group_count * group_width)


def head_scores(query_grp, key_grp, allowed):
    row_count = query_grp.shape[0]
    query_heads = query_grp.reshape(row_count, 4, HD)
    key_heads = key_grp.reshape(row_count, 4, HD)
    scores = jnp.einsum(
        "qhe,khe->hqk", query_heads, key_heads, preferred_element_type=jnp.float32
    ) * HD ** (-0.5)
    return jnp.where(allowed[None], scores, -1e30)


def norm_back(grad_normed, inputs_f, scale_rows, gain_row):
    gain_term = jnp.sum(grad_normed * inputs_f * scale_rows, axis=0)
    scaled = grad_normed * gain_row
    grad_inputs = scale_rows * (
        scaled
        - inputs_f * scale_rows * scale_rows * jnp.mean(scaled * inputs_f, axis=-1, keepdims=True)
    )
    return (grad_inputs, gain_term)


def layer(
    gather_set,
    reduce_set,
    tokens,
    seq_counts,
    segments,
    positions,
    norm_first,
    query_weight,
    key_weight,
    value_weight,
    output_weight,
    norm_second,
    gate_weight,
    up_weight,
    down_weight,
    out_cotangent,
    value_cotangent,
):
    slot_count, seq_length, model_width = tokens.shape
    row_count = slot_count * seq_length
    head_count = model_width // HD
    weights = gather_set(
        norm_first,
        norm_second,
        query_weight,
        key_weight,
        value_weight,
        output_weight,
        gate_weight,
        up_weight,
        down_weight,
    )
    gain_one, gain_two, query_full, key_full, value_full, output_full = weights[:6]
    gate_full, up_full, down_full = weights[6:]
    row_index = jnp.arange(row_count, dtype=jnp.int32)
    slot_index = row_index // seq_length
    live_rows = (slot_index < seq_counts[0]).astype(jnp.float32)[:, None]
    flat_segments = segments.reshape(row_count)
    allowed = (
        (slot_index[:, None] == slot_index[None, :])
        & (flat_segments[:, None] == flat_segments[None, :])
        & (row_index[:, None] >= row_index[None, :])
    )
    inputs_f = tokens.reshape(row_count, model_width).astype(jnp.float32)
    scale_one = rms_scale(inputs_f)
    normed = (inputs_f * scale_one * gain_one.astype(jnp.float32)).astype(jnp.bfloat16)
    cosine, sines = rotate_table(positions.reshape(row_count))

    def rotated(values_in, turn_sign):
        turned = apply_rotary(
            values_in.reshape(row_count, head_count, HD), cosine, turn_sign * sines
        )
        return turned.reshape(row_count, model_width).astype(jnp.bfloat16)

    query_rot = rotated(matmul(normed, query_full), 1.0)
    key_rot = rotated(matmul(normed, key_full), 1.0)
    value_low = matmul(normed, value_full).astype(jnp.bfloat16)

    def attend_group(operands):
        query_grp, key_grp, value_grp = operands
        scores = head_scores(query_grp, key_grp, allowed)
        row_max = jnp.max(scores, axis=-1, keepdims=True)
        log_total = row_max + jnp.log(jnp.sum(jnp.exp(scores - row_max), axis=-1, keepdims=True))
        probs_low = jnp.exp(scores - log_total).astype(jnp.bfloat16)
        value_heads = value_grp.reshape(row_count, 4, HD)
        mixed_heads = jnp.einsum(
            "hqk,khe->qhe", probs_low, value_heads, preferred_element_type=jnp.float32
        )
        return (mixed_heads.reshape(row_count, 4 * HD), log_total)

    query_groups = stack_groups(query_rot)
    key_groups = stack_groups(key_rot)
    value_groups = stack_groups(value_low)
    mixed_groups, log_totals = lax.map(attend_group, (query_groups, key_groups, value_groups))
    mixed_low = unstack_groups(mixed_groups).astype(jnp.bfloat16)
    middle = inputs_f + matmul(mixed_low, output_full)
    scale_two = rms_scale(middle)
    normed_two = (middle * scale_two * gain_two.astype(jnp.float32)).astype(jnp.bfloat16)
    gate_pre = matmul(normed_two, gate_full)
    upward = matmul(normed_two, up_full)
    sigmoid_gate = jax.nn.sigmoid(gate_pre)
    silu_gate = gate_pre * sigmoid_gate
    hidden = (silu_gate * upward).astype(jnp.bfloat16)
    block_out = (live_rows * (middle + matmul(hidden, down_full))).astype(jnp.bfloat16)
    first_values = (live_rows * value_low.astype(jnp.float32)).astype(jnp.bfloat16)
    grad_y = live_rows * out_cotangent.reshape(row_count, model_width).astype(jnp.float32)
    grad_branch = grad_y.astype(jnp.bfloat16)
    down_term = jnp.einsum("rf,rd->fd", hidden, grad_branch, preferred_element_type=jnp.float32)
    grad_hidden = jnp.einsum(
        "rd,fd->rf", grad_branch, down_full, preferred_element_type=jnp.float32
    )
    grad_gate = (
        grad_hidden * upward * sigmoid_gate * (1.0 + gate_pre * (1.0 - sigmoid_gate))
    ).astype(jnp.bfloat16)
    grad_up = (grad_hidden * silu_gate).astype(jnp.bfloat16)
    gate_term = jnp.einsum("rd,rf->df", normed_two, grad_gate, preferred_element_type=jnp.float32)
    up_term = jnp.einsum("rd,rf->df", normed_two, grad_up, preferred_element_type=jnp.float32)
    grad_normed_two = jnp.einsum(
        "rf,df->rd", grad_gate, gate_full, preferred_element_type=jnp.float32
    ) + jnp.einsum("rf,df->rd", grad_up, up_full, preferred_element_type=jnp.float32)
    grad_middle_norm, gain_two_term = norm_back(
        grad_normed_two, middle, scale_two, gain_two.astype(jnp.float32)
    )
    grad_middle = grad_y + grad_middle_norm
    grad_attended = grad_middle.astype(jnp.bfloat16)
    output_term = jnp.einsum(
        "rd,re->de", mixed_low, grad_attended, preferred_element_type=jnp.float32
    )
    grad_mixed = jnp.einsum(
        "re,de->rd", grad_attended, output_full, preferred_element_type=jnp.float32
    ).astype(jnp.bfloat16)

    def attend_back(operands):
        query_grp, key_grp, value_grp, grad_grp, log_total = operands
        scores = head_scores(query_grp, key_grp, allowed)
        probs_full = jnp.exp(scores - log_total)
        probs_low = probs_full.astype(jnp.bfloat16)
        grad_heads = grad_grp.reshape(row_count, 4, HD)
        value_heads = value_grp.reshape(row_count, 4, HD)
        query_heads = query_grp.reshape(row_count, 4, HD)
        key_heads = key_grp.reshape(row_count, 4, HD)
        grad_probs = jnp.einsum(
            "qhe,khe->hqk", grad_heads, value_heads, preferred_element_type=jnp.float32
        )
        row_term = jnp.sum(probs_full * grad_probs, axis=-1, keepdims=True)
        grad_scores = (probs_full * (grad_probs - row_term)).astype(jnp.bfloat16)
        score_scale = HD ** (-0.5)
        grad_query = (
            jnp.einsum("hqk,khe->qhe", grad_scores, key_heads, preferred_element_type=jnp.float32)
            * score_scale
        )
        grad_key = (
            jnp.einsum("hqk,qhe->khe", grad_scores, query_heads, preferred_element_type=jnp.float32)
            * score_scale
        )
        grad_value = jnp.einsum(
            "hqk,qhe->khe", probs_low, grad_heads, preferred_element_type=jnp.float32
        )
        group_width = 4 * HD
        return (
            grad_query.reshape(row_count, group_width),
            grad_key.reshape(row_count, group_width),
            grad_value.reshape(row_count, group_width),
        )

    grad_q_groups, grad_k_groups, grad_v_groups = lax.map(
        attend_back, (query_groups, key_groups, value_groups, stack_groups(grad_mixed), log_totals)
    )
    grad_query = rotated(unstack_groups(grad_q_groups), -1.0)
    grad_key = rotated(unstack_groups(grad_k_groups), -1.0)
    grad_value = (
        unstack_groups(grad_v_groups)
        + live_rows * value_cotangent.reshape(row_count, model_width).astype(jnp.float32)
    ).astype(jnp.bfloat16)
    query_term = jnp.einsum("rd,re->de", normed, grad_query, preferred_element_type=jnp.float32)
    key_term = jnp.einsum("rd,re->de", normed, grad_key, preferred_element_type=jnp.float32)
    value_term = jnp.einsum("rd,re->de", normed, grad_value, preferred_element_type=jnp.float32)
    grad_normed = jnp.einsum(
        "re,de->rd", grad_query, query_full, preferred_element_type=jnp.float32
    )
    grad_normed = grad_normed + jnp.einsum(
        "re,de->rd", grad_key, key_full, preferred_element_type=jnp.float32
    )
    grad_normed = grad_normed + jnp.einsum(
        "re,de->rd", grad_value, value_full, preferred_element_type=jnp.float32
    )
    grad_inputs_norm, gain_one_term = norm_back(
        grad_normed, inputs_f, scale_one, gain_one.astype(jnp.float32)
    )
    token_grad = (grad_middle + grad_inputs_norm).astype(jnp.bfloat16).reshape(tokens.shape)
    grads = reduce_set(
        gain_one_term,
        gain_two_term,
        query_term,
        key_term,
        value_term,
        output_term,
        gate_term,
        up_term,
        down_term,
    )
    return (
        block_out.reshape(tokens.shape),
        first_values.reshape(tokens.shape),
        token_grad,
        grads[0],
        grads[2],
        grads[3],
        grads[4],
        grads[5],
        grads[1],
        grads[6],
        grads[7],
        grads[8],
    )


def plain_gather(*shards_in):
    return tuple(lax.all_gather(s, BOTH, axis=0, tiled=True) for s in shards_in)


def plain_reduce(*terms):
    return tuple(lax.psum_scatter(t, BOTH, scatter_dimension=0, tiled=True) for t in terms)


def linked_layer(mesh, *args):
    tokens, counts, segments, positions, norm_first = args[:5]
    norm_second, out_cotangent, value_cotangent = args[9], args[13], args[14]
    weights = args[5:9] + args[10:13]
    each = norm_first.shape[0]
    first, block, token_grad, gains, grads = whole_layer(
        mesh, tokens, counts, segments, positions, norm_first, norm_second, weights, (out_cotangent, value_cotangent)
    )
    one, two, block, first, token_grad, *grads = hand_over(gains, each, [block, first, token_grad] + grads)
    streams = tuple(a.reshape(tokens.shape) for a in (block, first, token_grad))
    return streams + (one.reshape(each), *grads[:4], two.reshape(each), *grads[4:])


def fits(mesh, tokens, weights):
    return (
        dict(mesh.shape) == {DP: 4, FSDP: 8}
        and tokens == (4, 128, 1024)
        and all(w == (32, 1024) for w in weights[:4])
        and weights[4:] == ((32, 2816), (32, 2816), (88, 1024))
    )


def solution(mesh):
    one, two, three = P(BOTH), P(BOTH, None), P(BOTH, None, None)
    in_specs = (three, one, two, two, one, two, two, two, two, one, two, two, two, three, three)
    out_specs = (three, three, three, one, two, two, two, two, one, two, two, two)

    def shards(*args):
        weights = tuple(w.shape for w in args[5:9] + args[10:13])
        if fits(mesh, args[0].shape, weights):
            return linked_layer(mesh, *args)
        return layer(plain_gather, plain_reduce, *args)

    return jax.shard_map(shards, mesh=mesh, in_specs=in_specs, out_specs=out_specs, check_vma=False)
```

```python
import math
from typing import Any, NamedTuple

import jax
import jax.numpy as jnp
import numpy as np
from jax import lax
from jax.experimental import pallas as pl
from jax.experimental.pallas import tpu as pltpu
from jax.sharding import PartitionSpec as P

HD = 64
MESH = pl.DeviceIdType.MESH
DP, FSDP = "dp", "fsdp"
BOTH = (DP, FSDP)
LOW, FULL = jnp.bfloat16, jnp.float32
WIDE = 256

eps = 1e-06


class Weights(NamedTuple):
    gains: Any
    query: Any
    key: Any
    value: Any
    output: Any
    gate: Any
    up: Any
    down: Any


class Saved(NamedTuple):
    cos: Any
    sin: Any
    normed_t: Any
    q_rot: Any
    k_rot: Any
    v_low: Any
    probs: Any
    mixed_t: Any
    middle: Any
    two: Any
    two_t: Any
    first: Any
    hid_t: Any
    down: Any


W = Weights._make(range(len(Weights._fields)))
S = Saved._make(range(len(Saved._fields)))


class Place:
    def __init__(self, depth):
        dp, fsdp = lax.axis_index(DP), lax.axis_index(FSDP)
        self.x, self.c = dp // 2, dp % 2
        self.z, self.y = fsdp // 2, fsdp % 2
        self.depth = depth

    def at(self, x, c, z, y):
        return (x * 2 + c, z * 2 + y)

    def across_x(self):
        return self.at(1 - self.x, self.c, self.z, self.y)

    def across_y(self):
        return self.at(self.x, self.c, self.z, 1 - self.y)

    def sibling(self):
        return self.at(self.x, 1 - self.c, self.z, self.y)

    def above(self):
        return self.at(self.x, self.c, self.z + 1, self.y)

    def below(self):
        return self.at(self.x, self.c, self.z - 1, self.y)

    def greet(self):
        barrier = pltpu.get_barrier_semaphore()

        def call(who):
            pl.semaphore_signal(barrier, inc=1, device_id=who, device_id_type=MESH)

        call(self.across_x())
        call(self.across_y())
        call(self.sibling())
        not_top = self.z < self.depth - 1
        not_low = self.z > 0
        pl.when(not_top)(lambda: call(self.above()))
        pl.when(not_low)(lambda: call(self.below()))
        peers = 3 + not_top.astype(jnp.int32) + not_low.astype(jnp.int32)
        pl.semaphore_wait(barrier, peers)


def remote(src, dst, send_sem, recv_sem, who):
    return pltpu.make_async_remote_copy(
        src_ref=src,
        dst_ref=dst,
        send_sem=send_sem,
        recv_sem=recv_sem,
        device_id=who,
        device_id_type=MESH,
    )


def iota(shape, dim):
    return lax.broadcasted_iota(jnp.int32, shape, dim)


def dot(a, b, dims=((1,), (0,))):
    return lax.dot_general(a, b, (dims, ((), ())), preferred_element_type=FULL)


def to_column(row):
    n = row.shape[1]
    eye = iota((n, n), 0) == iota((n, n), 1)
    return jnp.sum(jnp.where(eye, jnp.broadcast_to(row, (n, n)), 0.0), axis=1, keepdims=True)


def turn(values, cosine, sines):
    outs = []
    first = iota((values.shape[0], 128), 1) % HD < HD // 2
    for g in range(values.shape[1] // 128):
        part = values[:, g * 128 : (g + 1) * 128]
        other = jnp.where(
            first, pltpu.roll(part, 128 - HD // 2, 1), pltpu.roll(part, HD // 2, 1)
        )
        outs.append(part * cosine + other * sines)
    return jnp.concatenate(outs, axis=1)


def gain_row(gains, row, each):
    count = gains.shape[0]
    rows = gains[:, row, :]
    whole = jnp.concatenate([rows] * (count * each // 128), axis=1)
    shape = whole.shape
    keep = iota(shape, 1) // each == iota(shape, 0)
    return jnp.sum(jnp.where(keep, whole, 0.0), axis=0, keepdims=True)


def split_pair(values):
    first = iota(values.shape, 1) < HD
    zero = jnp.zeros_like(values)
    return jnp.concatenate([jnp.where(first, values, zero), jnp.where(first, zero, values)], axis=0)


class Gather:
    def __init__(self, place, own, full, sends, receipts, local_sem, z_first):
        self.p, self.own, self.full, self.z_first = place, own, full, z_first
        self.sends, self.receipts, self.local_sem = sends, receipts, local_sem
        self.wide = own.shape[-1]

    def shard(self, x, y, z):
        return self.full.at[x, self.p.c, z, y]

    def zunit(self, z):
        if self.z_first:
            return self.full.at[self.p.x, self.p.c, z, self.p.y]
        return self.full.at[:, self.p.c, z]

    def runit(self, x, y, half=None):
        if self.z_first:
            if half is None:
                return self.full.at[x, self.p.c, :, y]
            count = self.p.depth // 2
            return self.full.at[x, self.p.c, half * count : (half + 1) * count, y]
        if half is None:
            return self.full.at[x, self.p.c, self.p.z, y]
        count = self.wide // 2
        return self.full.at[x, self.p.c, self.p.z, y, :, half * count : (half + 1) * count]

    def copy(self, ref, sent, slot, who, src=None):
        return remote(ref if src is None else src, ref, self.sends.at[sent], self.receipts.at[slot], who)

    def up(self, unit, src=None):
        return self.copy(self.zunit(unit), 0, unit, self.p.above(), src)

    def down(self, unit, src=None):
        return self.copy(self.zunit(unit), 1, unit - 1, self.p.below(), src)

    def ring(self, ref, i, who, src=None):
        return self.copy(ref, 2, self.p.depth - 1 + i, who, src)

    def sib(self, ref):
        return self.copy(ref, 3, self.p.depth + 3, self.p.sibling())

    def keep_own(self):
        p = self.p
        return pltpu.make_async_copy(self.own, self.shard(p.x, p.y, p.z), self.local_sem)

    def z_step(self, step):
        p = self.p
        top, low = p.depth - 1, 0
        src = self.own if (step == 0 and self.z_first) else None

        def from_below():
            if step > 0:
                self.up(p.z - step).wait_recv()
            if step < top:
                pl.when(p.z < top)(lambda: self.up(p.z - step, src).start())

        def from_above():
            if step > 0:
                self.down(p.z + step).wait_recv()
            if step < top:
                pl.when(p.z > low)(lambda: self.down(p.z + step, src).start())

        pl.when(p.z - step >= low)(from_below)
        pl.when(p.z + step <= top)(from_above)

    def ring_first(self):
        p = self.p
        mine = self.runit(p.x, p.y)
        src = None if self.z_first else self.own
        self.ring(mine, 0, p.across_x(), src).start()
        self.ring(mine, 1, p.across_y(), src).start()

    def ring_second(self):
        p = self.p
        from_x, from_y = self.runit(1 - p.x, p.y), self.runit(p.x, 1 - p.y)
        self.ring(from_x, 0, p.across_x()).wait_recv()
        self.ring(self.runit(1 - p.x, p.y, 0), 2, p.across_y()).start()
        self.ring(from_y, 1, p.across_y()).wait_recv()
        self.ring(self.runit(p.x, 1 - p.y, 1), 3, p.across_x()).start()

    def ring_last(self):
        p = self.p
        self.ring(self.runit(1 - p.x, 1 - p.y, 0), 2, p.across_y()).wait_recv()
        self.ring(self.runit(1 - p.x, 1 - p.y, 1), 3, p.across_x()).wait_recv()

    def mine(self, kind):
        p = self.p
        x, y = (1 - p.x if kind % 2 else p.x), (1 - p.y if kind // 2 else p.y)
        self.sib(self.full.at[x, p.c, :, y]).start()

    def pass_on(self, step):
        p = self.p

        def low():
            self.sib(self.full.at[:, p.c, p.z - step]).start()

        def high():
            self.sib(self.full.at[:, p.c, p.z + step]).start()

        pl.when(p.z - step >= 0)(low)
        if step > 0:
            pl.when(p.z + step <= p.depth - 1)(high)

    def steps(self):
        mine = self.mine
        if self.z_first:
            return [
                lambda: (self.keep_own().start(), self.z_step(0)),
                lambda: self.z_step(1),
                lambda: self.z_step(2),
                lambda: (self.z_step(3), self.keep_own().wait(), self.ring_first(), mine(0)),
                lambda: (self.ring_second(), mine(1), mine(2)),
                lambda: (self.ring_last(), mine(3)),
                self.finish,
            ]
        return [
            lambda: (self.keep_own().start(), self.ring_first()),
            self.ring_second,
            lambda: (self.ring_last(), self.keep_own().wait(), self.z_step(0), self.pass_on(0)),
            lambda: (self.z_step(1), self.pass_on(1)),
            lambda: (self.z_step(2), self.pass_on(2)),
            lambda: (self.z_step(3), self.pass_on(3)),
            self.finish,
        ]

    def finish(self):
        self.sib(self.full.at[:, 1 - self.p.c]).wait_recv()

    def sent(self):
        p = self.p
        top = p.depth - 1

        def units(count):
            if self.z_first:
                return self.full.at[p.x, p.c, :count, p.y]
            return self.full.at[:, p.c, :count]

        for z in range(top):
            pl.when(p.z == z)(lambda z=z: self.copy(units(z + 1), 0, 0, p.above()).wait_send())
        for z in range(1, p.depth):
            pl.when(p.z == z)(lambda z=z: self.copy(units(p.depth - z), 1, 0, p.below()).wait_send())
        three = self.full.at[:, p.c, :3] if self.z_first else self.full.at[p.x, p.c, :3, p.y]
        self.ring(three, 0, p.across_x()).wait_send()
        self.sib(self.full.at[:, p.c]).wait_send()


def add_block(into, other):
    into[...] = into[...] + other[...]


class Buffers(NamedTuple):
    acc: Any
    stage: Any
    sib: Any
    ring1: Any
    ring2: Any
    zed: Any
    sends: Any
    receipts: Any
    credit: Any


class Reduce:
    def __init__(self, place, index, count, slots, z_first, buffers, emit):
        self.p, self.z_first, self.b, self.emit = place, z_first, buffers, emit
        self.k, self.count, self.slots = index, count, slots
        rows = buffers.acc.shape[3]
        self.cut = (rows // 2 + 15) // 16 * 16

    def copy(self, src, dst, slot, who):
        sent = 0 if slot == 0 else 1 if slot < 5 else 2
        return remote(src, dst, self.b.sends.at[sent], self.b.receipts.at[slot], who)

    def sib_copy(self):
        return self.copy(self.b.stage, self.b.sib, 0, self.p.sibling())

    def free_stage(self):
        self.sib_copy().wait_send()

    def send(self):
        if self.k >= self.slots:
            pl.semaphore_wait(self.b.credit, 1)
        self.sib_copy().start()

    def merge(self):
        self.sib_copy().wait_recv()
        depth = self.p.depth

        def block(i, carry):
            at = (i // (2 * depth), i // 2 % depth, i % 2)
            self.b.acc[at] = self.b.acc[at] + self.b.sib[at]
            return carry

        lax.fori_loop(0, 4 * depth, block, 0)
        if self.k + self.slots < self.count:
            pl.semaphore_signal(
                self.b.credit, inc=1, device_id=self.p.sibling(), device_id_type=MESH
            )

    def bundle(self, x, y):
        if self.z_first:
            return self.b.acc.at[x, self.p.z, y]
        return self.b.acc.at[x, :, y]

    def halves(self, ref):
        cut = self.cut if self.z_first else self.p.depth // 2
        return ref.at[:cut], ref.at[cut:]

    def first_copies(self):
        p = self.p
        low, high = self.halves(self.bundle(1 - p.x, 1 - p.y))
        to_low, to_high = self.halves(self.b.ring1)
        return (
            self.copy(low, to_low, 1, p.across_x()),
            self.copy(high, to_high, 2, p.across_y()),
        )

    def second_copies(self):
        p = self.p
        return (
            self.copy(self.bundle(1 - p.x, p.y), self.b.ring2.at[0], 3, p.across_x()),
            self.copy(self.bundle(p.x, 1 - p.y), self.b.ring2.at[1], 4, p.across_y()),
        )

    def ring_first(self):
        for copy in self.first_copies():
            copy.start()

    def ring_second(self):
        p = self.p
        by_x, by_y = self.first_copies()
        to_x, to_y = self.second_copies()
        got_low, got_high = self.halves(self.b.ring1)
        by_x.wait_recv()
        add_block(self.halves(self.bundle(p.x, 1 - p.y))[0], got_low)
        to_y.start()
        by_y.wait_recv()
        add_block(self.halves(self.bundle(1 - p.x, p.y))[1], got_high)
        to_x.start()

    def ring_last(self):
        p = self.p
        for copy in self.second_copies():
            copy.wait_recv()
        both = self.b.ring2[0].astype(FULL) + self.b.ring2[1].astype(FULL)
        return self.bundle(p.x, p.y)[...].astype(FULL) + both

    def zunits(self, units):
        if self.z_first:
            return self.b.acc.at[:, units]
        return self.b.acc.at[self.p.x, units, self.p.y]

    def landing(self, side, units):
        if self.z_first:
            return self.b.zed.at[side, :, units]
        return self.b.zed.at[side, units]

    def up(self, step):
        top = self.p.depth - 1
        return self.copy(self.zunits(slice(step + 1, top + 1)), self.landing(0, slice(step, top)), 5, self.p.above())

    def down(self, step):
        count = self.p.depth - 1 - step
        return self.copy(self.zunits(slice(0, count)), self.landing(1, slice(0, count)), 6, self.p.below())

    def z_step(self, step):
        p, top = self.p, self.p.depth - 1

        def upward():
            if step > 0:
                self.up(step - 1).wait_recv()
            if step < top:
                if step > 0:
                    add_block(self.zunits(slice(step + 1, top + 1)), self.landing(0, slice(step, top)))
                self.up(step).start()

        def downward():
            if step > 0:
                self.down(step - 1).wait_recv()
            if step < top:
                if step > 0:
                    add_block(self.zunits(slice(0, top - step)), self.landing(1, slice(0, top - step)))
                self.down(step).start()

        pl.when(p.z == step)(upward)
        pl.when(p.z == top - step)(downward)

    def z_sum(self, put):
        p, top = self.p, self.p.depth - 1
        mine = self.zunits(p.z)[...].astype(FULL)

        @pl.when(p.z == 0)
        def _():
            put(mine + self.landing(1, 0)[...].astype(FULL))

        @pl.when(p.z == top)
        def _():
            put(mine + self.landing(0, top - 1)[...].astype(FULL))

        @pl.when((p.z > 0) & (p.z < top))
        def _():
            low, high = self.landing(0, p.z - 1)[...], self.landing(1, p.z)[...]
            put(mine + (low.astype(FULL) + high.astype(FULL)))

    def steps(self):
        kind = self.b.acc.dtype

        def keep_ring():
            self.bundle(self.p.x, self.p.y)[...] = self.ring_last().astype(kind)
            self.z_step(0)

        def keep_z(values):
            self.zunits(self.p.z)[...] = values.astype(kind)

        if self.z_first:
            return [
                self.send,
                lambda: (self.merge(), self.z_step(0)),
                lambda: self.z_step(1),
                lambda: self.z_step(2),
                lambda: (self.z_step(3), self.z_sum(keep_z), self.ring_first()),
                self.ring_second,
                lambda: self.emit(self.ring_last()),
            ]
        return [
            self.send,
            lambda: (self.merge(), self.ring_first()),
            self.ring_second,
            keep_ring,
            lambda: self.z_step(1),
            lambda: self.z_step(2),
            lambda: (self.z_step(3), self.z_sum(self.emit)),
        ]

    def sent(self):
        p = self.p
        if self.k + self.slots >= self.count:
            self.free_stage()
        three = self.b.acc.at[0, :3, 0] if self.z_first else self.b.acc.at[:, :3]
        self.copy(three, three, 1, p.across_x()).wait_send()
        units = self.zunits(slice(0, p.depth - 1))
        self.copy(units, units, 5, p.sibling()).wait_send()


GATHER_JOBS = (
    (W.gains, True, None),
    (W.query, True, None),
    (W.key, True, None),
    (W.value, True, None),
    (W.output, True, None),
    (W.down, False, (0, 1)),
    (W.down, True, (1, 2)),
    (W.gate, True, (0, 3)),
    (W.up, True, (0, 3)),
    (W.gate, True, (3, 6)),
    (W.up, True, (3, 6)),
    (W.gate, True, (6, 8)),
    (W.up, True, (6, 8)),
    (W.gate, False, (8, 11)),
    (W.up, False, (8, 11)),
)
DOWN, SIDE, SIDE_Z, GAIN = range(4)
SLOTS = (2, 2, 2, 1)
Z_FIRST = (False, False, True, False)
Z_CHUNKS = ((W.gate, 0), (W.gate, 1), (W.gate, 2), (W.gate, 4), (W.gate, 6), (W.gate, 8))
ORDER = (
    0, 28, 98, 35, 7, 91, 1, 99, 29, 2, 3, 36, 14, 30, 21, 8, 92, 4, 49, 31, 9, 10, 56, 70, 22, 42, 273, 5, 23, 32,
    15, 50, 11, 16, 17, 57, 43, 6, 274, 77, 58, 37, 24, 18, 12, 63, 13, 275, 44, 33, 34, 71, 25, 78, 276, 51, 38, 45,
    19, 277, 84, 20, 278, 26, 27, 280, 64, 59, 72, 279, 281, 282, 39, 85, 46, 93, 52, 286, 283, 60, 284, 285, 65, 79,
    100, 287, 47, 40, 86, 73, 288, 289, 41, 48, 290, 53, 94, 66, 61, 291, 292, 293, 54, 74, 62, 87, 55, 295, 297, 101,
    294, 296, 299, 133, 67, 298, 140, 80, 102, 134, 300, 75, 68, 147, 141, 95, 76, 69, 301, 103, 303, 148, 88, 81,
    302, 305, 154, 304, 89, 155, 82, 306, 168, 90, 83, 307, 309, 161, 96, 104, 156, 169, 308, 97, 311, 310, 182, 312,
    183, 313, 170, 315, 162, 314, 196, 184, 135, 316, 203, 197, 317, 105, 204, 318, 112, 106, 198, 319, 320, 119, 171,
    205, 113, 321, 142, 120, 126, 107, 175, 189, 322, 323, 324, 210, 127, 185, 176, 190, 149, 121, 172, 325, 114, 157,
    326, 327, 328, 217, 150, 128, 211, 329, 330, 224, 218, 177, 108, 122, 331, 225, 332, 231, 333, 163, 232, 238, 334,
    245, 219, 239, 191, 252, 335, 246, 336, 199, 253, 212, 206, 115, 186, 220, 337, 338, 178, 226, 339, 164, 340, 143,
    247, 259, 158, 129, 207, 233, 341, 192, 123, 227, 213, 254, 260, 200, 173, 116, 136, 109, 221, 240, 266, 248, 342,
    255, 130, 261, 234, 267, 110, 151, 165, 241, 228, 214, 124, 159, 179, 187, 137, 117, 111, 262, 144, 208, 256, 268,
    138, 180, 235, 222, 201, 152, 160, 145, 249, 269, 118, 131, 229, 193, 257, 174, 242, 263, 236, 166, 194, 209, 223,
    181, 215, 270, 243, 250, 216, 264, 258, 188, 244, 237, 139, 132, 271, 153, 230, 251, 146, 125, 195, 167, 202, 265,
    272,
)


def chunk_list(tiles, width):
    halves = width // (2 * WIDE)
    sides = [(W.gate, f) for f in range(tiles)]
    sides += [(w, half) for w in (W.output, W.query, W.key, W.value) for half in range(halves)]
    chunks = [(DOWN, W.down, n) for n in range(width // WIDE)]
    chunks += [(SIDE_Z if side in Z_CHUNKS else SIDE, *side) for side in sides]
    return chunks + [(GAIN, W.gains, 0)]


class Ahead(NamedTuple):
    tokens: Any
    normed: Any
    normed_t: Any
    q_rot: Any
    k_rot: Any
    v_low: Any
    first: Any
    probs: Any
    mixed: Any
    mixed_t: Any
    w: Any
    middle: Any
    two: Any
    two_t: Any
    cos: Any
    sin: Any
    bias: Any
    live: Any


class Hidden(NamedTuple):
    hid_t: Any
    branch: Any
    raw: Any
    down: Any
    two: Any
    two_t: Any
    middle: Any
    tile: Any
    both: Any


class Attention(NamedTuple):
    w: Any
    mixed_t: Any
    normed_t: Any
    v_low: Any
    probs: Any
    cos: Any
    sin: Any
    tokens: Any
    gmixed: Any
    gq: Any
    gk: Any
    gv: Any
    gnormed: Any


class Last(NamedTuple):
    hid_t: Any
    down: Any
    middle: Any
    out: Any


class Layer:
    def __init__(self, place, **refs):
        self.p = place
        self.__dict__.update(refs)
        self.slots, self.length = self.segments.shape
        self.rows, self.width = self.tokens.shape
        self.tiles = self.full.gate.shape[-1] // WIDE
        self.loads = 0
        self.pending = {}
        self.saving = []

    def fetch(self, key, src, dst):
        copy = pltpu.make_async_copy(src, dst, self.load_sems.at[self.loads])
        self.loads += 1
        self.pending[key] = copy
        copy.start()

    def arrived(self, *keys):
        for key in keys:
            self.pending.pop(key).wait()

    def save(self, *which):
        for i in which:
            copy = pltpu.make_async_copy(getattr(self.h, Saved._fields[i]), self.s[i], self.save_sems.at[i])
            copy.start()
            self.saving.append(copy)

    def saved(self):
        for copy in self.saving:
            copy.wait()
        self.saving = []

    def block_rows(self, b):
        return pl.ds(b * self.length, self.length)

    def live(self, b):
        return (jnp.int32(b) < self.counts[0]).astype(FULL)

    def own_shards(self):
        each = self.norm_first.shape[1]
        spread = (iota((each, 128), 1) % each == iota((each, 128), 0)).astype(LOW)
        sub = iota((8, 128), 0)
        one, two = dot(self.norm_first[...], spread), dot(self.norm_second[...], spread)
        self.own_gains[...] = jnp.where(sub == 0, one, jnp.where(sub == 1, two, 0.0))
        rows, half = self.down_weight.shape[0], self.down_weight.shape[1] // 2
        down = self.down_weight[...].astype(FULL)
        self.own_down[...] = jnp.concatenate([down[:, :half], down[:, half:]], axis=0).astype(LOW)

    def tables(self):
        h = self.h
        for b in range(self.slots):
            rows = pl.ds(b * self.length, self.length)
            angles = to_column(self.positions[b : b + 1, :].astype(FULL)) * self.inverse[...]
            first = iota(angles.shape, 1) % HD < HD // 2
            sines = jnp.sin(angles)
            h.cos[rows, :] = jnp.cos(angles)
            h.sin[rows, :] = jnp.where(first, -sines, sines)
            seg = self.segments[b : b + 1, :].astype(FULL)
            shape = (self.length, self.length)
            allowed = (to_column(seg) == seg) & (iota(shape, 0) >= iota(shape, 1))
            h.bias[b] = jnp.where(allowed, 0.0, -1e30)
        h.live[...] = (iota((self.rows, 128), 0) // self.length < self.counts[0]).astype(FULL)
        self.save(S.cos, S.sin)

    def gain_rows(self):
        self.fetch((W.gains,), self.full.gains, self.gains_near)
        self.arrived((W.gains,))
        near = self.gains_near
        count = math.prod(near.shape[:4])
        gains = near[...].reshape(count, 8, 128)
        self.gain[0:1, :] = gain_row(gains, 0, self.width // count)
        self.gain[1:2, :] = gain_row(gains, 1, self.width // count)

    def norm_one(self):
        h = self.h
        self.arrived(-3)
        for b in range(self.slots):
            rows = pl.ds(b * self.length, self.length)
            inputs = h.tokens[rows, :].astype(FULL)
            scale = lax.rsqrt(jnp.mean(inputs * inputs, axis=-1, keepdims=True) + eps)
            normed = (inputs * scale * self.gain[0:1, :]).astype(LOW)
            h.normed[rows, :] = normed
            h.normed_t[:, rows] = normed.T
        self.save(S.normed_t)

    def take(self, which):
        self.fetch((which,), self.full[which], self.h.w.at[which % 2])

    def weight(self, which, cols):
        w = self.h.w[which % 2, :, :, :, :, :, cols]
        return w.reshape(math.prod(w.shape[:5]), w.shape[5])

    def project(self, which):
        h = self.h
        self.arrived((which,))
        normed = h.normed[...]

        def tile(n, carry):
            cols = pl.ds(pl.multiple_of(n * WIDE, WIDE), WIDE)
            got = dot(normed, self.weight(which, cols))
            if which == W.value:
                low = got.astype(LOW)
                h.v_low[:, cols] = low
                h.first[:, cols] = (h.live[...][:, 0:1] * low.astype(FULL)).astype(LOW)
            else:
                into = h.q_rot if which == W.query else h.k_rot
                into[:, cols] = turn(got, h.cos[...], h.sin[...]).astype(LOW)
            return carry

        lax.fori_loop(0, self.width // WIDE, tile, 0)
        if which == W.value:
            self.save(S.v_low, S.first)
        else:
            self.save(S.q_rot if which == W.query else S.k_rot)

    def attend(self, b):
        h = self.h
        length = self.length
        rows = pl.ds(b * length, length)

        def pair(n, carry):
            cols = pl.ds(pl.multiple_of(n * 128, 128), 128)
            q, k, v = h.q_rot[rows, cols], h.k_rot[rows, cols], h.v_low[rows, cols]
            k2, v2 = split_pair(k), split_pair(v)
            scores = dot(q, k2, ((1,), (1,))) * HD ** (-0.5)
            bias = h.bias[b]
            probs = []
            for half in range(2):
                s = scores[:, half * length : (half + 1) * length] + bias
                e = jnp.exp(s - jnp.max(s, axis=-1, keepdims=True))
                probs.append(e * (1.0 / jnp.sum(e, axis=-1, keepdims=True)))
            probs = jnp.concatenate(probs, axis=1).astype(LOW)
            h.probs[b, n] = probs
            h.mixed[rows, cols] = dot(probs, v2).astype(LOW)
            return carry

        lax.fori_loop(0, self.width // 128, pair, 0, unroll=True)
        h.mixed_t[:, rows] = h.mixed[rows, :].T
        if b == self.slots - 1:
            self.save(S.probs, S.mixed_t)

    def join(self):
        h = self.h
        self.arrived((W.output,))
        mixed = h.mixed[...]

        def tile(n, carry):
            cols = pl.ds(pl.multiple_of(n * WIDE, WIDE), WIDE)
            got = dot(mixed, self.weight(W.output, cols))
            h.middle[:, cols] = h.tokens[:, cols].astype(FULL) + got
            return carry

        lax.fori_loop(0, self.width // WIDE, tile, 0)
        self.save(S.middle)

    def norm_two(self):
        h = self.h
        for b in range(self.slots):
            rows = pl.ds(b * self.length, self.length)
            middle = h.middle[rows, :]
            scale = lax.rsqrt(jnp.mean(middle * middle, axis=-1, keepdims=True) + eps)
            normed = (middle * scale * self.gain[1:2, :]).astype(LOW)
            h.two[rows, :] = normed
            h.two_t[:, rows] = normed.T
        self.save(S.two, S.two_t)

    def enter(self):
        h, s = self.h, self.s
        self.fetch(S.two, s.two, h.two)
        self.fetch(-1, self.out_cotangent, h.branch)
        self.fetch(S.two_t, s.two_t, h.two_t)
        self.fetch(S.middle, s.middle, h.middle)
        self.arrived(-1)
        for b in range(self.slots):
            rows = self.block_rows(b)
            h.branch[rows, :] = (h.branch[rows, :].astype(FULL) * self.live(b)).astype(LOW)

    def raw(self):
        self.fetch((W.down, 0), self.full.down.at[0, 0], self.h.raw)

    def down_quarter(self, i):
        self.arrived((W.down, i))
        depth, raw, down = self.p.depth, self.h.raw, self.h.down
        rows, half = raw.shape[2] // 2, raw.shape[3]
        for z in range(depth):
            pair = raw[z].astype(FULL)
            for side in range(2):
                part = pair[:, side * rows : (side + 1) * rows, :].reshape(2 * rows, half)
                at = (i * depth + z) * 2 * rows
                down[at : at + 2 * rows, side * half : (side + 1) * half] = part.astype(LOW)
        j = i + 1
        if j < 4:
            self.fetch((W.down, j), self.full.down.at[j // 2, j % 2], raw)
        else:
            self.save(S.down)

    def tile_load(self, f):
        cols = pl.ds(f * WIDE, WIDE)
        for which, side in ((W.gate, 0), (W.up, 1)):
            into = self.h.tile.at[f % 2, :, :, :, :, :, side * WIDE : (side + 1) * WIDE]
            self.fetch((which, f), self.full[which].at[:, :, :, :, :, cols], into)

    def ff_tile(self, f):
        h, slot = self.h, f % 2
        self.arrived((W.gate, f), (W.up, f))
        if f == 0:
            self.arrived(S.two, S.two_t)
        count = self.width // 4
        both = dot(h.two[...], h.tile[slot].reshape(self.width, 2 * WIDE))
        gate, upward = both[:, :WIDE], both[:, WIDE:]
        sig = 1.0 / (1.0 + jnp.exp(-gate))
        silu = gate * sig
        rows = slice(f * WIDE, (f + 1) * WIDE)
        h.hid_t[rows, :] = (silu * upward).astype(LOW).T
        grad = dot(h.branch[...], h.down[rows, :], ((1,), (1,)))
        h.both[:, :WIDE] = (grad * upward * sig * (1.0 + gate * (1.0 - sig))).astype(LOW)
        h.both[:, WIDE:] = (grad * silu).astype(LOW)
        self.side_by_side(self.job[W.gate, f], h.two_t, h.both)
        for xc in range(4):
            cols = slice(xc * count, (xc + 1) * count)
            weight = h.tile[slot, xc // 2, xc % 2].reshape(count, 2 * WIDE)
            got = dot(h.both[...], weight, ((1,), (1,)))
            if f == 0:
                self.grad[:, cols] = got
            else:
                self.grad[:, cols] += got
        if f == self.tiles - 1:
            self.save(S.hid_t)

    def spread(self, job, part):
        p = self.p
        if job.before is not None:
            job.before.free_stage()
        for x in range(2):
            part(x, 1 - p.c, job.b.stage)
            part(x, p.c, job.b.acc)

    def side_by_side(self, job, left, right):
        count = self.width // 4

        def part(x, c, into):
            at = pl.multiple_of((x * 2 + c) * count, count)
            got = dot(left[pl.ds(at, count), :], right[...]).astype(LOW)
            got = got.reshape(self.p.depth, 2, -1, 2 * WIDE)
            each = got.shape[2]
            into[x, :, :, :each, :] = got[..., :WIDE]
            into[x, :, :, each:, :] = got[..., WIDE:]

        self.spread(job, part)

    def down_chunk(self, n):
        h = self.h
        right = h.branch[:, n * WIDE : (n + 1) * WIDE]
        count = h.hid_t.shape[0] // 4

        def part(x, c, into):
            at = pl.multiple_of((x * 2 + c) * count, 16)
            got = dot(h.hid_t[pl.ds(at, count), :], right)
            got = got.reshape(2 * self.p.depth, -1, WIDE)
            got = jnp.concatenate([got[:, :, : WIDE // 2], got[:, :, WIDE // 2 :]], axis=1)
            into[x] = got.astype(LOW).reshape(into.shape[1:])

        self.spread(self.job[W.down, n], part)

    def norm_back(self, grads, inputs, gain):
        scale = lax.rsqrt(jnp.mean(inputs * inputs, axis=-1, keepdims=True) + eps)
        total = jnp.sum(grads * inputs * scale, axis=0, keepdims=True)
        scaled = grads * gain
        mean = jnp.mean(scaled * inputs, axis=-1, keepdims=True)
        return scale * (scaled - inputs * (scale * scale * mean)), total

    def norm_two_back(self):
        h = self.h
        self.arrived(S.middle)
        total = jnp.zeros((1, self.width), FULL)
        for b in range(self.slots):
            rows = self.block_rows(b)
            got, part = self.norm_back(self.grad[rows, :], h.middle[rows, :], self.gain[1:2, :])
            grad = h.branch[rows, :].astype(FULL) + got
            self.grad[rows, :] = grad
            self.attended[rows, :] = grad.astype(LOW)
            total = total + part
        self.gain_sum[1:2, :] = total

    def second(self):
        h, s = self.h, self.s
        self.fetch((W.output,), self.full.output, h.w.at[0])
        self.fetch(S.mixed_t, s.mixed_t, h.mixed_t)
        self.fetch(S.v_low, s.v_low, h.v_low)
        self.fetch(S.probs, s.probs, h.probs)
        self.fetch(S.q_rot, s.q_rot, h.gq)
        self.fetch(S.k_rot, s.k_rot, h.gk)
        self.fetch(-2, self.value_cotangent, h.gv)
        self.fetch(S.cos, s.cos, h.cos)
        self.fetch(S.sin, s.sin, h.sin)
        self.fetch(S.normed_t, s.normed_t, h.normed_t)
        self.fetch(-3, self.tokens, h.tokens)
        self.fetch((W.query,), self.full.query, h.w.at[1])

    def weight_rows(self, slot, xc):
        return self.h.w[slot, xc // 2, xc % 2].reshape(self.width // 4, self.width)

    def mixed_back(self):
        self.arrived((W.output,))
        for xc in range(4):
            got = dot(self.attended[...], self.weight_rows(0, xc), ((1,), (1,)))
            count = self.width // 4
            self.h.gmixed[:, xc * count : (xc + 1) * count] = got.astype(LOW)
        self.fetch((W.key,), self.full.key, self.h.w.at[0])

    def weight_chunk(self, which, half):
        h = self.h
        if half == 0 and which in (W.output, W.query):
            self.arrived(S.mixed_t if which == W.output else S.normed_t)
        left = h.mixed_t if which == W.output else h.normed_t
        right = {W.output: self.attended, W.query: h.gq, W.key: h.gk, W.value: h.gv}[which]
        cols = slice(half * 2 * WIDE, (half + 1) * 2 * WIDE)
        self.side_by_side(self.job[which, half], left, right.at[:, cols])

    def attend_back(self, b):
        h = self.h
        if b == 0:
            self.arrived(S.v_low, S.probs, S.q_rot, S.k_rot, -2, S.cos, S.sin)
        rows, length = self.block_rows(b), self.length
        first = iota((length, 128), 1) < HD
        live = self.live(b)
        cosine, sines = h.cos[rows, :], h.sin[rows, :]

        def fold(values):
            return jnp.where(first, values[:length], values[length:])

        def pair(n, carry):
            cols = pl.ds(pl.multiple_of(n * 128, 128), 128)
            q, k, v = h.gq[rows, cols], h.gk[rows, cols], h.v_low[rows, cols]
            grad = h.gmixed[rows, cols]
            probs = h.probs[b, n]
            k2, v2 = split_pair(k), split_pair(v)
            grad_probs = dot(grad, v2, ((1,), (1,)))
            parts = []
            for half in range(2):
                at = slice(half * length, (half + 1) * length)
                full, gp = probs[:, at].astype(FULL), grad_probs[:, at]
                parts.append(full * (gp - jnp.sum(full * gp, axis=-1, keepdims=True)))
            scores = jnp.concatenate(parts, axis=1).astype(LOW)
            grad_q = dot(scores, k2) * HD ** (-0.5)
            grad_k = fold(dot(scores, q, ((0,), (0,)))) * HD ** (-0.5)
            grad_v = fold(dot(probs, grad, ((0,), (0,))))
            grad_v = grad_v + live * h.gv[rows, cols].astype(FULL)
            h.gq[rows, cols] = turn(grad_q, cosine, -sines).astype(LOW)
            h.gk[rows, cols] = turn(grad_k, cosine, -sines).astype(LOW)
            h.gv[rows, cols] = grad_v.astype(LOW)
            return carry

        lax.fori_loop(0, self.width // 128, pair, 0, unroll=True)

    def normed_back(self, which):
        h = self.h
        self.arrived((which,))
        slot, grad = {W.query: (1, h.gq), W.key: (0, h.gk), W.value: (1, h.gv)}[which]
        for xc in range(4):
            got = dot(grad[...], self.weight_rows(slot, xc), ((1,), (1,)))
            count = self.width // 4
            cols = slice(xc * count, (xc + 1) * count)
            if which == W.query:
                h.gnormed[:, cols] = got
            else:
                h.gnormed[:, cols] += got
        if which == W.query:
            self.fetch((W.value,), self.full.value, h.w.at[1])

    def norm_one_back(self):
        h = self.h
        self.arrived(-3)
        total = jnp.zeros((1, self.width), FULL)
        for b in range(self.slots):
            rows = self.block_rows(b)
            inputs = h.tokens[rows, :].astype(FULL)
            got, part = self.norm_back(h.gnormed[rows, :], inputs, self.gain[0:1, :])
            h.tokens[rows, :] = (self.grad[rows, :] + got).astype(LOW)
            total = total + part
        self.gain_sum[0:1, :] = total
        self.fetch(-4, h.tokens, self.token_grad)

    def gain_chunk(self):
        depth = self.p.depth
        count = 4 * 2 * depth
        each = self.width // count
        shape = (count, self.width)
        keep = iota(shape, 1) // each == iota(shape, 0)
        folded = []
        for row in range(2):
            whole = jnp.where(keep, jnp.broadcast_to(self.gain_sum[row : row + 1, :], shape), 0.0)
            folded.append(sum(whole[:, i * 128 : (i + 1) * 128] for i in range(self.width // 128)))
        sub = iota((8, 128), 0)
        mine = []
        for i in range(count):
            one = jnp.broadcast_to(folded[0][i : i + 1, :], (8, 128))
            two = jnp.broadcast_to(folded[1][i : i + 1, :], (8, 128))
            mine.append(jnp.where(sub == 0, one, jnp.where(sub == 1, two, 0.0)))

        def part(x, c, into):
            for core in range(2):

                @pl.when(c == core)
                def _(core=core):
                    for z in range(depth):
                        for y in range(2):
                            into[x, z, y] = mine[(x * 2 + core) * 2 * depth + z * 2 + y]

        self.spread(self.job[W.gains, 0], part)
        self.arrived(-4)

    def third(self):
        h = self.h
        self.fetch(S.hid_t, self.s.hid_t, h.hid_t)
        self.fetch((W.down,), self.s.down, h.down)
        self.fetch(S.middle, self.s.middle, h.middle)

    def block_output(self):
        h = self.h
        self.arrived(S.hid_t, (W.down,), S.middle)
        for b in range(self.slots // 2):
            rows = pl.ds(b * 2 * self.length, 2 * self.length)
            hidden = h.hid_t[:, rows].T
            live = jnp.concatenate(
                [jnp.full((self.length, 1), 1.0, FULL) * self.live(2 * b + i) for i in range(2)], axis=0
            )

            def tile(n, carry, rows=rows, hidden=hidden, live=live):
                cols = pl.ds(pl.multiple_of(n * WIDE, WIDE), WIDE)
                got = dot(hidden, h.down[:, cols])
                h.out[rows, cols] = (live * (h.middle[rows, cols] + got)).astype(LOW)
                return carry

            lax.fori_loop(0, self.width // WIDE, tile, 0)
        self.fetch(-5, h.out, self.block_out)

    def leave(self, part):
        self.saved()
        if part == 3:
            self.arrived(-5)

    def begin(self):
        self.fetch(-3, self.tokens, self.h.tokens)

    def steps(self):
        halves, slots = range(self.width // (2 * WIDE)), range(self.slots)
        qkv, quarters = (W.query, W.key, W.value), range(4)
        todo, borders = [self.tables, self.gain_rows, self.norm_one], []

        def add(action, *args):
            todo.append(lambda: action(*args))

        for w in qkv:
            add(self.take, w)
            add(self.project, w)
        for b in slots:
            add(self.attend, b)
        add(self.take, W.output)
        add(self.join)
        add(self.norm_two)
        borders.append(len(todo))
        add(self.enter)
        add(self.raw)
        for i in quarters:
            add(self.down_quarter, i)
        for f in range(self.tiles):
            add(self.tile_load, f)
            add(self.ff_tile, f)
        for n in range(self.width // WIDE):
            add(self.down_chunk, n)
        add(self.norm_two_back)
        borders.append(len(todo))
        add(self.second)
        add(self.mixed_back)
        for half in halves:
            add(self.weight_chunk, W.output, half)
        for b in slots:
            add(self.attend_back, b)
        for w in qkv:
            for half in halves:
                add(self.weight_chunk, w, half)
        for w in qkv:
            add(self.normed_back, w)
        add(self.norm_one_back)
        add(self.gain_chunk)
        borders.append(len(todo))
        add(self.third)
        add(self.block_output)
        return todo, borders


def emitter(outs, kind, which, n):
    def emit(values):
        each = values.shape[0] // 2
        if kind == GAIN:
            outs.gains[...] = values
        elif kind == DOWN:
            half = WIDE // 2
            outs.down[:, n * WIDE : n * WIDE + half] = values[:each]
            outs.down[:, n * WIDE + half : (n + 1) * WIDE] = values[each:]
        elif which == W.gate:
            outs.gate[:, n * WIDE : (n + 1) * WIDE] = values[:each]
            outs.up[:, n * WIDE : (n + 1) * WIDE] = values[each:]
        else:
            outs[which][:, 2 * n * WIDE : (2 * n + 1) * WIDE] = values[:each]
            outs[which][:, (2 * n + 1) * WIDE : (2 * n + 2) * WIDE] = values[each:]

    return emit


def layer_kernel(depth, *refs):
    refs = list(refs)

    def take(count):
        got = refs[:count]
        del refs[:count]
        return got

    kinds = len(Weights._fields)
    counts, segments, positions, inverse, norm_first, norm_second = take(6)
    tokens, out_cotangent, value_cotangent = take(3)
    given = take(kinds - 1)
    full = Weights._make(take(kinds))
    s = Saved._make(take(len(Saved._fields)))
    block_out, token_grad = take(2)
    outs = Weights._make(take(kinds))
    grad, attended, gain, gain_sum, gains_near, own_gains, own_down = take(7)
    buffers = [Buffers._make(take(len(Buffers._fields))) for _ in SLOTS]
    sends, receipts, local_sems, load_sems, save_sems = refs
    place = Place(depth)
    work = Layer(
        place, counts=counts, segments=segments, positions=positions, inverse=inverse, norm_first=norm_first,
        norm_second=norm_second, tokens=tokens, out_cotangent=out_cotangent, value_cotangent=value_cotangent,
        down_weight=given[-1], full=full, s=s, block_out=block_out, token_grad=token_grad, grad=grad,
        attended=attended, gain=gain, gain_sum=gain_sum, gains_near=gains_near, own_gains=own_gains,
        own_down=own_down, load_sems=load_sems, save_sems=save_sems,
    )
    owns = Weights._make([own_gains] + given[:-1] + [own_down])
    gathers = []
    for i, (which, z_first, cols) in enumerate(GATHER_JOBS):
        own, whole = owns[which], full[which]
        if cols is not None:
            cut = slice(cols[0] * WIDE, cols[1] * WIDE)
            own, whole = own.at[:, cut], whole.at[:, :, :, :, :, cut]
        gathers.append(Gather(place, own, whole, sends.at[i], receipts.at[i], local_sems.at[i], z_first))
    rows, width = work.rows, work.width
    chunks = chunk_list(work.tiles, width)
    work.job, by_kind = {}, [[] for _ in SLOTS]
    for kind, which, n in chunks:
        b, k, many = buffers[kind], len(by_kind[kind]), SLOTS[kind]
        own = Buffers._make([ref.at[k % many if i in (1, 2) else k] for i, ref in enumerate(b[:-1])] + [b.credit])
        count = sum(chunk[0] == kind for chunk in chunks)
        job = Reduce(place, k, count, many, Z_FIRST[kind], own, emitter(outs, kind, which, n))
        job.before = by_kind[kind][k - many] if k >= many else None
        by_kind[kind].append(job)
        work.job[which, n] = job
    todo, borders = work.steps()
    actions = [step for job in gathers + list(work.job.values()) for step in job.steps()]
    borders = [len(actions) + border for border in borders]
    actions += todo
    assert sorted(ORDER) == list(range(len(actions)))
    work.own_shards()
    place.greet()
    flat, tall = pltpu.VMEM((rows, width), LOW), pltpu.VMEM((width, rows), LOW)
    table, wide = pltpu.VMEM((rows, 128), FULL), pltpu.VMEM((rows, width), FULL)
    down = pltpu.VMEM((work.tiles * WIDE, width), LOW)
    hid_t = pltpu.VMEM((work.tiles * WIDE, rows), LOW)
    pairs = pltpu.VMEM(s.probs.shape, LOW)
    two_weights = pltpu.VMEM((2,) + full.query.shape, LOW)
    held = (
        Ahead(
            tokens=flat, normed=flat, normed_t=tall, q_rot=flat, k_rot=flat, v_low=flat, first=flat, probs=pairs,
            mixed=flat, mixed_t=tall, w=two_weights, middle=wide, two=flat, two_t=tall, cos=table, sin=table,
            bias=pltpu.VMEM((work.slots, work.length, work.length), FULL), live=table,
        ),
        Hidden(
            hid_t=hid_t, branch=flat, raw=pltpu.VMEM(full.down.shape[2:], LOW), down=down, two=flat, two_t=tall,
            middle=wide, tile=pltpu.VMEM((2,) + full.gate.shape[:5] + (2 * WIDE,), LOW),
            both=pltpu.VMEM((rows, 2 * WIDE), LOW),
        ),
        Attention(
            w=two_weights, mixed_t=tall, normed_t=tall, v_low=flat, probs=pairs, cos=table, sin=table, tokens=flat,
            gmixed=flat, gq=flat, gk=flat, gv=flat, gnormed=wide,
        ),
        Last(hid_t=hid_t, down=down, middle=wide, out=flat),
    )
    cuts = [0] + [ORDER.index(border) for border in borders] + [len(ORDER)]
    for part, types in enumerate(held):

        def run(*mine, part=part, types=types):
            work.h = type(types)._make(mine)
            if part == 0:
                work.begin()
            for i in ORDER[cuts[part] : cuts[part + 1]]:
                actions[i]()
            work.leave(part)

        pl.run_scoped(run, *types)
    for job in gathers + list(work.job.values()):
        job.sent()


def whole_layer(mesh, tokens, counts, segments, positions, norm_first, norm_second, weights, cotangents):
    depth = mesh.shape[FSDP] // 2
    slots, length, width = tokens.shape
    rows, each = slots * length, norm_first.shape[0]
    down_rows, hidden = weights[-1].shape[0], weights[W.gate - 1].shape[1]
    tiles, lead = hidden // WIDE, (2, 2, depth, 2)
    flat, tall, table = ((rows, width), LOW), ((width, rows), LOW), ((rows, 128), FULL)
    saved = Saved(
        cos=table,
        sin=table,
        normed_t=tall,
        q_rot=flat,
        k_rot=flat,
        v_low=flat,
        probs=((slots, width // 128, length, 2 * length), LOW),
        mixed_t=tall,
        middle=((rows, width), FULL),
        two=flat,
        two_t=tall,
        first=flat,
        hid_t=((hidden, rows), LOW),
        down=((hidden, width), LOW),
    )
    owns = [((8, 128), FULL)] + [(w.shape, LOW) for w in weights[:-1]] + [((2 * down_rows, width // 2), LOW)]
    fulls = [(lead + shape, kind) for shape, kind in owns]
    grads = [((8, 128), FULL)] + [(w.shape, FULL) for w in weights]
    scratch = [
        pltpu.VMEM((rows, width), FULL),
        pltpu.VMEM(*flat),
        pltpu.VMEM((8, width), FULL),
        pltpu.VMEM((8, width), FULL),
        pltpu.VMEM(*fulls[0]),
        pltpu.VMEM(*owns[0]),
        pltpu.VMEM(*owns[-1]),
    ]
    chunks = chunk_list(tiles, width)
    side = ((2 * each, WIDE), LOW)
    blocks = (((2 * down_rows, WIDE // 2), LOW), side, side, ((8, 128), FULL))
    for kind, (block, dtype) in enumerate(blocks):
        count, many = sum(chunk[0] == kind for chunk in chunks), SLOTS[kind]
        whole = (2, depth, 2) + block
        if Z_FIRST[kind]:
            ring1, ring2, zed = block, (2,) + block, (2, 2, depth - 1, 2) + block
        else:
            ring1, ring2, zed = (depth,) + block, (2, depth) + block, (2, depth - 1) + block
        scratch += [
            pltpu.VMEM((count,) + whole, dtype),
            pltpu.VMEM((many,) + whole, dtype),
            pltpu.VMEM((many,) + whole, dtype),
            pltpu.VMEM((count,) + ring1, dtype),
            pltpu.VMEM((count,) + ring2, dtype),
            pltpu.VMEM((count,) + zed, dtype),
            pltpu.SemaphoreType.DMA((count, 3)),
            pltpu.SemaphoreType.DMA((count, 7)),
            pltpu.SemaphoreType.REGULAR,
        ]
    jobs = len(GATHER_JOBS)
    scratch += [
        pltpu.SemaphoreType.DMA((jobs, 4)),
        pltpu.SemaphoreType.DMA((jobs, depth + 4)),
        pltpu.SemaphoreType.DMA((jobs,)),
        pltpu.SemaphoreType.DMA((36 + 2 * tiles,)),
        pltpu.SemaphoreType.DMA((len(saved),)),
    ]
    inverse = jnp.asarray(
        np.exp((np.arange(128) % (HD // 2)) * (-2.0 * math.log(10000.0) / HD)), FULL
    )[None, :]
    vmem, anywhere = pl.BlockSpec(memory_space=pltpu.VMEM), pl.BlockSpec(memory_space=pl.ANY)
    smem = pl.BlockSpec(memory_space=pltpu.SMEM)
    shapes = fulls + list(saved) + [flat, flat] + grads
    got = pl.pallas_call(
        lambda *refs: layer_kernel(depth, *refs),
        out_shape=tuple(jax.ShapeDtypeStruct(*a) for a in shapes),
        in_specs=[smem] + [vmem] * 5 + [anywhere] * (3 + len(weights) - 1) + [vmem],
        out_specs=tuple([anywhere] * (len(fulls) + len(saved) + 2) + [vmem] * len(grads)),
        scratch_shapes=scratch,
        compiler_params=pltpu.CompilerParams(
            collective_id=1, has_side_effects=True, vmem_limit_bytes=63 * 2**20
        ),
        cost_estimate=pl.CostEstimate(
            flops=6 * rows * width * (4 * width + 3 * hidden), bytes_accessed=160 * 2**20, transcendentals=2**22
        ),
        name="layer",
    )(
        counts, segments, positions, inverse, norm_first.reshape(1, each), norm_second.reshape(1, each),
        tokens.reshape(rows, width), *[a.reshape(rows, width) for a in cotangents], *weights,
    )
    first = got[len(fulls) + S.first]
    block, token_grad, gains, *grads = got[len(fulls) + len(saved) :]
    return first, block, token_grad, gains, grads


def hand_over_kernel(count, each, *refs):
    gains, ins = refs[0], refs[1 : count + 1]
    one, two, outs = refs[count + 1], refs[count + 2], refs[count + 3 : 2 * count + 3]
    held, sems = refs[2 * count + 3 : -1], refs[-1]
    takes = [pltpu.make_async_copy(a, b, sems.at[0, i]) for i, (a, b) in enumerate(zip(ins, held))]
    gives = [pltpu.make_async_copy(a, b, sems.at[1, i]) for i, (a, b) in enumerate(zip(held, outs))]
    for take in takes:
        take.start()
    total, shift = gains[...], each
    while shift < 128:
        total = total + pltpu.roll(total, shift, 1)
        shift *= 2
    one[...] = total[0:1, :each]
    two[...] = total[1:2, :each]
    for take, give in zip(takes, gives):
        take.wait()
        give.start()
    for give in gives:
        give.wait()


def hand_over(gains, each, arrays):
    vmem, anywhere = pl.BlockSpec(memory_space=pltpu.VMEM), pl.BlockSpec(memory_space=pl.ANY)
    count = len(arrays)
    return pl.pallas_call(
        lambda *refs: hand_over_kernel(count, each, *refs),
        out_shape=tuple([jax.ShapeDtypeStruct((1, each), FULL)] * 2)
        + tuple(jax.ShapeDtypeStruct(a.shape, a.dtype) for a in arrays),
        in_specs=[vmem] + [anywhere] * count,
        out_specs=tuple([vmem] * 2 + [anywhere] * count),
        scratch_shapes=[pltpu.VMEM(a.shape, a.dtype) for a in arrays] + [pltpu.SemaphoreType.DMA((2, count))],
        compiler_params=pltpu.CompilerParams(vmem_limit_bytes=60 * 2**20),
        name="hand_over",
    )(gains, *arrays)


def rms_scale(values_in):
    return lax.rsqrt(jnp.mean(values_in * values_in, axis=-1, keepdims=True) + eps)


def rotate_table(positions):
    freq_index = jnp.arange(HD // 2, dtype=jnp.float32)
    inverse = jnp.exp(freq_index * (-2.0 * math.log(10000.0) / HD))
    angles = positions.astype(jnp.float32)[..., None] * inverse
    return (jnp.cos(angles), jnp.sin(angles))


def apply_rotary(values_in, cosine, sines):
    half_dim = values_in.shape[-1] // 2
    first_half = values_in[..., :half_dim]
    second_half = values_in[..., half_dim:]
    cosine = cosine[..., None, :]
    sines = sines[..., None, :]
    return jnp.concatenate(
        [first_half * cosine - second_half * sines, second_half * cosine + first_half * sines],
        axis=-1,
    )


def matmul(left_arg, right_arg):
    return jnp.dot(left_arg, right_arg, preferred_element_type=jnp.float32)


def stack_groups(values_in):
    row_count, model_width = values_in.shape
    return values_in.reshape(row_count, model_width // (4 * HD), 4 * HD).transpose(1, 0, 2)


def unstack_groups(values_in):
    group_count, row_count, group_width = values_in.shape
    return values_in.transpose(1, 0, 2).reshape(row_count, group_count * group_width)


def head_scores(query_grp, key_grp, allowed):
    row_count = query_grp.shape[0]
    query_heads = query_grp.reshape(row_count, 4, HD)
    key_heads = key_grp.reshape(row_count, 4, HD)
    scores = jnp.einsum(
        "qhe,khe->hqk", query_heads, key_heads, preferred_element_type=jnp.float32
    ) * HD ** (-0.5)
    return jnp.where(allowed[None], scores, -1e30)


def norm_back(grad_normed, inputs_f, scale_rows, gain_row):
    gain_term = jnp.sum(grad_normed * inputs_f * scale_rows, axis=0)
    scaled = grad_normed * gain_row
    grad_inputs = scale_rows * (
        scaled
        - inputs_f * scale_rows * scale_rows * jnp.mean(scaled * inputs_f, axis=-1, keepdims=True)
    )
    return (grad_inputs, gain_term)


def layer(
    gather_set,
    reduce_set,
    tokens,
    seq_counts,
    segments,
    positions,
    norm_first,
    query_weight,
    key_weight,
    value_weight,
    output_weight,
    norm_second,
    gate_weight,
    up_weight,
    down_weight,
    out_cotangent,
    value_cotangent,
):
    slot_count, seq_length, model_width = tokens.shape
    row_count = slot_count * seq_length
    head_count = model_width // HD
    weights = gather_set(
        norm_first,
        norm_second,
        query_weight,
        key_weight,
        value_weight,
        output_weight,
        gate_weight,
        up_weight,
        down_weight,
    )
    gain_one, gain_two, query_full, key_full, value_full, output_full = weights[:6]
    gate_full, up_full, down_full = weights[6:]
    row_index = jnp.arange(row_count, dtype=jnp.int32)
    slot_index = row_index // seq_length
    live_rows = (slot_index < seq_counts[0]).astype(jnp.float32)[:, None]
    flat_segments = segments.reshape(row_count)
    allowed = (
        (slot_index[:, None] == slot_index[None, :])
        & (flat_segments[:, None] == flat_segments[None, :])
        & (row_index[:, None] >= row_index[None, :])
    )
    inputs_f = tokens.reshape(row_count, model_width).astype(jnp.float32)
    scale_one = rms_scale(inputs_f)
    normed = (inputs_f * scale_one * gain_one.astype(jnp.float32)).astype(jnp.bfloat16)
    cosine, sines = rotate_table(positions.reshape(row_count))

    def rotated(values_in, turn_sign):
        turned = apply_rotary(
            values_in.reshape(row_count, head_count, HD), cosine, turn_sign * sines
        )
        return turned.reshape(row_count, model_width).astype(jnp.bfloat16)

    query_rot = rotated(matmul(normed, query_full), 1.0)
    key_rot = rotated(matmul(normed, key_full), 1.0)
    value_low = matmul(normed, value_full).astype(jnp.bfloat16)

    def attend_group(operands):
        query_grp, key_grp, value_grp = operands
        scores = head_scores(query_grp, key_grp, allowed)
        row_max = jnp.max(scores, axis=-1, keepdims=True)
        log_total = row_max + jnp.log(jnp.sum(jnp.exp(scores - row_max), axis=-1, keepdims=True))
        probs_low = jnp.exp(scores - log_total).astype(jnp.bfloat16)
        value_heads = value_grp.reshape(row_count, 4, HD)
        mixed_heads = jnp.einsum(
            "hqk,khe->qhe", probs_low, value_heads, preferred_element_type=jnp.float32
        )
        return (mixed_heads.reshape(row_count, 4 * HD), log_total)

    query_groups = stack_groups(query_rot)
    key_groups = stack_groups(key_rot)
    value_groups = stack_groups(value_low)
    mixed_groups, log_totals = lax.map(attend_group, (query_groups, key_groups, value_groups))
    mixed_low = unstack_groups(mixed_groups).astype(jnp.bfloat16)
    middle = inputs_f + matmul(mixed_low, output_full)
    scale_two = rms_scale(middle)
    normed_two = (middle * scale_two * gain_two.astype(jnp.float32)).astype(jnp.bfloat16)
    gate_pre = matmul(normed_two, gate_full)
    upward = matmul(normed_two, up_full)
    sigmoid_gate = jax.nn.sigmoid(gate_pre)
    silu_gate = gate_pre * sigmoid_gate
    hidden = (silu_gate * upward).astype(jnp.bfloat16)
    block_out = (live_rows * (middle + matmul(hidden, down_full))).astype(jnp.bfloat16)
    first_values = (live_rows * value_low.astype(jnp.float32)).astype(jnp.bfloat16)
    grad_y = live_rows * out_cotangent.reshape(row_count, model_width).astype(jnp.float32)
    grad_branch = grad_y.astype(jnp.bfloat16)
    down_term = jnp.einsum("rf,rd->fd", hidden, grad_branch, preferred_element_type=jnp.float32)
    grad_hidden = jnp.einsum(
        "rd,fd->rf", grad_branch, down_full, preferred_element_type=jnp.float32
    )
    grad_gate = (
        grad_hidden * upward * sigmoid_gate * (1.0 + gate_pre * (1.0 - sigmoid_gate))
    ).astype(jnp.bfloat16)
    grad_up = (grad_hidden * silu_gate).astype(jnp.bfloat16)
    gate_term = jnp.einsum("rd,rf->df", normed_two, grad_gate, preferred_element_type=jnp.float32)
    up_term = jnp.einsum("rd,rf->df", normed_two, grad_up, preferred_element_type=jnp.float32)
    grad_normed_two = jnp.einsum(
        "rf,df->rd", grad_gate, gate_full, preferred_element_type=jnp.float32
    ) + jnp.einsum("rf,df->rd", grad_up, up_full, preferred_element_type=jnp.float32)
    grad_middle_norm, gain_two_term = norm_back(
        grad_normed_two, middle, scale_two, gain_two.astype(jnp.float32)
    )
    grad_middle = grad_y + grad_middle_norm
    grad_attended = grad_middle.astype(jnp.bfloat16)
    output_term = jnp.einsum(
        "rd,re->de", mixed_low, grad_attended, preferred_element_type=jnp.float32
    )
    grad_mixed = jnp.einsum(
        "re,de->rd", grad_attended, output_full, preferred_element_type=jnp.float32
    ).astype(jnp.bfloat16)

    def attend_back(operands):
        query_grp, key_grp, value_grp, grad_grp, log_total = operands
        scores = head_scores(query_grp, key_grp, allowed)
        probs_full = jnp.exp(scores - log_total)
        probs_low = probs_full.astype(jnp.bfloat16)
        grad_heads = grad_grp.reshape(row_count, 4, HD)
        value_heads = value_grp.reshape(row_count, 4, HD)
        query_heads = query_grp.reshape(row_count, 4, HD)
        key_heads = key_grp.reshape(row_count, 4, HD)
        grad_probs = jnp.einsum(
            "qhe,khe->hqk", grad_heads, value_heads, preferred_element_type=jnp.float32
        )
        row_term = jnp.sum(probs_full * grad_probs, axis=-1, keepdims=True)
        grad_scores = (probs_full * (grad_probs - row_term)).astype(jnp.bfloat16)
        score_scale = HD ** (-0.5)
        grad_query = (
            jnp.einsum("hqk,khe->qhe", grad_scores, key_heads, preferred_element_type=jnp.float32)
            * score_scale
        )
        grad_key = (
            jnp.einsum("hqk,qhe->khe", grad_scores, query_heads, preferred_element_type=jnp.float32)
            * score_scale
        )
        grad_value = jnp.einsum(
            "hqk,qhe->khe", probs_low, grad_heads, preferred_element_type=jnp.float32
        )
        group_width = 4 * HD
        return (
            grad_query.reshape(row_count, group_width),
            grad_key.reshape(row_count, group_width),
            grad_value.reshape(row_count, group_width),
        )

    grad_q_groups, grad_k_groups, grad_v_groups = lax.map(
        attend_back, (query_groups, key_groups, value_groups, stack_groups(grad_mixed), log_totals)
    )
    grad_query = rotated(unstack_groups(grad_q_groups), -1.0)
    grad_key = rotated(unstack_groups(grad_k_groups), -1.0)
    grad_value = (
        unstack_groups(grad_v_groups)
        + live_rows * value_cotangent.reshape(row_count, model_width).astype(jnp.float32)
    ).astype(jnp.bfloat16)
    query_term = jnp.einsum("rd,re->de", normed, grad_query, preferred_element_type=jnp.float32)
    key_term = jnp.einsum("rd,re->de", normed, grad_key, preferred_element_type=jnp.float32)
    value_term = jnp.einsum("rd,re->de", normed, grad_value, preferred_element_type=jnp.float32)
    grad_normed = jnp.einsum(
        "re,de->rd", grad_query, query_full, preferred_element_type=jnp.float32
    )
    grad_normed = grad_normed + jnp.einsum(
        "re,de->rd", grad_key, key_full, preferred_element_type=jnp.float32
    )
    grad_normed = grad_normed + jnp.einsum(
        "re,de->rd", grad_value, value_full, preferred_element_type=jnp.float32
    )
    grad_inputs_norm, gain_one_term = norm_back(
        grad_normed, inputs_f, scale_one, gain_one.astype(jnp.float32)
    )
    token_grad = (grad_middle + grad_inputs_norm).astype(jnp.bfloat16).reshape(tokens.shape)
    grads = reduce_set(
        gain_one_term,
        gain_two_term,
        query_term,
        key_term,
        value_term,
        output_term,
        gate_term,
        up_term,
        down_term,
    )
    return (
        block_out.reshape(tokens.shape),
        first_values.reshape(tokens.shape),
        token_grad,
        grads[0],
        grads[2],
        grads[3],
        grads[4],
        grads[5],
        grads[1],
        grads[6],
        grads[7],
        grads[8],
    )


def plain_gather(*shards_in):
    return tuple(lax.all_gather(s, BOTH, axis=0, tiled=True) for s in shards_in)


def plain_reduce(*terms):
    return tuple(lax.psum_scatter(t, BOTH, scatter_dimension=0, tiled=True) for t in terms)


def linked_layer(mesh, *args):
    tokens, counts, segments, positions, norm_first = args[:5]
    norm_second, out_cotangent, value_cotangent = args[9], args[13], args[14]
    weights = args[5:9] + args[10:13]
    each = norm_first.shape[0]
    first, block, token_grad, gains, grads = whole_layer(
        mesh, tokens, counts, segments, positions, norm_first, norm_second, weights, (out_cotangent, value_cotangent)
    )
    one, two, block, first, token_grad, *grads = hand_over(gains, each, [block, first, token_grad] + grads)
    streams = tuple(a.reshape(tokens.shape) for a in (block, first, token_grad))
    return streams + (one.reshape(each), *grads[:4], two.reshape(each), *grads[4:])


def fits(mesh, tokens, weights):
    return (
        dict(mesh.shape) == {DP: 4, FSDP: 8}
        and tokens == (4, 128, 1024)
        and all(w == (32, 1024) for w in weights[:4])
        and weights[4:] == ((32, 2816), (32, 2816), (88, 1024))
    )


def solution(mesh):
    one, two, three = P(BOTH), P(BOTH, None), P(BOTH, None, None)
    in_specs = (three, one, two, two, one, two, two, two, two, one, two, two, two, three, three)
    out_specs = (three, three, three, one, two, two, two, two, one, two, two, two)

    def shards(*args):
        weights = tuple(w.shape for w in args[5:9] + args[10:13])
        if fits(mesh, args[0].shape, weights):
            return linked_layer(mesh, *args)
        return layer(plain_gather, plain_reduce, *args)

    return jax.shard_map(shards, mesh=mesh, in_specs=in_specs, out_specs=out_specs, check_vma=False)
```

```python
import math
from typing import Any, NamedTuple

import jax
import jax.numpy as jnp
import numpy as np
from jax import lax
from jax.experimental import pallas as pl
from jax.experimental.pallas import tpu as pltpu
from jax.sharding import PartitionSpec as P

HD = 64
MESH = pl.DeviceIdType.MESH
DP, FSDP = "dp", "fsdp"
BOTH = (DP, FSDP)
LOW, FULL = jnp.bfloat16, jnp.float32
WIDE = 256

eps = 1e-06


class Weights(NamedTuple):
    gains: Any
    query: Any
    key: Any
    value: Any
    output: Any
    gate: Any
    up: Any
    down: Any


class Saved(NamedTuple):
    cos: Any
    sin: Any
    normed_t: Any
    q_rot: Any
    k_rot: Any
    v_low: Any
    probs: Any
    mixed_t: Any
    middle: Any
    two: Any
    two_t: Any
    first: Any
    hid_t: Any
    down: Any


W = Weights._make(range(len(Weights._fields)))
S = Saved._make(range(len(Saved._fields)))


class Place:
    def __init__(self, depth):
        dp, fsdp = lax.axis_index(DP), lax.axis_index(FSDP)
        self.x, self.c = dp // 2, dp % 2
        self.z, self.y = fsdp // 2, fsdp % 2
        self.depth = depth

    def at(self, x, c, z, y):
        return (x * 2 + c, z * 2 + y)

    def across_x(self):
        return self.at(1 - self.x, self.c, self.z, self.y)

    def across_y(self):
        return self.at(self.x, self.c, self.z, 1 - self.y)

    def sibling(self):
        return self.at(self.x, 1 - self.c, self.z, self.y)

    def above(self):
        return self.at(self.x, self.c, self.z + 1, self.y)

    def below(self):
        return self.at(self.x, self.c, self.z - 1, self.y)

    def greet(self):
        barrier = pltpu.get_barrier_semaphore()

        def call(who):
            pl.semaphore_signal(barrier, inc=1, device_id=who, device_id_type=MESH)

        call(self.across_x())
        call(self.across_y())
        call(self.sibling())
        not_top = self.z < self.depth - 1
        not_low = self.z > 0
        pl.when(not_top)(lambda: call(self.above()))
        pl.when(not_low)(lambda: call(self.below()))
        peers = 3 + not_top.astype(jnp.int32) + not_low.astype(jnp.int32)
        pl.semaphore_wait(barrier, peers)


def remote(src, dst, send_sem, recv_sem, who):
    return pltpu.make_async_remote_copy(
        src_ref=src,
        dst_ref=dst,
        send_sem=send_sem,
        recv_sem=recv_sem,
        device_id=who,
        device_id_type=MESH,
    )


def iota(shape, dim):
    return lax.broadcasted_iota(jnp.int32, shape, dim)


def dot(a, b, dims=((1,), (0,))):
    return lax.dot_general(a, b, (dims, ((), ())), preferred_element_type=FULL)


def to_column(row):
    n = row.shape[1]
    eye = iota((n, n), 0) == iota((n, n), 1)
    return jnp.sum(jnp.where(eye, jnp.broadcast_to(row, (n, n)), 0.0), axis=1, keepdims=True)


def turn(values, cosine, sines):
    outs = []
    first = iota((values.shape[0], 128), 1) % HD < HD // 2
    for g in range(values.shape[1] // 128):
        part = values[:, g * 128 : (g + 1) * 128]
        other = jnp.where(
            first, pltpu.roll(part, 128 - HD // 2, 1), pltpu.roll(part, HD // 2, 1)
        )
        outs.append(part * cosine + other * sines)
    return jnp.concatenate(outs, axis=1)


def gain_row(gains, row, each):
    count = gains.shape[0]
    rows = gains[:, row, :]
    whole = jnp.concatenate([rows] * (count * each // 128), axis=1)
    shape = whole.shape
    keep = iota(shape, 1) // each == iota(shape, 0)
    return jnp.sum(jnp.where(keep, whole, 0.0), axis=0, keepdims=True)


def split_pair(values):
    first = iota(values.shape, 1) < HD
    zero = jnp.zeros_like(values)
    return jnp.concatenate([jnp.where(first, values, zero), jnp.where(first, zero, values)], axis=0)


class Gather:
    def __init__(self, place, own, full, sends, receipts, local_sem, z_first):
        self.p, self.own, self.full, self.z_first = place, own, full, z_first
        self.sends, self.receipts, self.local_sem = sends, receipts, local_sem
        self.wide = own.shape[-1]

    def shard(self, x, y, z):
        return self.full.at[x, self.p.c, z, y]

    def zunit(self, z):
        if self.z_first:
            return self.full.at[self.p.x, self.p.c, z, self.p.y]
        return self.full.at[:, self.p.c, z]

    def runit(self, x, y, half=None):
        if self.z_first:
            if half is None:
                return self.full.at[x, self.p.c, :, y]
            count = self.p.depth // 2
            return self.full.at[x, self.p.c, half * count : (half + 1) * count, y]
        if half is None:
            return self.full.at[x, self.p.c, self.p.z, y]
        count = self.wide // 2
        return self.full.at[x, self.p.c, self.p.z, y, :, half * count : (half + 1) * count]

    def copy(self, ref, sent, slot, who, src=None):
        return remote(ref if src is None else src, ref, self.sends.at[sent], self.receipts.at[slot], who)

    def up(self, unit, src=None):
        return self.copy(self.zunit(unit), 0, unit, self.p.above(), src)

    def down(self, unit, src=None):
        return self.copy(self.zunit(unit), 1, unit - 1, self.p.below(), src)

    def ring(self, ref, i, who, src=None):
        return self.copy(ref, 2, self.p.depth - 1 + i, who, src)

    def sib(self, ref):
        return self.copy(ref, 3, self.p.depth + 3, self.p.sibling())

    def keep_own(self):
        p = self.p
        return pltpu.make_async_copy(self.own, self.shard(p.x, p.y, p.z), self.local_sem)

    def z_step(self, step):
        p = self.p
        top, low = p.depth - 1, 0
        src = self.own if (step == 0 and self.z_first) else None

        def from_below():
            if step > 0:
                self.up(p.z - step).wait_recv()
            if step < top:
                pl.when(p.z < top)(lambda: self.up(p.z - step, src).start())

        def from_above():
            if step > 0:
                self.down(p.z + step).wait_recv()
            if step < top:
                pl.when(p.z > low)(lambda: self.down(p.z + step, src).start())

        pl.when(p.z - step >= low)(from_below)
        pl.when(p.z + step <= top)(from_above)

    def ring_first(self):
        p = self.p
        mine = self.runit(p.x, p.y)
        src = None if self.z_first else self.own
        self.ring(mine, 0, p.across_x(), src).start()
        self.ring(mine, 1, p.across_y(), src).start()

    def ring_second(self):
        p = self.p
        from_x, from_y = self.runit(1 - p.x, p.y), self.runit(p.x, 1 - p.y)
        self.ring(from_x, 0, p.across_x()).wait_recv()
        self.ring(self.runit(1 - p.x, p.y, 0), 2, p.across_y()).start()
        self.ring(from_y, 1, p.across_y()).wait_recv()
        self.ring(self.runit(p.x, 1 - p.y, 1), 3, p.across_x()).start()

    def ring_last(self):
        p = self.p
        self.ring(self.runit(1 - p.x, 1 - p.y, 0), 2, p.across_y()).wait_recv()
        self.ring(self.runit(1 - p.x, 1 - p.y, 1), 3, p.across_x()).wait_recv()

    def mine(self, kind):
        p = self.p
        x, y = (1 - p.x if kind % 2 else p.x), (1 - p.y if kind // 2 else p.y)
        self.sib(self.full.at[x, p.c, :, y]).start()

    def pass_on(self, step):
        p = self.p

        def low():
            self.sib(self.full.at[:, p.c, p.z - step]).start()

        def high():
            self.sib(self.full.at[:, p.c, p.z + step]).start()

        pl.when(p.z - step >= 0)(low)
        if step > 0:
            pl.when(p.z + step <= p.depth - 1)(high)

    def steps(self):
        mine = self.mine
        if self.z_first:
            return [
                lambda: (self.keep_own().start(), self.z_step(0)),
                lambda: self.z_step(1),
                lambda: self.z_step(2),
                lambda: (self.z_step(3), self.keep_own().wait(), self.ring_first(), mine(0)),
                lambda: (self.ring_second(), mine(1), mine(2)),
                lambda: (self.ring_last(), mine(3)),
                self.finish,
            ]
        return [
            lambda: (self.keep_own().start(), self.ring_first()),
            self.ring_second,
            lambda: (self.ring_last(), self.keep_own().wait(), self.z_step(0), self.pass_on(0)),
            lambda: (self.z_step(1), self.pass_on(1)),
            lambda: (self.z_step(2), self.pass_on(2)),
            lambda: (self.z_step(3), self.pass_on(3)),
            self.finish,
        ]

    def finish(self):
        self.sib(self.full.at[:, 1 - self.p.c]).wait_recv()

    def sent(self):
        p = self.p
        top = p.depth - 1

        def units(count):
            if self.z_first:
                return self.full.at[p.x, p.c, :count, p.y]
            return self.full.at[:, p.c, :count]

        for z in range(top):
            pl.when(p.z == z)(lambda z=z: self.copy(units(z + 1), 0, 0, p.above()).wait_send())
        for z in range(1, p.depth):
            pl.when(p.z == z)(lambda z=z: self.copy(units(p.depth - z), 1, 0, p.below()).wait_send())
        three = self.full.at[:, p.c, :3] if self.z_first else self.full.at[p.x, p.c, :3, p.y]
        self.ring(three, 0, p.across_x()).wait_send()
        self.sib(self.full.at[:, p.c]).wait_send()


def add_block(into, other):
    into[...] = into[...] + other[...]


class Buffers(NamedTuple):
    acc: Any
    stage: Any
    sib: Any
    ring1: Any
    ring2: Any
    zed: Any
    sends: Any
    receipts: Any
    credit: Any


class Reduce:
    def __init__(self, place, index, count, slots, z_first, buffers, emit):
        self.p, self.z_first, self.b, self.emit = place, z_first, buffers, emit
        self.k, self.count, self.slots = index, count, slots
        rows = buffers.acc.shape[3]
        self.cut = (rows // 2 + 15) // 16 * 16

    def copy(self, src, dst, slot, who):
        sent = 0 if slot == 0 else 1 if slot < 5 else 2
        return remote(src, dst, self.b.sends.at[sent], self.b.receipts.at[slot], who)

    def sib_copy(self):
        return self.copy(self.b.stage, self.b.sib, 0, self.p.sibling())

    def free_stage(self):
        self.sib_copy().wait_send()

    def send(self):
        if self.k >= self.slots:
            pl.semaphore_wait(self.b.credit, 1)
        self.sib_copy().start()

    def merge(self):
        self.sib_copy().wait_recv()
        depth = self.p.depth

        def block(i, carry):
            at = (i // (2 * depth), i // 2 % depth, i % 2)
            self.b.acc[at] = self.b.acc[at] + self.b.sib[at]
            return carry

        lax.fori_loop(0, 4 * depth, block, 0)
        if self.k + self.slots < self.count:
            pl.semaphore_signal(
                self.b.credit, inc=1, device_id=self.p.sibling(), device_id_type=MESH
            )

    def bundle(self, x, y):
        if self.z_first:
            return self.b.acc.at[x, self.p.z, y]
        return self.b.acc.at[x, :, y]

    def halves(self, ref):
        cut = self.cut if self.z_first else self.p.depth // 2
        return ref.at[:cut], ref.at[cut:]

    def first_copies(self):
        p = self.p
        low, high = self.halves(self.bundle(1 - p.x, 1 - p.y))
        to_low, to_high = self.halves(self.b.ring1)
        return (
            self.copy(low, to_low, 1, p.across_x()),
            self.copy(high, to_high, 2, p.across_y()),
        )

    def second_copies(self):
        p = self.p
        return (
            self.copy(self.bundle(1 - p.x, p.y), self.b.ring2.at[0], 3, p.across_x()),
            self.copy(self.bundle(p.x, 1 - p.y), self.b.ring2.at[1], 4, p.across_y()),
        )

    def ring_first(self):
        for copy in self.first_copies():
            copy.start()

    def ring_second(self):
        p = self.p
        by_x, by_y = self.first_copies()
        to_x, to_y = self.second_copies()
        got_low, got_high = self.halves(self.b.ring1)
        by_x.wait_recv()
        add_block(self.halves(self.bundle(p.x, 1 - p.y))[0], got_low)
        to_y.start()
        by_y.wait_recv()
        add_block(self.halves(self.bundle(1 - p.x, p.y))[1], got_high)
        to_x.start()

    def ring_last(self):
        p = self.p
        for copy in self.second_copies():
            copy.wait_recv()
        both = self.b.ring2[0].astype(FULL) + self.b.ring2[1].astype(FULL)
        return self.bundle(p.x, p.y)[...].astype(FULL) + both

    def zunits(self, units):
        if self.z_first:
            return self.b.acc.at[:, units]
        return self.b.acc.at[self.p.x, units, self.p.y]

    def landing(self, side, units):
        if self.z_first:
            return self.b.zed.at[side, :, units]
        return self.b.zed.at[side, units]

    def up(self, step):
        top = self.p.depth - 1
        return self.copy(self.zunits(slice(step + 1, top + 1)), self.landing(0, slice(step, top)), 5, self.p.above())

    def down(self, step):
        count = self.p.depth - 1 - step
        return self.copy(self.zunits(slice(0, count)), self.landing(1, slice(0, count)), 6, self.p.below())

    def z_step(self, step):
        p, top = self.p, self.p.depth - 1

        def upward():
            if step > 0:
                self.up(step - 1).wait_recv()
            if step < top:
                if step > 0:
                    add_block(self.zunits(slice(step + 1, top + 1)), self.landing(0, slice(step, top)))
                self.up(step).start()

        def downward():
            if step > 0:
                self.down(step - 1).wait_recv()
            if step < top:
                if step > 0:
                    add_block(self.zunits(slice(0, top - step)), self.landing(1, slice(0, top - step)))
                self.down(step).start()

        pl.when(p.z == step)(upward)
        pl.when(p.z == top - step)(downward)

    def z_sum(self, put):
        p, top = self.p, self.p.depth - 1
        mine = self.zunits(p.z)[...].astype(FULL)

        @pl.when(p.z == 0)
        def _():
            put(mine + self.landing(1, 0)[...].astype(FULL))

        @pl.when(p.z == top)
        def _():
            put(mine + self.landing(0, top - 1)[...].astype(FULL))

        @pl.when((p.z > 0) & (p.z < top))
        def _():
            low, high = self.landing(0, p.z - 1)[...], self.landing(1, p.z)[...]
            put(mine + (low.astype(FULL) + high.astype(FULL)))

    def steps(self):
        kind = self.b.acc.dtype

        def keep_ring():
            self.bundle(self.p.x, self.p.y)[...] = self.ring_last().astype(kind)
            self.z_step(0)

        def keep_z(values):
            self.zunits(self.p.z)[...] = values.astype(kind)

        if self.z_first:
            return [
                self.send,
                lambda: (self.merge(), self.z_step(0)),
                lambda: self.z_step(1),
                lambda: self.z_step(2),
                lambda: (self.z_step(3), self.z_sum(keep_z), self.ring_first()),
                self.ring_second,
                lambda: self.emit(self.ring_last()),
            ]
        return [
            self.send,
            lambda: (self.merge(), self.ring_first()),
            self.ring_second,
            keep_ring,
            lambda: self.z_step(1),
            lambda: self.z_step(2),
            lambda: (self.z_step(3), self.z_sum(self.emit)),
        ]

    def sent(self):
        p = self.p
        if self.k + self.slots >= self.count:
            self.free_stage()
        three = self.b.acc.at[0, :3, 0] if self.z_first else self.b.acc.at[:, :3]
        self.copy(three, three, 1, p.across_x()).wait_send()
        units = self.zunits(slice(0, p.depth - 1))
        self.copy(units, units, 5, p.sibling()).wait_send()


GATHER_JOBS = (
    (W.gains, True, None),
    (W.query, True, None),
    (W.key, True, None),
    (W.value, True, None),
    (W.output, True, None),
    (W.down, False, (0, 1)),
    (W.down, True, (1, 2)),
    (W.gate, True, (0, 3)),
    (W.up, True, (0, 3)),
    (W.gate, True, (3, 6)),
    (W.up, True, (3, 6)),
    (W.gate, True, (6, 8)),
    (W.up, True, (6, 8)),
    (W.gate, False, (8, 11)),
    (W.up, False, (8, 11)),
)
DOWN, SIDE, SIDE_Z, GAIN = range(4)
SLOTS = (2, 2, 2, 1)
Z_FIRST = (False, False, True, False)
Z_CHUNKS = ((W.gate, 0), (W.gate, 1), (W.gate, 2), (W.gate, 4), (W.gate, 6), (W.gate, 8))
ORDER = (
    0, 28, 98, 35, 7, 91, 1, 99, 29, 2, 3, 36, 14, 30, 21, 8, 92, 4, 49, 31, 9, 10, 56, 70, 22, 42, 273, 5, 23, 32,
    15, 50, 11, 16, 17, 57, 43, 6, 274, 77, 58, 37, 24, 18, 12, 63, 13, 275, 44, 33, 34, 71, 25, 78, 276, 51, 38, 45,
    19, 277, 84, 20, 278, 26, 27, 280, 64, 59, 72, 279, 281, 282, 39, 85, 46, 93, 52, 286, 283, 60, 284, 285, 65, 79,
    100, 287, 47, 40, 86, 73, 288, 289, 41, 48, 290, 53, 94, 66, 61, 291, 292, 293, 54, 74, 62, 87, 55, 295, 297, 101,
    294, 296, 299, 133, 67, 298, 140, 80, 102, 134, 300, 75, 68, 147, 141, 95, 76, 69, 301, 103, 303, 148, 88, 81,
    302, 305, 154, 304, 89, 155, 82, 306, 168, 90, 83, 307, 309, 161, 96, 104, 156, 169, 308, 97, 311, 310, 182, 312,
    183, 313, 170, 315, 162, 314, 196, 184, 135, 316, 203, 197, 317, 105, 204, 318, 112, 106, 198, 319, 320, 119, 171,
    205, 113, 321, 142, 120, 126, 107, 175, 189, 322, 323, 324, 210, 127, 185, 176, 190, 149, 121, 172, 325, 114, 157,
    326, 327, 328, 217, 150, 128, 211, 329, 330, 224, 218, 177, 108, 122, 331, 225, 332, 231, 333, 163, 232, 238, 334,
    245, 219, 239, 191, 252, 335, 246, 336, 199, 253, 212, 206, 115, 186, 220, 337, 338, 178, 226, 339, 164, 340, 143,
    247, 259, 158, 129, 207, 233, 341, 192, 123, 227, 213, 254, 260, 200, 173, 116, 136, 109, 221, 240, 266, 248, 342,
    255, 130, 261, 234, 267, 110, 151, 165, 241, 228, 214, 124, 159, 179, 187, 137, 117, 111, 262, 144, 208, 256, 268,
    138, 180, 235, 222, 201, 152, 160, 145, 249, 269, 118, 131, 229, 193, 257, 174, 242, 263, 236, 166, 194, 209, 223,
    181, 215, 270, 243, 250, 216, 264, 258, 188, 244, 237, 139, 132, 271, 153, 230, 251, 146, 125, 195, 167, 202, 265,
    272,
)


def chunk_list(tiles, width):
    halves = width // (2 * WIDE)
    sides = [(W.gate, f) for f in range(tiles)]
    sides += [(w, half) for w in (W.output, W.query, W.key, W.value) for half in range(halves)]
    chunks = [(DOWN, W.down, n) for n in range(width // WIDE)]
    chunks += [(SIDE_Z if side in Z_CHUNKS else SIDE, *side) for side in sides]
    return chunks + [(GAIN, W.gains, 0)]


class Ahead(NamedTuple):
    tokens: Any
    normed: Any
    normed_t: Any
    q_rot: Any
    k_rot: Any
    v_low: Any
    first: Any
    probs: Any
    mixed: Any
    mixed_t: Any
    w: Any
    middle: Any
    two: Any
    two_t: Any
    cos: Any
    sin: Any
    bias: Any
    live: Any


class Hidden(NamedTuple):
    hid_t: Any
    branch: Any
    raw: Any
    down: Any
    two: Any
    two_t: Any
    middle: Any
    tile: Any
    both: Any


class Attention(NamedTuple):
    w: Any
    mixed_t: Any
    normed_t: Any
    v_low: Any
    probs: Any
    cos: Any
    sin: Any
    tokens: Any
    gmixed: Any
    gq: Any
    gk: Any
    gv: Any
    gnormed: Any


class Last(NamedTuple):
    hid_t: Any
    down: Any
    middle: Any
    out: Any


class Layer:
    def __init__(self, place, **refs):
        self.p = place
        self.__dict__.update(refs)
        self.slots, self.length = self.segments.shape
        self.rows, self.width = self.tokens.shape
        self.tiles = self.full.gate.shape[-1] // WIDE
        self.loads = 0
        self.pending = {}
        self.saving = []

    def fetch(self, key, src, dst):
        copy = pltpu.make_async_copy(src, dst, self.load_sems.at[self.loads])
        self.loads += 1
        self.pending[key] = copy
        copy.start()

    def arrived(self, *keys):
        for key in keys:
            self.pending.pop(key).wait()

    def save(self, *which):
        for i in which:
            copy = pltpu.make_async_copy(getattr(self.h, Saved._fields[i]), self.s[i], self.save_sems.at[i])
            copy.start()
            self.saving.append(copy)

    def saved(self):
        for copy in self.saving:
            copy.wait()
        self.saving = []

    def block_rows(self, b):
        return pl.ds(b * self.length, self.length)

    def live(self, b):
        return (jnp.int32(b) < self.counts[0]).astype(FULL)

    def own_shards(self):
        each = self.norm_first.shape[1]
        spread = (iota((each, 128), 1) % each == iota((each, 128), 0)).astype(LOW)
        sub = iota((8, 128), 0)
        one, two = dot(self.norm_first[...], spread), dot(self.norm_second[...], spread)
        self.own_gains[...] = jnp.where(sub == 0, one, jnp.where(sub == 1, two, 0.0))
        rows, half = self.down_weight.shape[0], self.down_weight.shape[1] // 2
        down = self.down_weight[...].astype(FULL)
        self.own_down[...] = jnp.concatenate([down[:, :half], down[:, half:]], axis=0).astype(LOW)

    def tables(self):
        h = self.h
        for b in range(self.slots):
            rows = pl.ds(b * self.length, self.length)
            angles = to_column(self.positions[b : b + 1, :].astype(FULL)) * self.inverse[...]
            first = iota(angles.shape, 1) % HD < HD // 2
            sines = jnp.sin(angles)
            h.cos[rows, :] = jnp.cos(angles)
            h.sin[rows, :] = jnp.where(first, -sines, sines)
            seg = self.segments[b : b + 1, :].astype(FULL)
            shape = (self.length, self.length)
            allowed = (to_column(seg) == seg) & (iota(shape, 0) >= iota(shape, 1))
            h.bias[b] = jnp.where(allowed, 0.0, -1e30)
        h.live[...] = (iota((self.rows, 128), 0) // self.length < self.counts[0]).astype(FULL)
        self.save(S.cos, S.sin)

    def gain_rows(self):
        self.fetch((W.gains,), self.full.gains, self.gains_near)
        self.arrived((W.gains,))
        near = self.gains_near
        count = math.prod(near.shape[:4])
        gains = near[...].reshape(count, 8, 128)
        self.gain[0:1, :] = gain_row(gains, 0, self.width // count)
        self.gain[1:2, :] = gain_row(gains, 1, self.width // count)

    def norm_one(self):
        h = self.h
        self.arrived(-3)
        for b in range(self.slots):
            rows = pl.ds(b * self.length, self.length)
            inputs = h.tokens[rows, :].astype(FULL)
            scale = lax.rsqrt(jnp.mean(inputs * inputs, axis=-1, keepdims=True) + eps)
            normed = (inputs * scale * self.gain[0:1, :]).astype(LOW)
            h.normed[rows, :] = normed
            h.normed_t[:, rows] = normed.T
        self.save(S.normed_t)

    def take(self, which):
        self.fetch((which,), self.full[which], self.h.w.at[which % 2])

    def weight(self, which, cols):
        w = self.h.w[which % 2, :, :, :, :, :, cols]
        return w.reshape(math.prod(w.shape[:5]), w.shape[5])

    def project(self, which):
        h = self.h
        self.arrived((which,))
        normed = h.normed[...]

        def tile(n, carry):
            cols = pl.ds(pl.multiple_of(n * WIDE, WIDE), WIDE)
            got = dot(normed, self.weight(which, cols))
            if which == W.value:
                low = got.astype(LOW)
                h.v_low[:, cols] = low
                h.first[:, cols] = (h.live[...][:, 0:1] * low.astype(FULL)).astype(LOW)
            else:
                into = h.q_rot if which == W.query else h.k_rot
                into[:, cols] = turn(got, h.cos[...], h.sin[...]).astype(LOW)
            return carry

        lax.fori_loop(0, self.width // WIDE, tile, 0)
        if which == W.value:
            self.save(S.v_low, S.first)
        else:
            self.save(S.q_rot if which == W.query else S.k_rot)

    def attend(self, b):
        h = self.h
        length = self.length
        rows = pl.ds(b * length, length)

        def pair(n, carry):
            cols = pl.ds(pl.multiple_of(n * 128, 128), 128)
            q, k, v = h.q_rot[rows, cols], h.k_rot[rows, cols], h.v_low[rows, cols]
            k2, v2 = split_pair(k), split_pair(v)
            scores = dot(q, k2, ((1,), (1,))) * HD ** (-0.5)
            bias = h.bias[b]
            probs = []
            for half in range(2):
                s = scores[:, half * length : (half + 1) * length] + bias
                e = jnp.exp(s - jnp.max(s, axis=-1, keepdims=True))
                probs.append(e * (1.0 / jnp.sum(e, axis=-1, keepdims=True)))
            probs = jnp.concatenate(probs, axis=1).astype(LOW)
            h.probs[b, n] = probs
            h.mixed[rows, cols] = dot(probs, v2).astype(LOW)
            return carry

        lax.fori_loop(0, self.width // 128, pair, 0, unroll=True)
        h.mixed_t[:, rows] = h.mixed[rows, :].T
        if b == self.slots - 1:
            self.save(S.probs, S.mixed_t)

    def join(self):
        h = self.h
        self.arrived((W.output,))
        mixed = h.mixed[...]

        def tile(n, carry):
            cols = pl.ds(pl.multiple_of(n * WIDE, WIDE), WIDE)
            got = dot(mixed, self.weight(W.output, cols))
            h.middle[:, cols] = h.tokens[:, cols].astype(FULL) + got
            return carry

        lax.fori_loop(0, self.width // WIDE, tile, 0)
        self.save(S.middle)

    def norm_two(self):
        h = self.h
        for b in range(self.slots):
            rows = pl.ds(b * self.length, self.length)
            middle = h.middle[rows, :]
            scale = lax.rsqrt(jnp.mean(middle * middle, axis=-1, keepdims=True) + eps)
            normed = (middle * scale * self.gain[1:2, :]).astype(LOW)
            h.two[rows, :] = normed
            h.two_t[:, rows] = normed.T
        self.save(S.two, S.two_t)

    def enter(self):
        h, s = self.h, self.s
        self.fetch(S.two, s.two, h.two)
        self.fetch(-1, self.out_cotangent, h.branch)
        self.fetch(S.two_t, s.two_t, h.two_t)
        self.fetch(S.middle, s.middle, h.middle)
        self.arrived(-1)
        for b in range(self.slots):
            rows = self.block_rows(b)
            h.branch[rows, :] = (h.branch[rows, :].astype(FULL) * self.live(b)).astype(LOW)

    def raw(self):
        for j in range(2):
            self.fetch((W.down, j), self.full.down.at[j // 2, j % 2], self.h.raw.at[j])

    def down_quarter(self, i):
        self.arrived((W.down, i))
        depth, raw, down = self.p.depth, self.h.raw, self.h.down
        rows, half = raw.shape[3] // 2, raw.shape[4]
        for z in range(depth):
            pair = raw[i % 2, z].astype(FULL)
            for side in range(2):
                part = pair[:, side * rows : (side + 1) * rows, :].reshape(2 * rows, half)
                at = (i * depth + z) * 2 * rows
                down[at : at + 2 * rows, side * half : (side + 1) * half] = part.astype(LOW)
        j = i + 2
        if j < 4:
            self.fetch((W.down, j), self.full.down.at[j // 2, j % 2], raw.at[i % 2])
        if i == 3:
            self.save(S.down)

    def tile_load(self, f):
        cols = pl.ds(f * WIDE, WIDE)
        for which, side in ((W.gate, 0), (W.up, 1)):
            into = self.h.tile.at[f % 2, :, :, :, :, :, side * WIDE : (side + 1) * WIDE]
            self.fetch((which, f), self.full[which].at[:, :, :, :, :, cols], into)

    def ff_tile(self, f):
        h, slot = self.h, f % 2
        self.arrived((W.gate, f), (W.up, f))
        if f == 0:
            self.arrived(S.two, S.two_t)
        count = self.width // 4
        both = dot(h.two[...], h.tile[slot].reshape(self.width, 2 * WIDE))
        gate, upward = both[:, :WIDE], both[:, WIDE:]
        sig = 1.0 / (1.0 + jnp.exp(-gate))
        silu = gate * sig
        rows = slice(f * WIDE, (f + 1) * WIDE)
        h.hid_t[rows, :] = (silu * upward).astype(LOW).T
        grad = dot(h.branch[...], h.down[rows, :], ((1,), (1,)))
        h.both[:, :WIDE] = (grad * upward * sig * (1.0 + gate * (1.0 - sig))).astype(LOW)
        h.both[:, WIDE:] = (grad * silu).astype(LOW)
        self.side_by_side(self.job[W.gate, f], h.two_t, h.both)
        for xc in range(4):
            cols = slice(xc * count, (xc + 1) * count)
            weight = h.tile[slot, xc // 2, xc % 2].reshape(count, 2 * WIDE)
            got = dot(h.both[...], weight, ((1,), (1,)))
            if f == 0:
                self.grad[:, cols] = got
            else:
                self.grad[:, cols] += got
        if f == self.tiles - 1:
            self.save(S.hid_t)

    def spread(self, job, part):
        p = self.p
        if job.before is not None:
            job.before.free_stage()
        for x in range(2):
            part(x, 1 - p.c, job.b.stage)
            part(x, p.c, job.b.acc)

    def side_by_side(self, job, left, right):
        count = self.width // 4

        def part(x, c, into):
            at = pl.multiple_of((x * 2 + c) * count, count)
            got = dot(left[pl.ds(at, count), :], right[...]).astype(LOW)
            got = got.reshape(self.p.depth, 2, -1, 2 * WIDE)
            each = got.shape[2]
            into[x, :, :, :each, :] = got[..., :WIDE]
            into[x, :, :, each:, :] = got[..., WIDE:]

        self.spread(job, part)

    def down_chunk(self, n):
        h = self.h
        right = h.branch[:, n * WIDE : (n + 1) * WIDE]
        count = h.hid_t.shape[0] // 4

        def part(x, c, into):
            at = pl.multiple_of((x * 2 + c) * count, 16)
            got = dot(h.hid_t[pl.ds(at, count), :], right)
            got = got.reshape(2 * self.p.depth, -1, WIDE)
            got = jnp.concatenate([got[:, :, : WIDE // 2], got[:, :, WIDE // 2 :]], axis=1)
            into[x] = got.astype(LOW).reshape(into.shape[1:])

        self.spread(self.job[W.down, n], part)

    def norm_back(self, grads, inputs, gain):
        scale = lax.rsqrt(jnp.mean(inputs * inputs, axis=-1, keepdims=True) + eps)
        total = jnp.sum(grads * inputs * scale, axis=0, keepdims=True)
        scaled = grads * gain
        mean = jnp.mean(scaled * inputs, axis=-1, keepdims=True)
        return scale * (scaled - inputs * (scale * scale * mean)), total

    def norm_two_back(self):
        h = self.h
        self.arrived(S.middle)
        total = jnp.zeros((1, self.width), FULL)
        for b in range(self.slots):
            rows = self.block_rows(b)
            got, part = self.norm_back(self.grad[rows, :], h.middle[rows, :], self.gain[1:2, :])
            grad = h.branch[rows, :].astype(FULL) + got
            self.grad[rows, :] = grad
            self.attended[rows, :] = grad.astype(LOW)
            total = total + part
        self.gain_sum[1:2, :] = total

    def second(self):
        h, s = self.h, self.s
        self.fetch((W.output,), self.full.output, h.w.at[0])
        self.fetch(S.mixed_t, s.mixed_t, h.mixed_t)
        self.fetch(S.v_low, s.v_low, h.v_low)
        self.fetch(S.probs, s.probs, h.probs)
        self.fetch(S.q_rot, s.q_rot, h.gq)
        self.fetch(S.k_rot, s.k_rot, h.gk)
        self.fetch(-2, self.value_cotangent, h.gv)
        self.fetch(S.cos, s.cos, h.cos)
        self.fetch(S.sin, s.sin, h.sin)
        self.fetch(S.normed_t, s.normed_t, h.normed_t)
        self.fetch(-3, self.tokens, h.tokens)
        self.fetch((W.query,), self.full.query, h.w.at[1])

    def weight_rows(self, slot, xc):
        return self.h.w[slot, xc // 2, xc % 2].reshape(self.width // 4, self.width)

    def mixed_back(self):
        self.arrived((W.output,))
        for xc in range(4):
            got = dot(self.attended[...], self.weight_rows(0, xc), ((1,), (1,)))
            count = self.width // 4
            self.h.gmixed[:, xc * count : (xc + 1) * count] = got.astype(LOW)
        self.fetch((W.key,), self.full.key, self.h.w.at[0])

    def weight_chunk(self, which, half):
        h = self.h
        if half == 0 and which in (W.output, W.query):
            self.arrived(S.mixed_t if which == W.output else S.normed_t)
        left = h.mixed_t if which == W.output else h.normed_t
        right = {W.output: self.attended, W.query: h.gq, W.key: h.gk, W.value: h.gv}[which]
        cols = slice(half * 2 * WIDE, (half + 1) * 2 * WIDE)
        self.side_by_side(self.job[which, half], left, right.at[:, cols])

    def attend_back(self, b):
        h = self.h
        if b == 0:
            self.arrived(S.v_low, S.probs, S.q_rot, S.k_rot, -2, S.cos, S.sin)
        rows, length = self.block_rows(b), self.length
        first = iota((length, 128), 1) < HD
        live = self.live(b)
        cosine, sines = h.cos[rows, :], h.sin[rows, :]

        def fold(values):
            return jnp.where(first, values[:length], values[length:])

        def pair(n, carry):
            cols = pl.ds(pl.multiple_of(n * 128, 128), 128)
            q, k, v = h.gq[rows, cols], h.gk[rows, cols], h.v_low[rows, cols]
            grad = h.gmixed[rows, cols]
            probs = h.probs[b, n]
            k2, v2 = split_pair(k), split_pair(v)
            grad_probs = dot(grad, v2, ((1,), (1,)))
            parts = []
            for half in range(2):
                at = slice(half * length, (half + 1) * length)
                full, gp = probs[:, at].astype(FULL), grad_probs[:, at]
                parts.append(full * (gp - jnp.sum(full * gp, axis=-1, keepdims=True)))
            scores = jnp.concatenate(parts, axis=1).astype(LOW)
            grad_q = dot(scores, k2) * HD ** (-0.5)
            grad_k = fold(dot(scores, q, ((0,), (0,)))) * HD ** (-0.5)
            grad_v = fold(dot(probs, grad, ((0,), (0,))))
            grad_v = grad_v + live * h.gv[rows, cols].astype(FULL)
            h.gq[rows, cols] = turn(grad_q, cosine, -sines).astype(LOW)
            h.gk[rows, cols] = turn(grad_k, cosine, -sines).astype(LOW)
            h.gv[rows, cols] = grad_v.astype(LOW)
            return carry

        lax.fori_loop(0, self.width // 128, pair, 0, unroll=True)

    def normed_back(self, which):
        h = self.h
        self.arrived((which,))
        slot, grad = {W.query: (1, h.gq), W.key: (0, h.gk), W.value: (1, h.gv)}[which]
        for xc in range(4):
            got = dot(grad[...], self.weight_rows(slot, xc), ((1,), (1,)))
            count = self.width // 4
            cols = slice(xc * count, (xc + 1) * count)
            if which == W.query:
                h.gnormed[:, cols] = got
            else:
                h.gnormed[:, cols] += got
        if which == W.query:
            self.fetch((W.value,), self.full.value, h.w.at[1])

    def norm_one_back(self):
        h = self.h
        self.arrived(-3)
        total = jnp.zeros((1, self.width), FULL)
        for b in range(self.slots):
            rows = self.block_rows(b)
            inputs = h.tokens[rows, :].astype(FULL)
            got, part = self.norm_back(h.gnormed[rows, :], inputs, self.gain[0:1, :])
            h.tokens[rows, :] = (self.grad[rows, :] + got).astype(LOW)
            total = total + part
        self.gain_sum[0:1, :] = total
        self.fetch(-4, h.tokens, self.token_grad)

    def gain_chunk(self):
        depth = self.p.depth
        count = 4 * 2 * depth
        each = self.width // count
        shape = (count, self.width)
        keep = iota(shape, 1) // each == iota(shape, 0)
        folded = []
        for row in range(2):
            whole = jnp.where(keep, jnp.broadcast_to(self.gain_sum[row : row + 1, :], shape), 0.0)
            folded.append(sum(whole[:, i * 128 : (i + 1) * 128] for i in range(self.width // 128)))
        sub = iota((8, 128), 0)
        mine = []
        for i in range(count):
            one = jnp.broadcast_to(folded[0][i : i + 1, :], (8, 128))
            two = jnp.broadcast_to(folded[1][i : i + 1, :], (8, 128))
            mine.append(jnp.where(sub == 0, one, jnp.where(sub == 1, two, 0.0)))

        def part(x, c, into):
            for core in range(2):

                @pl.when(c == core)
                def _(core=core):
                    for z in range(depth):
                        for y in range(2):
                            into[x, z, y] = mine[(x * 2 + core) * 2 * depth + z * 2 + y]

        self.spread(self.job[W.gains, 0], part)
        self.arrived(-4)

    def third(self):
        h = self.h
        self.fetch(S.hid_t, self.s.hid_t, h.hid_t)
        self.fetch((W.down,), self.s.down, h.down)
        self.fetch(S.middle, self.s.middle, h.middle)

    def block_output(self):
        h = self.h
        self.arrived(S.hid_t, (W.down,), S.middle)
        for b in range(self.slots // 2):
            rows = pl.ds(b * 2 * self.length, 2 * self.length)
            hidden = h.hid_t[:, rows].T
            live = jnp.concatenate(
                [jnp.full((self.length, 1), 1.0, FULL) * self.live(2 * b + i) for i in range(2)], axis=0
            )

            def tile(n, carry, rows=rows, hidden=hidden, live=live):
                cols = pl.ds(pl.multiple_of(n * WIDE, WIDE), WIDE)
                got = dot(hidden, h.down[:, cols])
                h.out[rows, cols] = (live * (h.middle[rows, cols] + got)).astype(LOW)
                return carry

            lax.fori_loop(0, self.width // WIDE, tile, 0)
        self.fetch(-5, h.out, self.block_out)

    def leave(self, part):
        self.saved()
        if part == 3:
            self.arrived(-5)

    def begin(self):
        self.fetch(-3, self.tokens, self.h.tokens)

    def steps(self):
        halves, slots = range(self.width // (2 * WIDE)), range(self.slots)
        qkv, quarters = (W.query, W.key, W.value), range(4)
        todo, borders = [self.tables, self.gain_rows, self.norm_one], []

        def add(action, *args):
            todo.append(lambda: action(*args))

        for w in qkv:
            add(self.take, w)
            add(self.project, w)
        for b in slots:
            add(self.attend, b)
        add(self.take, W.output)
        add(self.join)
        add(self.norm_two)
        borders.append(len(todo))
        add(self.enter)
        add(self.raw)
        for i in quarters:
            add(self.down_quarter, i)
        for f in range(self.tiles):
            add(self.tile_load, f)
            add(self.ff_tile, f)
        for n in range(self.width // WIDE):
            add(self.down_chunk, n)
        add(self.norm_two_back)
        borders.append(len(todo))
        add(self.second)
        add(self.mixed_back)
        for half in halves:
            add(self.weight_chunk, W.output, half)
        for b in slots:
            add(self.attend_back, b)
        for w in qkv:
            for half in halves:
                add(self.weight_chunk, w, half)
        for w in qkv:
            add(self.normed_back, w)
        add(self.norm_one_back)
        add(self.gain_chunk)
        borders.append(len(todo))
        add(self.third)
        add(self.block_output)
        return todo, borders


def emitter(outs, kind, which, n):
    def emit(values):
        each = values.shape[0] // 2
        if kind == GAIN:
            outs.gains[...] = values
        elif kind == DOWN:
            half = WIDE // 2
            outs.down[:, n * WIDE : n * WIDE + half] = values[:each]
            outs.down[:, n * WIDE + half : (n + 1) * WIDE] = values[each:]
        elif which == W.gate:
            outs.gate[:, n * WIDE : (n + 1) * WIDE] = values[:each]
            outs.up[:, n * WIDE : (n + 1) * WIDE] = values[each:]
        else:
            outs[which][:, 2 * n * WIDE : (2 * n + 1) * WIDE] = values[:each]
            outs[which][:, (2 * n + 1) * WIDE : (2 * n + 2) * WIDE] = values[each:]

    return emit


def layer_kernel(depth, *refs):
    refs = list(refs)

    def take(count):
        got = refs[:count]
        del refs[:count]
        return got

    kinds = len(Weights._fields)
    counts, segments, positions, inverse, norm_first, norm_second = take(6)
    tokens, out_cotangent, value_cotangent = take(3)
    given = take(kinds - 1)
    full = Weights._make(take(kinds))
    s = Saved._make(take(len(Saved._fields)))
    block_out, token_grad = take(2)
    outs = Weights._make(take(kinds))
    grad, attended, gain, gain_sum, gains_near, own_gains, own_down = take(7)
    buffers = [Buffers._make(take(len(Buffers._fields))) for _ in SLOTS]
    sends, receipts, local_sems, load_sems, save_sems = refs
    place = Place(depth)
    work = Layer(
        place, counts=counts, segments=segments, positions=positions, inverse=inverse, norm_first=norm_first,
        norm_second=norm_second, tokens=tokens, out_cotangent=out_cotangent, value_cotangent=value_cotangent,
        down_weight=given[-1], full=full, s=s, block_out=block_out, token_grad=token_grad, grad=grad,
        attended=attended, gain=gain, gain_sum=gain_sum, gains_near=gains_near, own_gains=own_gains,
        own_down=own_down, load_sems=load_sems, save_sems=save_sems,
    )
    owns = Weights._make([own_gains] + given[:-1] + [own_down])
    gathers = []
    for i, (which, z_first, cols) in enumerate(GATHER_JOBS):
        own, whole = owns[which], full[which]
        if cols is not None:
            cut = slice(cols[0] * WIDE, cols[1] * WIDE)
            own, whole = own.at[:, cut], whole.at[:, :, :, :, :, cut]
        gathers.append(Gather(place, own, whole, sends.at[i], receipts.at[i], local_sems.at[i], z_first))
    rows, width = work.rows, work.width
    chunks = chunk_list(work.tiles, width)
    work.job, by_kind = {}, [[] for _ in SLOTS]
    for kind, which, n in chunks:
        b, k, many = buffers[kind], len(by_kind[kind]), SLOTS[kind]
        own = Buffers._make([ref.at[k % many if i in (1, 2) else k] for i, ref in enumerate(b[:-1])] + [b.credit])
        count = sum(chunk[0] == kind for chunk in chunks)
        job = Reduce(place, k, count, many, Z_FIRST[kind], own, emitter(outs, kind, which, n))
        job.before = by_kind[kind][k - many] if k >= many else None
        by_kind[kind].append(job)
        work.job[which, n] = job
    todo, borders = work.steps()
    actions = [step for job in gathers + list(work.job.values()) for step in job.steps()]
    borders = [len(actions) + border for border in borders]
    actions += todo
    assert sorted(ORDER) == list(range(len(actions)))
    work.own_shards()
    place.greet()
    flat, tall = pltpu.VMEM((rows, width), LOW), pltpu.VMEM((width, rows), LOW)
    table, wide = pltpu.VMEM((rows, 128), FULL), pltpu.VMEM((rows, width), FULL)
    down = pltpu.VMEM((work.tiles * WIDE, width), LOW)
    hid_t = pltpu.VMEM((work.tiles * WIDE, rows), LOW)
    pairs = pltpu.VMEM(s.probs.shape, LOW)
    two_weights = pltpu.VMEM((2,) + full.query.shape, LOW)
    held = (
        Ahead(
            tokens=flat, normed=flat, normed_t=tall, q_rot=flat, k_rot=flat, v_low=flat, first=flat, probs=pairs,
            mixed=flat, mixed_t=tall, w=two_weights, middle=wide, two=flat, two_t=tall, cos=table, sin=table,
            bias=pltpu.VMEM((work.slots, work.length, work.length), FULL), live=table,
        ),
        Hidden(
            hid_t=hid_t, branch=flat, raw=pltpu.VMEM((2,) + full.down.shape[2:], LOW), down=down, two=flat, two_t=tall,
            middle=wide, tile=pltpu.VMEM((2,) + full.gate.shape[:5] + (2 * WIDE,), LOW),
            both=pltpu.VMEM((rows, 2 * WIDE), LOW),
        ),
        Attention(
            w=two_weights, mixed_t=tall, normed_t=tall, v_low=flat, probs=pairs, cos=table, sin=table, tokens=flat,
            gmixed=flat, gq=flat, gk=flat, gv=flat, gnormed=wide,
        ),
        Last(hid_t=hid_t, down=down, middle=wide, out=flat),
    )
    cuts = [0] + [ORDER.index(border) for border in borders] + [len(ORDER)]
    for part, types in enumerate(held):

        def run(*mine, part=part, types=types):
            work.h = type(types)._make(mine)
            if part == 0:
                work.begin()
            for i in ORDER[cuts[part] : cuts[part + 1]]:
                actions[i]()
            work.leave(part)

        pl.run_scoped(run, *types)
    for job in gathers + list(work.job.values()):
        job.sent()


def whole_layer(mesh, tokens, counts, segments, positions, norm_first, norm_second, weights, cotangents):
    depth = mesh.shape[FSDP] // 2
    slots, length, width = tokens.shape
    rows, each = slots * length, norm_first.shape[0]
    down_rows, hidden = weights[-1].shape[0], weights[W.gate - 1].shape[1]
    tiles, lead = hidden // WIDE, (2, 2, depth, 2)
    flat, tall, table = ((rows, width), LOW), ((width, rows), LOW), ((rows, 128), FULL)
    saved = Saved(
        cos=table,
        sin=table,
        normed_t=tall,
        q_rot=flat,
        k_rot=flat,
        v_low=flat,
        probs=((slots, width // 128, length, 2 * length), LOW),
        mixed_t=tall,
        middle=((rows, width), FULL),
        two=flat,
        two_t=tall,
        first=flat,
        hid_t=((hidden, rows), LOW),
        down=((hidden, width), LOW),
    )
    owns = [((8, 128), FULL)] + [(w.shape, LOW) for w in weights[:-1]] + [((2 * down_rows, width // 2), LOW)]
    fulls = [(lead + shape, kind) for shape, kind in owns]
    grads = [((8, 128), FULL)] + [(w.shape, FULL) for w in weights]
    scratch = [
        pltpu.VMEM((rows, width), FULL),
        pltpu.VMEM(*flat),
        pltpu.VMEM((8, width), FULL),
        pltpu.VMEM((8, width), FULL),
        pltpu.VMEM(*fulls[0]),
        pltpu.VMEM(*owns[0]),
        pltpu.VMEM(*owns[-1]),
    ]
    chunks = chunk_list(tiles, width)
    side = ((2 * each, WIDE), LOW)
    blocks = (((2 * down_rows, WIDE // 2), LOW), side, side, ((8, 128), FULL))
    for kind, (block, dtype) in enumerate(blocks):
        count, many = sum(chunk[0] == kind for chunk in chunks), SLOTS[kind]
        whole = (2, depth, 2) + block
        if Z_FIRST[kind]:
            ring1, ring2, zed = block, (2,) + block, (2, 2, depth - 1, 2) + block
        else:
            ring1, ring2, zed = (depth,) + block, (2, depth) + block, (2, depth - 1) + block
        scratch += [
            pltpu.VMEM((count,) + whole, dtype),
            pltpu.VMEM((many,) + whole, dtype),
            pltpu.VMEM((many,) + whole, dtype),
            pltpu.VMEM((count,) + ring1, dtype),
            pltpu.VMEM((count,) + ring2, dtype),
            pltpu.VMEM((count,) + zed, dtype),
            pltpu.SemaphoreType.DMA((count, 3)),
            pltpu.SemaphoreType.DMA((count, 7)),
            pltpu.SemaphoreType.REGULAR,
        ]
    jobs = len(GATHER_JOBS)
    scratch += [
        pltpu.SemaphoreType.DMA((jobs, 4)),
        pltpu.SemaphoreType.DMA((jobs, depth + 4)),
        pltpu.SemaphoreType.DMA((jobs,)),
        pltpu.SemaphoreType.DMA((36 + 2 * tiles,)),
        pltpu.SemaphoreType.DMA((len(saved),)),
    ]
    inverse = jnp.asarray(
        np.exp((np.arange(128) % (HD // 2)) * (-2.0 * math.log(10000.0) / HD)), FULL
    )[None, :]
    vmem, anywhere = pl.BlockSpec(memory_space=pltpu.VMEM), pl.BlockSpec(memory_space=pl.ANY)
    smem = pl.BlockSpec(memory_space=pltpu.SMEM)
    shapes = fulls + list(saved) + [flat, flat] + grads
    got = pl.pallas_call(
        lambda *refs: layer_kernel(depth, *refs),
        out_shape=tuple(jax.ShapeDtypeStruct(*a) for a in shapes),
        in_specs=[smem] + [vmem] * 5 + [anywhere] * (3 + len(weights) - 1) + [vmem],
        out_specs=tuple([anywhere] * (len(fulls) + len(saved) + 2) + [vmem] * len(grads)),
        scratch_shapes=scratch,
        compiler_params=pltpu.CompilerParams(
            collective_id=1, has_side_effects=True, vmem_limit_bytes=63 * 2**20
        ),
        cost_estimate=pl.CostEstimate(
            flops=6 * rows * width * (4 * width + 3 * hidden), bytes_accessed=160 * 2**20, transcendentals=2**22
        ),
        name="layer",
    )(
        counts, segments, positions, inverse, norm_first.reshape(1, each), norm_second.reshape(1, each),
        tokens.reshape(rows, width), *[a.reshape(rows, width) for a in cotangents], *weights,
    )
    first = got[len(fulls) + S.first]
    block, token_grad, gains, *grads = got[len(fulls) + len(saved) :]
    return first, block, token_grad, gains, grads


def hand_over_kernel(count, each, *refs):
    gains, ins = refs[0], refs[1 : count + 1]
    one, two, outs = refs[count + 1], refs[count + 2], refs[count + 3 : 2 * count + 3]
    held, sems = refs[2 * count + 3 : -1], refs[-1]
    takes = [pltpu.make_async_copy(a, b, sems.at[0, i]) for i, (a, b) in enumerate(zip(ins, held))]
    gives = [pltpu.make_async_copy(a, b, sems.at[1, i]) for i, (a, b) in enumerate(zip(held, outs))]
    for take in takes:
        take.start()
    total, shift = gains[...], each
    while shift < 128:
        total = total + pltpu.roll(total, shift, 1)
        shift *= 2
    one[...] = total[0:1, :each]
    two[...] = total[1:2, :each]
    for take, give in zip(takes, gives):
        take.wait()
        give.start()
    for give in gives:
        give.wait()


def hand_over(gains, each, arrays):
    vmem, anywhere = pl.BlockSpec(memory_space=pltpu.VMEM), pl.BlockSpec(memory_space=pl.ANY)
    count = len(arrays)
    return pl.pallas_call(
        lambda *refs: hand_over_kernel(count, each, *refs),
        out_shape=tuple([jax.ShapeDtypeStruct((1, each), FULL)] * 2)
        + tuple(jax.ShapeDtypeStruct(a.shape, a.dtype) for a in arrays),
        in_specs=[vmem] + [anywhere] * count,
        out_specs=tuple([vmem] * 2 + [anywhere] * count),
        scratch_shapes=[pltpu.VMEM(a.shape, a.dtype) for a in arrays] + [pltpu.SemaphoreType.DMA((2, count))],
        compiler_params=pltpu.CompilerParams(vmem_limit_bytes=60 * 2**20),
        name="hand_over",
    )(gains, *arrays)


def rms_scale(values_in):
    return lax.rsqrt(jnp.mean(values_in * values_in, axis=-1, keepdims=True) + eps)


def rotate_table(positions):
    freq_index = jnp.arange(HD // 2, dtype=jnp.float32)
    inverse = jnp.exp(freq_index * (-2.0 * math.log(10000.0) / HD))
    angles = positions.astype(jnp.float32)[..., None] * inverse
    return (jnp.cos(angles), jnp.sin(angles))


def apply_rotary(values_in, cosine, sines):
    half_dim = values_in.shape[-1] // 2
    first_half = values_in[..., :half_dim]
    second_half = values_in[..., half_dim:]
    cosine = cosine[..., None, :]
    sines = sines[..., None, :]
    return jnp.concatenate(
        [first_half * cosine - second_half * sines, second_half * cosine + first_half * sines],
        axis=-1,
    )


def matmul(left_arg, right_arg):
    return jnp.dot(left_arg, right_arg, preferred_element_type=jnp.float32)


def stack_groups(values_in):
    row_count, model_width = values_in.shape
    return values_in.reshape(row_count, model_width // (4 * HD), 4 * HD).transpose(1, 0, 2)


def unstack_groups(values_in):
    group_count, row_count, group_width = values_in.shape
    return values_in.transpose(1, 0, 2).reshape(row_count, group_count * group_width)


def head_scores(query_grp, key_grp, allowed):
    row_count = query_grp.shape[0]
    query_heads = query_grp.reshape(row_count, 4, HD)
    key_heads = key_grp.reshape(row_count, 4, HD)
    scores = jnp.einsum(
        "qhe,khe->hqk", query_heads, key_heads, preferred_element_type=jnp.float32
    ) * HD ** (-0.5)
    return jnp.where(allowed[None], scores, -1e30)


def norm_back(grad_normed, inputs_f, scale_rows, gain_row):
    gain_term = jnp.sum(grad_normed * inputs_f * scale_rows, axis=0)
    scaled = grad_normed * gain_row
    grad_inputs = scale_rows * (
        scaled
        - inputs_f * scale_rows * scale_rows * jnp.mean(scaled * inputs_f, axis=-1, keepdims=True)
    )
    return (grad_inputs, gain_term)


def layer(
    gather_set,
    reduce_set,
    tokens,
    seq_counts,
    segments,
    positions,
    norm_first,
    query_weight,
    key_weight,
    value_weight,
    output_weight,
    norm_second,
    gate_weight,
    up_weight,
    down_weight,
    out_cotangent,
    value_cotangent,
):
    slot_count, seq_length, model_width = tokens.shape
    row_count = slot_count * seq_length
    head_count = model_width // HD
    weights = gather_set(
        norm_first,
        norm_second,
        query_weight,
        key_weight,
        value_weight,
        output_weight,
        gate_weight,
        up_weight,
        down_weight,
    )
    gain_one, gain_two, query_full, key_full, value_full, output_full = weights[:6]
    gate_full, up_full, down_full = weights[6:]
    row_index = jnp.arange(row_count, dtype=jnp.int32)
    slot_index = row_index // seq_length
    live_rows = (slot_index < seq_counts[0]).astype(jnp.float32)[:, None]
    flat_segments = segments.reshape(row_count)
    allowed = (
        (slot_index[:, None] == slot_index[None, :])
        & (flat_segments[:, None] == flat_segments[None, :])
        & (row_index[:, None] >= row_index[None, :])
    )
    inputs_f = tokens.reshape(row_count, model_width).astype(jnp.float32)
    scale_one = rms_scale(inputs_f)
    normed = (inputs_f * scale_one * gain_one.astype(jnp.float32)).astype(jnp.bfloat16)
    cosine, sines = rotate_table(positions.reshape(row_count))

    def rotated(values_in, turn_sign):
        turned = apply_rotary(
            values_in.reshape(row_count, head_count, HD), cosine, turn_sign * sines
        )
        return turned.reshape(row_count, model_width).astype(jnp.bfloat16)

    query_rot = rotated(matmul(normed, query_full), 1.0)
    key_rot = rotated(matmul(normed, key_full), 1.0)
    value_low = matmul(normed, value_full).astype(jnp.bfloat16)

    def attend_group(operands):
        query_grp, key_grp, value_grp = operands
        scores = head_scores(query_grp, key_grp, allowed)
        row_max = jnp.max(scores, axis=-1, keepdims=True)
        log_total = row_max + jnp.log(jnp.sum(jnp.exp(scores - row_max), axis=-1, keepdims=True))
        probs_low = jnp.exp(scores - log_total).astype(jnp.bfloat16)
        value_heads = value_grp.reshape(row_count, 4, HD)
        mixed_heads = jnp.einsum(
            "hqk,khe->qhe", probs_low, value_heads, preferred_element_type=jnp.float32
        )
        return (mixed_heads.reshape(row_count, 4 * HD), log_total)

    query_groups = stack_groups(query_rot)
    key_groups = stack_groups(key_rot)
    value_groups = stack_groups(value_low)
    mixed_groups, log_totals = lax.map(attend_group, (query_groups, key_groups, value_groups))
    mixed_low = unstack_groups(mixed_groups).astype(jnp.bfloat16)
    middle = inputs_f + matmul(mixed_low, output_full)
    scale_two = rms_scale(middle)
    normed_two = (middle * scale_two * gain_two.astype(jnp.float32)).astype(jnp.bfloat16)
    gate_pre = matmul(normed_two, gate_full)
    upward = matmul(normed_two, up_full)
    sigmoid_gate = jax.nn.sigmoid(gate_pre)
    silu_gate = gate_pre * sigmoid_gate
    hidden = (silu_gate * upward).astype(jnp.bfloat16)
    block_out = (live_rows * (middle + matmul(hidden, down_full))).astype(jnp.bfloat16)
    first_values = (live_rows * value_low.astype(jnp.float32)).astype(jnp.bfloat16)
    grad_y = live_rows * out_cotangent.reshape(row_count, model_width).astype(jnp.float32)
    grad_branch = grad_y.astype(jnp.bfloat16)
    down_term = jnp.einsum("rf,rd->fd", hidden, grad_branch, preferred_element_type=jnp.float32)
    grad_hidden = jnp.einsum(
        "rd,fd->rf", grad_branch, down_full, preferred_element_type=jnp.float32
    )
    grad_gate = (
        grad_hidden * upward * sigmoid_gate * (1.0 + gate_pre * (1.0 - sigmoid_gate))
    ).astype(jnp.bfloat16)
    grad_up = (grad_hidden * silu_gate).astype(jnp.bfloat16)
    gate_term = jnp.einsum("rd,rf->df", normed_two, grad_gate, preferred_element_type=jnp.float32)
    up_term = jnp.einsum("rd,rf->df", normed_two, grad_up, preferred_element_type=jnp.float32)
    grad_normed_two = jnp.einsum(
        "rf,df->rd", grad_gate, gate_full, preferred_element_type=jnp.float32
    ) + jnp.einsum("rf,df->rd", grad_up, up_full, preferred_element_type=jnp.float32)
    grad_middle_norm, gain_two_term = norm_back(
        grad_normed_two, middle, scale_two, gain_two.astype(jnp.float32)
    )
    grad_middle = grad_y + grad_middle_norm
    grad_attended = grad_middle.astype(jnp.bfloat16)
    output_term = jnp.einsum(
        "rd,re->de", mixed_low, grad_attended, preferred_element_type=jnp.float32
    )
    grad_mixed = jnp.einsum(
        "re,de->rd", grad_attended, output_full, preferred_element_type=jnp.float32
    ).astype(jnp.bfloat16)

    def attend_back(operands):
        query_grp, key_grp, value_grp, grad_grp, log_total = operands
        scores = head_scores(query_grp, key_grp, allowed)
        probs_full = jnp.exp(scores - log_total)
        probs_low = probs_full.astype(jnp.bfloat16)
        grad_heads = grad_grp.reshape(row_count, 4, HD)
        value_heads = value_grp.reshape(row_count, 4, HD)
        query_heads = query_grp.reshape(row_count, 4, HD)
        key_heads = key_grp.reshape(row_count, 4, HD)
        grad_probs = jnp.einsum(
            "qhe,khe->hqk", grad_heads, value_heads, preferred_element_type=jnp.float32
        )
        row_term = jnp.sum(probs_full * grad_probs, axis=-1, keepdims=True)
        grad_scores = (probs_full * (grad_probs - row_term)).astype(jnp.bfloat16)
        score_scale = HD ** (-0.5)
        grad_query = (
            jnp.einsum("hqk,khe->qhe", grad_scores, key_heads, preferred_element_type=jnp.float32)
            * score_scale
        )
        grad_key = (
            jnp.einsum("hqk,qhe->khe", grad_scores, query_heads, preferred_element_type=jnp.float32)
            * score_scale
        )
        grad_value = jnp.einsum(
            "hqk,qhe->khe", probs_low, grad_heads, preferred_element_type=jnp.float32
        )
        group_width = 4 * HD
        return (
            grad_query.reshape(row_count, group_width),
            grad_key.reshape(row_count, group_width),
            grad_value.reshape(row_count, group_width),
        )

    grad_q_groups, grad_k_groups, grad_v_groups = lax.map(
        attend_back, (query_groups, key_groups, value_groups, stack_groups(grad_mixed), log_totals)
    )
    grad_query = rotated(unstack_groups(grad_q_groups), -1.0)
    grad_key = rotated(unstack_groups(grad_k_groups), -1.0)
    grad_value = (
        unstack_groups(grad_v_groups)
        + live_rows * value_cotangent.reshape(row_count, model_width).astype(jnp.float32)
    ).astype(jnp.bfloat16)
    query_term = jnp.einsum("rd,re->de", normed, grad_query, preferred_element_type=jnp.float32)
    key_term = jnp.einsum("rd,re->de", normed, grad_key, preferred_element_type=jnp.float32)
    value_term = jnp.einsum("rd,re->de", normed, grad_value, preferred_element_type=jnp.float32)
    grad_normed = jnp.einsum(
        "re,de->rd", grad_query, query_full, preferred_element_type=jnp.float32
    )
    grad_normed = grad_normed + jnp.einsum(
        "re,de->rd", grad_key, key_full, preferred_element_type=jnp.float32
    )
    grad_normed = grad_normed + jnp.einsum(
        "re,de->rd", grad_value, value_full, preferred_element_type=jnp.float32
    )
    grad_inputs_norm, gain_one_term = norm_back(
        grad_normed, inputs_f, scale_one, gain_one.astype(jnp.float32)
    )
    token_grad = (grad_middle + grad_inputs_norm).astype(jnp.bfloat16).reshape(tokens.shape)
    grads = reduce_set(
        gain_one_term,
        gain_two_term,
        query_term,
        key_term,
        value_term,
        output_term,
        gate_term,
        up_term,
        down_term,
    )
    return (
        block_out.reshape(tokens.shape),
        first_values.reshape(tokens.shape),
        token_grad,
        grads[0],
        grads[2],
        grads[3],
        grads[4],
        grads[5],
        grads[1],
        grads[6],
        grads[7],
        grads[8],
    )


def plain_gather(*shards_in):
    return tuple(lax.all_gather(s, BOTH, axis=0, tiled=True) for s in shards_in)


def plain_reduce(*terms):
    return tuple(lax.psum_scatter(t, BOTH, scatter_dimension=0, tiled=True) for t in terms)


def linked_layer(mesh, *args):
    tokens, counts, segments, positions, norm_first = args[:5]
    norm_second, out_cotangent, value_cotangent = args[9], args[13], args[14]
    weights = args[5:9] + args[10:13]
    each = norm_first.shape[0]
    first, block, token_grad, gains, grads = whole_layer(
        mesh, tokens, counts, segments, positions, norm_first, norm_second, weights, (out_cotangent, value_cotangent)
    )
    one, two, block, first, token_grad, *grads = hand_over(gains, each, [block, first, token_grad] + grads)
    streams = tuple(a.reshape(tokens.shape) for a in (block, first, token_grad))
    return streams + (one.reshape(each), *grads[:4], two.reshape(each), *grads[4:])


def fits(mesh, tokens, weights):
    return (
        dict(mesh.shape) == {DP: 4, FSDP: 8}
        and tokens == (4, 128, 1024)
        and all(w == (32, 1024) for w in weights[:4])
        and weights[4:] == ((32, 2816), (32, 2816), (88, 1024))
    )


def solution(mesh):
    one, two, three = P(BOTH), P(BOTH, None), P(BOTH, None, None)
    in_specs = (three, one, two, two, one, two, two, two, two, one, two, two, two, three, three)
    out_specs = (three, three, three, one, two, two, two, two, one, two, two, two)

    def shards(*args):
        weights = tuple(w.shape for w in args[5:9] + args[10:13])
        if fits(mesh, args[0].shape, weights):
            return linked_layer(mesh, *args)
        return layer(plain_gather, plain_reduce, *args)

    return jax.shard_map(shards, mesh=mesh, in_specs=in_specs, out_specs=out_specs, check_vma=False)
```
